32 devices in a mesh: dp: 16 (over z, x, core), tensor: 2 (over y).
Axes of the slice: x: 2, y: 2, z: 4, core: 2. Of those that a mesh axis runs over, the one named last changes fastest.
Arguments:
- tokens: bfloat16 [8192, 1536], P(('dp', 'tensor')), may hold values from -6 to 6
- lengths: int32 [16, 4], P('dp'), may hold values from 1 to 256, 512 in all within a row
- first_gain: float32 [1536], replicated, may hold values from 0.25 to 1.75
- query_weight: bfloat16 [1536, 1536], P(None, 'tensor'), may hold values from -0.21875 to 0.21875
- key_weight: bfloat16 [1536, 768], P(None, 'tensor'), may hold values from -0.21875 to 0.21875
- value_weight: bfloat16 [1536, 768], P(None, 'tensor'), may hold values from -0.15625 to 0.15625
- output_weight: bfloat16 [1536, 1536], P('tensor'), may hold values from -0.875 to 0.875
- second_gain: float32 [1536], replicated, may hold values from 0.25 to 1.75
- gate_weight: bfloat16 [1536, 4096], P(None, 'tensor'), may hold values from -0.15625 to 0.15625
- up_weight: bfloat16 [1536, 4096], P(None, 'tensor'), may hold values from -0.15625 to 0.15625
- down_weight: bfloat16 [4096, 1536], P('tensor'), may hold values from -0.09375 to 0.09375
- out_cotangent: bfloat16 [8192, 1536], P(('dp', 'tensor')), may hold values from -6 to 6
Outputs:
- layer_out: bfloat16 [8192, 1536], P(('dp', 'tensor'))
- tokens_grad: float32 [8192, 1536], P(('dp', 'tensor'))
- first_gain_grad: float32 [1536], replicated
- query_grad: float32 [1536, 1536], P(None, 'tensor')
- key_grad: float32 [1536, 768], P(None, 'tensor')
- value_grad: float32 [1536, 768], P(None, 'tensor')
- output_grad: float32 [1536, 1536], P('tensor')
- second_gain_grad: float32 [1536], replicated
- gate_grad: float32 [1536, 4096], P(None, 'tensor')
- up_grad: float32 [1536, 4096], P(None, 'tensor')
- down_grad: float32 [4096, 1536], P('tensor')
- rms_values: float32 [3], replicated
The draws below stay inside these ranges and needn't reach their ends.
Inputs may be any that keep to these rules, and one draw needn't show every extreme that they name: Each row holds the lengths of the 4 sequences of one index of dp in packing order, summing to 512, the largest exactly 256.
All inputs are finite; a program needn't handle non-finite values.
Results may differ from the reference program's by a relative error of at most 0.014.
The reference program's roundings to bfloat16 on the way count: a program that leaves them out, or rounds other values in their place, can miss the bound.
Values may be sent and summed in bfloat16 or wider, within the bound.
A program may use at most 320 MiB of HBM per device.

```python
import math
import jax
import jax.numpy as jnp
import numpy as np
from jax import lax

D = 1536
HQ = 16
KVH = 8
HD = 96
FF = 4096
TOK_DEV = 512
NSEG = 4
LONGEST = 256
TOKENS = 8192
N_DP = 16


def steps_of(key, dims, shards, least, high):
    def one(axis_at, shards_of):
        heights = jax.random.uniform(jax.random.fold_in(jax.random.fold_in(key, 6), axis_at), (shards_of,), jnp.float32, least / len(shards), high / len(shards))
        return jnp.repeat(jnp.exp(heights), dims[axis_at] // shards_of).reshape((-1,) + (1,) * (len(dims) - axis_at - 1))

    level = one(*shards[0])
    for cut in shards[1:]:
        level = level * one(*cut)
    return level


def split_up(number_of, total, bound, lean):
    loads = [(1 << 20) // math.isqrt(grade ** lean) + 1 for grade in range(2, number_of + 1)]
    rest, counts = total - bound - (number_of - 1), [1] * (number_of - 1)
    while rest > 0:
        free = [i for i in range(number_of - 1) if counts[i] < bound]
        whole, left = sum([loads[i] for i in free]), rest
        for i in free:
            extra = min(bound - counts[i], max(1, left * loads[i] // whole), rest)
            counts[i] = counts[i] + extra
            rest = rest - extra
    return np.array([bound] + counts)


def ragged_sizes(key, number_of, total, most, skew):
    if number_of == 2:
        one = jax.random.randint(key, (), max(1, total - most), min(most, total - 1) + 1)
        return jnp.stack([one, total - one])
    sizes = jnp.asarray(split_up(number_of, total, most, skew), jnp.int32)
    couples = (number_of - 1) // 2
    donor, taker = sizes[1:1 + 2 * couples:2], sizes[2:2 + 2 * couples:2]
    margin = jnp.minimum(donor - 1, most - taker)
    shifted = jax.random.randint(jax.random.fold_in(key, 1), (couples,), 0, 1 << 20) % (margin + 1)
    sizes = sizes.at[1:1 + 2 * couples:2].set(donor - shifted).at[2:2 + 2 * couples:2].set(taker + shifted)
    return sizes[jax.random.permutation(jax.random.fold_in(key, 2), number_of)]


def gaussian(stream_key, extent, scale, limit, pieces=(), held_as=jnp.bfloat16):
    gain = steps_of(stream_key, extent, pieces, -0.22, 0.18) if pieces else 1.0
    values = jax.random.normal(stream_key, extent, jnp.float32) * scale * gain
    return jnp.minimum(jnp.maximum(values, -limit), limit).astype(held_as)


def setup_inputs(seed: int = 0) -> dict:
    seeds = jax.random.split(jax.random.key(seed), 13)
    return {
        "tokens": gaussian(seeds[0], (TOKENS, D), 1.0, 6.0, ((0, 32),)),
        "lengths": jax.vmap(lambda own: ragged_sizes(own, NSEG, TOK_DEV, LONGEST, 1))(jax.random.split(seeds[1], N_DP)).reshape((N_DP, NSEG)).astype(jnp.int32),
        "first_gain": jnp.clip(1.0 + 0.15 * jax.random.normal(seeds[2], (D,), jnp.float32), 0.25, 1.75),
        "query_weight": gaussian(seeds[3], (D, HQ * HD), (D // 2) ** -0.5, 0.21875, ((1, 2),)),
        "key_weight": gaussian(seeds[4], (D, KVH * HD), (D // 2) ** -0.5, 0.21875, ((1, 2),)),
        "value_weight": gaussian(seeds[5], (D, KVH * HD), D ** -0.5, 0.15625, ((1, 2),)),
        "output_weight": gaussian(seeds[6], (HQ * HD, D), (HD // 2) ** -0.5, 0.875, ((0, 2),)),
        "second_gain": jnp.clip(1.0 + 0.15 * jax.random.normal(seeds[7], (D,), jnp.float32), 0.25, 1.75),
        "gate_weight": gaussian(seeds[8], (D, FF), D ** -0.5, 0.15625, ((1, 2),)),
        "up_weight": gaussian(seeds[9], (D, FF), D ** -0.5, 0.15625, ((1, 2),)),
        "down_weight": gaussian(seeds[10], (FF, D), FF ** -0.5, 0.09375, ((0, 2),)),
        "out_cotangent": gaussian(seeds[11], (TOKENS, D), 1.0, 6.0, ((0, 32),)),
    }


epsilon = 1e-05
rope_base = 10000.0
masked_score = -1e+30

@jax.custom_vjp
def low(v):
    return lax.optimization_barrier(v.astype(jnp.bfloat16)).astype(jnp.float32)

@jax.custom_vjp
def low_back(v):
    return v

def low_keep(v):
    return (low(v), None)

def low_pass(kept, grad):
    return (grad,)

def back_keep(v):
    return (v, None)

def back_low(kept, grad):
    return (low(grad),)
low.defvjp(low_keep, low_pass)
low_back.defvjp(back_keep, back_low)

def exact_product(left_side, right_side):
    return jnp.dot(left_side, right_side, precision=lax.Precision.HIGHEST, preferred_element_type=jnp.float32)

def tables(lens_row, total_rows, half_size):
    seq_ends = jnp.cumsum(lens_row, dtype=jnp.int32)
    starts = seq_ends - lens_row
    places = jnp.arange(total_rows, dtype=jnp.int32)
    segment = lax.optimization_barrier(jnp.sum((places[:, None] >= seq_ends[None, :]).astype(jnp.int32), axis=1, dtype=jnp.int32))
    member = segment[:, None] == jnp.arange(lens_row.shape[0], dtype=jnp.int32)[None, :]
    position = places - lax.optimization_barrier(jnp.sum(jnp.where(member, starts[None, :], 0), axis=1, dtype=jnp.int32))
    inverse = rope_base ** (-2.0 * jnp.arange(half_size, dtype=jnp.float32) / (2 * half_size))
    angles = position.astype(jnp.float32)[:, None] * inverse[None, :]
    return (places, segment, jnp.cos(angles), jnp.sin(angles))

def rotate(values, cosine_table, sine_table):
    total_rows = values.shape[0]
    half_size = cosine_table.shape[1]
    shaped = values.reshape(total_rows, -1, 2 * half_size)
    first_half = shaped[..., :half_size]
    second = shaped[..., half_size:]
    cos_b = cosine_table[:, None, :]
    sin_b = sine_table[:, None, :]
    turned = jnp.concatenate([first_half * cos_b - second * sin_b, second * cos_b + first_half * sin_b], axis=-1)
    return turned.reshape(total_rows, -1)

def block_forward(inputs, weights, places, segment, cosine_table, sine_table):
    first_gain, query_weight, key_weight, value_weight, output_weight, second_gain, gate_weight, up_weight, down_weight = weights
    total_rows = inputs.shape[0]
    normed1 = low(inputs * lax.rsqrt(lax.optimization_barrier(jnp.mean(inputs * inputs, axis=-1, keepdims=True)) + epsilon) * first_gain)
    query_lin = low_back(exact_product(normed1, query_weight))
    key_lin = low_back(exact_product(normed1, key_weight))
    value_lin = low_back(exact_product(normed1, value_weight))
    query = low(rotate(query_lin, cosine_table, sine_table))
    keys = low(rotate(key_lin, cosine_table, sine_table))
    values = low(value_lin)
    groups = HQ // KVH
    query_four = query.reshape(total_rows, KVH, groups, HD)
    key_three = keys.reshape(total_rows, KVH, HD)
    value_three = values.reshape(total_rows, KVH, HD)
    raw = jnp.einsum('qcgd,kcd->cgqk', query_four, key_three, precision=lax.Precision.HIGHEST) * HD ** (-0.5)
    raw = low_back(raw)
    allowed = (segment[:, None] == segment[None, :]) & (places[:, None] >= places[None, :])
    masked = jnp.where(allowed[None, None], raw, masked_score)
    probs_low = low(jax.nn.softmax(masked, axis=-1))
    attended = jnp.einsum('cgqk,kcd->qcgd', probs_low, value_three, precision=lax.Precision.HIGHEST).reshape(total_rows, HQ * HD)
    attended = low(low_back(attended))
    attn_branch = low_back(exact_product(attended, output_weight))
    middle = inputs + attn_branch
    normed2 = low(middle * lax.rsqrt(lax.optimization_barrier(jnp.mean(middle * middle, axis=-1, keepdims=True)) + epsilon) * second_gain)
    gate_value = low_back(exact_product(normed2, gate_weight))
    upward = low_back(exact_product(normed2, up_weight))
    hidden = low(gate_value * jax.nn.sigmoid(gate_value) * upward)
    mlp_branch = low_back(exact_product(hidden, down_weight))
    result = middle + mlp_branch
    squares = jnp.stack([jnp.sum(result * result), jnp.sum(attn_branch * attn_branch), jnp.sum(mlp_branch * mlp_branch)])
    return (result, squares)

def reference(tokens, lengths, first_gain, query_weight, key_weight, value_weight, output_weight, second_gain, gate_weight, up_weight, down_weight, out_cotangent):
    weights = (first_gain.astype(jnp.float32), query_weight.astype(jnp.float32), key_weight.astype(jnp.float32), value_weight.astype(jnp.float32), output_weight.astype(jnp.float32), second_gain.astype(jnp.float32), gate_weight.astype(jnp.float32), up_weight.astype(jnp.float32), down_weight.astype(jnp.float32))
    token_packs = tokens.reshape(N_DP, TOK_DEV, D)
    grad_packs = out_cotangent.reshape(N_DP, TOK_DEV, D)

    def group_step(running, pack):
        pack_tokens, pack_grad, lens_row = pack
        places, segment, cosine_table, sine_table = tables(lens_row, TOK_DEV, HD // 2)

        def run_block(inputs, *weight_list):
            return block_forward(inputs, weight_list, places, segment, cosine_table, sine_table)
        result, pullback, squares = jax.vjp(run_block, pack_tokens.astype(jnp.float32), *weights, has_aux=True)
        grads = pullback(pack_grad.astype(jnp.float32))
        summed = tuple((acc + new for acc, new in zip(running[0], grads[1:])))
        return ((summed, running[1] + squares), (result, grads[0]))
    start_grads = tuple((jnp.zeros(weight.shape, jnp.float32) for weight in weights))
    start_state = (start_grads, jnp.zeros((3,), jnp.float32))
    (weight_grads, squares), (results, input_grads) = lax.scan(group_step, start_state, (token_packs, grad_packs, lengths))
    rms_values = jnp.sqrt(squares / TOKENS)
    return (results.reshape(TOKENS, D).astype(jnp.bfloat16), input_grads.reshape(TOKENS, D), weight_grads[0], weight_grads[1], weight_grads[2], weight_grads[3], weight_grads[4], weight_grads[5], weight_grads[6], weight_grads[7], weight_grads[8], rms_values)
```

```python
import jax
import jax.numpy as jnp
from jax import lax
from jax.sharding import PartitionSpec as P

HD = 96


epsilon = 1e-05
rope_base = 10000.0
masked_score = -1e30
block_limit = 512


def product(left_side, right_side):
    return jnp.dot(left_side, right_side, preferred_element_type=jnp.float32)


def times_rows(left_side, right_side):
    return lax.dot_general(
        left_side, right_side, (((0,), (0,)), ((), ())), preferred_element_type=jnp.float32
    )


def times_cols(left_side, right_side):
    return lax.dot_general(
        left_side, right_side, (((1,), (1,)), ((), ())), preferred_element_type=jnp.float32
    )


def tables(lens_row, total_rows, half_size):
    count = lens_row.shape[0]
    earlier = jnp.arange(count)[:, None] <= jnp.arange(count)[None, :]
    seq_ends = jnp.sum(jnp.where(earlier, lens_row[:, None], 0), axis=0, dtype=jnp.int32)
    starts = seq_ends - lens_row
    places = jnp.arange(total_rows, dtype=jnp.int32)
    segment = jnp.sum(
        (places[:, None] >= seq_ends[None, :]).astype(jnp.int32), axis=1, dtype=jnp.int32
    )
    member = segment[:, None] == jnp.arange(lens_row.shape[0], dtype=jnp.int32)[None, :]
    position = places - jnp.sum(jnp.where(member, starts[None, :], 0), axis=1, dtype=jnp.int32)
    inverse = rope_base ** (-2.0 * jnp.arange(half_size, dtype=jnp.float32) / (2 * half_size))
    angles = position.astype(jnp.float32)[:, None] * inverse[None, :]
    return (places, segment, jnp.cos(angles), jnp.sin(angles))


def rotate(values, cosine_table, sine_table, direction):
    total_rows = values.shape[0]
    half_size = cosine_table.shape[1]
    shaped = values.reshape(total_rows, -1, 2 * half_size)
    first_half = shaped[..., :half_size]
    second = shaped[..., half_size:]
    cos_b = cosine_table[:, None, :]
    sin_b = sine_table[:, None, :] * direction
    turned = jnp.concatenate(
        [first_half * cos_b - second * sin_b, second * cos_b + first_half * sin_b], axis=-1
    )
    return turned.reshape(total_rows, -1)


def norm_rows(values, gain):
    inv_rms = lax.rsqrt(jnp.mean(values * values, axis=-1, keepdims=True) + epsilon)
    return (values * inv_rms * gain, inv_rms)


def norm_back(values, inv_rms, gain, upstream):
    scaled = upstream * gain
    row_inner = jnp.mean(scaled * values, axis=-1, keepdims=True)
    gain_rows = jnp.sum(upstream * values * inv_rms, axis=0)
    return (gain_rows, inv_rms * (scaled - values * inv_rms * inv_rms * row_inner))


def dp_sum(terms):
    low = lax.psum(tuple(term.astype(jnp.bfloat16) for term in terms), "dp")
    return tuple(term.astype(jnp.float32) for term in low)


def low_scatter(partial):
    return lax.psum_scatter(
        partial.astype(jnp.bfloat16), "tensor", scatter_dimension=0, tiled=True
    ).astype(jnp.float32)


def body(
    tokens,
    lengths,
    first_gain,
    query_weight,
    key_weight,
    value_weight,
    output_weight,
    second_gain,
    gate_weight,
    up_weight,
    down_weight,
    out_cotangent,
):
    inputs = tokens.astype(jnp.float32)
    normed1, inv_first = norm_rows(inputs, first_gain)
    normed1 = normed1.astype(jnp.bfloat16)
    full_first = lax.all_gather(normed1, "tensor", axis=0, tiled=True)
    total_rows = full_first.shape[0]
    places, segment, cosine_table, sine_table = tables(lengths[0], total_rows, HD // 2)
    kv_heads = key_weight.shape[1] // HD
    groups = query_weight.shape[1] // key_weight.shape[1]
    query = rotate(product(full_first, query_weight), cosine_table, sine_table, 1.0).astype(
        jnp.bfloat16
    )
    keys = rotate(product(full_first, key_weight), cosine_table, sine_table, 1.0).astype(
        jnp.bfloat16
    )
    values = product(full_first, value_weight).astype(jnp.bfloat16)
    block_rows = min(block_limit, total_rows)
    block_count = total_rows // block_rows
    query_blocks = query.reshape(block_count, block_rows, kv_heads, groups, HD)
    seg_blocks = segment.reshape(block_count, block_rows)
    place_blocks = places.reshape(block_count, block_rows)
    key_three = keys.reshape(total_rows, kv_heads, HD)
    value_three = values.reshape(total_rows, kv_heads, HD)
    factor = HD ** (-0.5)

    def scores(query_block, seg_block, place_block):
        raw = (
            jnp.einsum("qcgd,kcd->cgqk", query_block, key_three, preferred_element_type=jnp.float32)
            * factor
        )
        allowed = (seg_block[:, None] == segment[None, :]) & (
            place_block[:, None] >= places[None, :]
        )
        return (jnp.where(allowed[None, None], raw, masked_score), allowed)

    def forward_block(piece_set):
        query_block, seg_block, place_block = piece_set
        masked, allowed = scores(query_block, seg_block, place_block)
        highest = jnp.max(masked, axis=-1, keepdims=True)
        exponent = jnp.exp(masked - highest)
        denominator = jnp.sum(exponent, axis=-1, keepdims=True)
        weights = exponent / denominator
        output = jnp.einsum(
            "cgqk,kcd->qcgd",
            weights.astype(jnp.bfloat16),
            value_three,
            preferred_element_type=jnp.float32,
        )
        stored = (highest + jnp.log(denominator))[..., 0]
        return (output.reshape(block_rows, -1), stored)

    out_blocks, kept_blocks = lax.map(forward_block, (query_blocks, seg_blocks, place_blocks))
    attended = out_blocks.reshape(total_rows, -1).astype(jnp.bfloat16)
    attn_rows = low_scatter(product(attended, output_weight))
    middle = inputs + attn_rows
    normed2, inv_second = norm_rows(middle, second_gain)
    normed2 = normed2.astype(jnp.bfloat16)
    full_second = lax.all_gather(normed2, "tensor", axis=0, tiled=True)
    gate_value = product(full_second, gate_weight)
    upward = product(full_second, up_weight)
    gate_sig = jax.nn.sigmoid(gate_value)
    hidden = (gate_value * gate_sig * upward).astype(jnp.bfloat16)
    mlp_rows = low_scatter(product(hidden, down_weight))
    layer_out = middle + mlp_rows
    squares = jnp.stack(
        [
            jnp.sum(layer_out * layer_out),
            jnp.sum(attn_rows * attn_rows),
            jnp.sum(mlp_rows * mlp_rows),
        ]
    )
    grad_full = lax.all_gather(out_cotangent, "tensor", axis=0, tiled=True)
    grad_hidden = times_cols(grad_full, down_weight)
    down_g = times_rows(hidden, grad_full)
    gate_slope = gate_sig * (1.0 + gate_value * (1.0 - gate_sig))
    grad_gate = (grad_hidden * upward * gate_slope).astype(jnp.bfloat16)
    grad_up = (grad_hidden * gate_value * gate_sig).astype(jnp.bfloat16)
    gate_g = times_rows(full_second, grad_gate)
    up_g = times_rows(full_second, grad_up)
    gate_g, up_g, down_g = dp_sum((gate_g, up_g, down_g))
    grad_normed2 = low_scatter(
        times_cols(grad_gate, gate_weight) + times_cols(grad_up, up_weight)
    )
    second_rows, grad_mid_norm = norm_back(middle, inv_second, second_gain, grad_normed2)
    grad_middle = out_cotangent.astype(jnp.float32) + grad_mid_norm
    grad_attn_full = lax.all_gather(grad_middle.astype(jnp.bfloat16), "tensor", axis=0, tiled=True)
    output_g = times_rows(attended, grad_attn_full)
    grad_out = times_cols(grad_attn_full, output_weight).astype(jnp.bfloat16)
    grad_blocks = grad_out.reshape(block_count, block_rows, kv_heads, groups, HD)

    def backward_block(running, piece_set):
        key_acc, value_acc = running
        query_block, seg_block, place_block, grad_block, stored = piece_set
        masked, allowed = scores(query_block, seg_block, place_block)
        weights = jnp.where(allowed[None, None], jnp.exp(masked - stored[..., None]), 0.0)
        grad_weights = jnp.einsum(
            "qcgd,kcd->cgqk", grad_block, value_three, preferred_element_type=jnp.float32
        )
        row_inner = jnp.sum(weights * grad_weights, axis=-1, keepdims=True)
        grad_scores = (weights * (grad_weights - row_inner)).astype(jnp.bfloat16)
        grad_query = (
            jnp.einsum("cgqk,kcd->qcgd", grad_scores, key_three, preferred_element_type=jnp.float32)
            * factor
        )
        key_acc = (
            key_acc
            + jnp.einsum(
                "cgqk,qcgd->kcd", grad_scores, query_block, preferred_element_type=jnp.float32
            )
            * factor
        )
        value_acc = value_acc + jnp.einsum(
            "cgqk,qcgd->kcd",
            weights.astype(jnp.bfloat16),
            grad_block,
            preferred_element_type=jnp.float32,
        )
        return ((key_acc, value_acc), grad_query.reshape(block_rows, -1))

    zeros_kv = jnp.zeros((total_rows, kv_heads, HD), jnp.float32)
    (key_rot_grad, value_acc_grad), query_rot_grad = lax.scan(
        backward_block,
        (zeros_kv, zeros_kv),
        (query_blocks, seg_blocks, place_blocks, grad_blocks, kept_blocks),
    )
    query_lin = rotate(
        query_rot_grad.reshape(total_rows, -1), cosine_table, sine_table, -1.0
    ).astype(jnp.bfloat16)
    key_lin = rotate(key_rot_grad.reshape(total_rows, -1), cosine_table, sine_table, -1.0).astype(
        jnp.bfloat16
    )
    value_lin = value_acc_grad.reshape(total_rows, -1).astype(jnp.bfloat16)
    query_g = times_rows(full_first, query_lin)
    key_g = times_rows(full_first, key_lin)
    value_g = times_rows(full_first, value_lin)
    grad_normed1 = low_scatter(
        times_cols(query_lin, query_weight)
        + times_cols(key_lin, key_weight)
        + times_cols(value_lin, value_weight)
    )
    first_rows, grad_in_norm = norm_back(inputs, inv_first, first_gain, grad_normed1)
    tokens_grad = grad_middle + grad_in_norm
    gain_rows = jnp.stack([first_rows, second_rows])
    query_g, key_g, value_g, output_g = dp_sum((query_g, key_g, value_g, output_g))
    gain_rows, squares = lax.psum((gain_rows, squares), ("dp", "tensor"))
    rms_values = jnp.sqrt(squares / (total_rows * lax.axis_size("dp")))
    return (
        layer_out.astype(jnp.bfloat16),
        tokens_grad,
        gain_rows[0],
        query_g,
        key_g,
        value_g,
        output_g,
        gain_rows[1],
        gate_g,
        up_g,
        down_g,
        rms_values,
    )


def solution(mesh):
    in_specs = (
        P(("dp", "tensor"), None),
        P("dp", None),
        P(),
        P(None, "tensor"),
        P(None, "tensor"),
        P(None, "tensor"),
        P("tensor", None),
        P(),
        P(None, "tensor"),
        P(None, "tensor"),
        P("tensor", None),
        P(("dp", "tensor"), None),
    )
    out_specs = (
        P(("dp", "tensor"), None),
        P(("dp", "tensor"), None),
        P(),
        P(None, "tensor"),
        P(None, "tensor"),
        P(None, "tensor"),
        P("tensor", None),
        P(),
        P(None, "tensor"),
        P(None, "tensor"),
        P("tensor", None),
        P(),
    )
    return jax.shard_map(body, mesh=mesh, in_specs=in_specs, out_specs=out_specs, check_vma=False)
```

```python
from functools import partial

import jax
import jax.numpy as jnp
from jax import lax
from jax.experimental import pallas as pl
from jax.experimental.pallas import tpu as pltpu
from jax.sharding import PartitionSpec as P

HD = 96


epsilon = 1e-05
rope_base = 10000.0
masked_score = -1e30
block_limit = 512


def product(left_side, right_side):
    return jnp.dot(left_side, right_side, preferred_element_type=jnp.float32)


def times_rows(left_side, right_side):
    return lax.dot_general(
        left_side, right_side, (((0,), (0,)), ((), ())), preferred_element_type=jnp.float32
    )


def times_cols(left_side, right_side):
    return lax.dot_general(
        left_side, right_side, (((1,), (1,)), ((), ())), preferred_element_type=jnp.float32
    )


def tables(lens_row, total_rows, half_size):
    count = lens_row.shape[0]
    earlier = jnp.arange(count)[:, None] <= jnp.arange(count)[None, :]
    seq_ends = jnp.sum(jnp.where(earlier, lens_row[:, None], 0), axis=0, dtype=jnp.int32)
    starts = seq_ends - lens_row
    places = jnp.arange(total_rows, dtype=jnp.int32)
    segment = jnp.sum(
        (places[:, None] >= seq_ends[None, :]).astype(jnp.int32), axis=1, dtype=jnp.int32
    )
    member = segment[:, None] == jnp.arange(lens_row.shape[0], dtype=jnp.int32)[None, :]
    position = places - jnp.sum(jnp.where(member, starts[None, :], 0), axis=1, dtype=jnp.int32)
    inverse = rope_base ** (-2.0 * jnp.arange(half_size, dtype=jnp.float32) / (2 * half_size))
    angles = position.astype(jnp.float32)[:, None] * inverse[None, :]
    return (places, segment, jnp.cos(angles), jnp.sin(angles))


def rotate(values, cosine_table, sine_table, direction):
    total_rows = values.shape[0]
    half_size = cosine_table.shape[1]
    shaped = values.reshape(total_rows, -1, 2 * half_size)
    first_half = shaped[..., :half_size]
    second = shaped[..., half_size:]
    cos_b = cosine_table[:, None, :]
    sin_b = sine_table[:, None, :] * direction
    turned = jnp.concatenate(
        [first_half * cos_b - second * sin_b, second * cos_b + first_half * sin_b], axis=-1
    )
    return turned.reshape(total_rows, -1)


def norm_rows(values, gain):
    inv_rms = lax.rsqrt(jnp.mean(values * values, axis=-1, keepdims=True) + epsilon)
    return (values * inv_rms * gain, inv_rms)


def norm_back(values, inv_rms, gain, upstream):
    scaled = upstream * gain
    row_inner = jnp.mean(scaled * values, axis=-1, keepdims=True)
    gain_rows = jnp.sum(upstream * values * inv_rms, axis=0)
    return (gain_rows, inv_rms * (scaled - values * inv_rms * inv_rms * row_inner))


ORDER = (
    0, 1, 5, 10, 11, 2, 6, 4, 11, 7, 3, 9, 14, 11, 8, 13, 10, 11, 11, 13, 13, 14, 11, 10, 13, 13,
    11, 10, 13, 12, 13, 14, 18, 10, 14, 11, 13, 12, 14, 10, 11, 12, 13, 18, 19, 10, 14, 11, 11, 17,
    12, 18, 16, 13, 13, 10, 10, 16, 19, 14, 18, 12, 19, 15, 14, 14, 17, 18, 16, 10, 17, 19, 19, 12,
    16, 17, 17, 15, 12, 14, 16, 19, 17, 19, 12, 12, 17, 15, 18, 16, 19, 15, 15, 17, 18, 12, 16, 15,
    19, 17, 18, 18, 15, 16, 16, 19, 19, 17, 17, 15, 18, 15, 16, 15, 15,
)


MESH = pl.DeviceIdType.MESH
LINE = 4
UNITS = (
    (2048, 1536, 640, 384, 256),
    (1536, 2048, 512, 256, 256),
    (1536, 2048, 384, 384, 256),
    (768, 1536, 256, 128, 128),
    (1536, 1536, 512, 256, 256),
)
COPIES = 16
TILE_BASE = 2 * len(UNITS) * COPIES
TILES = tuple(rows // 2 // tile for rows, _, _, _, tile in UNITS)
SMALL_BASE = TILE_BASE + sum(TILES)
SMALL_STEPS = 5
N_SEMS = SMALL_BASE + SMALL_STEPS


def rows_at(start, size):
    return pl.ds(pl.multiple_of(start, 16), size)


class Place:
    def __init__(self):
        dp = lax.axis_index("dp")
        self.dp = dp
        self.y = lax.axis_index("tensor")
        self.core = lax.rem(dp, 2)
        self.x = lax.rem(dp // 2, 2)
        self.z = dp // 4

    def at(self, z, x, core, y):
        return ((z * 2 + x) * 2 + core, y)

    def other_core(self):
        return self.at(self.z, self.x, 1 - self.core, self.y)

    def other_x(self):
        return self.at(self.z, 1 - self.x, self.core, self.y)

    def other_y(self):
        return self.at(self.z, self.x, self.core, 1 - self.y)

    def up(self):
        return self.at(self.z + 1, self.x, self.core, self.y)

    def down(self):
        return self.at(self.z - 1, self.x, self.core, self.y)

    def pair_z(self):
        return self.at(self.z + 1 - 2 * lax.rem(self.z, 2), self.x, self.core, self.y)

    def far_z(self):
        return self.at(lax.rem(self.z + 2, LINE), self.x, self.core, self.y)


class Mover:
    def __init__(self, send_sems, recv_sems):
        self.send_sems = send_sems
        self.recv_sems = recv_sems
        self.left = []

    def copy(self, source, target, index, device):
        return pltpu.make_async_remote_copy(
            src_ref=source,
            dst_ref=target,
            send_sem=self.send_sems.at[index],
            recv_sem=self.recv_sems.at[index],
            device_id=device,
            device_id_type=MESH,
        )

    def start(self, source, target, index, device, when=None):
        copy = self.copy(source, target, index, device)
        guarded(when, copy.start)
        self.left.append((when, copy.wait_send))

    def arrived(self, target, index, device):
        self.copy(target, target, index, device).wait_recv()


def guarded(when, action):
    if when is None:
        action()
    else:
        pl.when(when)(action)


def add_rows(target, target_row, source, source_row, size):
    step = 16

    def one(i, _):
        here = rows_at(target_row + i * step, step)
        there = rows_at(source_row + i * step, step)
        total = target[here, :].astype(jnp.float32) + source[there, :].astype(jnp.float32)
        target[here, :] = total.astype(target.dtype)
        return 0

    lax.fori_loop(0, size // step, one, 0)


class Block:
    def __init__(self, place, mover, held, across, along, result, base, start, size, half_rows, x_first):
        self.p = place
        self.m = mover
        self.held = held
        self.across = across
        self.along = along
        self.result = result
        self.base = base
        self.start = start
        self.size = size
        self.half_rows = half_rows
        self.x_first = x_first
        self.chunk = size // 8 if x_first else size // 4
        self.origin = start + place.x * (size // 2) if x_first else start

    def part(self, chunk):
        return self.held.at[rows_at(self.origin + chunk * self.chunk, self.chunk)]

    def final(self, row, size):
        return self.result.at[rows_at(self.p.core * self.half_rows + row, size)]

    def final_part(self, chunk):
        return self.final(self.origin + chunk * self.chunk, self.chunk)

    def keep(self, row, size):
        index = self.base // COPIES
        copy = pltpu.make_async_copy(
            self.held.at[rows_at(row, size)], self.final(row, size), self.m.keep_sems.at[index]
        )
        copy.start()
        self.kept = copy

    def events(self):
        line = [self.line_start, lambda: self.line_add(0), lambda: self.line_add(1), lambda: self.line_add(2)]
        spread = [lambda: self.spread(1), lambda: self.spread(2), lambda: self.spread(3)]
        if self.x_first:
            return [self.x_send, self.x_add] + line[1:] + spread + [self.x_return, self.x_done]
        return line + [self.pair_send, self.pair_add, self.pair_done] + spread + [self.z_done]

    def line_start(self):
        p = self.p
        for step in range(3):
            self.m.start(self.part(3 - step), self.along.at[step], self.base + step, p.up(), p.z == 0)
            self.m.start(self.part(step), self.along.at[3 + step], self.base + 3 + step, p.down(), p.z == LINE - 1)

    def line_add(self, step):
        p = self.p
        rising = jnp.minimum(p.z + 2 - step, 3)
        falling = jnp.maximum(p.z - 2 + step, 0)
        goes_up = (p.z >= 1) & (p.z <= step + 1)
        goes_down = (p.z <= 2) & (p.z >= 2 - step)

        def take_rising():
            self.m.arrived(self.along.at[step], self.base + step, p.down())
            add_rows(self.held, self.origin + rising * self.chunk, self.along.at[step], 0, self.chunk)

        def take_falling():
            self.m.arrived(self.along.at[3 + step], self.base + 3 + step, p.up())
            add_rows(self.held, self.origin + falling * self.chunk, self.along.at[3 + step], 0, self.chunk)

        pl.when(goes_up)(take_rising)
        if step < 2:
            self.m.start(self.part(rising), self.along.at[step + 1], self.base + step + 1, p.up(), goes_up)
        pl.when(goes_down)(take_falling)
        if step < 2:
            self.m.start(self.part(falling), self.along.at[4 + step], self.base + 4 + step, p.down(), goes_down)
        elif self.x_first:
            self.keep(self.origin + p.z * self.chunk, self.chunk)
            self.own_spread(self.part(p.z))

    def own_spread(self, source):
        p = self.p
        target = self.final_part(p.z)
        self.m.start(source, target, self.base + 6, p.up(), p.z < 3)
        self.m.start(source, target, self.base + 9, p.down(), p.z > 0)

    def spread(self, distance):
        p = self.p
        below = self.final_part(jnp.maximum(p.z - distance, 0))
        above = self.final_part(jnp.minimum(p.z + distance, 3))

        pl.when(p.z >= distance)(lambda: self.m.arrived(below, self.base + 5 + distance, p.down()))
        if distance < 3:
            self.m.start(below, below, self.base + 6 + distance, p.up(), (p.z >= distance) & (p.z < 3))
        pl.when(p.z <= 3 - distance)(lambda: self.m.arrived(above, self.base + 8 + distance, p.up()))
        if distance < 3:
            self.m.start(above, above, self.base + 9 + distance, p.down(), (p.z <= 3 - distance) & (p.z > 0))

    def x_part(self, which):
        half = self.size // 2
        return self.held.at[rows_at(self.start + which * half, half)]

    def x_send(self):
        self.m.start(self.x_part(1 - self.p.x), self.across, self.base + 12, self.p.other_x())

    def x_add(self):
        self.m.arrived(self.across, self.base + 12, self.p.other_x())
        add_rows(self.held, self.origin, self.across, 0, self.size // 2)
        self.line_start()

    def x_final(self, which):
        half = self.size // 2
        return self.final(self.start + which * half, half)

    def x_return(self):
        p = self.p
        self.kept.wait()
        mine = self.x_final(p.x)
        self.m.start(mine, mine, self.base + 13, p.other_x())
        self.give(p.x * (self.size // 2), self.size // 2, 14)

    def x_done(self):
        p = self.p
        self.m.arrived(self.x_final(1 - p.x), self.base + 13, p.other_x())
        self.give((1 - p.x) * (self.size // 2), self.size // 2, 15)

    def pair_row(self, which):
        return self.start + self.p.z * self.chunk + which * (self.chunk // 2)

    def pair_send(self):
        half = self.chunk // 2
        source = self.held.at[rows_at(self.pair_row(1 - self.p.x), half)]
        self.m.start(source, self.across, self.base + 12, self.p.other_x())

    def pair_add(self):
        p = self.p
        half = self.chunk // 2
        self.m.arrived(self.across, self.base + 12, p.other_x())
        row = self.pair_row(p.x)
        add_rows(self.held, row, self.across, 0, half)
        self.keep(row, half)
        self.m.start(self.held.at[rows_at(row, half)], self.final(row, half), self.base + 13, p.other_x())

    def pair_done(self):
        p = self.p
        half = self.chunk // 2
        self.m.arrived(self.final(self.pair_row(1 - p.x), half), self.base + 13, p.other_x())
        self.kept.wait()
        self.own_spread(self.final_part(p.z))

    def z_done(self):
        self.give(0, self.size, 14)

    def give(self, offset, size, slot):
        p = self.p
        source = self.final(self.start + offset, size)
        self.m.start(source, source, self.base + slot, p.other_core())
        other = self.result.at[rows_at((1 - p.core) * self.half_rows + self.start + offset, size)]
        self.m.left.append((None, lambda: self.m.arrived(other, self.base + slot, p.other_core())))


def product_tile(left, right, first, tile, width, part):
    columns = pl.ds(pl.multiple_of(first, 128), tile)
    return lax.dot_general(
        left[:, columns], right[:, part * width : (part + 1) * width],
        (((0,), (0,)), ((), ())), preferred_element_type=jnp.float32,
    )


class Unit:
    def __init__(self, index, place, mover, left, right, held, staged, stage_sems):
        self.index = index
        self.rows, self.columns, _, _, self.tile = UNITS[index]
        self.p, self.m = place, mover
        self.left, self.right, self.held = left, right, held
        self.staged, self.stage_sems = staged, stage_sems
        self.base = TILE_BASE + sum(TILES[:index])
        self.width = 512

    def tile_copy(self, i, slot):
        tile = self.tile
        return pltpu.make_async_remote_copy(
            src_ref=self.staged.at[slot, pl.ds(0, tile), pl.ds(0, self.columns)],
            dst_ref=self.held.at[rows_at(i * tile, tile)],
            send_sem=self.stage_sems.at[slot],
            recv_sem=self.m.recv_sems.at[self.base + i],
            device_id=self.p.other_core(),
            device_id_type=MESH,
        )

    def send(self):
        half, tile = self.rows // 2, self.tile

        def one(i, _):
            slot = lax.rem(i, 2)
            pl.when(i >= 2)(lambda: self.tile_copy(i, slot).wait_send())
            first = (1 - self.p.core) * half + i * tile
            for part in range(self.columns // self.width):
                got = product_tile(self.left, self.right, first, tile, self.width, part)
                self.staged[slot, pl.ds(0, tile), part * self.width : (part + 1) * self.width] = got.astype(
                    jnp.bfloat16
                )
            self.tile_copy(i, slot).start()
            return 0

        lax.fori_loop(0, half // tile, one, 0)
        for slot in range(min(2, half // tile)):
            self.tile_copy(0, slot).wait_send()

    def own(self):
        half, tile = self.rows // 2, self.tile

        def one(i, _):
            self.tile_copy(i, 0).wait_recv()
            first = self.p.core * half + i * tile
            here = rows_at(i * tile, tile)
            for part in range(self.columns // self.width):
                got = product_tile(self.left, self.right, first, tile, self.width, part)
                cut = slice(part * self.width, (part + 1) * self.width)
                total = got + self.held[here, cut].astype(jnp.float32)
                self.held[here, cut] = total.astype(jnp.bfloat16)
            return 0

        lax.fori_loop(0, half // tile, one, 0)


def sum_small(place, mover, total, slots, step):
    device = (place.other_core, place.other_x, place.other_y, place.pair_z, place.far_z)[step]()
    index = SMALL_BASE + step
    copy = mover.copy(total.at[step], slots.at[step], index, device)
    copy.start()
    copy.wait()
    total[step + 1] = total[step] + slots[step]


def grads_kernel(
    hid, g, h2, d_gate, d_up, o, d_attn, h1, d_qkv, small,
    down_out, gate_out, up_out, o_out, qkv_out, small_out,
    held0, held1, held2, held3, held4, staged,
    ax0, az0, ax1, az1, ax2, az2, ax3, az3, ax4, az4,
    lx0, lz0, lx1, lz1, lx2, lz2, lx3, lz3, lx4, lz4,
    totals, slots, stage_sems, send_sems, recv_sems, keep_sems,
):
    place = Place()
    mover = Mover(send_sems, recv_sems)
    mover.keep_sems = keep_sems
    enter(place)
    held = (held0, held1, held2, held3, held4)
    across = (ax0, az0, ax1, az1, ax2, az2, ax3, az3, ax4, az4)
    along = (lx0, lz0, lx1, lz1, lx2, lz2, lx3, lz3, lx4, lz4)
    lefts = (hid, h2, h2, o, h1)
    rights = (g, d_gate, d_up, d_attn, d_qkv)
    results = (down_out, gate_out, up_out, o_out, qkv_out)
    units = [
        Unit(i, place, mover, lefts[i], rights[i], held[i], staged, stage_sems) for i in range(len(UNITS))
    ]
    steps = []
    for i, (rows, columns, x_rows, z_rows, _) in enumerate(UNITS):
        for j in range(2):
            b = 2 * i + j
            block = Block(
                place, mover, held[i], across[b], along[b], results[i], b * COPIES,
                0 if j == 0 else x_rows, x_rows if j == 0 else z_rows, rows // 2, j == 0,
            )
            steps.append(block.events())
    totals[0] = small[...]
    small_at = 0
    for count, item in enumerate(ORDER):
        if item < 5:
            units[item].send()
        elif item < 10:
            units[item - 5].own()
        else:
            steps[item - 10].pop(0)()
        if count % 8 == 7 and small_at < SMALL_STEPS:
            sum_small(place, mover, totals, slots, small_at)
            small_at += 1
    small_out[...] = totals[SMALL_STEPS]
    for when, wait in mover.left:
        guarded(when, wait)


def enter(place):
    barrier = pltpu.get_barrier_semaphore()

    def greet(device):
        pl.semaphore_signal(barrier, inc=1, device_id=device, device_id_type=MESH)

    for device in (place.other_core(), place.other_x(), place.other_y(), place.pair_z(), place.far_z()):
        greet(device)
    middle = (place.z == 1) | (place.z == 2)
    pl.when(middle)(lambda: greet(place.at(3 - place.z, place.x, place.core, place.y)))
    pl.semaphore_wait(barrier, 5 + jnp.where(middle, 1, 0))


def weight_grads(hid, g, h2, d_gate, d_up, o, d_attn, h1, d_qkv, small):
    vmem = pl.BlockSpec(memory_space=pltpu.VMEM)
    hbm = pl.BlockSpec(memory_space=pl.ANY)
    low = jnp.bfloat16
    held = [pltpu.VMEM((rows // 2, columns), low) for rows, columns, *_ in UNITS]
    across, along = [], []
    for _, columns, x_rows, z_rows, _ in UNITS:
        across += [pltpu.VMEM((x_rows // 2, columns), low), pltpu.VMEM((z_rows // 8, columns), low)]
        along += [pltpu.VMEM((6, x_rows // 8, columns), low), pltpu.VMEM((6, z_rows // 4, columns), low)]
    flops = sum(2 * 512 * rows * columns for rows, columns, *_ in UNITS)
    return pl.pallas_call(
        grads_kernel,
        out_shape=[jax.ShapeDtypeStruct((rows, columns), low) for rows, columns, *_ in UNITS]
        + [jax.ShapeDtypeStruct(small.shape, jnp.float32)],
        in_specs=[vmem] * 10,
        out_specs=[hbm] * 5 + [vmem],
        scratch_shapes=held
        + [pltpu.VMEM((2, 256, 2048), low)]
        + across
        + along
        + [
            pltpu.VMEM((SMALL_STEPS + 1,) + small.shape, jnp.float32),
            pltpu.VMEM((SMALL_STEPS,) + small.shape, jnp.float32),
            pltpu.SemaphoreType.DMA((2,)),
            pltpu.SemaphoreType.DMA((N_SEMS,)),
            pltpu.SemaphoreType.DMA((N_SEMS,)),
            pltpu.SemaphoreType.DMA((2 * len(UNITS),)),
        ],
        compiler_params=pltpu.CompilerParams(
            collective_id=0, has_side_effects=True, vmem_limit_bytes=60 << 20
        ),
        cost_estimate=pl.CostEstimate(flops=flops, bytes_accessed=80 << 20, transcendentals=0),
        name="weight_grads",
    )(hid, g, h2, d_gate, d_up, o, d_attn, h1, d_qkv, small)


def dp_sum(terms):
    low = lax.psum(tuple(term.astype(jnp.bfloat16) for term in terms), "dp")
    return tuple(term.astype(jnp.float32) for term in low)


def low_scatter(partial):
    return lax.psum_scatter(
        partial.astype(jnp.bfloat16), "tensor", scatter_dimension=0, tiled=True
    ).astype(jnp.float32)


def body(
    fused,
    tokens,
    lengths,
    first_gain,
    query_weight,
    key_weight,
    value_weight,
    output_weight,
    second_gain,
    gate_weight,
    up_weight,
    down_weight,
    out_cotangent,
):
    inputs = tokens.astype(jnp.float32)
    normed1, inv_first = norm_rows(inputs, first_gain)
    normed1 = normed1.astype(jnp.bfloat16)
    full_first = lax.all_gather(normed1, "tensor", axis=0, tiled=True)
    total_rows = full_first.shape[0]
    places, segment, cosine_table, sine_table = tables(lengths[0], total_rows, HD // 2)
    kv_heads = key_weight.shape[1] // HD
    groups = query_weight.shape[1] // key_weight.shape[1]
    query = rotate(product(full_first, query_weight), cosine_table, sine_table, 1.0).astype(
        jnp.bfloat16
    )
    keys = rotate(product(full_first, key_weight), cosine_table, sine_table, 1.0).astype(
        jnp.bfloat16
    )
    values = product(full_first, value_weight).astype(jnp.bfloat16)
    block_rows = min(block_limit, total_rows)
    block_count = total_rows // block_rows
    query_blocks = query.reshape(block_count, block_rows, kv_heads, groups, HD)
    seg_blocks = segment.reshape(block_count, block_rows)
    place_blocks = places.reshape(block_count, block_rows)
    key_three = keys.reshape(total_rows, kv_heads, HD)
    value_three = values.reshape(total_rows, kv_heads, HD)
    factor = HD ** (-0.5)

    def scores(query_block, seg_block, place_block):
        raw = (
            jnp.einsum("qcgd,kcd->cgqk", query_block, key_three, preferred_element_type=jnp.float32)
            * factor
        )
        allowed = (seg_block[:, None] == segment[None, :]) & (
            place_block[:, None] >= places[None, :]
        )
        return (jnp.where(allowed[None, None], raw, masked_score), allowed)

    def forward_block(piece_set):
        query_block, seg_block, place_block = piece_set
        masked, allowed = scores(query_block, seg_block, place_block)
        highest = jnp.max(masked, axis=-1, keepdims=True)
        exponent = jnp.exp(masked - highest)
        denominator = jnp.sum(exponent, axis=-1, keepdims=True)
        weights = exponent / denominator
        output = jnp.einsum(
            "cgqk,kcd->qcgd",
            weights.astype(jnp.bfloat16),
            value_three,
            preferred_element_type=jnp.float32,
        )
        stored = (highest + jnp.log(denominator))[..., 0]
        return (output.reshape(block_rows, -1), stored)

    out_blocks, kept_blocks = lax.map(forward_block, (query_blocks, seg_blocks, place_blocks))
    attended = out_blocks.reshape(total_rows, -1).astype(jnp.bfloat16)
    attn_rows = low_scatter(product(attended, output_weight))
    middle = inputs + attn_rows
    normed2, inv_second = norm_rows(middle, second_gain)
    normed2 = normed2.astype(jnp.bfloat16)
    full_second = lax.all_gather(normed2, "tensor", axis=0, tiled=True)
    gate_value = product(full_second, gate_weight)
    upward = product(full_second, up_weight)
    gate_sig = jax.nn.sigmoid(gate_value)
    hidden = (gate_value * gate_sig * upward).astype(jnp.bfloat16)
    mlp_rows = low_scatter(product(hidden, down_weight))
    layer_out = middle + mlp_rows
    squares = jnp.stack(
        [
            jnp.sum(layer_out * layer_out),
            jnp.sum(attn_rows * attn_rows),
            jnp.sum(mlp_rows * mlp_rows),
        ]
    )
    grad_full = lax.all_gather(out_cotangent, "tensor", axis=0, tiled=True)
    grad_hidden = times_cols(grad_full, down_weight)
    down_g = times_rows(hidden, grad_full)
    gate_slope = gate_sig * (1.0 + gate_value * (1.0 - gate_sig))
    grad_gate = (grad_hidden * upward * gate_slope).astype(jnp.bfloat16)
    grad_up = (grad_hidden * gate_value * gate_sig).astype(jnp.bfloat16)
    gate_g = times_rows(full_second, grad_gate)
    up_g = times_rows(full_second, grad_up)
    if not fused:
        gate_g, up_g, down_g = dp_sum((gate_g, up_g, down_g))
    grad_normed2 = low_scatter(
        times_cols(grad_gate, gate_weight) + times_cols(grad_up, up_weight)
    )
    second_rows, grad_mid_norm = norm_back(middle, inv_second, second_gain, grad_normed2)
    grad_middle = out_cotangent.astype(jnp.float32) + grad_mid_norm
    grad_attn_full = lax.all_gather(grad_middle.astype(jnp.bfloat16), "tensor", axis=0, tiled=True)
    output_g = times_rows(attended, grad_attn_full)
    grad_out = times_cols(grad_attn_full, output_weight).astype(jnp.bfloat16)
    grad_blocks = grad_out.reshape(block_count, block_rows, kv_heads, groups, HD)

    def backward_block(running, piece_set):
        key_acc, value_acc = running
        query_block, seg_block, place_block, grad_block, stored = piece_set
        masked, allowed = scores(query_block, seg_block, place_block)
        weights = jnp.where(allowed[None, None], jnp.exp(masked - stored[..., None]), 0.0)
        grad_weights = jnp.einsum(
            "qcgd,kcd->cgqk", grad_block, value_three, preferred_element_type=jnp.float32
        )
        row_inner = jnp.sum(weights * grad_weights, axis=-1, keepdims=True)
        grad_scores = (weights * (grad_weights - row_inner)).astype(jnp.bfloat16)
        grad_query = (
            jnp.einsum("cgqk,kcd->qcgd", grad_scores, key_three, preferred_element_type=jnp.float32)
            * factor
        )
        key_acc = (
            key_acc
            + jnp.einsum(
                "cgqk,qcgd->kcd", grad_scores, query_block, preferred_element_type=jnp.float32
            )
            * factor
        )
        value_acc = value_acc + jnp.einsum(
            "cgqk,qcgd->kcd",
            weights.astype(jnp.bfloat16),
            grad_block,
            preferred_element_type=jnp.float32,
        )
        return ((key_acc, value_acc), grad_query.reshape(block_rows, -1))

    zeros_kv = jnp.zeros((total_rows, kv_heads, HD), jnp.float32)
    (key_rot_grad, value_acc_grad), query_rot_grad = lax.scan(
        backward_block,
        (zeros_kv, zeros_kv),
        (query_blocks, seg_blocks, place_blocks, grad_blocks, kept_blocks),
    )
    query_lin = rotate(
        query_rot_grad.reshape(total_rows, -1), cosine_table, sine_table, -1.0
    ).astype(jnp.bfloat16)
    key_lin = rotate(key_rot_grad.reshape(total_rows, -1), cosine_table, sine_table, -1.0).astype(
        jnp.bfloat16
    )
    value_lin = value_acc_grad.reshape(total_rows, -1).astype(jnp.bfloat16)
    query_g = times_rows(full_first, query_lin)
    key_g = times_rows(full_first, key_lin)
    value_g = times_rows(full_first, value_lin)
    grad_normed1 = low_scatter(
        times_cols(query_lin, query_weight)
        + times_cols(key_lin, key_weight)
        + times_cols(value_lin, value_weight)
    )
    first_rows, grad_in_norm = norm_back(inputs, inv_first, first_gain, grad_normed1)
    tokens_grad = grad_middle + grad_in_norm
    gain_rows = jnp.stack([first_rows, second_rows])
    if fused:
        small = jnp.concatenate(
            [gain_rows, jnp.pad(squares, (0, gain_rows.shape[1] - 3))[None]], axis=0
        )
        small = jnp.pad(small, ((0, 5), (0, 0)))
        *sums, small = weight_grads(
            hidden, grad_full, full_second, grad_gate, grad_up, attended, grad_attn_full, full_first,
            jnp.concatenate([query_lin, key_lin, value_lin], axis=1), small,
        )
        down_g, gate_g, up_g, output_g, qkv_g = (part.astype(jnp.float32) for part in sums)
        q_cols, k_cols = query_lin.shape[1], key_lin.shape[1]
        query_g = qkv_g[:, :q_cols]
        key_g = qkv_g[:, q_cols : q_cols + k_cols]
        value_g = qkv_g[:, q_cols + k_cols :]
        gain_rows, squares = small[:2], small[2, :3]
    else:
        query_g, key_g, value_g, output_g = dp_sum((query_g, key_g, value_g, output_g))
        gain_rows, squares = lax.psum((gain_rows, squares), ("dp", "tensor"))
    rms_values = jnp.sqrt(squares / (total_rows * lax.axis_size("dp")))
    return (
        layer_out.astype(jnp.bfloat16),
        tokens_grad,
        gain_rows[0],
        query_g,
        key_g,
        value_g,
        output_g,
        gain_rows[1],
        gate_g,
        up_g,
        down_g,
        rms_values,
    )


def solution(mesh):
    in_specs = (
        P(("dp", "tensor"), None),
        P("dp", None),
        P(),
        P(None, "tensor"),
        P(None, "tensor"),
        P(None, "tensor"),
        P("tensor", None),
        P(),
        P(None, "tensor"),
        P(None, "tensor"),
        P("tensor", None),
        P(("dp", "tensor"), None),
    )
    out_specs = (
        P(("dp", "tensor"), None),
        P(("dp", "tensor"), None),
        P(),
        P(None, "tensor"),
        P(None, "tensor"),
        P(None, "tensor"),
        P("tensor", None),
        P(),
        P(None, "tensor"),
        P(None, "tensor"),
        P("tensor", None),
        P(),
    )
    fused = dict(mesh.shape) == {"dp": 16, "tensor": 2}
    return jax.shard_map(partial(body, fused), mesh=mesh, in_specs=in_specs, out_specs=out_specs, check_vma=False)
```

```python
from functools import partial

import jax
import jax.numpy as jnp
from jax import lax
from jax.experimental import pallas as pl
from jax.experimental.pallas import tpu as pltpu
from jax.sharding import PartitionSpec as P

HD = 96


epsilon = 1e-05
rope_base = 10000.0
masked_score = -1e30
block_limit = 512


def product(left_side, right_side):
    return jnp.dot(left_side, right_side, preferred_element_type=jnp.float32)


def times_rows(left_side, right_side):
    return lax.dot_general(
        left_side, right_side, (((0,), (0,)), ((), ())), preferred_element_type=jnp.float32
    )


def times_cols(left_side, right_side):
    return lax.dot_general(
        left_side, right_side, (((1,), (1,)), ((), ())), preferred_element_type=jnp.float32
    )


def tables(lens_row, total_rows, half_size):
    count = lens_row.shape[0]
    earlier = jnp.arange(count)[:, None] <= jnp.arange(count)[None, :]
    seq_ends = jnp.sum(jnp.where(earlier, lens_row[:, None], 0), axis=0, dtype=jnp.int32)
    starts = seq_ends - lens_row
    places = jnp.arange(total_rows, dtype=jnp.int32)
    segment = jnp.sum(
        (places[:, None] >= seq_ends[None, :]).astype(jnp.int32), axis=1, dtype=jnp.int32
    )
    member = segment[:, None] == jnp.arange(lens_row.shape[0], dtype=jnp.int32)[None, :]
    firsts = jnp.sum(jnp.where(member, starts[None, :], 0), axis=1, dtype=jnp.int32)
    position = places - firsts
    inverse = rope_base ** (-2.0 * jnp.arange(half_size, dtype=jnp.float32) / (2 * half_size))
    angles = position.astype(jnp.float32)[:, None] * inverse[None, :]
    return (places, segment, jnp.cos(angles), jnp.sin(angles), firsts)


def rotate(values, cosine_table, sine_table, direction):
    total_rows = values.shape[0]
    half_size = cosine_table.shape[1]
    shaped = values.reshape(total_rows, -1, 2 * half_size)
    first_half = shaped[..., :half_size]
    second = shaped[..., half_size:]
    cos_b = cosine_table[:, None, :]
    sin_b = sine_table[:, None, :] * direction
    turned = jnp.concatenate(
        [first_half * cos_b - second * sin_b, second * cos_b + first_half * sin_b], axis=-1
    )
    return turned.reshape(total_rows, -1)


def norm_rows(values, gain):
    inv_rms = lax.rsqrt(jnp.mean(values * values, axis=-1, keepdims=True) + epsilon)
    return (values * inv_rms * gain, inv_rms)


def norm_back(values, inv_rms, gain, upstream):
    scaled = upstream * gain
    row_inner = jnp.mean(scaled * values, axis=-1, keepdims=True)
    gain_rows = jnp.sum(upstream * values * inv_rms, axis=0)
    return (gain_rows, inv_rms * (scaled - values * inv_rms * inv_rms * row_inner))


ORDER = (
    20, 0, 1, 5, 10, 11, 2, 6, 7, 11, 21, 11, 10, 13, 11, 11, 10, 12, 11, 22, 3, 10, 23, 8, 10, 13,
    24, 25, 11, 13, 12, 10, 26, 27, 11, 28, 4, 13, 13, 12, 9, 10, 13, 15, 11, 13, 16, 10, 10, 12,
    29, 11, 11, 15, 16, 14, 12, 30, 15, 31, 32, 10, 13, 16, 33, 34, 35, 15, 15, 12, 13, 16, 18, 14,
    12, 15, 14, 13, 13, 16, 14, 12, 12, 16, 14, 18, 16, 15, 14, 19, 16, 16, 18, 14, 17, 18, 14, 14,
    12, 15, 18, 19, 16, 15, 17, 19, 17, 18, 15, 15, 14, 19, 19, 17, 17, 19, 17, 18, 19, 17, 18, 18,
    19, 17, 19, 17, 19, 19, 18, 17, 17,
)


MESH = pl.DeviceIdType.MESH
LINE = 4
UNITS = (
    (2048, 1536, 640, 384, 256),
    (1536, 2048, 512, 256, 256),
    (1536, 2048, 384, 384, 256),
    (768, 1536, 256, 128, 128),
    (1536, 1536, 512, 256, 256),
)
COPIES = 16
TILE_BASE = 2 * len(UNITS) * COPIES
TILES = tuple(rows // 2 // tile for rows, _, _, _, tile in UNITS)
SMALL_BASE = TILE_BASE + sum(TILES)
SMALL_STEPS = 5
Y_BASE = SMALL_BASE + SMALL_STEPS
N_SEMS = Y_BASE + 4


def rows_at(start, size):
    return pl.ds(pl.multiple_of(start, 16), size)


class Place:
    def __init__(self):
        dp = lax.axis_index("dp")
        self.dp = dp
        self.y = lax.axis_index("tensor")
        self.core = lax.rem(dp, 2)
        self.x = lax.rem(dp // 2, 2)
        self.z = dp // 4

    def at(self, z, x, core, y):
        return ((z * 2 + x) * 2 + core, y)

    def other_core(self):
        return self.at(self.z, self.x, 1 - self.core, self.y)

    def other_x(self):
        return self.at(self.z, 1 - self.x, self.core, self.y)

    def other_y(self):
        return self.at(self.z, self.x, self.core, 1 - self.y)

    def up(self):
        return self.at(self.z + 1, self.x, self.core, self.y)

    def down(self):
        return self.at(self.z - 1, self.x, self.core, self.y)

    def pair_z(self):
        return self.at(self.z + 1 - 2 * lax.rem(self.z, 2), self.x, self.core, self.y)

    def far_z(self):
        return self.at(lax.rem(self.z + 2, LINE), self.x, self.core, self.y)


class Mover:
    def __init__(self, send_sems, recv_sems):
        self.send_sems = send_sems
        self.recv_sems = recv_sems
        self.left = []

    def copy(self, source, target, index, device):
        return pltpu.make_async_remote_copy(
            src_ref=source,
            dst_ref=target,
            send_sem=self.send_sems.at[index],
            recv_sem=self.recv_sems.at[index],
            device_id=device,
            device_id_type=MESH,
        )

    def start(self, source, target, index, device, when=None):
        copy = self.copy(source, target, index, device)
        guarded(when, copy.start)
        self.left.append((when, copy.wait_send))

    def arrived(self, target, index, device):
        self.copy(target, target, index, device).wait_recv()


def guarded(when, action):
    if when is None:
        action()
    else:
        pl.when(when)(action)


def add_rows(target, target_row, source, source_row, size):
    step = 16

    def one(i, _):
        here = rows_at(target_row + i * step, step)
        there = rows_at(source_row + i * step, step)
        total = target[here, :].astype(jnp.float32) + source[there, :].astype(jnp.float32)
        target[here, :] = total.astype(target.dtype)
        return 0

    lax.fori_loop(0, size // step, one, 0)


def fall_slot(step):
    return 0 if step == 0 else 2 + step


class Block:
    def __init__(self, place, mover, held, across, along, result, base, start, size, half_rows, x_first):
        self.p = place
        self.m = mover
        self.held = held
        self.across = across
        self.along = along
        self.result = result
        self.base = base
        self.start = start
        self.size = size
        self.half_rows = half_rows
        self.x_first = x_first
        self.chunk = size // 8 if x_first else size // 4
        self.origin = start + place.x * (size // 2) if x_first else start

    def part(self, chunk):
        return self.held.at[rows_at(self.origin + chunk * self.chunk, self.chunk)]

    def final(self, row, size):
        return self.result.at[rows_at(self.p.core * self.half_rows + row, size)]

    def final_part(self, chunk):
        return self.final(self.origin + chunk * self.chunk, self.chunk)

    def keep(self, row, size):
        index = self.base // COPIES
        copy = pltpu.make_async_copy(
            self.held.at[rows_at(row, size)], self.final(row, size), self.m.keep_sems.at[index]
        )
        copy.start()
        self.kept = copy

    def events(self):
        line = [self.line_start, lambda: self.line_add(0), lambda: self.line_add(1), lambda: self.line_add(2)]
        spread = [lambda: self.spread(1), lambda: self.spread(2), lambda: self.spread(3)]
        if self.x_first:
            return [self.x_send, self.x_add] + line[1:] + spread + [self.x_return, self.x_done]
        return line + [self.pair_send, self.pair_add, self.pair_done] + spread + [self.z_done]

    def line_start(self):
        p = self.p
        for step in range(3):
            self.m.start(self.part(3 - step), self.along.at[step], self.base + step, p.up(), p.z == 0)
            self.m.start(self.part(step), self.along.at[fall_slot(step)], self.base + 3 + step, p.down(), p.z == LINE - 1)

    def line_add(self, step):
        p = self.p
        rising = jnp.minimum(p.z + 2 - step, 3)
        falling = jnp.maximum(p.z - 2 + step, 0)
        goes_up = (p.z >= 1) & (p.z <= step + 1)
        goes_down = (p.z <= 2) & (p.z >= 2 - step)

        def take_rising():
            self.m.arrived(self.along.at[step], self.base + step, p.down())
            add_rows(self.held, self.origin + rising * self.chunk, self.along.at[step], 0, self.chunk)

        def take_falling():
            self.m.arrived(self.along.at[fall_slot(step)], self.base + 3 + step, p.up())
            add_rows(self.held, self.origin + falling * self.chunk, self.along.at[fall_slot(step)], 0, self.chunk)

        pl.when(goes_up)(take_rising)
        if step < 2:
            self.m.start(self.part(rising), self.along.at[step + 1], self.base + step + 1, p.up(), goes_up)
        pl.when(goes_down)(take_falling)
        if step < 2:
            self.m.start(self.part(falling), self.along.at[fall_slot(step + 1)], self.base + 4 + step, p.down(), goes_down)
        elif self.x_first:
            self.keep(self.origin + p.z * self.chunk, self.chunk)
            self.own_spread(self.part(p.z))

    def own_spread(self, source):
        p = self.p
        target = self.final_part(p.z)
        self.m.start(source, target, self.base + 6, p.up(), p.z < 3)
        self.m.start(source, target, self.base + 9, p.down(), p.z > 0)

    def spread(self, distance):
        p = self.p
        below = self.final_part(jnp.maximum(p.z - distance, 0))
        above = self.final_part(jnp.minimum(p.z + distance, 3))

        pl.when(p.z >= distance)(lambda: self.m.arrived(below, self.base + 5 + distance, p.down()))
        if distance < 3:
            self.m.start(below, below, self.base + 6 + distance, p.up(), (p.z >= distance) & (p.z < 3))
        pl.when(p.z <= 3 - distance)(lambda: self.m.arrived(above, self.base + 8 + distance, p.up()))
        if distance < 3:
            self.m.start(above, above, self.base + 9 + distance, p.down(), (p.z <= 3 - distance) & (p.z > 0))

    def x_part(self, which):
        half = self.size // 2
        return self.held.at[rows_at(self.start + which * half, half)]

    def x_send(self):
        self.m.start(self.x_part(1 - self.p.x), self.across, self.base + 12, self.p.other_x())

    def x_add(self):
        self.m.arrived(self.across, self.base + 12, self.p.other_x())
        add_rows(self.held, self.origin, self.across, 0, self.size // 2)
        self.line_start()

    def x_final(self, which):
        half = self.size // 2
        return self.final(self.start + which * half, half)

    def x_return(self):
        p = self.p
        self.kept.wait()
        mine = self.x_final(p.x)
        self.m.start(mine, mine, self.base + 13, p.other_x())
        self.give(p.x * (self.size // 2), self.size // 2, 14)

    def x_done(self):
        p = self.p
        self.m.arrived(self.x_final(1 - p.x), self.base + 13, p.other_x())
        self.give((1 - p.x) * (self.size // 2), self.size // 2, 15)

    def pair_row(self, which):
        return self.start + self.p.z * self.chunk + which * (self.chunk // 2)

    def pair_send(self):
        half = self.chunk // 2
        source = self.held.at[rows_at(self.pair_row(1 - self.p.x), half)]
        self.m.start(source, self.across, self.base + 12, self.p.other_x())

    def pair_add(self):
        p = self.p
        half = self.chunk // 2
        self.m.arrived(self.across, self.base + 12, p.other_x())
        row = self.pair_row(p.x)
        add_rows(self.held, row, self.across, 0, half)
        self.keep(row, half)
        self.m.start(self.held.at[rows_at(row, half)], self.final(row, half), self.base + 13, p.other_x())

    def pair_done(self):
        p = self.p
        half = self.chunk // 2
        self.m.arrived(self.final(self.pair_row(1 - p.x), half), self.base + 13, p.other_x())
        self.kept.wait()
        self.own_spread(self.final_part(p.z))

    def z_done(self):
        self.give(0, self.size, 14)

    def give(self, offset, size, slot):
        p = self.p
        source = self.final(self.start + offset, size)
        self.m.start(source, source, self.base + slot, p.other_core())
        other = self.result.at[rows_at((1 - p.core) * self.half_rows + self.start + offset, size)]
        self.m.left.append((None, lambda: self.m.arrived(other, self.base + slot, p.other_core())))


def product_tile(left, right, first, tile, width, part):
    columns = pl.ds(pl.multiple_of(first, 128), tile)
    return lax.dot_general(
        left[:, columns], right[:, part * width : (part + 1) * width],
        (((0,), (0,)), ((), ())), preferred_element_type=jnp.float32,
    )


class Unit:
    def __init__(self, index, place, mover, left, right, held, staged, stage_sems):
        self.index = index
        self.rows, self.columns, _, _, self.tile = UNITS[index]
        self.p, self.m = place, mover
        self.left, self.right, self.held = left, right, held
        self.staged, self.stage_sems = staged, stage_sems
        self.base = TILE_BASE + sum(TILES[:index])
        self.width = 512

    def tile_copy(self, i, slot):
        tile = self.tile
        return pltpu.make_async_remote_copy(
            src_ref=self.staged.at[slot, pl.ds(0, tile), pl.ds(0, self.columns)],
            dst_ref=self.held.at[rows_at(i * tile, tile)],
            send_sem=self.stage_sems.at[slot],
            recv_sem=self.m.recv_sems.at[self.base + i],
            device_id=self.p.other_core(),
            device_id_type=MESH,
        )

    def send(self):
        half, tile = self.rows // 2, self.tile

        def one(i, _):
            slot = lax.rem(i, 2)
            pl.when(i >= 2)(lambda: self.tile_copy(i, slot).wait_send())
            first = (1 - self.p.core) * half + i * tile
            for part in range(self.columns // self.width):
                got = product_tile(self.left, self.right, first, tile, self.width, part)
                self.staged[slot, pl.ds(0, tile), part * self.width : (part + 1) * self.width] = got.astype(
                    jnp.bfloat16
                )
            self.tile_copy(i, slot).start()
            return 0

        lax.fori_loop(0, half // tile, one, 0)
        for slot in range(min(2, half // tile)):
            self.tile_copy(0, slot).wait_send()

    def own(self):
        half, tile = self.rows // 2, self.tile

        def one(i, _):
            self.tile_copy(i, 0).wait_recv()
            first = self.p.core * half + i * tile
            here = rows_at(i * tile, tile)
            for part in range(self.columns // self.width):
                got = product_tile(self.left, self.right, first, tile, self.width, part)
                cut = slice(part * self.width, (part + 1) * self.width)
                total = got + self.held[here, cut].astype(jnp.float32)
                self.held[here, cut] = total.astype(jnp.bfloat16)
            return 0

        lax.fori_loop(0, half // tile, one, 0)


def row_scale(values):
    return lax.rsqrt(jnp.mean(values * values, axis=-1, keepdims=True) + epsilon)


def eight(values):
    rows, columns = values.shape
    return jnp.sum(values.reshape(rows // 8, 8, columns), axis=0)


def turn_back(values, cosines, sines):
    half = values.shape[1] // 2
    swapped = jnp.concatenate([values[:, half:], values[:, :half]], axis=1)
    return values * cosines + swapped * sines


def nt(left_side, right_side):
    return lax.dot_general(
        left_side, right_side, (((1,), (1,)), ((), ())), preferred_element_type=jnp.float32
    )


def tn(left_side, right_side):
    return lax.dot_general(
        left_side, right_side, (((0,), (0,)), ((), ())), preferred_element_type=jnp.float32
    )


class Layer:
    def __init__(self, place, mover, **refs):
        self.p, self.m = place, mover
        self.__dict__.update(refs)
        self.rows = self.x1.shape[0]
        self.mine = rows_at(place.y * self.rows, self.rows)
        self.theirs = rows_at((1 - place.y) * self.rows, self.rows)

    def load(self, source, target, index):
        copy = pltpu.make_async_copy(source, target, self.local_sems.at[index])
        copy.start()
        return copy

    def begin(self):
        self.m.start(self.h2_parts.at[self.theirs], self.h2_in, Y_BASE, self.p.other_y())
        self.hid_load = self.load(self.hid_hbm, self.hid, 0)
        self.h_load = self.load(self.h2_hbm, self.hbuf, 1)
        self.own_load = self.load(self.h2_parts.at[self.mine], self.own, 2)
        self.out_load = self.load(self.out_w, self.wbuf.at[pl.ds(0, 768)], 3)

    def tiles(self, step, body):
        lax.fori_loop(0, self.rows // step, lambda i, _: (body(i * step, step), 0)[1], 0)

    def middle(self):
        self.own_load.wait()
        self.m.arrived(self.h2_in, Y_BASE, self.p.other_y())
        self.gains[...] = jnp.zeros_like(self.gains)

        def body(start, step):
            here = rows_at(start, step)
            there = rows_at(self.p.y * self.rows + start, step)
            d = self.own[here, :].astype(jnp.float32) + self.h2_in[here, :].astype(jnp.float32)
            x1 = self.x1[here, :]
            inv = row_scale(x1)
            scaled = d * self.gain2[...]
            inner = jnp.mean(scaled * x1, axis=-1, keepdims=True)
            self.gains[1] += eight(d * x1 * inv)
            d_x1 = self.g[there, :].astype(jnp.float32) + inv * (scaled - x1 * inv * inv * inner)
            self.d_x1[here, :] = d_x1
            self.d_attn[there, :] = d_x1.astype(jnp.bfloat16)

        self.tiles(16, body)
        own = self.d_attn.at[self.mine]
        self.m.start(own, own, Y_BASE + 1, self.p.other_y())

    def outward(self):
        self.m.arrived(self.d_attn.at[self.theirs], Y_BASE + 1, self.p.other_y())
        self.out_load.wait()
        for part in range(3):
            cut = slice(part * 256, (part + 1) * 256)
            self.d_o[:, cut] = nt(self.d_attn[...], self.wbuf[cut, :]).astype(jnp.bfloat16)
        self.w_loads = [
            self.load(self.q_w, self.wbuf.at[:, pl.ds(0, 768)], 3),
            self.load(self.k_w, self.wbuf.at[:, pl.ds(768, 384)], 4),
            self.load(self.v_w, self.wbuf.at[:, pl.ds(1152, 384)], 5),
        ]

    def attention(self, key_head):
        factor = HD ** (-0.5)
        c = key_head * HD
        keys, values = self.k[:, c : c + HD], self.v[:, c : c + HD]
        block = 256
        d_k = [jnp.zeros((block, HD), jnp.float32)] * 2
        d_v = [jnp.zeros((block, HD), jnp.float32)] * 2
        for head in (2 * key_head, 2 * key_head + 1):
            h = head * HD
            for i in range(2):
                here = slice(i * block, (i + 1) * block)
                n = block * (i + 1)
                query, d_out = self.q[here, h : h + HD], self.d_o[here, h : h + HD]
                column = lax.broadcasted_iota(jnp.int32, (block, n), 1)
                row = lax.broadcasted_iota(jnp.int32, (block, n), 0) + i * block
                allowed = (column <= row) & (column >= self.starts[here, :])
                masked = jnp.where(allowed, nt(query, keys[:n]) * factor, masked_score)
                exponent = jnp.exp(masked - jnp.max(masked, axis=1, keepdims=True))
                weights = exponent / jnp.sum(exponent, axis=1, keepdims=True)
                d_weights = nt(d_out, values[:n])
                inner = jnp.sum(weights * d_weights, axis=1, keepdims=True)
                d_scores = (weights * (d_weights - inner)).astype(jnp.bfloat16)
                low = weights.astype(jnp.bfloat16)
                d_query = jnp.dot(d_scores, keys[:n], preferred_element_type=jnp.float32) * factor
                turned = turn_back(d_query, self.cosines[here, :], self.sines[here, :])
                self.d_qkv[here, h : h + HD] = turned.astype(jnp.bfloat16)
                for j in range(i + 1):
                    cut = slice(j * block, (j + 1) * block)
                    d_k[j] = d_k[j] + tn(d_scores[:, cut], query) * factor
                    d_v[j] = d_v[j] + tn(low[:, cut], d_out)
        for j in range(2):
            cut = slice(j * block, (j + 1) * block)
            turned = turn_back(d_k[j], self.cosines[cut, :], self.sines[cut, :])
            self.d_qkv[cut, 768 + c : 768 + c + HD] = turned.astype(jnp.bfloat16)
            self.d_qkv[cut, 1152 + c : 1152 + c + HD] = d_v[j].astype(jnp.bfloat16)

    def h1_part(self, rows, put):
        def body(i, _):
            cut = pl.ds(pl.multiple_of(i * 256, 256), 256)
            put(cut, nt(self.d_qkv[rows, 0:1536], self.wbuf[cut, :]))
            return 0

        lax.fori_loop(0, 6, body, 0)

    def inward(self):
        for copy in self.w_loads:
            copy.wait()

        def put(cut, got):
            self.h1_out[:, cut] = got.astype(jnp.bfloat16)

        self.h1_part(self.theirs, put)
        self.m.start(self.h1_out, self.h1_in, Y_BASE + 2, self.p.other_y())

    def mlp_send(self):
        self.m.start(self.mlp_parts.at[self.theirs], self.mlp_in, Y_BASE + 3, self.p.other_y())
        self.own_load = self.load(self.mlp_parts.at[self.mine], self.own, 2)

    def finish(self):
        def put(cut, got):
            self.fbuf[:, cut] = got

        self.h1_part(self.mine, put)
        self.m.arrived(self.h1_in, Y_BASE + 2, self.p.other_y())

        def body(start, step):
            here = rows_at(start, step)
            d = self.fbuf[here, :] + self.h1_in[here, :].astype(jnp.float32)
            x = self.x[here, :].astype(jnp.float32)
            inv = row_scale(x)
            scaled = d * self.gain1[...]
            inner = jnp.mean(scaled * x, axis=-1, keepdims=True)
            self.gains[0] += eight(d * x * inv)
            self.d_x1[here, :] = self.d_x1[here, :] + inv * (scaled - x * inv * inv * inner)

        self.tiles(16, body)
        copy = self.load(self.d_x1, self.tokens_out, 6)
        self.m.left.append((None, copy.wait))

    def layer_end(self):
        self.own_load.wait()
        self.m.arrived(self.mlp_in, Y_BASE + 3, self.p.other_y())

        def body(start, step):
            here = rows_at(start, step)
            mlp = self.own[here, :].astype(jnp.float32) + self.mlp_in[here, :].astype(jnp.float32)
            out = self.x1[here, :] + mlp
            self.gains[2] += eight(out * out)
            self.gains[3] += eight(mlp * mlp)
            self.y_low[here, :] = out.astype(jnp.bfloat16)

        self.tiles(16, body)
        copy = self.load(self.y_low, self.layer_out, 7)
        self.m.left.append((None, copy.wait))
        self.totals[0] = jnp.zeros(self.totals.shape[1:], jnp.float32)
        for row in range(4):
            self.totals[0, row : row + 1, :] = jnp.sum(self.gains[row], axis=0, keepdims=True)
        self.totals[0, 4:5, :] = self.attn_squares[...]


def sum_small(place, mover, total, slots, step):
    device = (place.other_core, place.other_x, place.other_y, place.pair_z, place.far_z)[step]()
    copy = mover.copy(total.at[step], slots.at[step], SMALL_BASE + step, device)
    copy.start()
    copy.wait()
    total[step + 1] = total[step] + slots[step]


INPUTS = (
    "hid_hbm", "g", "h2_hbm", "d_gate", "d_up", "o", "h1_hbm", "q", "k", "v", "out_w", "q_w", "k_w", "v_w",
    "x1", "x", "h2_parts", "mlp_parts", "cosines", "sines", "starts", "gain1", "gain2", "attn_squares",
)
IN_HBM = ("hid_hbm", "h2_hbm", "h1_hbm", "out_w", "q_w", "k_w", "v_w", "h2_parts", "mlp_parts")
RESULTS = ("down_out", "gate_out", "up_out", "o_out", "qkv_out", "tokens_out", "layer_out", "small_out")
PLAIN = (
    "staged", "hid", "hbuf", "own", "h2_in", "d_attn", "d_x1", "wbuf", "d_o", "h1_out", "h1_in", "mlp_in",
    "y_low", "fbuf", "gains", "totals", "slots", "stage_sems", "send_sems", "recv_sems", "keep_sems", "local_sems",
)


def backward_kernel(*refs):
    n = len(UNITS)
    names = INPUTS + RESULTS
    r = dict(zip(names, refs[: len(names)]))
    rest = refs[len(names) :]
    held, across, along = rest[:n], rest[n : 3 * n], rest[3 * n : 5 * n]
    r.update(zip(PLAIN, rest[5 * n :]))
    r["d_qkv"] = r["hid"]
    place = Place()
    mover = Mover(r["send_sems"], r["recv_sems"])
    mover.keep_sems = r["keep_sems"]
    enter(place)
    layer = Layer(place, mover, **r)
    lefts = (r["hid"], r["hbuf"], r["hbuf"], r["o"], r["hbuf"])
    rights = (r["g"], r["d_gate"], r["d_up"], r["d_attn"], r["d_qkv"])
    results = tuple(r[name] for name in RESULTS[:n])
    units = [
        Unit(i, place, mover, lefts[i], rights[i], held[i], r["staged"], r["stage_sems"]) for i in range(n)
    ]
    steps = []
    for i, (rows, columns, x_rows, z_rows, _) in enumerate(UNITS):
        for j in range(2):
            b = 2 * i + j
            block = Block(
                place, mover, held[i], across[b], along[b], results[i], b * COPIES,
                0 if j == 0 else x_rows, x_rows if j == 0 else z_rows, rows // 2, j == 0,
            )
            steps.append(block.events())

    def send(i):
        if i == 0:
            layer.hid_load.wait()
        if i == 1:
            layer.h_load.wait()
        if i == 4:
            layer.h_load = layer.load(layer.h1_hbm, layer.hbuf, 1)
            layer.h_load.wait()
        units[i].send()

    tasks = [layer.begin, layer.middle, layer.outward]
    tasks += [partial(layer.attention, i) for i in range(4)]
    tasks += [layer.inward, layer.mlp_send, layer.finish, layer.layer_end]
    tasks += [partial(sum_small, place, mover, r["totals"], r["slots"], i) for i in range(SMALL_STEPS)]
    for item in ORDER:
        if item < 5:
            send(item)
        elif item < 10:
            units[item - 5].own()
        elif item < 20:
            steps[item - 10].pop(0)()
        else:
            tasks[item - 20]()
    r["small_out"][...] = r["totals"][SMALL_STEPS]
    for when, wait in mover.left:
        guarded(when, wait)


def enter(place):
    barrier = pltpu.get_barrier_semaphore()

    def greet(device):
        pl.semaphore_signal(barrier, inc=1, device_id=device, device_id_type=MESH)

    for device in (place.other_core(), place.other_x(), place.other_y(), place.pair_z(), place.far_z()):
        greet(device)
    middle = (place.z == 1) | (place.z == 2)
    pl.when(middle)(lambda: greet(place.at(3 - place.z, place.x, place.core, place.y)))
    pl.semaphore_wait(barrier, 5 + jnp.where(middle, 1, 0))


def backward(**given):
    vmem = pl.BlockSpec(memory_space=pltpu.VMEM)
    hbm = pl.BlockSpec(memory_space=pl.ANY)
    low, full = jnp.bfloat16, jnp.float32
    own_rows, width = given["x1"].shape
    held = [pltpu.VMEM((rows // 2, columns), low) for rows, columns, *_ in UNITS]
    across, along = [], []
    for _, columns, x_rows, z_rows, _ in UNITS:
        across += [pltpu.VMEM((x_rows // 2, columns), low), pltpu.VMEM((z_rows // 8, columns), low)]
        along += [pltpu.VMEM((5, x_rows // 8, columns), low), pltpu.VMEM((5, z_rows // 4, columns), low)]
    part = pltpu.VMEM((own_rows, width), low)
    plain = dict(
        staged=pltpu.VMEM((2, 256, 2048), low),
        hid=pltpu.VMEM((512, 2048), low),
        hbuf=pltpu.VMEM((512, width), low),
        own=part,
        h2_in=part,
        d_attn=pltpu.VMEM((512, width), low),
        d_x1=pltpu.VMEM((own_rows, width), full),
        wbuf=pltpu.VMEM((1536, 1536), low),
        d_o=pltpu.VMEM((512, 768), low),
        h1_out=part,
        h1_in=part,
        mlp_in=part,
        y_low=part,
        fbuf=pltpu.VMEM((own_rows, width), full),
        gains=pltpu.VMEM((4, 8, width), full),
        totals=pltpu.VMEM((SMALL_STEPS + 1, 8, width), full),
        slots=pltpu.VMEM((SMALL_STEPS, 8, width), full),
        stage_sems=pltpu.SemaphoreType.DMA((2,)),
        send_sems=pltpu.SemaphoreType.DMA((N_SEMS,)),
        recv_sems=pltpu.SemaphoreType.DMA((N_SEMS,)),
        keep_sems=pltpu.SemaphoreType.DMA((2 * len(UNITS),)),
        local_sems=pltpu.SemaphoreType.DMA((8,)),
    )
    flops = sum(2 * 512 * rows * columns for rows, columns, *_ in UNITS)
    return pl.pallas_call(
        backward_kernel,
        out_shape=[jax.ShapeDtypeStruct((rows, columns), low) for rows, columns, *_ in UNITS]
        + [
            jax.ShapeDtypeStruct((own_rows, width), full),
            jax.ShapeDtypeStruct((own_rows, width), low),
            jax.ShapeDtypeStruct((8, width), full),
        ],
        in_specs=[hbm if name in IN_HBM else vmem for name in INPUTS],
        out_specs=[hbm] * 7 + [vmem],
        scratch_shapes=held + across + along + [plain[name] for name in PLAIN],
        compiler_params=pltpu.CompilerParams(
            collective_id=0, has_side_effects=True, vmem_limit_bytes=62 << 20
        ),
        cost_estimate=pl.CostEstimate(flops=flops, bytes_accessed=80 << 20, transcendentals=0),
        name="backward",
    )(*(given[name] for name in INPUTS))


def dp_sum(terms):
    low = lax.psum(tuple(term.astype(jnp.bfloat16) for term in terms), "dp")
    return tuple(term.astype(jnp.float32) for term in low)


def low_scatter(partial):
    return lax.psum_scatter(
        partial.astype(jnp.bfloat16), "tensor", scatter_dimension=0, tiled=True
    ).astype(jnp.float32)


def body(
    tokens,
    lengths,
    first_gain,
    query_weight,
    key_weight,
    value_weight,
    output_weight,
    second_gain,
    gate_weight,
    up_weight,
    down_weight,
    out_cotangent,
):
    inputs = tokens.astype(jnp.float32)
    normed1, inv_first = norm_rows(inputs, first_gain)
    normed1 = normed1.astype(jnp.bfloat16)
    full_first = lax.all_gather(normed1, "tensor", axis=0, tiled=True)
    total_rows = full_first.shape[0]
    places, segment, cosine_table, sine_table, _ = tables(lengths[0], total_rows, HD // 2)
    kv_heads = key_weight.shape[1] // HD
    groups = query_weight.shape[1] // key_weight.shape[1]
    query = rotate(product(full_first, query_weight), cosine_table, sine_table, 1.0).astype(
        jnp.bfloat16
    )
    keys = rotate(product(full_first, key_weight), cosine_table, sine_table, 1.0).astype(
        jnp.bfloat16
    )
    values = product(full_first, value_weight).astype(jnp.bfloat16)
    block_rows = min(block_limit, total_rows)
    block_count = total_rows // block_rows
    query_blocks = query.reshape(block_count, block_rows, kv_heads, groups, HD)
    seg_blocks = segment.reshape(block_count, block_rows)
    place_blocks = places.reshape(block_count, block_rows)
    key_three = keys.reshape(total_rows, kv_heads, HD)
    value_three = values.reshape(total_rows, kv_heads, HD)
    factor = HD ** (-0.5)

    def scores(query_block, seg_block, place_block):
        raw = (
            jnp.einsum("qcgd,kcd->cgqk", query_block, key_three, preferred_element_type=jnp.float32)
            * factor
        )
        allowed = (seg_block[:, None] == segment[None, :]) & (
            place_block[:, None] >= places[None, :]
        )
        return (jnp.where(allowed[None, None], raw, masked_score), allowed)

    def forward_block(piece_set):
        query_block, seg_block, place_block = piece_set
        masked, allowed = scores(query_block, seg_block, place_block)
        highest = jnp.max(masked, axis=-1, keepdims=True)
        exponent = jnp.exp(masked - highest)
        denominator = jnp.sum(exponent, axis=-1, keepdims=True)
        weights = exponent / denominator
        output = jnp.einsum(
            "cgqk,kcd->qcgd",
            weights.astype(jnp.bfloat16),
            value_three,
            preferred_element_type=jnp.float32,
        )
        stored = (highest + jnp.log(denominator))[..., 0]
        return (output.reshape(block_rows, -1), stored)

    out_blocks, kept_blocks = lax.map(forward_block, (query_blocks, seg_blocks, place_blocks))
    attended = out_blocks.reshape(total_rows, -1).astype(jnp.bfloat16)
    attn_rows = low_scatter(product(attended, output_weight))
    middle = inputs + attn_rows
    normed2, inv_second = norm_rows(middle, second_gain)
    normed2 = normed2.astype(jnp.bfloat16)
    full_second = lax.all_gather(normed2, "tensor", axis=0, tiled=True)
    gate_value = product(full_second, gate_weight)
    upward = product(full_second, up_weight)
    gate_sig = jax.nn.sigmoid(gate_value)
    hidden = (gate_value * gate_sig * upward).astype(jnp.bfloat16)
    mlp_rows = low_scatter(product(hidden, down_weight))
    layer_out = middle + mlp_rows
    squares = jnp.stack(
        [
            jnp.sum(layer_out * layer_out),
            jnp.sum(attn_rows * attn_rows),
            jnp.sum(mlp_rows * mlp_rows),
        ]
    )
    grad_full = lax.all_gather(out_cotangent, "tensor", axis=0, tiled=True)
    grad_hidden = times_cols(grad_full, down_weight)
    down_g = times_rows(hidden, grad_full)
    gate_slope = gate_sig * (1.0 + gate_value * (1.0 - gate_sig))
    grad_gate = (grad_hidden * upward * gate_slope).astype(jnp.bfloat16)
    grad_up = (grad_hidden * gate_value * gate_sig).astype(jnp.bfloat16)
    gate_g = times_rows(full_second, grad_gate)
    up_g = times_rows(full_second, grad_up)
    gate_g, up_g, down_g = dp_sum((gate_g, up_g, down_g))
    grad_normed2 = low_scatter(
        times_cols(grad_gate, gate_weight) + times_cols(grad_up, up_weight)
    )
    second_rows, grad_mid_norm = norm_back(middle, inv_second, second_gain, grad_normed2)
    grad_middle = out_cotangent.astype(jnp.float32) + grad_mid_norm
    grad_attn_full = lax.all_gather(grad_middle.astype(jnp.bfloat16), "tensor", axis=0, tiled=True)
    output_g = times_rows(attended, grad_attn_full)
    grad_out = times_cols(grad_attn_full, output_weight).astype(jnp.bfloat16)
    grad_blocks = grad_out.reshape(block_count, block_rows, kv_heads, groups, HD)

    def backward_block(running, piece_set):
        key_acc, value_acc = running
        query_block, seg_block, place_block, grad_block, stored = piece_set
        masked, allowed = scores(query_block, seg_block, place_block)
        weights = jnp.where(allowed[None, None], jnp.exp(masked - stored[..., None]), 0.0)
        grad_weights = jnp.einsum(
            "qcgd,kcd->cgqk", grad_block, value_three, preferred_element_type=jnp.float32
        )
        row_inner = jnp.sum(weights * grad_weights, axis=-1, keepdims=True)
        grad_scores = (weights * (grad_weights - row_inner)).astype(jnp.bfloat16)
        grad_query = (
            jnp.einsum("cgqk,kcd->qcgd", grad_scores, key_three, preferred_element_type=jnp.float32)
            * factor
        )
        key_acc = (
            key_acc
            + jnp.einsum(
                "cgqk,qcgd->kcd", grad_scores, query_block, preferred_element_type=jnp.float32
            )
            * factor
        )
        value_acc = value_acc + jnp.einsum(
            "cgqk,qcgd->kcd",
            weights.astype(jnp.bfloat16),
            grad_block,
            preferred_element_type=jnp.float32,
        )
        return ((key_acc, value_acc), grad_query.reshape(block_rows, -1))

    zeros_kv = jnp.zeros((total_rows, kv_heads, HD), jnp.float32)
    (key_rot_grad, value_acc_grad), query_rot_grad = lax.scan(
        backward_block,
        (zeros_kv, zeros_kv),
        (query_blocks, seg_blocks, place_blocks, grad_blocks, kept_blocks),
    )
    query_lin = rotate(
        query_rot_grad.reshape(total_rows, -1), cosine_table, sine_table, -1.0
    ).astype(jnp.bfloat16)
    key_lin = rotate(key_rot_grad.reshape(total_rows, -1), cosine_table, sine_table, -1.0).astype(
        jnp.bfloat16
    )
    value_lin = value_acc_grad.reshape(total_rows, -1).astype(jnp.bfloat16)
    query_g = times_rows(full_first, query_lin)
    key_g = times_rows(full_first, key_lin)
    value_g = times_rows(full_first, value_lin)
    grad_normed1 = low_scatter(
        times_cols(query_lin, query_weight)
        + times_cols(key_lin, key_weight)
        + times_cols(value_lin, value_weight)
    )
    first_rows, grad_in_norm = norm_back(inputs, inv_first, first_gain, grad_normed1)
    tokens_grad = grad_middle + grad_in_norm
    gain_rows = jnp.stack([first_rows, second_rows])
    query_g, key_g, value_g, output_g = dp_sum((query_g, key_g, value_g, output_g))
    gain_rows, squares = lax.psum((gain_rows, squares), ("dp", "tensor"))
    rms_values = jnp.sqrt(squares / (total_rows * lax.axis_size("dp")))
    return (
        layer_out.astype(jnp.bfloat16),
        tokens_grad,
        gain_rows[0],
        query_g,
        key_g,
        value_g,
        output_g,
        gain_rows[1],
        gate_g,
        up_g,
        down_g,
        rms_values,
    )


def fused_body(
    tokens,
    lengths,
    first_gain,
    query_weight,
    key_weight,
    value_weight,
    output_weight,
    second_gain,
    gate_weight,
    up_weight,
    down_weight,
    out_cotangent,
):
    inputs = tokens.astype(jnp.float32)
    normed1, _ = norm_rows(inputs, first_gain)
    full_first = lax.all_gather(normed1.astype(jnp.bfloat16), "tensor", axis=0, tiled=True)
    total_rows = full_first.shape[0]
    places, segment, cosine_table, sine_table, firsts = tables(lengths[0], total_rows, HD // 2)
    kv_heads = key_weight.shape[1] // HD
    groups = query_weight.shape[1] // key_weight.shape[1]
    query = rotate(product(full_first, query_weight), cosine_table, sine_table, 1.0).astype(
        jnp.bfloat16
    )
    keys = rotate(product(full_first, key_weight), cosine_table, sine_table, 1.0).astype(
        jnp.bfloat16
    )
    values = product(full_first, value_weight).astype(jnp.bfloat16)
    raw = jnp.einsum(
        "qcgd,kcd->cgqk",
        query.reshape(total_rows, kv_heads, groups, HD),
        keys.reshape(total_rows, kv_heads, HD),
        preferred_element_type=jnp.float32,
    ) * HD ** (-0.5)
    allowed = (segment[:, None] == segment[None, :]) & (places[:, None] >= places[None, :])
    masked = jnp.where(allowed[None, None], raw, masked_score)
    exponent = jnp.exp(masked - jnp.max(masked, axis=-1, keepdims=True))
    weights = exponent / jnp.sum(exponent, axis=-1, keepdims=True)
    attended = (
        jnp.einsum(
            "cgqk,kcd->qcgd",
            weights.astype(jnp.bfloat16),
            values.reshape(total_rows, kv_heads, HD),
            preferred_element_type=jnp.float32,
        )
        .reshape(total_rows, -1)
        .astype(jnp.bfloat16)
    )
    attn_rows = low_scatter(product(attended, output_weight))
    middle = inputs + attn_rows
    normed2, _ = norm_rows(middle, second_gain)
    full_second = lax.all_gather(normed2.astype(jnp.bfloat16), "tensor", axis=0, tiled=True)
    gate_value = product(full_second, gate_weight)
    upward = product(full_second, up_weight)
    gate_sig = jax.nn.sigmoid(gate_value)
    hidden = (gate_value * gate_sig * upward).astype(jnp.bfloat16)
    mlp_parts = product(hidden, down_weight).astype(jnp.bfloat16)
    grad_full = lax.all_gather(out_cotangent, "tensor", axis=0, tiled=True)
    grad_hidden = times_cols(grad_full, down_weight)
    gate_slope = gate_sig * (1.0 + gate_value * (1.0 - gate_sig))
    grad_gate = (grad_hidden * upward * gate_slope).astype(jnp.bfloat16)
    grad_up = (grad_hidden * gate_value * gate_sig).astype(jnp.bfloat16)
    h2_parts = (times_cols(grad_gate, gate_weight) + times_cols(grad_up, up_weight)).astype(
        jnp.bfloat16
    )
    *sums, tokens_grad, layer_out, small = backward(
        hid_hbm=hidden,
        g=grad_full,
        h2_hbm=full_second,
        d_gate=grad_gate,
        d_up=grad_up,
        o=attended,
        h1_hbm=full_first,
        q=query,
        k=keys,
        v=values,
        out_w=output_weight,
        q_w=query_weight,
        k_w=key_weight,
        v_w=value_weight,
        x1=middle,
        x=tokens,
        h2_parts=h2_parts,
        mlp_parts=mlp_parts,
        cosines=jnp.concatenate([cosine_table, cosine_table], axis=1),
        sines=jnp.concatenate([sine_table, -sine_table], axis=1),
        starts=firsts[:, None],
        gain1=first_gain[None],
        gain2=second_gain[None],
        attn_squares=jnp.sum(attn_rows * attn_rows, axis=0)[None],
    )
    down_g, gate_g, up_g, output_g, qkv_g = (part.astype(jnp.float32) for part in sums)
    q_cols, k_cols = query.shape[1], keys.shape[1]
    squares = jnp.stack([jnp.sum(small[2]), jnp.sum(small[4]), jnp.sum(small[3])])
    rms_values = jnp.sqrt(squares / (total_rows * lax.axis_size("dp")))
    return (
        layer_out,
        tokens_grad,
        small[0],
        qkv_g[:, :q_cols],
        qkv_g[:, q_cols : q_cols + k_cols],
        qkv_g[:, q_cols + k_cols :],
        output_g,
        small[1],
        gate_g,
        up_g,
        down_g,
        rms_values,
    )


def solution(mesh):
    in_specs = (
        P(("dp", "tensor"), None),
        P("dp", None),
        P(),
        P(None, "tensor"),
        P(None, "tensor"),
        P(None, "tensor"),
        P("tensor", None),
        P(),
        P(None, "tensor"),
        P(None, "tensor"),
        P("tensor", None),
        P(("dp", "tensor"), None),
    )
    out_specs = (
        P(("dp", "tensor"), None),
        P(("dp", "tensor"), None),
        P(),
        P(None, "tensor"),
        P(None, "tensor"),
        P(None, "tensor"),
        P("tensor", None),
        P(),
        P(None, "tensor"),
        P(None, "tensor"),
        P("tensor", None),
        P(),
    )
    fused = dict(mesh.shape) == {"dp": 16, "tensor": 2}
    chosen = fused_body if fused else body
    return jax.shard_map(chosen, mesh=mesh, in_specs=in_specs, out_specs=out_specs, check_vma=False)
```

```python
from functools import partial

import jax
import jax.numpy as jnp
from jax import lax
from jax.experimental import pallas as pl
from jax.experimental.pallas import tpu as pltpu
from jax.sharding import PartitionSpec as P

HD = 96


epsilon = 1e-05
rope_base = 10000.0
masked_score = -1e30
block_limit = 512


def product(left_side, right_side):
    return jnp.dot(left_side, right_side, preferred_element_type=jnp.float32)


def times_rows(left_side, right_side):
    return lax.dot_general(
        left_side, right_side, (((0,), (0,)), ((), ())), preferred_element_type=jnp.float32
    )


def times_cols(left_side, right_side):
    return lax.dot_general(
        left_side, right_side, (((1,), (1,)), ((), ())), preferred_element_type=jnp.float32
    )


def tables(lens_row, total_rows, half_size):
    count = lens_row.shape[0]
    earlier = jnp.arange(count)[:, None] <= jnp.arange(count)[None, :]
    seq_ends = jnp.sum(jnp.where(earlier, lens_row[:, None], 0), axis=0, dtype=jnp.int32)
    starts = seq_ends - lens_row
    places = jnp.arange(total_rows, dtype=jnp.int32)
    segment = jnp.sum(
        (places[:, None] >= seq_ends[None, :]).astype(jnp.int32), axis=1, dtype=jnp.int32
    )
    member = segment[:, None] == jnp.arange(lens_row.shape[0], dtype=jnp.int32)[None, :]
    firsts = jnp.sum(jnp.where(member, starts[None, :], 0), axis=1, dtype=jnp.int32)
    position = places - firsts
    inverse = rope_base ** (-2.0 * jnp.arange(half_size, dtype=jnp.float32) / (2 * half_size))
    angles = position.astype(jnp.float32)[:, None] * inverse[None, :]
    return (places, segment, jnp.cos(angles), jnp.sin(angles), firsts)


def rotate(values, cosine_table, sine_table, direction):
    total_rows = values.shape[0]
    half_size = cosine_table.shape[1]
    shaped = values.reshape(total_rows, -1, 2 * half_size)
    first_half = shaped[..., :half_size]
    second = shaped[..., half_size:]
    cos_b = cosine_table[:, None, :]
    sin_b = sine_table[:, None, :] * direction
    turned = jnp.concatenate(
        [first_half * cos_b - second * sin_b, second * cos_b + first_half * sin_b], axis=-1
    )
    return turned.reshape(total_rows, -1)


def norm_rows(values, gain):
    inv_rms = lax.rsqrt(jnp.mean(values * values, axis=-1, keepdims=True) + epsilon)
    return (values * inv_rms * gain, inv_rms)


def norm_back(values, inv_rms, gain, upstream):
    scaled = upstream * gain
    row_inner = jnp.mean(scaled * values, axis=-1, keepdims=True)
    gain_rows = jnp.sum(upstream * values * inv_rms, axis=0)
    return (gain_rows, inv_rms * (scaled - values * inv_rms * inv_rms * row_inner))


ORDER = (
    20, 0, 1, 5, 10, 11, 2, 6, 7, 11, 21, 11, 10, 13, 11, 11, 10, 12, 11, 22, 3, 10, 23, 8, 10, 13,
    24, 25, 11, 13, 12, 10, 26, 27, 11, 28, 4, 13, 13, 12, 9, 10, 13, 15, 11, 13, 16, 10, 10, 12,
    29, 11, 11, 15, 16, 14, 12, 30, 15, 31, 32, 10, 13, 16, 33, 34, 35, 15, 15, 12, 13, 16, 18, 14,
    12, 15, 14, 13, 13, 16, 14, 12, 12, 16, 14, 18, 16, 15, 14, 19, 16, 16, 18, 14, 17, 18, 14, 14,
    12, 15, 18, 19, 16, 15, 17, 19, 17, 18, 15, 15, 14, 19, 19, 17, 17, 19, 17, 18, 19, 17, 18, 18,
    19, 17, 19, 17, 19, 19, 18, 17, 17,
)


MESH = pl.DeviceIdType.MESH
LINE = 4
UNITS = (
    (2048, 1536, 640, 384, 256),
    (1536, 2048, 512, 256, 256),
    (1536, 2048, 384, 384, 256),
    (768, 1536, 256, 128, 128),
    (1536, 1536, 512, 256, 256),
)
COPIES = 16
TILE_BASE = 2 * len(UNITS) * COPIES
TILES = tuple(rows // 2 // tile for rows, _, _, _, tile in UNITS)
SMALL_BASE = TILE_BASE + sum(TILES)
SMALL_STEPS = 5
Y_BASE = SMALL_BASE + SMALL_STEPS
N_SEMS = Y_BASE + 4


def rows_at(start, size):
    return pl.ds(pl.multiple_of(start, 16), size)


class Place:
    def __init__(self):
        dp = lax.axis_index("dp")
        self.dp = dp
        self.y = lax.axis_index("tensor")
        self.core = lax.rem(dp, 2)
        self.x = lax.rem(dp // 2, 2)
        self.z = dp // 4

    def at(self, z, x, core, y):
        return ((z * 2 + x) * 2 + core, y)

    def other_core(self):
        return self.at(self.z, self.x, 1 - self.core, self.y)

    def other_x(self):
        return self.at(self.z, 1 - self.x, self.core, self.y)

    def other_y(self):
        return self.at(self.z, self.x, self.core, 1 - self.y)

    def up(self):
        return self.at(self.z + 1, self.x, self.core, self.y)

    def down(self):
        return self.at(self.z - 1, self.x, self.core, self.y)

    def pair_z(self):
        return self.at(self.z + 1 - 2 * lax.rem(self.z, 2), self.x, self.core, self.y)

    def far_z(self):
        return self.at(lax.rem(self.z + 2, LINE), self.x, self.core, self.y)


class Mover:
    def __init__(self, send_sems, recv_sems):
        self.send_sems = send_sems
        self.recv_sems = recv_sems
        self.left = []

    def copy(self, source, target, index, device):
        return pltpu.make_async_remote_copy(
            src_ref=source,
            dst_ref=target,
            send_sem=self.send_sems.at[index],
            recv_sem=self.recv_sems.at[index],
            device_id=device,
            device_id_type=MESH,
        )

    def start(self, source, target, index, device, when=None):
        copy = self.copy(source, target, index, device)
        guarded(when, copy.start)
        self.left.append((when, copy.wait_send))

    def arrived(self, target, index, device):
        self.copy(target, target, index, device).wait_recv()


def guarded(when, action):
    if when is None:
        action()
    else:
        pl.when(when)(action)


def add_rows(target, target_row, source, source_row, size):
    step = 16

    def one(i, _):
        here = rows_at(target_row + i * step, step)
        there = rows_at(source_row + i * step, step)
        total = target[here, :].astype(jnp.float32) + source[there, :].astype(jnp.float32)
        target[here, :] = total.astype(target.dtype)
        return 0

    lax.fori_loop(0, size // step, one, 0)


def fall_slot(step):
    return 0 if step == 0 else 2 + step


class Block:
    def __init__(self, place, mover, held, across, along, result, base, start, size, half_rows, x_first):
        self.p = place
        self.m = mover
        self.held = held
        self.across = across
        self.along = along
        self.result = result
        self.base = base
        self.start = start
        self.size = size
        self.half_rows = half_rows
        self.x_first = x_first
        self.chunk = size // 8 if x_first else size // 4
        self.origin = start + place.x * (size // 2) if x_first else start

    def part(self, chunk):
        return self.held.at[rows_at(self.origin + chunk * self.chunk, self.chunk)]

    def final(self, row, size):
        return self.result.at[rows_at(self.p.core * self.half_rows + row, size)]

    def final_part(self, chunk):
        return self.final(self.origin + chunk * self.chunk, self.chunk)

    def keep(self, row, size):
        index = self.base // COPIES
        copy = pltpu.make_async_copy(
            self.held.at[rows_at(row, size)], self.final(row, size), self.m.keep_sems.at[index]
        )
        copy.start()
        self.kept = copy

    def events(self):
        line = [self.line_start, lambda: self.line_add(0), lambda: self.line_add(1), lambda: self.line_add(2)]
        spread = [lambda: self.spread(1), lambda: self.spread(2), lambda: self.spread(3)]
        if self.x_first:
            return [self.x_send, self.x_add] + line[1:] + spread + [self.x_return, self.x_done]
        return line + [self.pair_send, self.pair_add, self.pair_done] + spread + [self.z_done]

    def line_start(self):
        p = self.p
        for step in range(3):
            self.m.start(self.part(3 - step), self.along.at[step], self.base + step, p.up(), p.z == 0)
            self.m.start(self.part(step), self.along.at[fall_slot(step)], self.base + 3 + step, p.down(), p.z == LINE - 1)

    def line_add(self, step):
        p = self.p
        rising = jnp.minimum(p.z + 2 - step, 3)
        falling = jnp.maximum(p.z - 2 + step, 0)
        goes_up = (p.z >= 1) & (p.z <= step + 1)
        goes_down = (p.z <= 2) & (p.z >= 2 - step)

        def take_rising():
            self.m.arrived(self.along.at[step], self.base + step, p.down())
            add_rows(self.held, self.origin + rising * self.chunk, self.along.at[step], 0, self.chunk)

        def take_falling():
            self.m.arrived(self.along.at[fall_slot(step)], self.base + 3 + step, p.up())
            add_rows(self.held, self.origin + falling * self.chunk, self.along.at[fall_slot(step)], 0, self.chunk)

        pl.when(goes_up)(take_rising)
        if step < 2:
            self.m.start(self.part(rising), self.along.at[step + 1], self.base + step + 1, p.up(), goes_up)
        pl.when(goes_down)(take_falling)
        if step < 2:
            self.m.start(self.part(falling), self.along.at[fall_slot(step + 1)], self.base + 4 + step, p.down(), goes_down)
        elif self.x_first:
            self.keep(self.origin + p.z * self.chunk, self.chunk)
            self.own_spread(self.part(p.z))

    def own_spread(self, source):
        p = self.p
        target = self.final_part(p.z)
        self.m.start(source, target, self.base + 6, p.up(), p.z < 3)
        self.m.start(source, target, self.base + 9, p.down(), p.z > 0)

    def spread(self, distance):
        p = self.p
        below = self.final_part(jnp.maximum(p.z - distance, 0))
        above = self.final_part(jnp.minimum(p.z + distance, 3))

        pl.when(p.z >= distance)(lambda: self.m.arrived(below, self.base + 5 + distance, p.down()))
        if distance < 3:
            self.m.start(below, below, self.base + 6 + distance, p.up(), (p.z >= distance) & (p.z < 3))
        pl.when(p.z <= 3 - distance)(lambda: self.m.arrived(above, self.base + 8 + distance, p.up()))
        if distance < 3:
            self.m.start(above, above, self.base + 9 + distance, p.down(), (p.z <= 3 - distance) & (p.z > 0))

    def x_part(self, which):
        half = self.size // 2
        return self.held.at[rows_at(self.start + which * half, half)]

    def x_send(self):
        self.m.start(self.x_part(1 - self.p.x), self.across, self.base + 12, self.p.other_x())

    def x_add(self):
        self.m.arrived(self.across, self.base + 12, self.p.other_x())
        add_rows(self.held, self.origin, self.across, 0, self.size // 2)
        self.line_start()

    def x_final(self, which):
        half = self.size // 2
        return self.final(self.start + which * half, half)

    def x_return(self):
        p = self.p
        self.kept.wait()
        mine = self.x_final(p.x)
        self.m.start(mine, mine, self.base + 13, p.other_x())
        self.give(p.x * (self.size // 2), self.size // 2, 14)

    def x_done(self):
        p = self.p
        self.m.arrived(self.x_final(1 - p.x), self.base + 13, p.other_x())
        self.give((1 - p.x) * (self.size // 2), self.size // 2, 15)

    def pair_row(self, which):
        return self.start + self.p.z * self.chunk + which * (self.chunk // 2)

    def pair_send(self):
        half = self.chunk // 2
        source = self.held.at[rows_at(self.pair_row(1 - self.p.x), half)]
        self.m.start(source, self.across, self.base + 12, self.p.other_x())

    def pair_add(self):
        p = self.p
        half = self.chunk // 2
        self.m.arrived(self.across, self.base + 12, p.other_x())
        row = self.pair_row(p.x)
        add_rows(self.held, row, self.across, 0, half)
        self.keep(row, half)
        self.m.start(self.held.at[rows_at(row, half)], self.final(row, half), self.base + 13, p.other_x())

    def pair_done(self):
        p = self.p
        half = self.chunk // 2
        self.m.arrived(self.final(self.pair_row(1 - p.x), half), self.base + 13, p.other_x())
        self.kept.wait()
        self.own_spread(self.final_part(p.z))

    def z_done(self):
        self.give(0, self.size, 14)

    def give(self, offset, size, slot):
        p = self.p
        source = self.final(self.start + offset, size)
        self.m.start(source, source, self.base + slot, p.other_core())
        other = self.result.at[rows_at((1 - p.core) * self.half_rows + self.start + offset, size)]
        self.m.left.append((None, lambda: self.m.arrived(other, self.base + slot, p.other_core())))


def product_tile(left, right, first, tile, width, part):
    columns = pl.ds(pl.multiple_of(first, 128), tile)
    return lax.dot_general(
        left[:, columns], right[:, part * width : (part + 1) * width],
        (((0,), (0,)), ((), ())), preferred_element_type=jnp.float32,
    )


class Unit:
    def __init__(self, index, place, mover, left, right, held, staged, stage_sems):
        self.index = index
        self.rows, self.columns, _, _, self.tile = UNITS[index]
        self.p, self.m = place, mover
        self.left, self.right, self.held = left, right, held
        self.staged, self.stage_sems = staged, stage_sems
        self.base = TILE_BASE + sum(TILES[:index])
        self.width = 512

    def tile_copy(self, i, slot):
        tile = self.tile
        return pltpu.make_async_remote_copy(
            src_ref=self.staged.at[slot, pl.ds(0, tile), pl.ds(0, self.columns)],
            dst_ref=self.held.at[rows_at(i * tile, tile)],
            send_sem=self.stage_sems.at[slot],
            recv_sem=self.m.recv_sems.at[self.base + i],
            device_id=self.p.other_core(),
            device_id_type=MESH,
        )

    def send(self):
        half, tile = self.rows // 2, self.tile

        def one(i, _):
            slot = lax.rem(i, 2)
            pl.when(i >= 2)(lambda: self.tile_copy(i, slot).wait_send())
            first = (1 - self.p.core) * half + i * tile
            for part in range(self.columns // self.width):
                got = product_tile(self.left, self.right, first, tile, self.width, part)
                self.staged[slot, pl.ds(0, tile), part * self.width : (part + 1) * self.width] = got.astype(
                    jnp.bfloat16
                )
            self.tile_copy(i, slot).start()
            return 0

        lax.fori_loop(0, half // tile, one, 0)
        for slot in range(min(2, half // tile)):
            self.tile_copy(0, slot).wait_send()

    def own(self):
        half, tile = self.rows // 2, self.tile

        def one(i, _):
            self.tile_copy(i, 0).wait_recv()
            first = self.p.core * half + i * tile
            here = rows_at(i * tile, tile)
            for part in range(self.columns // self.width):
                got = product_tile(self.left, self.right, first, tile, self.width, part)
                cut = slice(part * self.width, (part + 1) * self.width)
                total = got + self.held[here, cut].astype(jnp.float32)
                self.held[here, cut] = total.astype(jnp.bfloat16)
            return 0

        lax.fori_loop(0, half // tile, one, 0)


def row_scale(values):
    return lax.rsqrt(jnp.mean(values * values, axis=-1, keepdims=True) + epsilon)


def eight(values):
    rows, columns = values.shape
    return jnp.sum(values.reshape(rows // 8, 8, columns), axis=0)


def turn_back(values, cosines, sines):
    half = values.shape[1] // 2
    swapped = jnp.concatenate([values[:, half:], values[:, :half]], axis=1)
    return values * cosines + swapped * sines


def nt(left_side, right_side):
    return lax.dot_general(
        left_side, right_side, (((1,), (1,)), ((), ())), preferred_element_type=jnp.float32
    )


def tn(left_side, right_side):
    return lax.dot_general(
        left_side, right_side, (((0,), (0,)), ((), ())), preferred_element_type=jnp.float32
    )


class Layer:
    def __init__(self, place, mover, **refs):
        self.p, self.m = place, mover
        self.__dict__.update(refs)
        self.rows = self.x1.shape[0]
        self.mine = rows_at(place.y * self.rows, self.rows)
        self.theirs = rows_at((1 - place.y) * self.rows, self.rows)

    def load(self, source, target, index):
        copy = pltpu.make_async_copy(source, target, self.local_sems.at[index])
        copy.start()
        return copy

    def begin(self):
        self.m.start(self.h2_parts.at[self.theirs], self.h2_in, Y_BASE, self.p.other_y())
        self.hid_load = self.load(self.hid_hbm, self.hid, 0)
        self.h_load = self.load(self.h2_hbm, self.hbuf, 1)
        self.own_load = self.load(self.h2_parts.at[self.mine], self.own, 2)
        self.out_load = self.load(self.out_w, self.wbuf.at[pl.ds(0, 768)], 3)

    def tiles(self, step, body):
        lax.fori_loop(0, self.rows // step, lambda i, _: (body(i * step, step), 0)[1], 0)

    def middle(self):
        self.own_load.wait()
        self.m.arrived(self.h2_in, Y_BASE, self.p.other_y())
        self.gains[...] = jnp.zeros_like(self.gains)

        def body(start, step):
            here = rows_at(start, step)
            there = rows_at(self.p.y * self.rows + start, step)
            d = self.own[here, :].astype(jnp.float32) + self.h2_in[here, :].astype(jnp.float32)
            x1 = self.x1[here, :]
            inv = row_scale(x1)
            scaled = d * self.gain2[...]
            inner = jnp.mean(scaled * x1, axis=-1, keepdims=True)
            self.gains[1] += eight(d * x1 * inv)
            d_x1 = self.g[there, :].astype(jnp.float32) + inv * (scaled - x1 * inv * inv * inner)
            self.d_x1[here, :] = d_x1
            self.d_attn[there, :] = d_x1.astype(jnp.bfloat16)

        self.tiles(16, body)
        own = self.d_attn.at[self.mine]
        self.m.start(own, own, Y_BASE + 1, self.p.other_y())

    def outward(self):
        self.m.arrived(self.d_attn.at[self.theirs], Y_BASE + 1, self.p.other_y())
        self.out_load.wait()
        for part in range(3):
            cut = slice(part * 256, (part + 1) * 256)
            self.d_o[:, cut] = nt(self.d_attn[...], self.wbuf[cut, :]).astype(jnp.bfloat16)
        self.w_loads = [
            self.load(self.q_w, self.wbuf.at[:, pl.ds(0, 768)], 3),
            self.load(self.k_w, self.wbuf.at[:, pl.ds(768, 384)], 4),
            self.load(self.v_w, self.wbuf.at[:, pl.ds(1152, 384)], 5),
        ]

    def attention(self, key_head):
        factor = HD ** (-0.5)
        c = key_head * HD
        keys, values = self.k[:, c : c + HD], self.v[:, c : c + HD]
        block = 256
        d_k = [jnp.zeros((block, HD), jnp.float32)] * 2
        d_v = [jnp.zeros((block, HD), jnp.float32)] * 2
        for head in (2 * key_head, 2 * key_head + 1):
            h = head * HD
            for i in range(2):
                here = slice(i * block, (i + 1) * block)
                n = block * (i + 1)
                query, d_out = self.q[here, h : h + HD], self.d_o[here, h : h + HD]
                column = lax.broadcasted_iota(jnp.int32, (block, n), 1)
                row = lax.broadcasted_iota(jnp.int32, (block, n), 0) + i * block
                allowed = (column <= row) & (column >= self.starts[here, :])
                masked = jnp.where(allowed, nt(query, keys[:n]) * factor, masked_score)
                exponent = jnp.exp(masked - jnp.max(masked, axis=1, keepdims=True))
                weights = exponent / jnp.sum(exponent, axis=1, keepdims=True)
                d_weights = nt(d_out, values[:n])
                inner = jnp.sum(weights * d_weights, axis=1, keepdims=True)
                d_scores = (weights * (d_weights - inner)).astype(jnp.bfloat16)
                low = weights.astype(jnp.bfloat16)
                d_query = jnp.dot(d_scores, keys[:n], preferred_element_type=jnp.float32) * factor
                turned = turn_back(d_query, self.cosines[here, :], self.sines[here, :])
                self.d_qkv[here, h : h + HD] = turned.astype(jnp.bfloat16)
                for j in range(i + 1):
                    cut = slice(j * block, (j + 1) * block)
                    d_k[j] = d_k[j] + tn(d_scores[:, cut], query) * factor
                    d_v[j] = d_v[j] + tn(low[:, cut], d_out)
        for j in range(2):
            cut = slice(j * block, (j + 1) * block)
            turned = turn_back(d_k[j], self.cosines[cut, :], self.sines[cut, :])
            self.d_qkv[cut, 768 + c : 768 + c + HD] = turned.astype(jnp.bfloat16)
            self.d_qkv[cut, 1152 + c : 1152 + c + HD] = d_v[j].astype(jnp.bfloat16)

    def h1_part(self, rows, put):
        def body(i, _):
            cut = pl.ds(pl.multiple_of(i * 256, 256), 256)
            put(cut, nt(self.d_qkv[rows, 0:1536], self.wbuf[cut, :]))
            return 0

        lax.fori_loop(0, 6, body, 0)

    def inward(self):
        for copy in self.w_loads:
            copy.wait()

        def put(cut, got):
            self.h1_out[:, cut] = got.astype(jnp.bfloat16)

        self.h1_part(self.theirs, put)
        self.m.start(self.h1_out, self.h1_in, Y_BASE + 2, self.p.other_y())

    def mlp_send(self):
        self.m.start(self.mlp_parts.at[self.theirs], self.mlp_in, Y_BASE + 3, self.p.other_y())
        self.own_load = self.load(self.mlp_parts.at[self.mine], self.own, 2)

    def finish(self):
        def put(cut, got):
            self.fbuf[:, cut] = got

        self.h1_part(self.mine, put)
        self.m.arrived(self.h1_in, Y_BASE + 2, self.p.other_y())

        def body(start, step):
            here = rows_at(start, step)
            d = self.fbuf[here, :] + self.h1_in[here, :].astype(jnp.float32)
            x = self.x[here, :].astype(jnp.float32)
            inv = row_scale(x)
            scaled = d * self.gain1[...]
            inner = jnp.mean(scaled * x, axis=-1, keepdims=True)
            self.gains[0] += eight(d * x * inv)
            self.d_x1[here, :] = self.d_x1[here, :] + inv * (scaled - x * inv * inv * inner)

        self.tiles(16, body)
        copy = self.load(self.d_x1, self.tokens_out, 6)
        self.m.left.append((None, copy.wait))

    def layer_end(self):
        self.own_load.wait()
        self.m.arrived(self.mlp_in, Y_BASE + 3, self.p.other_y())

        def body(start, step):
            here = rows_at(start, step)
            mlp = self.own[here, :].astype(jnp.float32) + self.mlp_in[here, :].astype(jnp.float32)
            out = self.x1[here, :] + mlp
            self.gains[2] += eight(out * out)
            self.gains[3] += eight(mlp * mlp)
            self.y_low[here, :] = out.astype(jnp.bfloat16)

        self.tiles(16, body)
        copy = self.load(self.y_low, self.layer_out, 7)
        self.m.left.append((None, copy.wait))
        self.totals[0] = jnp.zeros(self.totals.shape[1:], jnp.float32)
        for row in range(4):
            self.totals[0, row : row + 1, :] = jnp.sum(self.gains[row], axis=0, keepdims=True)
        self.totals[0, 4:5, :] = self.attn_squares[...]


def sum_small(place, mover, total, slots, step):
    device = (place.other_core, place.other_x, place.other_y, place.pair_z, place.far_z)[step]()
    copy = mover.copy(total.at[step], slots.at[step], SMALL_BASE + step, device)
    copy.start()
    copy.wait()
    total[step + 1] = total[step] + slots[step]


INPUTS = (
    "hid_hbm", "g", "h2_hbm", "d_gate", "d_up", "o", "h1_hbm", "q", "k", "v", "out_w", "q_w", "k_w", "v_w",
    "x1", "x", "h2_parts", "mlp_parts", "cosines", "sines", "starts", "gain1", "gain2", "attn_squares",
)
IN_HBM = ("hid_hbm", "h2_hbm", "h1_hbm", "out_w", "q_w", "k_w", "v_w", "h2_parts", "mlp_parts")
RESULTS = ("down_out", "gate_out", "up_out", "o_out", "qkv_out", "tokens_out", "layer_out", "small_out")
PLAIN = (
    "staged", "hid", "hbuf", "own", "h2_in", "d_attn", "d_x1", "wbuf", "d_o", "h1_out", "h1_in", "mlp_in",
    "y_low", "fbuf", "gains", "totals", "slots", "stage_sems", "send_sems", "recv_sems", "keep_sems", "local_sems",
)


def backward_kernel(*refs):
    n = len(UNITS)
    names = INPUTS + RESULTS
    r = dict(zip(names, refs[: len(names)]))
    rest = refs[len(names) :]
    held, across, along = rest[:n], rest[n : 3 * n], rest[3 * n : 5 * n]
    r.update(zip(PLAIN, rest[5 * n :]))
    r["d_qkv"] = r["hid"]
    place = Place()
    mover = Mover(r["send_sems"], r["recv_sems"])
    mover.keep_sems = r["keep_sems"]
    enter(place)
    layer = Layer(place, mover, **r)
    lefts = (r["hid"], r["hbuf"], r["hbuf"], r["o"], r["hbuf"])
    rights = (r["g"], r["d_gate"], r["d_up"], r["d_attn"], r["d_qkv"])
    results = tuple(r[name] for name in RESULTS[:n])
    units = [
        Unit(i, place, mover, lefts[i], rights[i], held[i], r["staged"], r["stage_sems"]) for i in range(n)
    ]
    steps = []
    for i, (rows, columns, x_rows, z_rows, _) in enumerate(UNITS):
        for j in range(2):
            b = 2 * i + j
            block = Block(
                place, mover, held[i], across[b], along[b], results[i], b * COPIES,
                0 if j == 0 else x_rows, x_rows if j == 0 else z_rows, rows // 2, j == 0,
            )
            steps.append(block.events())

    def send(i):
        if i == 0:
            layer.hid_load.wait()
        if i == 1:
            layer.h_load.wait()
        if i == 4:
            layer.h_load = layer.load(layer.h1_hbm, layer.hbuf, 1)
            layer.h_load.wait()
        units[i].send()

    tasks = [layer.begin, layer.middle, layer.outward]
    tasks += [partial(layer.attention, i) for i in range(4)]
    tasks += [layer.inward, layer.mlp_send, layer.finish, layer.layer_end]
    tasks += [partial(sum_small, place, mover, r["totals"], r["slots"], i) for i in range(SMALL_STEPS)]
    for item in ORDER:
        if item < 5:
            send(item)
        elif item < 10:
            units[item - 5].own()
        elif item < 20:
            steps[item - 10].pop(0)()
        else:
            tasks[item - 20]()
    r["small_out"][...] = r["totals"][SMALL_STEPS]
    for when, wait in mover.left:
        guarded(when, wait)


def enter(place):
    barrier = pltpu.get_barrier_semaphore()

    def greet(device):
        pl.semaphore_signal(barrier, inc=1, device_id=device, device_id_type=MESH)

    for device in (place.other_core(), place.other_x(), place.other_y(), place.pair_z(), place.far_z()):
        greet(device)
    middle = (place.z == 1) | (place.z == 2)
    pl.when(middle)(lambda: greet(place.at(3 - place.z, place.x, place.core, place.y)))
    pl.semaphore_wait(barrier, 5 + jnp.where(middle, 1, 0))


def backward(**given):
    vmem = pl.BlockSpec(memory_space=pltpu.VMEM)
    hbm = pl.BlockSpec(memory_space=pl.ANY)
    low, full = jnp.bfloat16, jnp.float32
    own_rows, width = given["x1"].shape
    held = [pltpu.VMEM((rows // 2, columns), low) for rows, columns, *_ in UNITS]
    across, along = [], []
    for _, columns, x_rows, z_rows, _ in UNITS:
        across += [pltpu.VMEM((x_rows // 2, columns), low), pltpu.VMEM((z_rows // 8, columns), low)]
        along += [pltpu.VMEM((5, x_rows // 8, columns), low), pltpu.VMEM((5, z_rows // 4, columns), low)]
    part = pltpu.VMEM((own_rows, width), low)
    plain = dict(
        staged=pltpu.VMEM((2, 256, 2048), low),
        hid=pltpu.VMEM((512, 2048), low),
        hbuf=pltpu.VMEM((512, width), low),
        own=part,
        h2_in=part,
        d_attn=pltpu.VMEM((512, width), low),
        d_x1=pltpu.VMEM((own_rows, width), full),
        wbuf=pltpu.VMEM((1536, 1536), low),
        d_o=pltpu.VMEM((512, 768), low),
        h1_out=part,
        h1_in=part,
        mlp_in=part,
        y_low=part,
        fbuf=pltpu.VMEM((own_rows, width), full),
        gains=pltpu.VMEM((4, 8, width), full),
        totals=pltpu.VMEM((SMALL_STEPS + 1, 8, width), full),
        slots=pltpu.VMEM((SMALL_STEPS, 8, width), full),
        stage_sems=pltpu.SemaphoreType.DMA((2,)),
        send_sems=pltpu.SemaphoreType.DMA((N_SEMS,)),
        recv_sems=pltpu.SemaphoreType.DMA((N_SEMS,)),
        keep_sems=pltpu.SemaphoreType.DMA((2 * len(UNITS),)),
        local_sems=pltpu.SemaphoreType.DMA((8,)),
    )
    flops = sum(2 * 512 * rows * columns for rows, columns, *_ in UNITS)
    return pl.pallas_call(
        backward_kernel,
        out_shape=[jax.ShapeDtypeStruct((rows, columns), low) for rows, columns, *_ in UNITS]
        + [
            jax.ShapeDtypeStruct((own_rows, width), full),
            jax.ShapeDtypeStruct((own_rows, width), low),
            jax.ShapeDtypeStruct((8, width), full),
        ],
        in_specs=[hbm if name in IN_HBM else vmem for name in INPUTS],
        out_specs=[hbm] * 7 + [vmem],
        scratch_shapes=held + across + along + [plain[name] for name in PLAIN],
        compiler_params=pltpu.CompilerParams(
            collective_id=0, has_side_effects=True, vmem_limit_bytes=62 << 20
        ),
        cost_estimate=pl.CostEstimate(flops=flops, bytes_accessed=80 << 20, transcendentals=0),
        name="backward",
    )(*(given[name] for name in INPUTS))


FORWARD_INPUTS = (
    "x", "lengths", "gain1", "gain2", "inverse", "q_w", "k_w", "v_w", "out_w", "gate_w", "up_w", "down_w", "g_own",
)
FORWARD_RESULTS = (
    "hid_to", "g_to", "h2_to", "d_gate_to", "d_up_to", "o_to", "h1_to", "q_to", "k_to", "v_to", "x1_to",
    "h2_parts_to", "mlp_parts_to", "cosines", "sines", "starts", "attn_squares",
)
FORWARD_PLAIN = (
    "x_in", "w_qkv", "w_out", "w_gate", "w_up", "w_down", "g", "h1", "lin", "q", "k", "v", "o", "own_part",
    "sent_part", "got_part", "x1", "h2", "d_hid", "hid", "d_gate", "d_up", "h2_parts", "mlp_parts", "squares",
    "send_sems", "recv_sems", "load_sems", "store_sems",
)
CHUNKS = 2


class Forward:
    def __init__(self, refs):
        self.__dict__.update(refs)
        self.p = Place()
        self.m = Mover(self.send_sems, self.recv_sems)
        self.rows = self.x.shape[0]
        self.step = self.rows // CHUNKS
        self.base = self.p.y * self.rows
        self.far = (1 - self.p.y) * self.rows
        self.stores = 0

    def load(self, source, target, index):
        copy = pltpu.make_async_copy(source, target, self.load_sems.at[index])
        copy.start()
        return copy

    def store(self, source, target):
        copy = pltpu.make_async_copy(source, target, self.store_sems.at[self.stores])
        self.stores += 1
        copy.start()
        self.m.left.append((None, copy.wait))

    def across(self, source, target, index):
        self.m.start(source, target, index, self.p.other_y())

    def arrived(self, target, index):
        self.m.arrived(target, index, self.p.other_y())

    def tiles(self, first, count, step, body):
        lax.fori_loop(0, count // step, lambda i, _: (body(first + i * step, step), 0)[1], 0)

    def run(self):
        step = self.step
        barrier = pltpu.get_barrier_semaphore()
        pl.semaphore_signal(barrier, inc=1, device_id=self.p.other_y(), device_id_type=MESH)
        pl.semaphore_wait(barrier, 1)
        for c in range(CHUNKS):
            part = pl.ds(c * step, step)
            self.across(self.x.at[part], self.x_in.at[part], c)
        self.across(self.g_own, self.g.at[rows_at(self.base, self.rows)], 2 * CHUNKS)
        qkv_loads = [
            self.load(self.q_w, self.w_qkv.at[:, pl.ds(0, 768)], 0),
            self.load(self.k_w, self.w_qkv.at[:, pl.ds(768, 384)], 1),
            self.load(self.v_w, self.w_qkv.at[:, pl.ds(1152, 384)], 2),
        ]
        g_load = self.load(self.g_own, self.g.at[rows_at(self.base, self.rows)], 3)
        out_load = self.load(self.out_w, self.w_out, 4)
        down_load = self.load(self.down_w, self.w_down, 5)
        gate_load = self.load(self.gate_w, self.w_gate, 6)
        up_load = self.load(self.up_w, self.w_up, 7)
        self.tables()
        self.norm1(self.x, 0, self.base, self.rows)
        for copy in qkv_loads:
            copy.wait()
        self.qkv(self.base, self.rows)
        for c in range(CHUNKS):
            self.arrived(self.x_in.at[pl.ds(c * step, step)], c)
            self.norm1(self.x_in, c * step, self.far + c * step, step)
            self.qkv(self.far + c * step, step)
        self.store(self.h1, self.h1_to)
        self.store(self.q, self.q_to)
        self.store(self.k, self.k_to)
        self.store(self.v, self.v_to)
        self.attention(self.far)
        out_load.wait()
        for c in range(CHUNKS):
            part = pl.ds(c * step, step)
            self.project(self.far + c * step, self.sent_part, c * step, step)
            self.across(self.sent_part.at[part], self.got_part.at[part], CHUNKS + c)
        self.attention(self.base)
        self.store(self.o, self.o_to)
        self.project(self.base, self.own_part, 0, self.rows)
        g_load.wait()
        down_load.wait()
        self.hidden_grad(self.base, self.rows)
        self.arrived(self.g.at[rows_at(self.far, self.rows)], 2 * CHUNKS)
        self.store(self.g, self.g_to)
        self.hidden_grad(self.far, self.rows)
        self.squares[...] = jnp.zeros_like(self.squares)
        for c in range(CHUNKS):
            self.arrived(self.got_part.at[pl.ds(c * step, step)], CHUNKS + c)
            self.norm2(c * step)
            mine = self.h2.at[rows_at(self.base + c * step, step)]
            self.across(mine, mine, 2 * CHUNKS + 1 + c)
        self.store(self.x1, self.x1_to)
        self.attn_squares[...] = jnp.sum(self.squares[...], axis=0, keepdims=True)
        gate_load.wait()
        up_load.wait()
        self.feed(self.base, self.rows)
        for c in range(CHUNKS):
            self.arrived(self.h2.at[rows_at(self.far + c * step, step)], 2 * CHUNKS + 1 + c)
            self.feed(self.far + c * step, step)
        for name in ("h2", "hid", "d_gate", "d_up", "h2_parts", "mlp_parts"):
            self.store(getattr(self, name), getattr(self, name + "_to"))
        for when, wait in self.m.left:
            guarded(when, wait)

    def tables(self):
        total = self.starts.shape[0]
        row = lax.broadcasted_iota(jnp.int32, (total, 1), 0)
        first = jnp.zeros((total, 1), jnp.int32)
        end = jnp.int32(0)
        for j in range(self.lengths.shape[1]):
            first = jnp.where(row >= end, end, first)
            end = end + self.lengths[0, j]
        self.starts[...] = first
        angles = (row - first).astype(jnp.float32) * self.inverse[...]
        self.cosines[...] = jnp.cos(angles)
        half = lax.broadcasted_iota(jnp.int32, (total, HD), 1) < HD // 2
        sines = jnp.sin(angles)
        self.sines[...] = jnp.where(half, sines, -sines)

    def norm1(self, source, source_row, row, count):
        def body(i, step):
            x = source[rows_at(source_row + i, step), :].astype(jnp.float32)
            self.h1[rows_at(row + i, step), :] = (x * row_scale(x) * self.gain1[...]).astype(jnp.bfloat16)

        self.tiles(0, count, 32, body)

    def qkv(self, row, count):
        here = rows_at(row, count)
        values = self.h1[here, :]
        for part in range(3):
            cut = slice(part * 512, (part + 1) * 512)
            self.lin[0:count, cut] = product(values, self.w_qkv[:, cut])
        cosines, sines = self.cosines[here, :], -self.sines[here, :]
        for target, first in ((self.q, 0), (self.k, 768)):
            for head in range(target.shape[1] // HD):
                linear = self.lin[0:count, first + head * HD : first + (head + 1) * HD]
                turned = turn_back(linear, cosines, sines)
                target[here, head * HD : (head + 1) * HD] = turned.astype(jnp.bfloat16)
        self.v[here, :] = self.lin[0:count, 1152:1536].astype(jnp.bfloat16)

    def attention(self, row):
        count, total = self.rows, self.q.shape[0]
        here = rows_at(row, count)
        column = lax.broadcasted_iota(jnp.int32, (count, total), 1)
        own = lax.broadcasted_iota(jnp.int32, (count, total), 0) + row
        allowed = (column <= own) & (column >= self.starts[here, :])
        for key_head in range(self.k.shape[1] // HD):
            c = key_head * HD
            keys, values = self.k[:, c : c + HD], self.v[:, c : c + HD]
            for head in (2 * key_head, 2 * key_head + 1):
                h = head * HD
                raw = nt(self.q[here, h : h + HD], keys) * HD ** (-0.5)
                masked = jnp.where(allowed, raw, masked_score)
                exponent = jnp.exp(masked - jnp.max(masked, axis=1, keepdims=True))
                weights = exponent / jnp.sum(exponent, axis=1, keepdims=True)
                out = product(weights.astype(jnp.bfloat16), values)
                self.o[here, h : h + HD] = out.astype(jnp.bfloat16)

    def project(self, row, target, target_row, count):
        values = self.o[rows_at(row, count), :]
        for part in range(3):
            cut = slice(part * 512, (part + 1) * 512)
            target[target_row : target_row + count, cut] = product(values, self.w_out[:, cut]).astype(target.dtype)

    def hidden_grad(self, row, count):
        here = rows_at(row, count)

        def body(i, _):
            cut = pl.ds(pl.multiple_of(i * 256, 256), 256)
            self.d_hid[here, cut] = nt(self.g[here, :], self.w_down[cut, :])
            return 0

        lax.fori_loop(0, self.w_down.shape[0] // 256, body, 0)

    def norm2(self, start):
        def body(i, step):
            here = rows_at(i, step)
            attn = self.own_part[here, :] + self.got_part[here, :].astype(jnp.float32)
            self.squares[...] += eight(attn * attn)
            x1 = self.x[here, :].astype(jnp.float32) + attn
            self.x1[here, :] = x1
            self.h2[rows_at(self.base + i, step), :] = (x1 * row_scale(x1) * self.gain2[...]).astype(jnp.bfloat16)

        self.tiles(start, self.step, 16, body)

    def feed(self, row, count):
        here = rows_at(row, count)

        def body(i, _):
            cut = pl.ds(pl.multiple_of(i * 256, 256), 256)
            values = self.h2[here, :]
            gate = product(values, self.w_gate[:, cut])
            up = product(values, self.w_up[:, cut])
            d_hid = self.d_hid[here, cut]
            sig = 1.0 / (1.0 + jnp.exp(-gate))
            self.hid[here, cut] = (gate * sig * up).astype(jnp.bfloat16)
            self.d_gate[here, cut] = (d_hid * up * sig * (1.0 + gate * (1.0 - sig))).astype(jnp.bfloat16)
            self.d_up[here, cut] = (d_hid * gate * sig).astype(jnp.bfloat16)
            return 0

        lax.fori_loop(0, self.w_gate.shape[1] // 256, body, 0)

        def back(i, _):
            cut = pl.ds(pl.multiple_of(i * 256, 256), 256)
            total = nt(self.d_gate[here, :], self.w_gate[cut, :]) + nt(self.d_up[here, :], self.w_up[cut, :])
            self.h2_parts[here, cut] = total.astype(jnp.bfloat16)
            self.mlp_parts[here, cut] = product(self.hid[here, :], self.w_down[:, cut]).astype(jnp.bfloat16)
            return 0

        lax.fori_loop(0, self.w_down.shape[1] // 256, back, 0)


def forward_kernel(*refs):
    names = FORWARD_INPUTS + FORWARD_RESULTS + FORWARD_PLAIN
    Forward(dict(zip(names, refs))).run()


def forward(**given):
    vmem = pl.BlockSpec(memory_space=pltpu.VMEM)
    hbm = pl.BlockSpec(memory_space=pl.ANY)
    smem = pl.BlockSpec(memory_space=pltpu.SMEM)
    low, full = jnp.bfloat16, jnp.float32
    own, width = given["x"].shape
    total = 2 * own
    units = given["gate_w"].shape[1]
    q_cols, k_cols = given["q_w"].shape[1], given["k_w"].shape[1]
    shapes = dict(
        hid_to=((total, units), low), g_to=((total, width), low), h2_to=((total, width), low),
        d_gate_to=((total, units), low), d_up_to=((total, units), low), o_to=((total, q_cols), low),
        h1_to=((total, width), low), q_to=((total, q_cols), low), k_to=((total, k_cols), low),
        v_to=((total, k_cols), low), x1_to=((own, width), full), h2_parts_to=((total, width), low),
        mlp_parts_to=((total, width), low), cosines=((total, HD), full), sines=((total, HD), full),
        starts=((total, 1), jnp.int32), attn_squares=((1, width), full),
    )
    plain = dict(
        x_in=((own, width), low), w_qkv=((width, q_cols + 2 * k_cols), low), w_out=((q_cols, width), low),
        w_gate=((width, units), low), w_up=((width, units), low), w_down=((units, width), low),
        g=((total, width), low), h1=((total, width), low), lin=((own, q_cols + 2 * k_cols), full),
        q=((total, q_cols), low), k=((total, k_cols), low), v=((total, k_cols), low), o=((total, q_cols), low),
        own_part=((own, width), full), sent_part=((own, width), low), got_part=((own, width), low),
        x1=((own, width), full), h2=((total, width), low), d_hid=((total, units), full), hid=((total, units), low),
        d_gate=((total, units), low), d_up=((total, units), low), h2_parts=((total, width), low),
        mlp_parts=((total, width), low), squares=((8, width), full),
    )
    scratch = [pltpu.VMEM(*plain[name]) for name in FORWARD_PLAIN if name in plain]
    copies = 3 * CHUNKS + 1
    scratch += [pltpu.SemaphoreType.DMA((n,)) for n in (copies, copies, 8, 16)]
    spaces = dict.fromkeys(("q_w", "k_w", "v_w", "out_w", "gate_w", "up_w", "down_w", "g_own"), hbm)
    spaces["lengths"] = smem
    out = pl.pallas_call(
        forward_kernel,
        out_shape=[jax.ShapeDtypeStruct(*shapes[name]) for name in FORWARD_RESULTS],
        in_specs=[spaces.get(name, vmem) for name in FORWARD_INPUTS],
        out_specs=[hbm if name.endswith("_to") else vmem for name in FORWARD_RESULTS],
        scratch_shapes=scratch,
        compiler_params=pltpu.CompilerParams(
            collective_id=1, has_side_effects=True, vmem_limit_bytes=62 << 20
        ),
        cost_estimate=pl.CostEstimate(flops=26 * 10**9, bytes_accessed=60 << 20, transcendentals=0),
        name="forward",
    )(*(given[name] for name in FORWARD_INPUTS))
    return dict(zip(FORWARD_RESULTS, out))


def dp_sum(terms):
    low = lax.psum(tuple(term.astype(jnp.bfloat16) for term in terms), "dp")
    return tuple(term.astype(jnp.float32) for term in low)


def low_scatter(partial):
    return lax.psum_scatter(
        partial.astype(jnp.bfloat16), "tensor", scatter_dimension=0, tiled=True
    ).astype(jnp.float32)


def body(
    tokens,
    lengths,
    first_gain,
    query_weight,
    key_weight,
    value_weight,
    output_weight,
    second_gain,
    gate_weight,
    up_weight,
    down_weight,
    out_cotangent,
):
    inputs = tokens.astype(jnp.float32)
    normed1, inv_first = norm_rows(inputs, first_gain)
    normed1 = normed1.astype(jnp.bfloat16)
    full_first = lax.all_gather(normed1, "tensor", axis=0, tiled=True)
    total_rows = full_first.shape[0]
    places, segment, cosine_table, sine_table, _ = tables(lengths[0], total_rows, HD // 2)
    kv_heads = key_weight.shape[1] // HD
    groups = query_weight.shape[1] // key_weight.shape[1]
    query = rotate(product(full_first, query_weight), cosine_table, sine_table, 1.0).astype(
        jnp.bfloat16
    )
    keys = rotate(product(full_first, key_weight), cosine_table, sine_table, 1.0).astype(
        jnp.bfloat16
    )
    values = product(full_first, value_weight).astype(jnp.bfloat16)
    block_rows = min(block_limit, total_rows)
    block_count = total_rows // block_rows
    query_blocks = query.reshape(block_count, block_rows, kv_heads, groups, HD)
    seg_blocks = segment.reshape(block_count, block_rows)
    place_blocks = places.reshape(block_count, block_rows)
    key_three = keys.reshape(total_rows, kv_heads, HD)
    value_three = values.reshape(total_rows, kv_heads, HD)
    factor = HD ** (-0.5)

    def scores(query_block, seg_block, place_block):
        raw = (
            jnp.einsum("qcgd,kcd->cgqk", query_block, key_three, preferred_element_type=jnp.float32)
            * factor
        )
        allowed = (seg_block[:, None] == segment[None, :]) & (
            place_block[:, None] >= places[None, :]
        )
        return (jnp.where(allowed[None, None], raw, masked_score), allowed)

    def forward_block(piece_set):
        query_block, seg_block, place_block = piece_set
        masked, allowed = scores(query_block, seg_block, place_block)
        highest = jnp.max(masked, axis=-1, keepdims=True)
        exponent = jnp.exp(masked - highest)
        denominator = jnp.sum(exponent, axis=-1, keepdims=True)
        weights = exponent / denominator
        output = jnp.einsum(
            "cgqk,kcd->qcgd",
            weights.astype(jnp.bfloat16),
            value_three,
            preferred_element_type=jnp.float32,
        )
        stored = (highest + jnp.log(denominator))[..., 0]
        return (output.reshape(block_rows, -1), stored)

    out_blocks, kept_blocks = lax.map(forward_block, (query_blocks, seg_blocks, place_blocks))
    attended = out_blocks.reshape(total_rows, -1).astype(jnp.bfloat16)
    attn_rows = low_scatter(product(attended, output_weight))
    middle = inputs + attn_rows
    normed2, inv_second = norm_rows(middle, second_gain)
    normed2 = normed2.astype(jnp.bfloat16)
    full_second = lax.all_gather(normed2, "tensor", axis=0, tiled=True)
    gate_value = product(full_second, gate_weight)
    upward = product(full_second, up_weight)
    gate_sig = jax.nn.sigmoid(gate_value)
    hidden = (gate_value * gate_sig * upward).astype(jnp.bfloat16)
    mlp_rows = low_scatter(product(hidden, down_weight))
    layer_out = middle + mlp_rows
    squares = jnp.stack(
        [
            jnp.sum(layer_out * layer_out),
            jnp.sum(attn_rows * attn_rows),
            jnp.sum(mlp_rows * mlp_rows),
        ]
    )
    grad_full = lax.all_gather(out_cotangent, "tensor", axis=0, tiled=True)
    grad_hidden = times_cols(grad_full, down_weight)
    down_g = times_rows(hidden, grad_full)
    gate_slope = gate_sig * (1.0 + gate_value * (1.0 - gate_sig))
    grad_gate = (grad_hidden * upward * gate_slope).astype(jnp.bfloat16)
    grad_up = (grad_hidden * gate_value * gate_sig).astype(jnp.bfloat16)
    gate_g = times_rows(full_second, grad_gate)
    up_g = times_rows(full_second, grad_up)
    gate_g, up_g, down_g = dp_sum((gate_g, up_g, down_g))
    grad_normed2 = low_scatter(
        times_cols(grad_gate, gate_weight) + times_cols(grad_up, up_weight)
    )
    second_rows, grad_mid_norm = norm_back(middle, inv_second, second_gain, grad_normed2)
    grad_middle = out_cotangent.astype(jnp.float32) + grad_mid_norm
    grad_attn_full = lax.all_gather(grad_middle.astype(jnp.bfloat16), "tensor", axis=0, tiled=True)
    output_g = times_rows(attended, grad_attn_full)
    grad_out = times_cols(grad_attn_full, output_weight).astype(jnp.bfloat16)
    grad_blocks = grad_out.reshape(block_count, block_rows, kv_heads, groups, HD)

    def backward_block(running, piece_set):
        key_acc, value_acc = running
        query_block, seg_block, place_block, grad_block, stored = piece_set
        masked, allowed = scores(query_block, seg_block, place_block)
        weights = jnp.where(allowed[None, None], jnp.exp(masked - stored[..., None]), 0.0)
        grad_weights = jnp.einsum(
            "qcgd,kcd->cgqk", grad_block, value_three, preferred_element_type=jnp.float32
        )
        row_inner = jnp.sum(weights * grad_weights, axis=-1, keepdims=True)
        grad_scores = (weights * (grad_weights - row_inner)).astype(jnp.bfloat16)
        grad_query = (
            jnp.einsum("cgqk,kcd->qcgd", grad_scores, key_three, preferred_element_type=jnp.float32)
            * factor
        )
        key_acc = (
            key_acc
            + jnp.einsum(
                "cgqk,qcgd->kcd", grad_scores, query_block, preferred_element_type=jnp.float32
            )
            * factor
        )
        value_acc = value_acc + jnp.einsum(
            "cgqk,qcgd->kcd",
            weights.astype(jnp.bfloat16),
            grad_block,
            preferred_element_type=jnp.float32,
        )
        return ((key_acc, value_acc), grad_query.reshape(block_rows, -1))

    zeros_kv = jnp.zeros((total_rows, kv_heads, HD), jnp.float32)
    (key_rot_grad, value_acc_grad), query_rot_grad = lax.scan(
        backward_block,
        (zeros_kv, zeros_kv),
        (query_blocks, seg_blocks, place_blocks, grad_blocks, kept_blocks),
    )
    query_lin = rotate(
        query_rot_grad.reshape(total_rows, -1), cosine_table, sine_table, -1.0
    ).astype(jnp.bfloat16)
    key_lin = rotate(key_rot_grad.reshape(total_rows, -1), cosine_table, sine_table, -1.0).astype(
        jnp.bfloat16
    )
    value_lin = value_acc_grad.reshape(total_rows, -1).astype(jnp.bfloat16)
    query_g = times_rows(full_first, query_lin)
    key_g = times_rows(full_first, key_lin)
    value_g = times_rows(full_first, value_lin)
    grad_normed1 = low_scatter(
        times_cols(query_lin, query_weight)
        + times_cols(key_lin, key_weight)
        + times_cols(value_lin, value_weight)
    )
    first_rows, grad_in_norm = norm_back(inputs, inv_first, first_gain, grad_normed1)
    tokens_grad = grad_middle + grad_in_norm
    gain_rows = jnp.stack([first_rows, second_rows])
    query_g, key_g, value_g, output_g = dp_sum((query_g, key_g, value_g, output_g))
    gain_rows, squares = lax.psum((gain_rows, squares), ("dp", "tensor"))
    rms_values = jnp.sqrt(squares / (total_rows * lax.axis_size("dp")))
    return (
        layer_out.astype(jnp.bfloat16),
        tokens_grad,
        gain_rows[0],
        query_g,
        key_g,
        value_g,
        output_g,
        gain_rows[1],
        gate_g,
        up_g,
        down_g,
        rms_values,
    )


def fused_body(
    tokens,
    lengths,
    first_gain,
    query_weight,
    key_weight,
    value_weight,
    output_weight,
    second_gain,
    gate_weight,
    up_weight,
    down_weight,
    out_cotangent,
):
    half_size = HD // 2
    inverse = rope_base ** (-2.0 * jnp.arange(half_size, dtype=jnp.float32) / (2 * half_size))
    made = forward(
        x=tokens,
        lengths=lengths,
        gain1=first_gain[None],
        gain2=second_gain[None],
        inverse=jnp.concatenate([inverse, inverse])[None],
        q_w=query_weight,
        k_w=key_weight,
        v_w=value_weight,
        out_w=output_weight,
        gate_w=gate_weight,
        up_w=up_weight,
        down_w=down_weight,
        g_own=out_cotangent,
    )
    *sums, tokens_grad, layer_out, small = backward(
        hid_hbm=made["hid_to"],
        g=made["g_to"],
        h2_hbm=made["h2_to"],
        d_gate=made["d_gate_to"],
        d_up=made["d_up_to"],
        o=made["o_to"],
        h1_hbm=made["h1_to"],
        q=made["q_to"],
        k=made["k_to"],
        v=made["v_to"],
        out_w=output_weight,
        q_w=query_weight,
        k_w=key_weight,
        v_w=value_weight,
        x1=made["x1_to"],
        x=tokens,
        h2_parts=made["h2_parts_to"],
        mlp_parts=made["mlp_parts_to"],
        cosines=made["cosines"],
        sines=made["sines"],
        starts=made["starts"],
        gain1=first_gain[None],
        gain2=second_gain[None],
        attn_squares=made["attn_squares"],
    )
    down_g, gate_g, up_g, output_g, qkv_g = (part.astype(jnp.float32) for part in sums)
    q_cols, k_cols = query_weight.shape[1], key_weight.shape[1]
    squares = jnp.stack([jnp.sum(small[2]), jnp.sum(small[4]), jnp.sum(small[3])])
    rms_values = jnp.sqrt(squares / (2 * tokens.shape[0] * lax.axis_size("dp")))
    return (
        layer_out,
        tokens_grad,
        small[0],
        qkv_g[:, :q_cols],
        qkv_g[:, q_cols : q_cols + k_cols],
        qkv_g[:, q_cols + k_cols :],
        output_g,
        small[1],
        gate_g,
        up_g,
        down_g,
        rms_values,
    )


def solution(mesh):
    in_specs = (
        P(("dp", "tensor"), None),
        P("dp", None),
        P(),
        P(None, "tensor"),
        P(None, "tensor"),
        P(None, "tensor"),
        P("tensor", None),
        P(),
        P(None, "tensor"),
        P(None, "tensor"),
        P("tensor", None),
        P(("dp", "tensor"), None),
    )
    out_specs = (
        P(("dp", "tensor"), None),
        P(("dp", "tensor"), None),
        P(),
        P(None, "tensor"),
        P(None, "tensor"),
        P(None, "tensor"),
        P("tensor", None),
        P(),
        P(None, "tensor"),
        P(None, "tensor"),
        P("tensor", None),
        P(),
    )
    fused = dict(mesh.shape) == {"dp": 16, "tensor": 2}
    chosen = fused_body if fused else body
    return jax.shard_map(chosen, mesh=mesh, in_specs=in_specs, out_specs=out_specs, check_vma=False)
```

```python
from functools import partial

import jax
import jax.numpy as jnp
import numpy as np
from jax import lax
from jax.experimental import pallas as pl
from jax.experimental.pallas import tpu as pltpu
from jax.sharding import PartitionSpec as P

HD = 96


epsilon = 1e-05
rope_base = 10000.0
masked_score = -1e30
block_limit = 512


def product(left_side, right_side):
    return jnp.dot(left_side, right_side, preferred_element_type=jnp.float32)


def times_rows(left_side, right_side):
    return lax.dot_general(
        left_side, right_side, (((0,), (0,)), ((), ())), preferred_element_type=jnp.float32
    )


def times_cols(left_side, right_side):
    return lax.dot_general(
        left_side, right_side, (((1,), (1,)), ((), ())), preferred_element_type=jnp.float32
    )


def tables(lens_row, total_rows, half_size):
    count = lens_row.shape[0]
    earlier = jnp.arange(count)[:, None] <= jnp.arange(count)[None, :]
    seq_ends = jnp.sum(jnp.where(earlier, lens_row[:, None], 0), axis=0, dtype=jnp.int32)
    starts = seq_ends - lens_row
    places = jnp.arange(total_rows, dtype=jnp.int32)
    segment = jnp.sum(
        (places[:, None] >= seq_ends[None, :]).astype(jnp.int32), axis=1, dtype=jnp.int32
    )
    member = segment[:, None] == jnp.arange(lens_row.shape[0], dtype=jnp.int32)[None, :]
    firsts = jnp.sum(jnp.where(member, starts[None, :], 0), axis=1, dtype=jnp.int32)
    position = places - firsts
    inverse = rope_base ** (-2.0 * jnp.arange(half_size, dtype=jnp.float32) / (2 * half_size))
    angles = position.astype(jnp.float32)[:, None] * inverse[None, :]
    return (places, segment, jnp.cos(angles), jnp.sin(angles), firsts)


def rotate(values, cosine_table, sine_table, direction):
    total_rows = values.shape[0]
    half_size = cosine_table.shape[1]
    shaped = values.reshape(total_rows, -1, 2 * half_size)
    first_half = shaped[..., :half_size]
    second = shaped[..., half_size:]
    cos_b = cosine_table[:, None, :]
    sin_b = sine_table[:, None, :] * direction
    turned = jnp.concatenate(
        [first_half * cos_b - second * sin_b, second * cos_b + first_half * sin_b], axis=-1
    )
    return turned.reshape(total_rows, -1)


def norm_rows(values, gain):
    inv_rms = lax.rsqrt(jnp.mean(values * values, axis=-1, keepdims=True) + epsilon)
    return (values * inv_rms * gain, inv_rms)


def norm_back(values, inv_rms, gain, upstream):
    scaled = upstream * gain
    row_inner = jnp.mean(scaled * values, axis=-1, keepdims=True)
    gain_rows = jnp.sum(upstream * values * inv_rms, axis=0)
    return (gain_rows, inv_rms * (scaled - values * inv_rms * inv_rms * row_inner))


ORDER = (
    20, 0, 1, 5, 10, 11, 2, 6, 7, 11, 21, 11, 10, 13, 11, 11, 10, 12, 11, 22, 3, 10, 23, 8, 10, 13,
    24, 25, 11, 13, 12, 10, 26, 27, 11, 28, 4, 13, 13, 12, 9, 10, 13, 15, 11, 13, 16, 10, 10, 12,
    29, 11, 11, 15, 16, 14, 12, 30, 15, 31, 32, 10, 13, 16, 33, 34, 35, 15, 15, 12, 13, 16, 18, 14,
    12, 15, 14, 13, 13, 16, 14, 12, 12, 16, 14, 18, 16, 15, 14, 19, 16, 16, 18, 14, 17, 18, 14, 14,
    12, 15, 18, 19, 16, 15, 17, 19, 17, 18, 15, 15, 14, 19, 19, 17, 17, 19, 17, 18, 19, 17, 18, 18,
    19, 17, 19, 17, 19, 19, 18, 17, 17,
)


MESH = pl.DeviceIdType.MESH
LINE = 4
UNITS = (
    (2048, 1536, 640, 384, 256),
    (1536, 2048, 512, 256, 256),
    (1536, 2048, 384, 384, 256),
    (768, 1536, 256, 128, 128),
    (1536, 1536, 512, 256, 256),
)
COPIES = 16
TILE_BASE = 2 * len(UNITS) * COPIES
TILES = tuple(rows // 2 // tile for rows, _, _, _, tile in UNITS)
SMALL_BASE = TILE_BASE + sum(TILES)
SMALL_STEPS = 5
Y_BASE = SMALL_BASE + SMALL_STEPS
N_SEMS = Y_BASE + 4


def rows_at(start, size):
    return pl.ds(pl.multiple_of(start, 16), size)


class Place:
    def __init__(self):
        dp = lax.axis_index("dp")
        self.dp = dp
        self.y = lax.axis_index("tensor")
        self.core = lax.rem(dp, 2)
        self.x = lax.rem(dp // 2, 2)
        self.z = dp // 4

    def at(self, z, x, core, y):
        return ((z * 2 + x) * 2 + core, y)

    def other_core(self):
        return self.at(self.z, self.x, 1 - self.core, self.y)

    def other_x(self):
        return self.at(self.z, 1 - self.x, self.core, self.y)

    def other_y(self):
        return self.at(self.z, self.x, self.core, 1 - self.y)

    def up(self):
        return self.at(self.z + 1, self.x, self.core, self.y)

    def down(self):
        return self.at(self.z - 1, self.x, self.core, self.y)

    def pair_z(self):
        return self.at(self.z + 1 - 2 * lax.rem(self.z, 2), self.x, self.core, self.y)

    def far_z(self):
        return self.at(lax.rem(self.z + 2, LINE), self.x, self.core, self.y)


class Mover:
    def __init__(self, send_sems, recv_sems):
        self.send_sems = send_sems
        self.recv_sems = recv_sems
        self.left = []

    def copy(self, source, target, index, device):
        return pltpu.make_async_remote_copy(
            src_ref=source,
            dst_ref=target,
            send_sem=self.send_sems.at[index],
            recv_sem=self.recv_sems.at[index],
            device_id=device,
            device_id_type=MESH,
        )

    def start(self, source, target, index, device, when=None):
        copy = self.copy(source, target, index, device)
        guarded(when, copy.start)
        self.left.append((when, copy.wait_send))

    def arrived(self, target, index, device):
        self.copy(target, target, index, device).wait_recv()


def guarded(when, action):
    if when is None:
        action()
    else:
        pl.when(when)(action)


def add_rows(target, target_row, source, source_row, size):
    step = 16

    def one(i, _):
        here = rows_at(target_row + i * step, step)
        there = rows_at(source_row + i * step, step)
        total = target[here, :].astype(jnp.float32) + source[there, :].astype(jnp.float32)
        target[here, :] = total.astype(target.dtype)
        return 0

    lax.fori_loop(0, size // step, one, 0)


def fall_slot(step):
    return 0 if step == 0 else 2 + step


class Block:
    def __init__(self, place, mover, held, across, along, result, base, start, size, half_rows, x_first):
        self.p = place
        self.m = mover
        self.held = held
        self.across = across
        self.along = along
        self.result = result
        self.base = base
        self.start = start
        self.size = size
        self.half_rows = half_rows
        self.x_first = x_first
        self.chunk = size // 8 if x_first else size // 4
        self.origin = start + place.x * (size // 2) if x_first else start

    def part(self, chunk):
        return self.held.at[rows_at(self.origin + chunk * self.chunk, self.chunk)]

    def final(self, row, size):
        return self.result.at[rows_at(self.p.core * self.half_rows + row, size)]

    def final_part(self, chunk):
        return self.final(self.origin + chunk * self.chunk, self.chunk)

    def keep(self, row, size):
        index = self.base // COPIES
        copy = pltpu.make_async_copy(
            self.held.at[rows_at(row, size)], self.final(row, size), self.m.keep_sems.at[index]
        )
        copy.start()
        self.kept = copy

    def events(self):
        line = [self.line_start, lambda: self.line_add(0), lambda: self.line_add(1), lambda: self.line_add(2)]
        spread = [lambda: self.spread(1), lambda: self.spread(2), lambda: self.spread(3)]
        if self.x_first:
            return [self.x_send, self.x_add] + line[1:] + spread + [self.x_return, self.x_done]
        return line + [self.pair_send, self.pair_add, self.pair_done] + spread + [self.z_done]

    def line_start(self):
        p = self.p
        for step in range(3):
            self.m.start(self.part(3 - step), self.along.at[step], self.base + step, p.up(), p.z == 0)
            self.m.start(self.part(step), self.along.at[fall_slot(step)], self.base + 3 + step, p.down(), p.z == LINE - 1)

    def line_add(self, step):
        p = self.p
        rising = jnp.minimum(p.z + 2 - step, 3)
        falling = jnp.maximum(p.z - 2 + step, 0)
        goes_up = (p.z >= 1) & (p.z <= step + 1)
        goes_down = (p.z <= 2) & (p.z >= 2 - step)

        def take_rising():
            self.m.arrived(self.along.at[step], self.base + step, p.down())
            add_rows(self.held, self.origin + rising * self.chunk, self.along.at[step], 0, self.chunk)

        def take_falling():
            self.m.arrived(self.along.at[fall_slot(step)], self.base + 3 + step, p.up())
            add_rows(self.held, self.origin + falling * self.chunk, self.along.at[fall_slot(step)], 0, self.chunk)

        pl.when(goes_up)(take_rising)
        if step < 2:
            self.m.start(self.part(rising), self.along.at[step + 1], self.base + step + 1, p.up(), goes_up)
        pl.when(goes_down)(take_falling)
        if step < 2:
            self.m.start(self.part(falling), self.along.at[fall_slot(step + 1)], self.base + 4 + step, p.down(), goes_down)
        elif self.x_first:
            self.keep(self.origin + p.z * self.chunk, self.chunk)
            self.own_spread(self.part(p.z))

    def own_spread(self, source):
        p = self.p
        target = self.final_part(p.z)
        self.m.start(source, target, self.base + 6, p.up(), p.z < 3)
        self.m.start(source, target, self.base + 9, p.down(), p.z > 0)

    def spread(self, distance):
        p = self.p
        below = self.final_part(jnp.maximum(p.z - distance, 0))
        above = self.final_part(jnp.minimum(p.z + distance, 3))

        pl.when(p.z >= distance)(lambda: self.m.arrived(below, self.base + 5 + distance, p.down()))
        if distance < 3:
            self.m.start(below, below, self.base + 6 + distance, p.up(), (p.z >= distance) & (p.z < 3))
        pl.when(p.z <= 3 - distance)(lambda: self.m.arrived(above, self.base + 8 + distance, p.up()))
        if distance < 3:
            self.m.start(above, above, self.base + 9 + distance, p.down(), (p.z <= 3 - distance) & (p.z > 0))

    def x_part(self, which):
        half = self.size // 2
        return self.held.at[rows_at(self.start + which * half, half)]

    def x_send(self):
        self.m.start(self.x_part(1 - self.p.x), self.across, self.base + 12, self.p.other_x())

    def x_add(self):
        self.m.arrived(self.across, self.base + 12, self.p.other_x())
        add_rows(self.held, self.origin, self.across, 0, self.size // 2)
        self.line_start()

    def x_final(self, which):
        half = self.size // 2
        return self.final(self.start + which * half, half)

    def x_return(self):
        p = self.p
        self.kept.wait()
        mine = self.x_final(p.x)
        self.m.start(mine, mine, self.base + 13, p.other_x())
        self.give(p.x * (self.size // 2), self.size // 2, 14)

    def x_done(self):
        p = self.p
        self.m.arrived(self.x_final(1 - p.x), self.base + 13, p.other_x())
        self.give((1 - p.x) * (self.size // 2), self.size // 2, 15)

    def pair_row(self, which):
        return self.start + self.p.z * self.chunk + which * (self.chunk // 2)

    def pair_send(self):
        half = self.chunk // 2
        source = self.held.at[rows_at(self.pair_row(1 - self.p.x), half)]
        self.m.start(source, self.across, self.base + 12, self.p.other_x())

    def pair_add(self):
        p = self.p
        half = self.chunk // 2
        self.m.arrived(self.across, self.base + 12, p.other_x())
        row = self.pair_row(p.x)
        add_rows(self.held, row, self.across, 0, half)
        self.keep(row, half)
        self.m.start(self.held.at[rows_at(row, half)], self.final(row, half), self.base + 13, p.other_x())

    def pair_done(self):
        p = self.p
        half = self.chunk // 2
        self.m.arrived(self.final(self.pair_row(1 - p.x), half), self.base + 13, p.other_x())
        self.kept.wait()
        self.own_spread(self.final_part(p.z))

    def z_done(self):
        self.give(0, self.size, 14)

    def give(self, offset, size, slot):
        p = self.p
        source = self.final(self.start + offset, size)
        self.m.start(source, source, self.base + slot, p.other_core())
        other = self.result.at[rows_at((1 - p.core) * self.half_rows + self.start + offset, size)]
        self.m.left.append((None, lambda: self.m.arrived(other, self.base + slot, p.other_core())))


def product_tile(left, right, first, tile, width, part):
    columns = pl.ds(pl.multiple_of(first, 128), tile)
    return lax.dot_general(
        left[:, columns], right[:, part * width : (part + 1) * width],
        (((0,), (0,)), ((), ())), preferred_element_type=jnp.float32,
    )


class Unit:
    def __init__(self, index, place, mover, left, right, held, staged, stage_sems):
        self.index = index
        self.rows, self.columns, _, _, self.tile = UNITS[index]
        self.p, self.m = place, mover
        self.left, self.right, self.held = left, right, held
        self.staged, self.stage_sems = staged, stage_sems
        self.base = TILE_BASE + sum(TILES[:index])
        self.width = 512

    def tile_copy(self, i, slot):
        tile = self.tile
        return pltpu.make_async_remote_copy(
            src_ref=self.staged.at[slot, pl.ds(0, tile), pl.ds(0, self.columns)],
            dst_ref=self.held.at[rows_at(i * tile, tile)],
            send_sem=self.stage_sems.at[slot],
            recv_sem=self.m.recv_sems.at[self.base + i],
            device_id=self.p.other_core(),
            device_id_type=MESH,
        )

    def send(self):
        half, tile = self.rows // 2, self.tile

        def one(i, _):
            slot = lax.rem(i, 2)
            pl.when(i >= 2)(lambda: self.tile_copy(i, slot).wait_send())
            first = (1 - self.p.core) * half + i * tile
            for part in range(self.columns // self.width):
                got = product_tile(self.left, self.right, first, tile, self.width, part)
                self.staged[slot, pl.ds(0, tile), part * self.width : (part + 1) * self.width] = got.astype(
                    jnp.bfloat16
                )
            self.tile_copy(i, slot).start()
            return 0

        lax.fori_loop(0, half // tile, one, 0)
        for slot in range(min(2, half // tile)):
            self.tile_copy(0, slot).wait_send()

    def own(self):
        half, tile = self.rows // 2, self.tile

        def one(i, _):
            self.tile_copy(i, 0).wait_recv()
            first = self.p.core * half + i * tile
            here = rows_at(i * tile, tile)
            for part in range(self.columns // self.width):
                got = product_tile(self.left, self.right, first, tile, self.width, part)
                cut = slice(part * self.width, (part + 1) * self.width)
                total = got + self.held[here, cut].astype(jnp.float32)
                self.held[here, cut] = total.astype(jnp.bfloat16)
            return 0

        lax.fori_loop(0, half // tile, one, 0)


def row_scale(values):
    return lax.rsqrt(jnp.mean(values * values, axis=-1, keepdims=True) + epsilon)


def eight(values):
    rows, columns = values.shape
    return jnp.sum(values.reshape(rows // 8, 8, columns), axis=0)


def turn_back(values, cosines, sines):
    half = values.shape[1] // 2
    swapped = jnp.concatenate([values[:, half:], values[:, :half]], axis=1)
    return values * cosines + swapped * sines


def nt(left_side, right_side):
    return lax.dot_general(
        left_side, right_side, (((1,), (1,)), ((), ())), preferred_element_type=jnp.float32
    )


def tn(left_side, right_side):
    return lax.dot_general(
        left_side, right_side, (((0,), (0,)), ((), ())), preferred_element_type=jnp.float32
    )


class Layer:
    def __init__(self, place, mover, **refs):
        self.p, self.m = place, mover
        self.__dict__.update(refs)
        self.rows = self.x1.shape[0]
        self.mine = rows_at(place.y * self.rows, self.rows)
        self.theirs = rows_at((1 - place.y) * self.rows, self.rows)

    def load(self, source, target, index):
        copy = pltpu.make_async_copy(source, target, self.local_sems.at[index])
        copy.start()
        return copy

    def begin(self):
        self.m.start(self.h2_parts.at[self.theirs], self.h2_in, Y_BASE, self.p.other_y())
        self.hid_load = self.load(self.hid_hbm, self.hid, 0)
        self.h_load = self.load(self.h2_hbm, self.hbuf, 1)
        self.own_load = self.load(self.h2_parts.at[self.mine], self.own, 2)
        self.out_load = self.load(self.out_w, self.wbuf.at[pl.ds(0, 768)], 3)

    def tiles(self, step, body):
        lax.fori_loop(0, self.rows // step, lambda i, _: (body(i * step, step), 0)[1], 0)

    def middle(self):
        self.own_load.wait()
        self.m.arrived(self.h2_in, Y_BASE, self.p.other_y())
        self.gains[...] = jnp.zeros_like(self.gains)

        def body(start, step):
            here = rows_at(start, step)
            there = rows_at(self.p.y * self.rows + start, step)
            d = self.own[here, :].astype(jnp.float32) + self.h2_in[here, :].astype(jnp.float32)
            x1 = self.x1[here, :]
            inv = row_scale(x1)
            scaled = d * self.gain2[...].reshape(1, -1)
            inner = jnp.mean(scaled * x1, axis=-1, keepdims=True)
            self.gains[1] += eight(d * x1 * inv)
            d_x1 = self.g[there, :].astype(jnp.float32) + inv * (scaled - x1 * inv * inv * inner)
            self.d_x1[here, :] = d_x1
            self.d_attn[there, :] = d_x1.astype(jnp.bfloat16)

        self.tiles(16, body)
        own = self.d_attn.at[self.mine]
        self.m.start(own, own, Y_BASE + 1, self.p.other_y())

    def outward(self):
        self.m.arrived(self.d_attn.at[self.theirs], Y_BASE + 1, self.p.other_y())
        self.out_load.wait()
        for part in range(3):
            cut = slice(part * 256, (part + 1) * 256)
            self.d_o[:, cut] = nt(self.d_attn[...], self.wbuf[cut, :]).astype(jnp.bfloat16)
        self.w_loads = [
            self.load(self.q_w, self.wbuf.at[:, pl.ds(0, 768)], 3),
            self.load(self.k_w, self.wbuf.at[:, pl.ds(768, 384)], 4),
            self.load(self.v_w, self.wbuf.at[:, pl.ds(1152, 384)], 5),
        ]

    def attention(self, key_head):
        factor = HD ** (-0.5)
        c = key_head * HD
        keys, values = self.k[:, c : c + HD], self.v[:, c : c + HD]
        block = 256
        d_k = [jnp.zeros((block, HD), jnp.float32)] * 2
        d_v = [jnp.zeros((block, HD), jnp.float32)] * 2
        for head in (2 * key_head, 2 * key_head + 1):
            h = head * HD
            for i in range(2):
                here = slice(i * block, (i + 1) * block)
                n = block * (i + 1)
                query, d_out = self.q[here, h : h + HD], self.d_o[here, h : h + HD]
                column = lax.broadcasted_iota(jnp.int32, (block, n), 1)
                row = lax.broadcasted_iota(jnp.int32, (block, n), 0) + i * block
                allowed = (column <= row) & (column >= self.starts[here, :])
                masked = jnp.where(allowed, nt(query, keys[:n]) * factor, masked_score)
                exponent = jnp.exp(masked - jnp.max(masked, axis=1, keepdims=True))
                weights = exponent / jnp.sum(exponent, axis=1, keepdims=True)
                d_weights = nt(d_out, values[:n])
                inner = jnp.sum(weights * d_weights, axis=1, keepdims=True)
                d_scores = (weights * (d_weights - inner)).astype(jnp.bfloat16)
                low = weights.astype(jnp.bfloat16)
                d_query = jnp.dot(d_scores, keys[:n], preferred_element_type=jnp.float32) * factor
                turned = turn_back(d_query, self.cosines[here, :], self.sines[here, :])
                self.d_qkv[here, h : h + HD] = turned.astype(jnp.bfloat16)
                for j in range(i + 1):
                    cut = slice(j * block, (j + 1) * block)
                    d_k[j] = d_k[j] + tn(d_scores[:, cut], query) * factor
                    d_v[j] = d_v[j] + tn(low[:, cut], d_out)
        for j in range(2):
            cut = slice(j * block, (j + 1) * block)
            turned = turn_back(d_k[j], self.cosines[cut, :], self.sines[cut, :])
            self.d_qkv[cut, 768 + c : 768 + c + HD] = turned.astype(jnp.bfloat16)
            self.d_qkv[cut, 1152 + c : 1152 + c + HD] = d_v[j].astype(jnp.bfloat16)

    def h1_part(self, rows, put):
        def body(i, _):
            cut = pl.ds(pl.multiple_of(i * 256, 256), 256)
            put(cut, nt(self.d_qkv[rows, 0:1536], self.wbuf[cut, :]))
            return 0

        lax.fori_loop(0, 6, body, 0)

    def inward(self):
        for copy in self.w_loads:
            copy.wait()

        def put(cut, got):
            self.h1_out[:, cut] = got.astype(jnp.bfloat16)

        self.h1_part(self.theirs, put)
        self.m.start(self.h1_out, self.h1_in, Y_BASE + 2, self.p.other_y())

    def mlp_send(self):
        self.m.start(self.mlp_parts.at[self.theirs], self.mlp_in, Y_BASE + 3, self.p.other_y())
        self.own_load = self.load(self.mlp_parts.at[self.mine], self.own, 2)

    def finish(self):
        def put(cut, got):
            self.fbuf[:, cut] = got

        self.h1_part(self.mine, put)
        self.m.arrived(self.h1_in, Y_BASE + 2, self.p.other_y())

        def body(start, step):
            here = rows_at(start, step)
            d = self.fbuf[here, :] + self.h1_in[here, :].astype(jnp.float32)
            x = self.x[here, :].astype(jnp.float32)
            inv = row_scale(x)
            scaled = d * self.gain1[...].reshape(1, -1)
            inner = jnp.mean(scaled * x, axis=-1, keepdims=True)
            self.gains[0] += eight(d * x * inv)
            self.d_x1[here, :] = self.d_x1[here, :] + inv * (scaled - x * inv * inv * inner)

        self.tiles(16, body)
        copy = self.load(self.d_x1, self.tokens_out, 6)
        self.m.left.append((None, copy.wait))

    def layer_end(self):
        self.own_load.wait()
        self.m.arrived(self.mlp_in, Y_BASE + 3, self.p.other_y())

        def body(start, step):
            here = rows_at(start, step)
            mlp = self.own[here, :].astype(jnp.float32) + self.mlp_in[here, :].astype(jnp.float32)
            out = self.x1[here, :] + mlp
            self.gains[2] += eight(out * out)
            self.gains[3] += eight(mlp * mlp)
            self.y_low[here, :] = out.astype(jnp.bfloat16)

        self.tiles(16, body)
        copy = self.load(self.y_low, self.layer_out, 7)
        self.m.left.append((None, copy.wait))
        self.totals[0] = jnp.zeros(self.totals.shape[1:], jnp.float32)
        for row in range(4):
            self.totals[0, row : row + 1, :] = jnp.sum(self.gains[row], axis=0, keepdims=True)
        self.totals[0, 4:5, :] = self.attn_squares[...]


def sum_small(place, mover, total, slots, step):
    device = (place.other_core, place.other_x, place.other_y, place.pair_z, place.far_z)[step]()
    copy = mover.copy(total.at[step], slots.at[step], SMALL_BASE + step, device)
    copy.start()
    copy.wait()
    total[step + 1] = total[step] + slots[step]


INPUTS = (
    "hid_hbm", "g", "h2_hbm", "d_gate", "d_up", "o", "h1_hbm", "q", "k", "v", "out_w", "q_w", "k_w", "v_w",
    "x1", "x", "h2_parts", "mlp_parts", "cosines", "sines", "starts", "gain1", "gain2", "attn_squares",
)
IN_HBM = ("hid_hbm", "h2_hbm", "h1_hbm", "out_w", "q_w", "k_w", "v_w", "h2_parts", "mlp_parts")
RESULTS = ("down_out", "gate_out", "up_out", "o_out", "qkv_out", "tokens_out", "layer_out", "small_out")
PLAIN = (
    "staged", "hid", "hbuf", "own", "h2_in", "d_attn", "d_x1", "wbuf", "d_o", "h1_out", "h1_in", "mlp_in",
    "y_low", "fbuf", "gains", "totals", "slots", "stage_sems", "send_sems", "recv_sems", "keep_sems", "local_sems",
)


def backward_kernel(*refs):
    n = len(UNITS)
    names = INPUTS + RESULTS
    r = dict(zip(names, refs[: len(names)]))
    rest = refs[len(names) :]
    held, across, along = rest[:n], rest[n : 3 * n], rest[3 * n : 5 * n]
    r.update(zip(PLAIN, rest[5 * n :]))
    r["d_qkv"] = r["hid"]
    place = Place()
    mover = Mover(r["send_sems"], r["recv_sems"])
    mover.keep_sems = r["keep_sems"]
    enter(place)
    layer = Layer(place, mover, **r)
    lefts = (r["hid"], r["hbuf"], r["hbuf"], r["o"], r["hbuf"])
    rights = (r["g"], r["d_gate"], r["d_up"], r["d_attn"], r["d_qkv"])
    results = tuple(r[name] for name in RESULTS[:n])
    units = [
        Unit(i, place, mover, lefts[i], rights[i], held[i], r["staged"], r["stage_sems"]) for i in range(n)
    ]
    steps = []
    for i, (rows, columns, x_rows, z_rows, _) in enumerate(UNITS):
        for j in range(2):
            b = 2 * i + j
            block = Block(
                place, mover, held[i], across[b], along[b], results[i], b * COPIES,
                0 if j == 0 else x_rows, x_rows if j == 0 else z_rows, rows // 2, j == 0,
            )
            steps.append(block.events())

    def send(i):
        if i == 0:
            layer.hid_load.wait()
        if i == 1:
            layer.h_load.wait()
        if i == 4:
            layer.h_load = layer.load(layer.h1_hbm, layer.hbuf, 1)
            layer.h_load.wait()
        units[i].send()

    tasks = [layer.begin, layer.middle, layer.outward]
    tasks += [partial(layer.attention, i) for i in range(4)]
    tasks += [layer.inward, layer.mlp_send, layer.finish, layer.layer_end]
    tasks += [partial(sum_small, place, mover, r["totals"], r["slots"], i) for i in range(SMALL_STEPS)]
    for item in ORDER:
        if item < 5:
            send(item)
        elif item < 10:
            units[item - 5].own()
        elif item < 20:
            steps[item - 10].pop(0)()
        else:
            tasks[item - 20]()
    r["small_out"][...] = r["totals"][SMALL_STEPS]
    for when, wait in mover.left:
        guarded(when, wait)


def enter(place):
    barrier = pltpu.get_barrier_semaphore()

    def greet(device):
        pl.semaphore_signal(barrier, inc=1, device_id=device, device_id_type=MESH)

    for device in (place.other_core(), place.other_x(), place.other_y(), place.pair_z(), place.far_z()):
        greet(device)
    middle = (place.z == 1) | (place.z == 2)
    pl.when(middle)(lambda: greet(place.at(3 - place.z, place.x, place.core, place.y)))
    pl.semaphore_wait(barrier, 5 + jnp.where(middle, 1, 0))


def backward(**given):
    vmem = pl.BlockSpec(memory_space=pltpu.VMEM)
    hbm = pl.BlockSpec(memory_space=pl.ANY)
    low, full = jnp.bfloat16, jnp.float32
    own_rows, width = given["x1"].shape
    held = [pltpu.VMEM((rows // 2, columns), low) for rows, columns, *_ in UNITS]
    across, along = [], []
    for _, columns, x_rows, z_rows, _ in UNITS:
        across += [pltpu.VMEM((x_rows // 2, columns), low), pltpu.VMEM((z_rows // 8, columns), low)]
        along += [pltpu.VMEM((5, x_rows // 8, columns), low), pltpu.VMEM((5, z_rows // 4, columns), low)]
    part = pltpu.VMEM((own_rows, width), low)
    plain = dict(
        staged=pltpu.VMEM((2, 256, 2048), low),
        hid=pltpu.VMEM((512, 2048), low),
        hbuf=pltpu.VMEM((512, width), low),
        own=part,
        h2_in=part,
        d_attn=pltpu.VMEM((512, width), low),
        d_x1=pltpu.VMEM((own_rows, width), full),
        wbuf=pltpu.VMEM((1536, 1536), low),
        d_o=pltpu.VMEM((512, 768), low),
        h1_out=part,
        h1_in=part,
        mlp_in=part,
        y_low=part,
        fbuf=pltpu.VMEM((own_rows, width), full),
        gains=pltpu.VMEM((4, 8, width), full),
        totals=pltpu.VMEM((SMALL_STEPS + 1, 8, width), full),
        slots=pltpu.VMEM((SMALL_STEPS, 8, width), full),
        stage_sems=pltpu.SemaphoreType.DMA((2,)),
        send_sems=pltpu.SemaphoreType.DMA((N_SEMS,)),
        recv_sems=pltpu.SemaphoreType.DMA((N_SEMS,)),
        keep_sems=pltpu.SemaphoreType.DMA((2 * len(UNITS),)),
        local_sems=pltpu.SemaphoreType.DMA((8,)),
    )
    flops = sum(2 * 512 * rows * columns for rows, columns, *_ in UNITS)
    return pl.pallas_call(
        backward_kernel,
        out_shape=[jax.ShapeDtypeStruct((rows, columns), low) for rows, columns, *_ in UNITS]
        + [
            jax.ShapeDtypeStruct((own_rows, width), full),
            jax.ShapeDtypeStruct((own_rows, width), low),
            jax.ShapeDtypeStruct((8, width), full),
        ],
        in_specs=[hbm if name in IN_HBM else vmem for name in INPUTS],
        out_specs=[hbm] * 7 + [vmem],
        scratch_shapes=held + across + along + [plain[name] for name in PLAIN],
        compiler_params=pltpu.CompilerParams(
            collective_id=0, has_side_effects=True, vmem_limit_bytes=62 << 20
        ),
        cost_estimate=pl.CostEstimate(flops=flops, bytes_accessed=80 << 20, transcendentals=0),
        name="backward",
    )(*(given[name] for name in INPUTS))


FORWARD_INPUTS = (
    "x", "lengths", "gain1", "gain2", "inverse", "q_w", "k_w", "v_w", "out_w", "gate_w", "up_w", "down_w", "g_own",
)
FORWARD_RESULTS = (
    "hid_to", "g_to", "h2_to", "d_gate_to", "d_up_to", "o_to", "h1_to", "q_to", "k_to", "v_to", "x1_to",
    "h2_parts_to", "mlp_parts_to", "cosines", "sines", "starts", "attn_squares",
)
FORWARD_PLAIN = (
    "x_in", "w_qkv", "w_out", "w_gate", "w_up", "w_down", "g", "h1", "lin", "q", "k", "v", "o", "own_part",
    "sent_part", "got_part", "x1", "h2", "d_hid", "hid", "d_gate", "d_up", "h2_parts", "mlp_parts", "squares",
    "send_sems", "recv_sems", "load_sems", "store_sems",
)
CHUNKS = 2


class Forward:
    def __init__(self, refs):
        self.__dict__.update(refs)
        self.p = Place()
        self.m = Mover(self.send_sems, self.recv_sems)
        self.rows = self.x.shape[0]
        self.step = self.rows // CHUNKS
        self.base = self.p.y * self.rows
        self.far = (1 - self.p.y) * self.rows
        self.stores = 0

    def load(self, source, target, index):
        copy = pltpu.make_async_copy(source, target, self.load_sems.at[index])
        copy.start()
        return copy

    def store(self, source, target):
        copy = pltpu.make_async_copy(source, target, self.store_sems.at[self.stores])
        self.stores += 1
        copy.start()
        self.m.left.append((None, copy.wait))

    def across(self, source, target, index):
        self.m.start(source, target, index, self.p.other_y())

    def arrived(self, target, index):
        self.m.arrived(target, index, self.p.other_y())

    def tiles(self, first, count, step, body):
        lax.fori_loop(0, count // step, lambda i, _: (body(first + i * step, step), 0)[1], 0)

    def run(self):
        step = self.step
        barrier = pltpu.get_barrier_semaphore()
        pl.semaphore_signal(barrier, inc=1, device_id=self.p.other_y(), device_id_type=MESH)
        pl.semaphore_wait(barrier, 1)
        for c in range(CHUNKS):
            part = pl.ds(c * step, step)
            self.across(self.x.at[part], self.x_in.at[part], c)
        self.across(self.g_own, self.g.at[rows_at(self.base, self.rows)], 2 * CHUNKS)
        qkv_loads = [
            self.load(self.q_w, self.w_qkv.at[:, pl.ds(0, 768)], 0),
            self.load(self.k_w, self.w_qkv.at[:, pl.ds(768, 384)], 1),
            self.load(self.v_w, self.w_qkv.at[:, pl.ds(1152, 384)], 2),
        ]
        g_load = self.load(self.g_own, self.g.at[rows_at(self.base, self.rows)], 3)
        out_load = self.load(self.out_w, self.w_out, 4)
        down_load = self.load(self.down_w, self.w_down, 5)
        gate_load = self.load(self.gate_w, self.w_gate, 6)
        up_load = self.load(self.up_w, self.w_up, 7)
        self.tables()
        self.norm1(self.x, 0, self.base, self.rows)
        for copy in qkv_loads:
            copy.wait()
        self.qkv(self.base, self.rows)
        for c in range(CHUNKS):
            self.arrived(self.x_in.at[pl.ds(c * step, step)], c)
            self.norm1(self.x_in, c * step, self.far + c * step, step)
            self.qkv(self.far + c * step, step)
        self.store(self.h1, self.h1_to)
        self.store(self.q, self.q_to)
        self.store(self.k, self.k_to)
        self.store(self.v, self.v_to)
        self.attention(self.far)
        out_load.wait()
        for c in range(CHUNKS):
            part = pl.ds(c * step, step)
            self.project(self.far + c * step, self.sent_part, c * step, step)
            self.across(self.sent_part.at[part], self.got_part.at[part], CHUNKS + c)
        self.attention(self.base)
        self.store(self.o, self.o_to)
        self.project(self.base, self.own_part, 0, self.rows)
        g_load.wait()
        down_load.wait()
        self.hidden_grad(self.base, self.rows)
        self.arrived(self.g.at[rows_at(self.far, self.rows)], 2 * CHUNKS)
        self.store(self.g, self.g_to)
        self.hidden_grad(self.far, self.rows)
        self.squares[...] = jnp.zeros_like(self.squares)
        for c in range(CHUNKS):
            self.arrived(self.got_part.at[pl.ds(c * step, step)], CHUNKS + c)
            self.norm2(c * step)
            mine = self.h2.at[rows_at(self.base + c * step, step)]
            self.across(mine, mine, 2 * CHUNKS + 1 + c)
        self.store(self.x1, self.x1_to)
        self.attn_squares[...] = jnp.sum(self.squares[...], axis=0, keepdims=True)
        gate_load.wait()
        up_load.wait()
        self.feed(self.base, self.rows)
        for c in range(CHUNKS):
            self.arrived(self.h2.at[rows_at(self.far + c * step, step)], 2 * CHUNKS + 1 + c)
            self.feed(self.far + c * step, step)
        for name in ("h2", "hid", "d_gate", "d_up", "h2_parts", "mlp_parts"):
            self.store(getattr(self, name), getattr(self, name + "_to"))
        for when, wait in self.m.left:
            guarded(when, wait)

    def tables(self):
        total = self.starts.shape[0]
        row = lax.broadcasted_iota(jnp.int32, (total, 1), 0)
        first = jnp.zeros((total, 1), jnp.int32)
        end = jnp.int32(0)
        for j in range(self.lengths.shape[1]):
            first = jnp.where(row >= end, end, first)
            end = end + self.lengths[0, j]
        self.starts[...] = first
        angles = (row - first).astype(jnp.float32) * self.inverse[...]
        self.cosines[...] = jnp.cos(angles)
        half = lax.broadcasted_iota(jnp.int32, (total, HD), 1) < HD // 2
        sines = jnp.sin(angles)
        self.sines[...] = jnp.where(half, sines, -sines)

    def norm1(self, source, source_row, row, count):
        def body(i, step):
            x = source[rows_at(source_row + i, step), :].astype(jnp.float32)
            self.h1[rows_at(row + i, step), :] = (x * row_scale(x) * self.gain1[...].reshape(1, -1)).astype(jnp.bfloat16)

        self.tiles(0, count, 32, body)

    def qkv(self, row, count):
        here = rows_at(row, count)
        values = self.h1[here, :]
        for part in range(3):
            cut = slice(part * 512, (part + 1) * 512)
            self.lin[0:count, cut] = product(values, self.w_qkv[:, cut])
        cosines, sines = self.cosines[here, :], -self.sines[here, :]
        for target, first in ((self.q, 0), (self.k, 768)):
            for head in range(target.shape[1] // HD):
                linear = self.lin[0:count, first + head * HD : first + (head + 1) * HD]
                turned = turn_back(linear, cosines, sines)
                target[here, head * HD : (head + 1) * HD] = turned.astype(jnp.bfloat16)
        self.v[here, :] = self.lin[0:count, 1152:1536].astype(jnp.bfloat16)

    def attention(self, row):
        count, total = self.rows, self.q.shape[0]
        here = rows_at(row, count)
        column = lax.broadcasted_iota(jnp.int32, (count, total), 1)
        own = lax.broadcasted_iota(jnp.int32, (count, total), 0) + row
        allowed = (column <= own) & (column >= self.starts[here, :])
        for key_head in range(self.k.shape[1] // HD):
            c = key_head * HD
            keys, values = self.k[:, c : c + HD], self.v[:, c : c + HD]
            for head in (2 * key_head, 2 * key_head + 1):
                h = head * HD
                raw = nt(self.q[here, h : h + HD], keys) * HD ** (-0.5)
                masked = jnp.where(allowed, raw, masked_score)
                exponent = jnp.exp(masked - jnp.max(masked, axis=1, keepdims=True))
                weights = exponent / jnp.sum(exponent, axis=1, keepdims=True)
                out = product(weights.astype(jnp.bfloat16), values)
                self.o[here, h : h + HD] = out.astype(jnp.bfloat16)

    def project(self, row, target, target_row, count):
        values = self.o[rows_at(row, count), :]
        for part in range(3):
            cut = slice(part * 512, (part + 1) * 512)
            target[target_row : target_row + count, cut] = product(values, self.w_out[:, cut]).astype(target.dtype)

    def hidden_grad(self, row, count):
        here = rows_at(row, count)

        def body(i, _):
            cut = pl.ds(pl.multiple_of(i * 256, 256), 256)
            self.d_hid[here, cut] = nt(self.g[here, :], self.w_down[cut, :])
            return 0

        lax.fori_loop(0, self.w_down.shape[0] // 256, body, 0)

    def norm2(self, start):
        def body(i, step):
            here = rows_at(i, step)
            attn = self.own_part[here, :] + self.got_part[here, :].astype(jnp.float32)
            self.squares[...] += eight(attn * attn)
            x1 = self.x[here, :].astype(jnp.float32) + attn
            self.x1[here, :] = x1
            self.h2[rows_at(self.base + i, step), :] = (x1 * row_scale(x1) * self.gain2[...].reshape(1, -1)).astype(jnp.bfloat16)

        self.tiles(start, self.step, 16, body)

    def feed(self, row, count):
        here = rows_at(row, count)

        def body(i, _):
            cut = pl.ds(pl.multiple_of(i * 256, 256), 256)
            values = self.h2[here, :]
            gate = product(values, self.w_gate[:, cut])
            up = product(values, self.w_up[:, cut])
            d_hid = self.d_hid[here, cut]
            sig = 1.0 / (1.0 + jnp.exp(-gate))
            self.hid[here, cut] = (gate * sig * up).astype(jnp.bfloat16)
            self.d_gate[here, cut] = (d_hid * up * sig * (1.0 + gate * (1.0 - sig))).astype(jnp.bfloat16)
            self.d_up[here, cut] = (d_hid * gate * sig).astype(jnp.bfloat16)
            return 0

        lax.fori_loop(0, self.w_gate.shape[1] // 256, body, 0)

        def back(i, _):
            cut = pl.ds(pl.multiple_of(i * 256, 256), 256)
            total = nt(self.d_gate[here, :], self.w_gate[cut, :]) + nt(self.d_up[here, :], self.w_up[cut, :])
            self.h2_parts[here, cut] = total.astype(jnp.bfloat16)
            self.mlp_parts[here, cut] = product(self.hid[here, :], self.w_down[:, cut]).astype(jnp.bfloat16)
            return 0

        lax.fori_loop(0, self.w_down.shape[1] // 256, back, 0)


def forward_kernel(*refs):
    names = FORWARD_INPUTS + FORWARD_RESULTS + FORWARD_PLAIN
    Forward(dict(zip(names, refs))).run()


def forward(**given):
    vmem = pl.BlockSpec(memory_space=pltpu.VMEM)
    hbm = pl.BlockSpec(memory_space=pl.ANY)
    smem = pl.BlockSpec(memory_space=pltpu.SMEM)
    low, full = jnp.bfloat16, jnp.float32
    own, width = given["x"].shape
    total = 2 * own
    units = given["gate_w"].shape[1]
    q_cols, k_cols = given["q_w"].shape[1], given["k_w"].shape[1]
    shapes = dict(
        hid_to=((total, units), low), g_to=((total, width), low), h2_to=((total, width), low),
        d_gate_to=((total, units), low), d_up_to=((total, units), low), o_to=((total, q_cols), low),
        h1_to=((total, width), low), q_to=((total, q_cols), low), k_to=((total, k_cols), low),
        v_to=((total, k_cols), low), x1_to=((own, width), full), h2_parts_to=((total, width), low),
        mlp_parts_to=((total, width), low), cosines=((total, HD), full), sines=((total, HD), full),
        starts=((total, 1), jnp.int32), attn_squares=((1, width), full),
    )
    plain = dict(
        x_in=((own, width), low), w_qkv=((width, q_cols + 2 * k_cols), low), w_out=((q_cols, width), low),
        w_gate=((width, units), low), w_up=((width, units), low), w_down=((units, width), low),
        g=((total, width), low), h1=((total, width), low), lin=((own, q_cols + 2 * k_cols), full),
        q=((total, q_cols), low), k=((total, k_cols), low), v=((total, k_cols), low), o=((total, q_cols), low),
        own_part=((own, width), full), sent_part=((own, width), low), got_part=((own, width), low),
        x1=((own, width), full), h2=((total, width), low), d_hid=((total, units), full), hid=((total, units), low),
        d_gate=((total, units), low), d_up=((total, units), low), h2_parts=((total, width), low),
        mlp_parts=((total, width), low), squares=((8, width), full),
    )
    scratch = [pltpu.VMEM(*plain[name]) for name in FORWARD_PLAIN if name in plain]
    copies = 3 * CHUNKS + 1
    scratch += [pltpu.SemaphoreType.DMA((n,)) for n in (copies, copies, 8, 16)]
    spaces = dict.fromkeys(("q_w", "k_w", "v_w", "out_w", "gate_w", "up_w", "down_w", "g_own"), hbm)
    spaces["lengths"] = smem
    out = pl.pallas_call(
        forward_kernel,
        out_shape=[jax.ShapeDtypeStruct(*shapes[name]) for name in FORWARD_RESULTS],
        in_specs=[spaces.get(name, vmem) for name in FORWARD_INPUTS],
        out_specs=[hbm if name.endswith("_to") else vmem for name in FORWARD_RESULTS],
        scratch_shapes=scratch,
        compiler_params=pltpu.CompilerParams(
            collective_id=1, has_side_effects=True, vmem_limit_bytes=62 << 20
        ),
        cost_estimate=pl.CostEstimate(flops=26 * 10**9, bytes_accessed=60 << 20, transcendentals=0),
        name="forward",
    )(*(given[name] for name in FORWARD_INPUTS))
    return dict(zip(FORWARD_RESULTS, out))


def results_kernel(
    down, gate, up, o, qkv, tokens_in, layer_in, small,
    layer_out, tokens_out, gain1_out, q_out, k_out, v_out, o_out, gain2_out, gate_out, up_out, down_out, rms_out,
    taken, made, in_sems, out_sems, whole_sems, *, tokens,
):
    whole = [
        pltpu.make_async_copy(tokens_in, tokens_out, whole_sems.at[0]),
        pltpu.make_async_copy(layer_in, layer_out, whole_sems.at[1]),
    ]
    for copy in whole:
        copy.start()
    q_cols, k_cols = q_out.shape[1], k_out.shape[1]
    tile = taken.shape[1]
    work = []
    for source, targets in (
        (down, ((down_out, 0),)),
        (gate, ((gate_out, 0),)),
        (up, ((up_out, 0),)),
        (qkv, ((q_out, 0), (k_out, q_cols), (v_out, q_cols + k_cols))),
        (o, ((o_out, 0),)),
    ):
        work += [(source, targets, row) for row in range(0, source.shape[0], tile)]
    slots = taken.shape[0]

    def take(i):
        source, _, row = work[i]
        return pltpu.make_async_copy(
            source.at[pl.ds(row, tile)], taken.at[i % slots, :, pl.ds(0, source.shape[1])], in_sems.at[i % slots]
        )

    def give(i):
        _, targets, row = work[i]
        return [
            pltpu.make_async_copy(
                made.at[i % slots, :, pl.ds(first, target.shape[1])],
                target.at[pl.ds(row, tile)],
                out_sems.at[i % slots, j],
            )
            for j, (target, first) in enumerate(targets)
        ]

    for i in range(min(slots - 1, len(work))):
        take(i).start()
    for i in range(len(work)):
        if i + slots - 1 < len(work):
            take(i + slots - 1).start()
        take(i).wait()
        if i >= slots:
            for copy in give(i - slots):
                copy.wait()
        columns = work[i][0].shape[1]

        def one(j, _, slot=i % slots, columns=columns):
            here = rows_at(j * 16, 16)
            made[slot, here, 0:columns] = taken[slot, here, 0:columns].astype(jnp.float32)
            return 0

        lax.fori_loop(0, tile // 16, one, 0)
        for copy in give(i):
            copy.start()
    gain1_out[...] = small[0:1, :]
    gain2_out[...] = small[1:2, :]
    lane = lax.broadcasted_iota(jnp.int32, (1, 3), 1)
    sums = [jnp.sum(small[row : row + 1, :], axis=1, keepdims=True) for row in (2, 4, 3)]
    squares = jnp.where(lane == 0, sums[0], jnp.where(lane == 1, sums[1], sums[2]))
    rms_out[...] = jnp.sqrt(squares / tokens)
    for i in range(max(0, len(work) - slots), len(work)):
        for copy in give(i):
            copy.wait()
    for copy in whole:
        copy.wait()


def results(sums, tokens_grad, layer_out, small, q_cols, k_cols, tokens):
    vmem = pl.BlockSpec(memory_space=pltpu.VMEM)
    hbm = pl.BlockSpec(memory_space=pl.ANY)
    full = jnp.float32
    down, gate, up, o, qkv = sums
    width = small.shape[1]
    rows = qkv.shape[0]
    shapes = (
        (layer_out.shape, layer_out.dtype, hbm), (tokens_grad.shape, full, hbm), ((1, width), full, vmem),
        ((rows, q_cols), full, hbm), ((rows, k_cols), full, hbm), ((rows, k_cols), full, hbm),
        (o.shape, full, hbm), ((1, width), full, vmem), (gate.shape, full, hbm), (up.shape, full, hbm),
        (down.shape, full, hbm), ((1, 3), full, vmem),
    )
    slots, tile = 4, 256
    columns = max(part.shape[1] for part in sums)
    out = pl.pallas_call(
        partial(results_kernel, tokens=tokens),
        out_shape=[jax.ShapeDtypeStruct(shape, dtype) for shape, dtype, _ in shapes],
        in_specs=[hbm] * 7 + [vmem],
        out_specs=[space for _, _, space in shapes],
        scratch_shapes=[
            pltpu.VMEM((slots, tile, columns), jnp.bfloat16),
            pltpu.VMEM((slots, tile, columns), full),
            pltpu.SemaphoreType.DMA((slots,)),
            pltpu.SemaphoreType.DMA((slots, 3)),
            pltpu.SemaphoreType.DMA((2,)),
        ],
        compiler_params=pltpu.CompilerParams(vmem_limit_bytes=40 << 20),
        cost_estimate=pl.CostEstimate(flops=0, bytes_accessed=78 * 10**6, transcendentals=0),
        name="results",
    )(*sums, tokens_grad, layer_out, small)
    return tuple(part.reshape(-1) if part.shape[0] == 1 else part for part in out)


def dp_sum(terms):
    low = lax.psum(tuple(term.astype(jnp.bfloat16) for term in terms), "dp")
    return tuple(term.astype(jnp.float32) for term in low)


def low_scatter(partial):
    return lax.psum_scatter(
        partial.astype(jnp.bfloat16), "tensor", scatter_dimension=0, tiled=True
    ).astype(jnp.float32)


def body(
    tokens,
    lengths,
    first_gain,
    query_weight,
    key_weight,
    value_weight,
    output_weight,
    second_gain,
    gate_weight,
    up_weight,
    down_weight,
    out_cotangent,
):
    inputs = tokens.astype(jnp.float32)
    normed1, inv_first = norm_rows(inputs, first_gain)
    normed1 = normed1.astype(jnp.bfloat16)
    full_first = lax.all_gather(normed1, "tensor", axis=0, tiled=True)
    total_rows = full_first.shape[0]
    places, segment, cosine_table, sine_table, _ = tables(lengths[0], total_rows, HD // 2)
    kv_heads = key_weight.shape[1] // HD
    groups = query_weight.shape[1] // key_weight.shape[1]
    query = rotate(product(full_first, query_weight), cosine_table, sine_table, 1.0).astype(
        jnp.bfloat16
    )
    keys = rotate(product(full_first, key_weight), cosine_table, sine_table, 1.0).astype(
        jnp.bfloat16
    )
    values = product(full_first, value_weight).astype(jnp.bfloat16)
    block_rows = min(block_limit, total_rows)
    block_count = total_rows // block_rows
    query_blocks = query.reshape(block_count, block_rows, kv_heads, groups, HD)
    seg_blocks = segment.reshape(block_count, block_rows)
    place_blocks = places.reshape(block_count, block_rows)
    key_three = keys.reshape(total_rows, kv_heads, HD)
    value_three = values.reshape(total_rows, kv_heads, HD)
    factor = HD ** (-0.5)

    def scores(query_block, seg_block, place_block):
        raw = (
            jnp.einsum("qcgd,kcd->cgqk", query_block, key_three, preferred_element_type=jnp.float32)
            * factor
        )
        allowed = (seg_block[:, None] == segment[None, :]) & (
            place_block[:, None] >= places[None, :]
        )
        return (jnp.where(allowed[None, None], raw, masked_score), allowed)

    def forward_block(piece_set):
        query_block, seg_block, place_block = piece_set
        masked, allowed = scores(query_block, seg_block, place_block)
        highest = jnp.max(masked, axis=-1, keepdims=True)
        exponent = jnp.exp(masked - highest)
        denominator = jnp.sum(exponent, axis=-1, keepdims=True)
        weights = exponent / denominator
        output = jnp.einsum(
            "cgqk,kcd->qcgd",
            weights.astype(jnp.bfloat16),
            value_three,
            preferred_element_type=jnp.float32,
        )
        stored = (highest + jnp.log(denominator))[..., 0]
        return (output.reshape(block_rows, -1), stored)

    out_blocks, kept_blocks = lax.map(forward_block, (query_blocks, seg_blocks, place_blocks))
    attended = out_blocks.reshape(total_rows, -1).astype(jnp.bfloat16)
    attn_rows = low_scatter(product(attended, output_weight))
    middle = inputs + attn_rows
    normed2, inv_second = norm_rows(middle, second_gain)
    normed2 = normed2.astype(jnp.bfloat16)
    full_second = lax.all_gather(normed2, "tensor", axis=0, tiled=True)
    gate_value = product(full_second, gate_weight)
    upward = product(full_second, up_weight)
    gate_sig = jax.nn.sigmoid(gate_value)
    hidden = (gate_value * gate_sig * upward).astype(jnp.bfloat16)
    mlp_rows = low_scatter(product(hidden, down_weight))
    layer_out = middle + mlp_rows
    squares = jnp.stack(
        [
            jnp.sum(layer_out * layer_out),
            jnp.sum(attn_rows * attn_rows),
            jnp.sum(mlp_rows * mlp_rows),
        ]
    )
    grad_full = lax.all_gather(out_cotangent, "tensor", axis=0, tiled=True)
    grad_hidden = times_cols(grad_full, down_weight)
    down_g = times_rows(hidden, grad_full)
    gate_slope = gate_sig * (1.0 + gate_value * (1.0 - gate_sig))
    grad_gate = (grad_hidden * upward * gate_slope).astype(jnp.bfloat16)
    grad_up = (grad_hidden * gate_value * gate_sig).astype(jnp.bfloat16)
    gate_g = times_rows(full_second, grad_gate)
    up_g = times_rows(full_second, grad_up)
    gate_g, up_g, down_g = dp_sum((gate_g, up_g, down_g))
    grad_normed2 = low_scatter(
        times_cols(grad_gate, gate_weight) + times_cols(grad_up, up_weight)
    )
    second_rows, grad_mid_norm = norm_back(middle, inv_second, second_gain, grad_normed2)
    grad_middle = out_cotangent.astype(jnp.float32) + grad_mid_norm
    grad_attn_full = lax.all_gather(grad_middle.astype(jnp.bfloat16), "tensor", axis=0, tiled=True)
    output_g = times_rows(attended, grad_attn_full)
    grad_out = times_cols(grad_attn_full, output_weight).astype(jnp.bfloat16)
    grad_blocks = grad_out.reshape(block_count, block_rows, kv_heads, groups, HD)

    def backward_block(running, piece_set):
        key_acc, value_acc = running
        query_block, seg_block, place_block, grad_block, stored = piece_set
        masked, allowed = scores(query_block, seg_block, place_block)
        weights = jnp.where(allowed[None, None], jnp.exp(masked - stored[..., None]), 0.0)
        grad_weights = jnp.einsum(
            "qcgd,kcd->cgqk", grad_block, value_three, preferred_element_type=jnp.float32
        )
        row_inner = jnp.sum(weights * grad_weights, axis=-1, keepdims=True)
        grad_scores = (weights * (grad_weights - row_inner)).astype(jnp.bfloat16)
        grad_query = (
            jnp.einsum("cgqk,kcd->qcgd", grad_scores, key_three, preferred_element_type=jnp.float32)
            * factor
        )
        key_acc = (
            key_acc
            + jnp.einsum(
                "cgqk,qcgd->kcd", grad_scores, query_block, preferred_element_type=jnp.float32
            )
            * factor
        )
        value_acc = value_acc + jnp.einsum(
            "cgqk,qcgd->kcd",
            weights.astype(jnp.bfloat16),
            grad_block,
            preferred_element_type=jnp.float32,
        )
        return ((key_acc, value_acc), grad_query.reshape(block_rows, -1))

    zeros_kv = jnp.zeros((total_rows, kv_heads, HD), jnp.float32)
    (key_rot_grad, value_acc_grad), query_rot_grad = lax.scan(
        backward_block,
        (zeros_kv, zeros_kv),
        (query_blocks, seg_blocks, place_blocks, grad_blocks, kept_blocks),
    )
    query_lin = rotate(
        query_rot_grad.reshape(total_rows, -1), cosine_table, sine_table, -1.0
    ).astype(jnp.bfloat16)
    key_lin = rotate(key_rot_grad.reshape(total_rows, -1), cosine_table, sine_table, -1.0).astype(
        jnp.bfloat16
    )
    value_lin = value_acc_grad.reshape(total_rows, -1).astype(jnp.bfloat16)
    query_g = times_rows(full_first, query_lin)
    key_g = times_rows(full_first, key_lin)
    value_g = times_rows(full_first, value_lin)
    grad_normed1 = low_scatter(
        times_cols(query_lin, query_weight)
        + times_cols(key_lin, key_weight)
        + times_cols(value_lin, value_weight)
    )
    first_rows, grad_in_norm = norm_back(inputs, inv_first, first_gain, grad_normed1)
    tokens_grad = grad_middle + grad_in_norm
    gain_rows = jnp.stack([first_rows, second_rows])
    query_g, key_g, value_g, output_g = dp_sum((query_g, key_g, value_g, output_g))
    gain_rows, squares = lax.psum((gain_rows, squares), ("dp", "tensor"))
    rms_values = jnp.sqrt(squares / (total_rows * lax.axis_size("dp")))
    return (
        layer_out.astype(jnp.bfloat16),
        tokens_grad,
        gain_rows[0],
        query_g,
        key_g,
        value_g,
        output_g,
        gain_rows[1],
        gate_g,
        up_g,
        down_g,
        rms_values,
    )


def fused_body(
    tokens,
    lengths,
    first_gain,
    query_weight,
    key_weight,
    value_weight,
    output_weight,
    second_gain,
    gate_weight,
    up_weight,
    down_weight,
    out_cotangent,
):
    half_size = HD // 2
    inverse = (rope_base ** (-2.0 * np.arange(half_size) / (2 * half_size))).astype(np.float32)
    made = forward(
        x=tokens,
        lengths=lengths,
        gain1=first_gain,
        gain2=second_gain,
        inverse=jnp.asarray(np.concatenate([inverse, inverse])[None]),
        q_w=query_weight,
        k_w=key_weight,
        v_w=value_weight,
        out_w=output_weight,
        gate_w=gate_weight,
        up_w=up_weight,
        down_w=down_weight,
        g_own=out_cotangent,
    )
    *sums, tokens_grad, layer_out, small = backward(
        hid_hbm=made["hid_to"],
        g=made["g_to"],
        h2_hbm=made["h2_to"],
        d_gate=made["d_gate_to"],
        d_up=made["d_up_to"],
        o=made["o_to"],
        h1_hbm=made["h1_to"],
        q=made["q_to"],
        k=made["k_to"],
        v=made["v_to"],
        out_w=output_weight,
        q_w=query_weight,
        k_w=key_weight,
        v_w=value_weight,
        x1=made["x1_to"],
        x=tokens,
        h2_parts=made["h2_parts_to"],
        mlp_parts=made["mlp_parts_to"],
        cosines=made["cosines"],
        sines=made["sines"],
        starts=made["starts"],
        gain1=first_gain,
        gain2=second_gain,
        attn_squares=made["attn_squares"],
    )
    return results(
        sums, tokens_grad, layer_out, small, query_weight.shape[1], key_weight.shape[1],
        2 * tokens.shape[0] * lax.axis_size("dp"),
    )


def solution(mesh):
    in_specs = (
        P(("dp", "tensor"), None),
        P("dp", None),
        P(),
        P(None, "tensor"),
        P(None, "tensor"),
        P(None, "tensor"),
        P("tensor", None),
        P(),
        P(None, "tensor"),
        P(None, "tensor"),
        P("tensor", None),
        P(("dp", "tensor"), None),
    )
    out_specs = (
        P(("dp", "tensor"), None),
        P(("dp", "tensor"), None),
        P(),
        P(None, "tensor"),
        P(None, "tensor"),
        P(None, "tensor"),
        P("tensor", None),
        P(),
        P(None, "tensor"),
        P(None, "tensor"),
        P("tensor", None),
        P(),
    )
    fused = dict(mesh.shape) == {"dp": 16, "tensor": 2}
    chosen = fused_body if fused else body
    return jax.shard_map(chosen, mesh=mesh, in_specs=in_specs, out_specs=out_specs, check_vma=False)
```

```python
from functools import partial

import jax
import jax.numpy as jnp
import numpy as np
from jax import lax
from jax.experimental import pallas as pl
from jax.experimental.pallas import tpu as pltpu
from jax.sharding import PartitionSpec as P

HD = 96


epsilon = 1e-05
rope_base = 10000.0
masked_score = -1e30
block_limit = 512


def product(left_side, right_side):
    return jnp.dot(left_side, right_side, preferred_element_type=jnp.float32)


def times_rows(left_side, right_side):
    return lax.dot_general(
        left_side, right_side, (((0,), (0,)), ((), ())), preferred_element_type=jnp.float32
    )


def times_cols(left_side, right_side):
    return lax.dot_general(
        left_side, right_side, (((1,), (1,)), ((), ())), preferred_element_type=jnp.float32
    )


def tables(lens_row, total_rows, half_size):
    count = lens_row.shape[0]
    earlier = jnp.arange(count)[:, None] <= jnp.arange(count)[None, :]
    seq_ends = jnp.sum(jnp.where(earlier, lens_row[:, None], 0), axis=0, dtype=jnp.int32)
    starts = seq_ends - lens_row
    places = jnp.arange(total_rows, dtype=jnp.int32)
    segment = jnp.sum(
        (places[:, None] >= seq_ends[None, :]).astype(jnp.int32), axis=1, dtype=jnp.int32
    )
    member = segment[:, None] == jnp.arange(lens_row.shape[0], dtype=jnp.int32)[None, :]
    position = places - jnp.sum(jnp.where(member, starts[None, :], 0), axis=1, dtype=jnp.int32)
    inverse = rope_base ** (-2.0 * jnp.arange(half_size, dtype=jnp.float32) / (2 * half_size))
    angles = position.astype(jnp.float32)[:, None] * inverse[None, :]
    return (places, segment, jnp.cos(angles), jnp.sin(angles))


def rotate(values, cosine_table, sine_table, direction):
    total_rows = values.shape[0]
    half_size = cosine_table.shape[1]
    shaped = values.reshape(total_rows, -1, 2 * half_size)
    first_half = shaped[..., :half_size]
    second = shaped[..., half_size:]
    cos_b = cosine_table[:, None, :]
    sin_b = sine_table[:, None, :] * direction
    turned = jnp.concatenate(
        [first_half * cos_b - second * sin_b, second * cos_b + first_half * sin_b], axis=-1
    )
    return turned.reshape(total_rows, -1)


def norm_rows(values, gain):
    inv_rms = lax.rsqrt(jnp.mean(values * values, axis=-1, keepdims=True) + epsilon)
    return (values * inv_rms * gain, inv_rms)


def norm_back(values, inv_rms, gain, upstream):
    scaled = upstream * gain
    row_inner = jnp.mean(scaled * values, axis=-1, keepdims=True)
    gain_rows = jnp.sum(upstream * values * inv_rms, axis=0)
    return (gain_rows, inv_rms * (scaled - values * inv_rms * inv_rms * row_inner))


ORDER = (
    1000, 0, 100, 201, 200, 1, 2, 201, 1001, 101, 201, 1002, 203, 201, 201, 203, 1003, 201, 102,
    202, 200, 203, 200, 203, 201, 200, 203, 1004, 1011, 205, 201, 203, 201, 1012, 203, 205, 200,
    1005, 3, 1006, 202, 204, 205, 203, 1007, 205, 205, 202, 200, 103, 203, 1008, 205, 204, 202,
    1009, 200, 204, 1010, 4, 205, 204, 202, 200, 206, 104, 208, 201, 207, 204, 209, 1013, 205, 204,
    1014, 205, 208, 202, 206, 205, 1015, 1016, 209, 207, 200, 209, 203, 204, 201, 207, 206, 209,
    209, 203, 1017, 202, 204, 208, 202, 206, 209, 208, 1018, 206, 207, 207, 209, 206, 202, 208, 207,
    209, 208, 206, 207, 208, 209, 206, 1019, 208, 205, 206, 207, 204, 1020, 208, 207, 209, 209, 207,
    207,
)


MESH = pl.DeviceIdType.MESH
LINE = 4
DOWN, GATE, UP, OUT, QKV = range(5)
UNITS = (
    (2048, 1536, 640, 384, 256, 0, 0),
    (1536, 2048, 512, 256, 256, 1, 0),
    (1536, 2048, 384, 384, 256, 2, 0),
    (768, 1536, 256, 128, 128, 3, 0),
    (1536, 1536, 512, 256, 256, 4, 0),
)
WHOLE = tuple(
    (sum(unit[0] for unit in UNITS if unit[5] == kind), next(unit[1] for unit in UNITS if unit[5] == kind))
    for kind in range(5)
)
COPIES = 20
TILE_BASE = 2 * len(UNITS) * COPIES
TILES = tuple(rows // 2 // tile for rows, _, _, _, tile, _, _ in UNITS)
SMALL_BASE = TILE_BASE + sum(TILES)
SMALL_STEPS = 5
Y_BASE = SMALL_BASE + SMALL_STEPS
N_SEMS = Y_BASE + 4


def rows_at(start, size):
    return pl.ds(pl.multiple_of(start, 16), size)


class Place:
    def __init__(self):
        dp = lax.axis_index("dp")
        self.dp = dp
        self.y = lax.axis_index("tensor")
        self.core = lax.rem(dp, 2)
        self.x = lax.rem(dp // 2, 2)
        self.z = dp // 4

    def at(self, z, x, core, y):
        return ((z * 2 + x) * 2 + core, y)

    def other_core(self):
        return self.at(self.z, self.x, 1 - self.core, self.y)

    def other_x(self):
        return self.at(self.z, 1 - self.x, self.core, self.y)

    def other_y(self):
        return self.at(self.z, self.x, self.core, 1 - self.y)

    def up(self):
        return self.at(self.z + 1, self.x, self.core, self.y)

    def down(self):
        return self.at(self.z - 1, self.x, self.core, self.y)

    def pair_z(self):
        return self.at(self.z + 1 - 2 * lax.rem(self.z, 2), self.x, self.core, self.y)

    def far_z(self):
        return self.at(lax.rem(self.z + 2, LINE), self.x, self.core, self.y)


class Mover:
    def __init__(self, send_sems, recv_sems):
        self.send_sems = send_sems
        self.recv_sems = recv_sems
        self.left = []

    def copy(self, source, target, index, device):
        return pltpu.make_async_remote_copy(
            src_ref=source,
            dst_ref=target,
            send_sem=self.send_sems.at[index],
            recv_sem=self.recv_sems.at[index],
            device_id=device,
            device_id_type=MESH,
        )

    def start(self, source, target, index, device, when=None):
        copy = self.copy(source, target, index, device)
        guarded(when, copy.start)
        self.left.append((when, copy.wait_send))

    def arrived(self, target, index, device):
        self.copy(target, target, index, device).wait_recv()


def guarded(when, action):
    if when is None:
        action()
    else:
        pl.when(when)(action)


def add_rows(target, target_row, source, source_row, size):
    step = 16

    def one(i, _):
        here = rows_at(target_row + i * step, step)
        there = rows_at(source_row + i * step, step)
        total = target[here, :].astype(jnp.float32) + source[there, :].astype(jnp.float32)
        target[here, :] = total.astype(target.dtype)
        return 0

    lax.fori_loop(0, size // step, one, 0)


def fall_slot(step):
    return 0 if step == 0 else 2 + step


class Block:
    def __init__(self, place, mover, held, across, along, result, base, start, size, half_rows, x_first, first):
        self.p = place
        self.m = mover
        self.held = held
        self.across = across
        self.along = along
        self.result = result
        self.base = base
        self.start = start
        self.size = size
        self.half_rows = half_rows
        self.x_first = x_first
        self.first = first
        self.chunk = size // 8 if x_first else size // 4
        self.origin = start + place.x * (size // 2) if x_first else start

    def part(self, chunk):
        return self.held.at[rows_at(self.origin + chunk * self.chunk, self.chunk)]

    def final(self, row, size):
        return self.result.at[rows_at(self.first + self.p.core * self.half_rows + row, size)]

    def final_part(self, chunk):
        return self.final(self.origin + chunk * self.chunk, self.chunk)

    def keep(self, row, size):
        index = self.base // COPIES
        copy = pltpu.make_async_copy(
            self.held.at[rows_at(row, size)], self.final(row, size), self.m.keep_sems.at[index]
        )
        copy.start()
        self.kept = copy

    def events(self):
        line = [self.line_start, lambda: self.line_add(0), lambda: self.line_add(1), lambda: self.line_add(2)]
        spread = [lambda: self.spread(1), lambda: self.spread(2), lambda: self.spread(3)]
        if self.x_first:
            return [self.x_send, self.x_add] + line[1:] + spread + [self.x_done]
        return line + [self.pair_send, self.pair_add, self.pair_done] + spread + [self.z_done]

    def line_start(self):
        p = self.p
        for step in range(3):
            self.m.start(self.part(3 - step), self.along.at[step], self.base + step, p.up(), p.z == 0)
            self.m.start(self.part(step), self.along.at[fall_slot(step)], self.base + 3 + step, p.down(), p.z == LINE - 1)

    def line_add(self, step):
        p = self.p
        rising = jnp.minimum(p.z + 2 - step, 3)
        falling = jnp.maximum(p.z - 2 + step, 0)
        goes_up = (p.z >= 1) & (p.z <= step + 1)
        goes_down = (p.z <= 2) & (p.z >= 2 - step)

        def take_rising():
            self.m.arrived(self.along.at[step], self.base + step, p.down())
            add_rows(self.held, self.origin + rising * self.chunk, self.along.at[step], 0, self.chunk)

        def take_falling():
            self.m.arrived(self.along.at[fall_slot(step)], self.base + 3 + step, p.up())
            add_rows(self.held, self.origin + falling * self.chunk, self.along.at[fall_slot(step)], 0, self.chunk)

        pl.when(goes_up)(take_rising)
        if step < 2:
            self.m.start(self.part(rising), self.along.at[step + 1], self.base + step + 1, p.up(), goes_up)
        pl.when(goes_down)(take_falling)
        if step < 2:
            self.m.start(self.part(falling), self.along.at[fall_slot(step + 1)], self.base + 4 + step, p.down(), goes_down)
        elif self.x_first:
            self.keep(self.origin + p.z * self.chunk, self.chunk)
            self.own_spread(self.part(p.z))
            self.x_return(self.part(p.z), p.z, None)

    def own_spread(self, source):
        p = self.p
        target = self.final_part(p.z)
        self.m.start(source, target, self.base + 6, p.up(), p.z < 3)
        self.m.start(source, target, self.base + 9, p.down(), p.z > 0)

    def spread(self, distance):
        p = self.p
        below = self.final_part(jnp.maximum(p.z - distance, 0))
        above = self.final_part(jnp.minimum(p.z + distance, 3))

        pl.when(p.z >= distance)(lambda: self.m.arrived(below, self.base + 5 + distance, p.down()))
        if distance < 3:
            self.m.start(below, below, self.base + 6 + distance, p.up(), (p.z >= distance) & (p.z < 3))
        if self.x_first:
            self.x_return(below, jnp.maximum(p.z - distance, 0), p.z >= distance)
        pl.when(p.z <= 3 - distance)(lambda: self.m.arrived(above, self.base + 8 + distance, p.up()))
        if distance < 3:
            self.m.start(above, above, self.base + 9 + distance, p.down(), (p.z <= 3 - distance) & (p.z > 0))
        if self.x_first:
            self.x_return(above, jnp.minimum(p.z + distance, 3), p.z <= 3 - distance)
            if distance == 3:
                self.kept.wait()
                self.give(p.x * (self.size // 2), self.size // 2, 14)

    def x_part(self, which):
        half = self.size // 2
        return self.held.at[rows_at(self.start + which * half, half)]

    def x_send(self):
        self.m.start(self.x_part(1 - self.p.x), self.across, self.base + 12, self.p.other_x())

    def x_add(self):
        self.m.arrived(self.across, self.base + 12, self.p.other_x())
        add_rows(self.held, self.origin, self.across, 0, self.size // 2)
        self.line_start()

    def x_return(self, source, chunk, when):
        self.m.start(source, self.final_part(chunk), self.base + 16 + chunk, self.p.other_x(), when)

    def x_done(self):
        p = self.p
        half = (1 - p.x) * (self.size // 2)
        for chunk in range(4):
            place = self.final(self.start + half + chunk * self.chunk, self.chunk)
            self.m.arrived(place, self.base + 16 + chunk, p.other_x())
        self.give(half, self.size // 2, 15)

    def pair_row(self, which):
        return self.start + self.p.z * self.chunk + which * (self.chunk // 2)

    def pair_send(self):
        half = self.chunk // 2
        source = self.held.at[rows_at(self.pair_row(1 - self.p.x), half)]
        self.m.start(source, self.across, self.base + 12, self.p.other_x())

    def pair_add(self):
        p = self.p
        half = self.chunk // 2
        self.m.arrived(self.across, self.base + 12, p.other_x())
        row = self.pair_row(p.x)
        add_rows(self.held, row, self.across, 0, half)
        self.keep(row, half)
        self.m.start(self.held.at[rows_at(row, half)], self.final(row, half), self.base + 13, p.other_x())

    def pair_done(self):
        p = self.p
        half = self.chunk // 2
        self.m.arrived(self.final(self.pair_row(1 - p.x), half), self.base + 13, p.other_x())
        self.kept.wait()
        self.own_spread(self.final_part(p.z))

    def z_done(self):
        self.give(0, self.size, 14)

    def give(self, offset, size, slot):
        p = self.p
        source = self.final(self.start + offset, size)
        self.m.start(source, source, self.base + slot, p.other_core())
        other = self.result.at[
            rows_at(self.first + (1 - p.core) * self.half_rows + self.start + offset, size)
        ]
        self.m.left.append((None, lambda: self.m.arrived(other, self.base + slot, p.other_core())))


def product_tile(left, right, first, tile, width, part):
    columns = pl.ds(pl.multiple_of(first, 128), tile)
    return lax.dot_general(
        left[:, columns], right[:, part * width : (part + 1) * width],
        (((0,), (0,)), ((), ())), preferred_element_type=jnp.float32,
    )


class Unit:
    def __init__(self, index, place, mover, left, right, held, staged, stage_sems):
        self.index = index
        self.rows, self.columns, _, _, self.tile, _, self.first = UNITS[index]
        self.p, self.m = place, mover
        self.left, self.right, self.held = left, right, held
        self.staged, self.stage_sems = staged, stage_sems
        self.base = TILE_BASE + sum(TILES[:index])
        self.width = 512

    def tile_copy(self, i, slot):
        tile = self.tile
        return pltpu.make_async_remote_copy(
            src_ref=self.staged.at[slot, pl.ds(0, tile), pl.ds(0, self.columns)],
            dst_ref=self.held.at[rows_at(i * tile, tile)],
            send_sem=self.stage_sems.at[slot],
            recv_sem=self.m.recv_sems.at[self.base + i],
            device_id=self.p.other_core(),
            device_id_type=MESH,
        )

    def send(self):
        half, tile = self.rows // 2, self.tile

        def one(i, _):
            slot = lax.rem(i, 2)
            pl.when(i >= 2)(lambda: self.tile_copy(i, slot).wait_send())
            first = self.first + (1 - self.p.core) * half + i * tile
            for part in range(self.columns // self.width):
                got = product_tile(self.left, self.right, first, tile, self.width, part)
                self.staged[slot, pl.ds(0, tile), part * self.width : (part + 1) * self.width] = got.astype(
                    jnp.bfloat16
                )
            self.tile_copy(i, slot).start()
            return 0

        lax.fori_loop(0, half // tile, one, 0)
        for slot in range(min(2, half // tile)):
            self.tile_copy(0, slot).wait_send()

    def own(self):
        half, tile = self.rows // 2, self.tile

        def one(i, _):
            self.tile_copy(i, 0).wait_recv()
            first = self.first + self.p.core * half + i * tile
            here = rows_at(i * tile, tile)
            for part in range(self.columns // self.width):
                got = product_tile(self.left, self.right, first, tile, self.width, part)
                cut = slice(part * self.width, (part + 1) * self.width)
                total = got + self.held[here, cut].astype(jnp.float32)
                self.held[here, cut] = total.astype(jnp.bfloat16)
            return 0

        lax.fori_loop(0, half // tile, one, 0)


def row_scale(values):
    return lax.rsqrt(jnp.mean(values * values, axis=-1, keepdims=True) + epsilon)


def eight(values):
    rows, columns = values.shape
    return jnp.sum(values.reshape(rows // 8, 8, columns), axis=0)


def turn_back(values, cosines, sines):
    half = values.shape[1] // 2
    swapped = jnp.concatenate([values[:, half:], values[:, :half]], axis=1)
    return values * cosines + swapped * sines


def nt(left_side, right_side):
    return lax.dot_general(
        left_side, right_side, (((1,), (1,)), ((), ())), preferred_element_type=jnp.float32
    )


def tn(left_side, right_side):
    return lax.dot_general(
        left_side, right_side, (((0,), (0,)), ((), ())), preferred_element_type=jnp.float32
    )


class Layer:
    def __init__(self, place, mover, **refs):
        self.p, self.m = place, mover
        self.__dict__.update(refs)
        self.rows = self.x1.shape[0]
        self.mine = rows_at(place.y * self.rows, self.rows)
        self.theirs = rows_at((1 - place.y) * self.rows, self.rows)

    def load(self, source, target, index):
        copy = pltpu.make_async_copy(source, target, self.local_sems.at[index])
        copy.start()
        return copy

    def begin(self):
        self.waits = {}
        for i, (name, target) in enumerate(LOADED):
            self.waits[target] = self.load(getattr(self, name), getattr(self, target), 16 + i)
        self.waits["out_w"] = self.load(self.out_w, self.wbuf.at[pl.ds(0, 768)], 3)

    def need(self, *targets):
        for target in targets:
            if target in self.waits:
                self.waits.pop(target).wait()

    def stream(self, first, count, fetch, use):
        def go(i):
            for j, (source, target) in enumerate(fetch(i)):
                pltpu.make_async_copy(source, target, self.local_sems.at[8 + 2 * lax.rem(i, 2) + j]).start()

        go(jnp.int32(first))

        def body(i, _):
            pl.when(i + 1 < first + count)(lambda: go(i + 1))
            for j, (source, target) in enumerate(fetch(i)):
                pltpu.make_async_copy(source, target, self.local_sems.at[8 + 2 * lax.rem(i, 2) + j]).wait()
            use(i, lax.rem(i, 2))
            return 0

        lax.fori_loop(first, first + count, body, 0)

    def h2_third(self, third):
        self.need("d_gate", "d_up")

        def fetch(i):
            slot, here = lax.rem(i, 2), rows_at(i * 128, 128)
            return (
                (self.gate_w.at[here], self.staged.at[slot, pl.ds(0, 128)]),
                (self.up_w.at[here], self.staged.at[slot, pl.ds(128, 128)]),
            )

        def use(i, slot):
            cut = pl.ds(pl.multiple_of(i * 128, 128), 128)
            gate_w, up_w = self.staged[slot, 0:128, :], self.staged[slot, 128:256, :]
            for rows, target in ((self.theirs, self.h2_out), (self.mine, self.fbuf)):
                total = nt(self.d_gate[rows, :], gate_w) + nt(self.d_up[rows, :], up_w)
                target[:, cut] = total.astype(target.dtype)

        self.stream(4 * third, 4, fetch, use)
        if third == 2:
            self.h2_sent = self.m.copy(self.h2_out, self.h2_in, Y_BASE, self.p.other_y())
            self.h2_sent.start()

    def mlp_half(self, half):
        self.need("hid")

        rows, target = ((self.theirs, self.mlp_out), (self.mine, self.own))[half]
        self.fbuf[...] = jnp.zeros_like(self.fbuf)

        def fetch(i):
            return ((self.down_w.at[rows_at(i * 256, 256)], self.staged.at[lax.rem(i, 2), :, pl.ds(0, 1536)]),)

        def use(i, slot):
            cut = pl.ds(pl.multiple_of(i * 256, 256), 256)
            self.fbuf[...] += product(self.hid[rows, cut], self.staged[slot, :, 0:1536])

        self.stream(0, self.down_w.shape[0] // 256, fetch, use)
        target[...] = self.fbuf[...].astype(target.dtype)

    def tiles(self, step, body):
        lax.fori_loop(0, self.rows // step, lambda i, _: (body(i * step, step), 0)[1], 0)

    def middle(self):
        self.need("x1", "g")
        self.m.arrived(self.h2_in, Y_BASE, self.p.other_y())
        self.gains[...] = jnp.zeros_like(self.gains)

        def body(start, step):
            here = rows_at(start, step)
            there = rows_at(self.p.y * self.rows + start, step)
            d = self.fbuf[here, :] + self.h2_in[here, :].astype(jnp.float32)
            x1 = self.x1[here, :]
            inv = row_scale(x1)
            scaled = d * self.gain2[...].reshape(1, -1)
            inner = jnp.mean(scaled * x1, axis=-1, keepdims=True)
            self.gains[1] += eight(d * x1 * inv)
            d_x1 = self.g[there, :].astype(jnp.float32) + inv * (scaled - x1 * inv * inv * inner)
            self.d_x1[here, :] = d_x1
            self.d_attn[there, :] = d_x1.astype(jnp.bfloat16)

        self.tiles(16, body)
        own = self.d_attn.at[self.mine]
        self.m.start(own, own, Y_BASE + 1, self.p.other_y())

    def outward(self):
        self.m.arrived(self.d_attn.at[self.theirs], Y_BASE + 1, self.p.other_y())
        self.need("out_w")
        for part in range(3):
            cut = slice(part * 256, (part + 1) * 256)
            self.d_o[:, cut] = nt(self.d_attn[...], self.wbuf[cut, :]).astype(jnp.bfloat16)
        self.w_loads = [
            self.load(self.q_w, self.wbuf.at[:, pl.ds(0, 768)], 3),
            self.load(self.k_w, self.wbuf.at[:, pl.ds(768, 384)], 4),
            self.load(self.v_w, self.wbuf.at[:, pl.ds(1152, 384)], 5),
        ]

    def attention(self, key_head):
        self.need("q", "k", "v", "cosines", "sines", "starts")
        factor = HD ** (-0.5)
        c = key_head * HD
        keys, values = self.k[:, c : c + HD], self.v[:, c : c + HD]
        block = 256
        d_k = [jnp.zeros((block, HD), jnp.float32)] * 2
        d_v = [jnp.zeros((block, HD), jnp.float32)] * 2
        for head in (2 * key_head, 2 * key_head + 1):
            h = head * HD
            for i in range(2):
                here = slice(i * block, (i + 1) * block)
                n = block * (i + 1)
                query, d_out = self.q[here, h : h + HD], self.d_o[here, h : h + HD]
                column = lax.broadcasted_iota(jnp.int32, (block, n), 1)
                row = lax.broadcasted_iota(jnp.int32, (block, n), 0) + i * block
                allowed = (column <= row) & (column >= self.starts[here, :])
                masked = jnp.where(allowed, nt(query, keys[:n]) * factor, masked_score)
                exponent = jnp.exp(masked - jnp.max(masked, axis=1, keepdims=True))
                weights = exponent / jnp.sum(exponent, axis=1, keepdims=True)
                d_weights = nt(d_out, values[:n])
                inner = jnp.sum(weights * d_weights, axis=1, keepdims=True)
                d_scores = (weights * (d_weights - inner)).astype(jnp.bfloat16)
                low = weights.astype(jnp.bfloat16)
                d_query = jnp.dot(d_scores, keys[:n], preferred_element_type=jnp.float32) * factor
                turned = turn_back(d_query, self.cosines[here, :], self.sines[here, :])
                self.d_qkv[here, h : h + HD] = turned.astype(jnp.bfloat16)
                for j in range(i + 1):
                    cut = slice(j * block, (j + 1) * block)
                    d_k[j] = d_k[j] + tn(d_scores[:, cut], query) * factor
                    d_v[j] = d_v[j] + tn(low[:, cut], d_out)
        for j in range(2):
            cut = slice(j * block, (j + 1) * block)
            turned = turn_back(d_k[j], self.cosines[cut, :], self.sines[cut, :])
            self.d_qkv[cut, 768 + c : 768 + c + HD] = turned.astype(jnp.bfloat16)
            self.d_qkv[cut, 1152 + c : 1152 + c + HD] = d_v[j].astype(jnp.bfloat16)

    def h1_part(self, rows, put):
        def body(i, _):
            cut = pl.ds(pl.multiple_of(i * 256, 256), 256)
            put(cut, nt(self.d_qkv[rows, 0:1536], self.wbuf[cut, :]))
            return 0

        lax.fori_loop(0, 6, body, 0)

    def inward(self):
        for copy in self.w_loads:
            copy.wait()

        self.h2_sent.wait_send()
        self.waits["x"] = self.load(self.x_hbm, self.h2_in, 0)

        def put(cut, got):
            self.h2_out[:, cut] = got.astype(jnp.bfloat16)

        self.h1_part(self.theirs, put)
        self.m.start(self.h2_out, self.h1_in, Y_BASE + 2, self.p.other_y())

    def mlp_send(self):
        self.m.start(self.mlp_out, self.mlp_in, Y_BASE + 3, self.p.other_y())

    def finish(self):
        def put(cut, got):
            self.fbuf[:, cut] = got

        self.waits.pop("x").wait()
        self.h1_part(self.mine, put)
        self.m.arrived(self.h1_in, Y_BASE + 2, self.p.other_y())

        def body(start, step):
            here = rows_at(start, step)
            d = self.fbuf[here, :] + self.h1_in[here, :].astype(jnp.float32)
            x = self.h2_in[here, :].astype(jnp.float32)
            inv = row_scale(x)
            scaled = d * self.gain1[...].reshape(1, -1)
            inner = jnp.mean(scaled * x, axis=-1, keepdims=True)
            self.gains[0] += eight(d * x * inv)
            self.d_x1[here, :] = self.d_x1[here, :] + inv * (scaled - x * inv * inv * inner)

        self.tiles(16, body)
        copy = self.load(self.d_x1, self.tokens_out, 6)
        self.m.left.append((None, copy.wait))

    def layer_end(self):
        self.m.arrived(self.mlp_in, Y_BASE + 3, self.p.other_y())

        def body(start, step):
            here = rows_at(start, step)
            mlp = self.own[here, :].astype(jnp.float32) + self.mlp_in[here, :].astype(jnp.float32)
            out = self.x1[here, :] + mlp
            self.gains[2] += eight(out * out)
            self.gains[3] += eight(mlp * mlp)
            self.own[here, :] = out.astype(jnp.bfloat16)

        self.tiles(16, body)
        copy = self.load(self.own, self.layer_out, 7)
        self.m.left.append((None, copy.wait))
        self.totals[0] = jnp.zeros(self.totals.shape[1:], jnp.float32)
        for row in range(4):
            self.totals[0, row : row + 1, :] = jnp.sum(self.gains[row], axis=0, keepdims=True)
        self.totals[0, 4:5, :] = self.attn_squares[...]


def sum_small(place, mover, total, slots, step):
    device = (place.other_core, place.other_x, place.other_y, place.pair_z, place.far_z)[step]()
    copy = mover.copy(total.at[step], slots.at[step], SMALL_BASE + step, device)
    copy.start()
    copy.wait()
    total[step + 1] = total[step] + slots[step]


INPUTS = (
    "hid_hbm", "g_hbm", "h2_hbm", "d_gate_hbm", "d_up_hbm", "o_hbm", "h1_hbm", "q_hbm", "k_hbm", "v_hbm",
    "out_w", "q_w", "k_w", "v_w", "gate_w", "up_w", "down_w", "x1_hbm", "x_hbm", "cosines_hbm", "sines_hbm",
    "starts_hbm", "gain1", "gain2", "attn_squares",
)
IN_VMEM = ("gain1", "gain2", "attn_squares")
LOADED = (
    ("hid_hbm", "hid"), ("g_hbm", "g"), ("h2_hbm", "hbuf"), ("d_gate_hbm", "d_gate"), ("d_up_hbm", "d_up"),
    ("x1_hbm", "x1"), ("o_hbm", "o"), ("q_hbm", "q"), ("k_hbm", "k"), ("v_hbm", "v"),
    ("cosines_hbm", "cosines"), ("sines_hbm", "sines"), ("starts_hbm", "starts"),
)
RESULTS = ("down_out", "gate_out", "up_out", "o_out", "qkv_out", "tokens_out", "layer_out", "small_out")
PLAIN = (
    "staged", "hid", "hbuf", "own", "h2_in", "d_attn", "d_x1", "wbuf", "d_o", "h1_in", "mlp_in", "h2_out",
    "mlp_out", "fbuf", "gains", "totals", "slots", "g", "d_gate", "d_up", "o", "q", "k", "v", "x1",
    "cosines", "sines", "starts",
    "stage_sems", "send_sems", "recv_sems", "keep_sems", "local_sems",
)


def backward_kernel(*refs):
    n = len(UNITS)
    names = INPUTS + RESULTS
    r = dict(zip(names, refs[: len(names)]))
    rest = refs[len(names) :]
    held, across, along = rest[:n], rest[n : 3 * n], rest[3 * n : 5 * n]
    r.update(zip(PLAIN, rest[5 * n :]))
    r["d_qkv"] = r["hid"]
    place = Place()
    mover = Mover(r["send_sems"], r["recv_sems"])
    mover.keep_sems = r["keep_sems"]
    enter(place)
    layer = Layer(place, mover, **r)
    lefts = (r["hid"], r["hbuf"], r["hbuf"], r["o"], r["hbuf"])
    rights = (r["g"], r["d_gate"], r["d_up"], r["d_attn"], r["d_qkv"])
    results = tuple(r[name] for name in RESULTS[:5])
    units = [
        Unit(i, place, mover, lefts[unit[5]], rights[unit[5]], held[i], r["staged"], r["stage_sems"])
        for i, unit in enumerate(UNITS)
    ]
    steps = []
    for i, (rows, columns, x_rows, z_rows, _, kind, first) in enumerate(UNITS):
        for j in range(2):
            b = 2 * i + j
            block = Block(
                place, mover, held[i], across[b], along[b], results[kind], b * COPIES,
                0 if j == 0 else x_rows, x_rows if j == 0 else z_rows, rows // 2, j == 0, first,
            )
            steps.append(block.events())

    def send(i):
        kind, first = UNITS[i][5:]
        layer.need(*((("hid", "g"), ("hbuf", "d_gate"), ("hbuf", "d_up"), ("o",), ())[kind]))
        if kind == QKV and first == 0:
            layer.load(layer.h1_hbm, layer.hbuf, 1).wait()
        units[i].send()

    tasks = [layer.begin]
    tasks += [partial(layer.h2_third, i) for i in range(3)]
    tasks += [layer.middle, layer.outward]
    tasks += [partial(layer.attention, i) for i in range(4)]
    tasks += [layer.inward]
    tasks += [partial(layer.mlp_half, i) for i in range(2)]
    tasks += [layer.mlp_send, layer.finish, layer.layer_end]
    tasks += [partial(sum_small, place, mover, r["totals"], r["slots"], i) for i in range(SMALL_STEPS)]
    for item in ORDER:
        if item < 100:
            send(item)
        elif item < 200:
            units[item - 100].own()
        elif item < 1000:
            steps[item - 200].pop(0)()
        else:
            tasks[item - 1000]()
    r["small_out"][...] = r["totals"][SMALL_STEPS]
    for when, wait in mover.left:
        guarded(when, wait)


def enter(place):
    barrier = pltpu.get_barrier_semaphore()

    def greet(device):
        pl.semaphore_signal(barrier, inc=1, device_id=device, device_id_type=MESH)

    for device in (place.other_core(), place.other_x(), place.other_y(), place.pair_z(), place.far_z()):
        greet(device)
    middle = (place.z == 1) | (place.z == 2)
    pl.when(middle)(lambda: greet(place.at(3 - place.z, place.x, place.core, place.y)))
    pl.semaphore_wait(barrier, 5 + jnp.where(middle, 1, 0))


def backward(**given):
    vmem = pl.BlockSpec(memory_space=pltpu.VMEM)
    hbm = pl.BlockSpec(memory_space=pl.ANY)
    low, full = jnp.bfloat16, jnp.float32
    own_rows, width = given["x1_hbm"].shape
    held = [pltpu.VMEM((rows // 2, columns), low) for rows, columns, *_ in UNITS]
    across, along = [], []
    for _, columns, x_rows, z_rows, *_ in UNITS:
        across += [pltpu.VMEM((x_rows // 2, columns), low), pltpu.VMEM((z_rows // 8, columns), low)]
        along += [pltpu.VMEM((5, x_rows // 8, columns), low), pltpu.VMEM((5, z_rows // 4, columns), low)]
    part = pltpu.VMEM((own_rows, width), low)
    plain = dict(
        staged=pltpu.VMEM((2, 256, 2048), low),
        hid=pltpu.VMEM((512, 2048), low),
        hbuf=pltpu.VMEM((512, width), low),
        own=part,
        h2_in=part,
        d_attn=pltpu.VMEM((512, width), low),
        d_x1=pltpu.VMEM((own_rows, width), full),
        wbuf=pltpu.VMEM((1536, 1536), low),
        d_o=pltpu.VMEM((512, 768), low),
        h1_in=part,
        mlp_in=part,
        h2_out=part,
        mlp_out=part,
        fbuf=pltpu.VMEM((own_rows, width), full),
        gains=pltpu.VMEM((4, 8, width), full),
        totals=pltpu.VMEM((SMALL_STEPS + 1, 8, width), full),
        slots=pltpu.VMEM((SMALL_STEPS, 8, width), full),
        stage_sems=pltpu.SemaphoreType.DMA((2,)),
        send_sems=pltpu.SemaphoreType.DMA((N_SEMS,)),
        recv_sems=pltpu.SemaphoreType.DMA((N_SEMS,)),
        keep_sems=pltpu.SemaphoreType.DMA((2 * len(UNITS),)),
        local_sems=pltpu.SemaphoreType.DMA((16 + len(LOADED),)),
    )
    for name, target in LOADED:
        plain.setdefault(target, pltpu.VMEM(given[name].shape, given[name].dtype))
    flops = sum(2 * 512 * rows * columns for rows, columns, *_ in UNITS)
    return pl.pallas_call(
        backward_kernel,
        out_shape=[jax.ShapeDtypeStruct(shape, low) for shape in WHOLE]
        + [
            jax.ShapeDtypeStruct((own_rows, width), full),
            jax.ShapeDtypeStruct((own_rows, width), low),
            jax.ShapeDtypeStruct((8, width), full),
        ],
        in_specs=[vmem if name in IN_VMEM else hbm for name in INPUTS],
        out_specs=[hbm] * 7 + [vmem],
        scratch_shapes=held + across + along + [plain[name] for name in PLAIN],
        compiler_params=pltpu.CompilerParams(
            collective_id=0, has_side_effects=True, vmem_limit_bytes=62 << 20
        ),
        cost_estimate=pl.CostEstimate(flops=flops, bytes_accessed=80 << 20, transcendentals=0),
        name="backward",
    )(*(given[name] for name in INPUTS))


FORWARD_INPUTS = (
    "x", "lengths", "gain1", "gain2", "inverse", "q_w", "k_w", "v_w", "out_w", "gate_w", "up_w", "down_w", "g_own",
)
FORWARD_RESULTS = (
    "hid_to", "g_to", "h2_to", "d_gate_to", "d_up_to", "o_to", "h1_to", "q_to", "k_to", "v_to", "x1_to",
    "cosines", "sines", "starts", "attn_squares",
)
FORWARD_PLAIN = (
    "x_in", "w_qkv", "w_out", "w_gate", "w_up", "w_down", "g", "h1", "lin", "q", "k", "v", "o", "own_part",
    "sent_part", "got_part", "x1", "h2", "d_hid", "hid", "d_gate", "d_up", "squares",
    "send_sems", "recv_sems", "load_sems", "store_sems",
)
CHUNKS = 2


class Forward:
    def __init__(self, refs):
        self.__dict__.update(refs)
        self.p = Place()
        self.m = Mover(self.send_sems, self.recv_sems)
        self.rows = self.x.shape[0]
        self.step = self.rows // CHUNKS
        self.base = self.p.y * self.rows
        self.far = (1 - self.p.y) * self.rows
        self.stores = 0

    def load(self, source, target, index):
        copy = pltpu.make_async_copy(source, target, self.load_sems.at[index])
        copy.start()
        return copy

    def store(self, source, target):
        copy = pltpu.make_async_copy(source, target, self.store_sems.at[self.stores])
        self.stores += 1
        copy.start()
        self.m.left.append((None, copy.wait))

    def across(self, source, target, index):
        self.m.start(source, target, index, self.p.other_y())

    def arrived(self, target, index):
        self.m.arrived(target, index, self.p.other_y())

    def tiles(self, first, count, step, body):
        lax.fori_loop(0, count // step, lambda i, _: (body(first + i * step, step), 0)[1], 0)

    def run(self):
        step = self.step
        barrier = pltpu.get_barrier_semaphore()
        pl.semaphore_signal(barrier, inc=1, device_id=self.p.other_y(), device_id_type=MESH)
        pl.semaphore_wait(barrier, 1)
        for c in range(CHUNKS):
            part = pl.ds(c * step, step)
            self.across(self.x.at[part], self.x_in.at[part], c)
        self.across(self.g_own, self.g.at[rows_at(self.base, self.rows)], 2 * CHUNKS)
        qkv_loads = [
            self.load(self.q_w, self.w_qkv.at[:, pl.ds(0, 768)], 0),
            self.load(self.k_w, self.w_qkv.at[:, pl.ds(768, 384)], 1),
            self.load(self.v_w, self.w_qkv.at[:, pl.ds(1152, 384)], 2),
        ]
        g_load = self.load(self.g_own, self.g.at[rows_at(self.base, self.rows)], 3)
        out_load = self.load(self.out_w, self.w_out, 4)
        down_load = self.load(self.down_w, self.w_down, 5)
        gate_load = self.load(self.gate_w, self.w_gate, 6)
        up_load = self.load(self.up_w, self.w_up, 7)
        self.tables()
        self.norm1(self.x, 0, self.base, self.rows)
        for copy in qkv_loads:
            copy.wait()
        self.qkv(self.base, self.rows)
        for c in range(CHUNKS):
            self.arrived(self.x_in.at[pl.ds(c * step, step)], c)
            self.norm1(self.x_in, c * step, self.far + c * step, step)
            self.qkv(self.far + c * step, step)
        self.store(self.h1, self.h1_to)
        self.store(self.q, self.q_to)
        self.store(self.k, self.k_to)
        self.store(self.v, self.v_to)
        self.attention(self.far)
        out_load.wait()
        for c in range(CHUNKS):
            part = pl.ds(c * step, step)
            self.project(self.far + c * step, self.sent_part, c * step, step)
            self.across(self.sent_part.at[part], self.got_part.at[part], CHUNKS + c)
        self.attention(self.base)
        self.store(self.o, self.o_to)
        self.project(self.base, self.own_part, 0, self.rows)
        g_load.wait()
        down_load.wait()
        self.hidden_grad(self.base, self.rows)
        self.arrived(self.g.at[rows_at(self.far, self.rows)], 2 * CHUNKS)
        self.store(self.g, self.g_to)
        self.hidden_grad(self.far, self.rows)
        self.squares[...] = jnp.zeros_like(self.squares)
        for c in range(CHUNKS):
            self.arrived(self.got_part.at[pl.ds(c * step, step)], CHUNKS + c)
            self.norm2(c * step)
            mine = self.h2.at[rows_at(self.base + c * step, step)]
            self.across(mine, mine, 2 * CHUNKS + 1 + c)
        self.store(self.x1, self.x1_to)
        self.attn_squares[...] = jnp.sum(self.squares[...], axis=0, keepdims=True)
        gate_load.wait()
        up_load.wait()
        self.feed(self.base, self.rows)
        for c in range(CHUNKS):
            self.arrived(self.h2.at[rows_at(self.far + c * step, step)], 2 * CHUNKS + 1 + c)
            self.feed(self.far + c * step, step)
        for name in ("h2", "hid", "d_gate", "d_up"):
            self.store(getattr(self, name), getattr(self, name + "_to"))
        for when, wait in self.m.left:
            guarded(when, wait)

    def tables(self):
        total = self.starts.shape[0]
        row = lax.broadcasted_iota(jnp.int32, (total, 1), 0)
        first = jnp.zeros((total, 1), jnp.int32)
        end = jnp.int32(0)
        for j in range(self.lengths.shape[1]):
            first = jnp.where(row >= end, end, first)
            end = end + self.lengths[0, j]
        self.starts[...] = first
        angles = (row - first).astype(jnp.float32) * self.inverse[...]
        self.cosines[...] = jnp.cos(angles)
        half = lax.broadcasted_iota(jnp.int32, (total, HD), 1) < HD // 2
        sines = jnp.sin(angles)
        self.sines[...] = jnp.where(half, sines, -sines)

    def norm1(self, source, source_row, row, count):
        def body(i, step):
            x = source[rows_at(source_row + i, step), :].astype(jnp.float32)
            self.h1[rows_at(row + i, step), :] = (x * row_scale(x) * self.gain1[...].reshape(1, -1)).astype(jnp.bfloat16)

        self.tiles(0, count, 32, body)

    def qkv(self, row, count):
        here = rows_at(row, count)
        values = self.h1[here, :]
        for part in range(3):
            cut = slice(part * 512, (part + 1) * 512)
            self.lin[0:count, cut] = product(values, self.w_qkv[:, cut])
        cosines, sines = self.cosines[here, :], -self.sines[here, :]
        for target, first in ((self.q, 0), (self.k, 768)):
            for head in range(target.shape[1] // HD):
                linear = self.lin[0:count, first + head * HD : first + (head + 1) * HD]
                turned = turn_back(linear, cosines, sines)
                target[here, head * HD : (head + 1) * HD] = turned.astype(jnp.bfloat16)
        self.v[here, :] = self.lin[0:count, 1152:1536].astype(jnp.bfloat16)

    def attention(self, row):
        count, total = self.rows, self.q.shape[0]
        here = rows_at(row, count)
        column = lax.broadcasted_iota(jnp.int32, (count, total), 1)
        own = lax.broadcasted_iota(jnp.int32, (count, total), 0) + row
        allowed = (column <= own) & (column >= self.starts[here, :])
        for key_head in range(self.k.shape[1] // HD):
            c = key_head * HD
            keys, values = self.k[:, c : c + HD], self.v[:, c : c + HD]
            for head in (2 * key_head, 2 * key_head + 1):
                h = head * HD
                raw = nt(self.q[here, h : h + HD], keys) * HD ** (-0.5)
                masked = jnp.where(allowed, raw, masked_score)
                exponent = jnp.exp(masked - jnp.max(masked, axis=1, keepdims=True))
                weights = exponent / jnp.sum(exponent, axis=1, keepdims=True)
                out = product(weights.astype(jnp.bfloat16), values)
                self.o[here, h : h + HD] = out.astype(jnp.bfloat16)

    def project(self, row, target, target_row, count):
        values = self.o[rows_at(row, count), :]
        for part in range(3):
            cut = slice(part * 512, (part + 1) * 512)
            target[target_row : target_row + count, cut] = product(values, self.w_out[:, cut]).astype(target.dtype)

    def hidden_grad(self, row, count):
        here = rows_at(row, count)

        def body(i, _):
            cut = pl.ds(pl.multiple_of(i * 256, 256), 256)
            self.d_hid[here, cut] = nt(self.g[here, :], self.w_down[cut, :])
            return 0

        lax.fori_loop(0, self.w_down.shape[0] // 256, body, 0)

    def norm2(self, start):
        def body(i, step):
            here = rows_at(i, step)
            attn = self.own_part[here, :] + self.got_part[here, :].astype(jnp.float32)
            self.squares[...] += eight(attn * attn)
            x1 = self.x[here, :].astype(jnp.float32) + attn
            self.x1[here, :] = x1
            self.h2[rows_at(self.base + i, step), :] = (x1 * row_scale(x1) * self.gain2[...].reshape(1, -1)).astype(jnp.bfloat16)

        self.tiles(start, self.step, 16, body)

    def feed(self, row, count):
        here = rows_at(row, count)

        def body(i, _):
            cut = pl.ds(pl.multiple_of(i * 256, 256), 256)
            values = self.h2[here, :]
            gate = product(values, self.w_gate[:, cut])
            up = product(values, self.w_up[:, cut])
            d_hid = self.d_hid[here, cut]
            sig = 1.0 / (1.0 + jnp.exp(-gate))
            self.hid[here, cut] = (gate * sig * up).astype(jnp.bfloat16)
            self.d_gate[here, cut] = (d_hid * up * sig * (1.0 + gate * (1.0 - sig))).astype(jnp.bfloat16)
            self.d_up[here, cut] = (d_hid * gate * sig).astype(jnp.bfloat16)
            return 0

        lax.fori_loop(0, self.w_gate.shape[1] // 256, body, 0)


def forward_kernel(*refs):
    names = FORWARD_INPUTS + FORWARD_RESULTS + FORWARD_PLAIN
    Forward(dict(zip(names, refs))).run()


def forward(**given):
    vmem = pl.BlockSpec(memory_space=pltpu.VMEM)
    hbm = pl.BlockSpec(memory_space=pl.ANY)
    smem = pl.BlockSpec(memory_space=pltpu.SMEM)
    low, full = jnp.bfloat16, jnp.float32
    own, width = given["x"].shape
    total = 2 * own
    units = given["gate_w"].shape[1]
    q_cols, k_cols = given["q_w"].shape[1], given["k_w"].shape[1]
    shapes = dict(
        hid_to=((total, units), low), g_to=((total, width), low), h2_to=((total, width), low),
        d_gate_to=((total, units), low), d_up_to=((total, units), low), o_to=((total, q_cols), low),
        h1_to=((total, width), low), q_to=((total, q_cols), low), k_to=((total, k_cols), low),
        v_to=((total, k_cols), low), x1_to=((own, width), full), cosines=((total, HD), full), sines=((total, HD), full),
        starts=((total, 1), jnp.int32), attn_squares=((1, width), full),
    )
    plain = dict(
        x_in=((own, width), low), w_qkv=((width, q_cols + 2 * k_cols), low), w_out=((q_cols, width), low),
        w_gate=((width, units), low), w_up=((width, units), low), w_down=((units, width), low),
        g=((total, width), low), h1=((total, width), low), lin=((own, q_cols + 2 * k_cols), full),
        q=((total, q_cols), low), k=((total, k_cols), low), v=((total, k_cols), low), o=((total, q_cols), low),
        own_part=((own, width), full), sent_part=((own, width), low), got_part=((own, width), low),
        x1=((own, width), full), h2=((total, width), low), d_hid=((total, units), full), hid=((total, units), low),
        d_gate=((total, units), low), d_up=((total, units), low), squares=((8, width), full),
    )
    scratch = [pltpu.VMEM(*plain[name]) for name in FORWARD_PLAIN if name in plain]
    copies = 3 * CHUNKS + 1
    scratch += [pltpu.SemaphoreType.DMA((n,)) for n in (copies, copies, 8, 16)]
    spaces = dict.fromkeys(("q_w", "k_w", "v_w", "out_w", "gate_w", "up_w", "down_w", "g_own"), hbm)
    spaces["lengths"] = smem
    out = pl.pallas_call(
        forward_kernel,
        out_shape=[jax.ShapeDtypeStruct(*shapes[name]) for name in FORWARD_RESULTS],
        in_specs=[spaces.get(name, vmem) for name in FORWARD_INPUTS],
        out_specs=[hbm if name.endswith("_to") else vmem for name in FORWARD_RESULTS],
        scratch_shapes=scratch,
        compiler_params=pltpu.CompilerParams(
            collective_id=1, has_side_effects=True, vmem_limit_bytes=62 << 20
        ),
        cost_estimate=pl.CostEstimate(flops=26 * 10**9, bytes_accessed=60 << 20, transcendentals=0),
        name="forward",
    )(*(given[name] for name in FORWARD_INPUTS))
    return dict(zip(FORWARD_RESULTS, out))


def results_kernel(
    down, gate, up, o, qkv, tokens_in, layer_in, small,
    layer_out, tokens_out, gain1_out, q_out, k_out, v_out, o_out, gain2_out, gate_out, up_out, down_out, rms_out,
    taken, made, tokens_held, layer_held, in_sems, out_sems, whole_sems, *, tokens,
):
    held = ((tokens_in, tokens_held, tokens_out), (layer_in, layer_held, layer_out))
    inward = [pltpu.make_async_copy(a, b, whole_sems.at[i]) for i, (a, b, _) in enumerate(held)]
    outward = [pltpu.make_async_copy(b, c, whole_sems.at[i]) for i, (_, b, c) in enumerate(held)]
    for copy in inward:
        copy.start()
    q_cols, k_cols = q_out.shape[1], k_out.shape[1]
    tile = taken.shape[1]
    work = []
    for source, targets in (
        (down, ((down_out, 0),)),
        (gate, ((gate_out, 0),)),
        (up, ((up_out, 0),)),
        (qkv, ((q_out, 0), (k_out, q_cols), (v_out, q_cols + k_cols))),
        (o, ((o_out, 0),)),
    ):
        work += [(source, targets, row) for row in range(0, source.shape[0], tile)]
    slots = taken.shape[0]

    def take(i):
        source, _, row = work[i]
        return pltpu.make_async_copy(
            source.at[pl.ds(row, tile)], taken.at[i % slots, :, pl.ds(0, source.shape[1])], in_sems.at[i % slots]
        )

    def give(i):
        _, targets, row = work[i]
        return [
            pltpu.make_async_copy(
                made.at[i % slots, :, pl.ds(first, target.shape[1])],
                target.at[pl.ds(row, tile)],
                out_sems.at[i % slots, j],
            )
            for j, (target, first) in enumerate(targets)
        ]

    for i in range(min(slots - 1, len(work))):
        take(i).start()
    for i in range(len(work)):
        if i + slots - 1 < len(work):
            take(i + slots - 1).start()
        take(i).wait()
        if i >= slots:
            for copy in give(i - slots):
                copy.wait()
        columns = work[i][0].shape[1]

        def one(j, _, slot=i % slots, columns=columns):
            here = rows_at(j * 16, 16)
            made[slot, here, 0:columns] = taken[slot, here, 0:columns].astype(jnp.float32)
            return 0

        lax.fori_loop(0, tile // 16, one, 0)
        for copy in give(i):
            copy.start()
    for i in range(2):
        inward[i].wait()
        outward[i].start()
    gain1_out[...] = small[0, :]
    gain2_out[...] = small[1, :]
    lane = lax.broadcasted_iota(jnp.int32, (1, 3), 1)
    sums = [jnp.sum(small[row : row + 1, :], axis=1, keepdims=True) for row in (2, 4, 3)]
    squares = jnp.where(lane == 0, sums[0], jnp.where(lane == 1, sums[1], sums[2]))
    rms_out[...] = jnp.sqrt(squares / tokens)
    for i in range(max(0, len(work) - slots), len(work)):
        for copy in give(i):
            copy.wait()
    for copy in outward:
        copy.wait()


def results(sums, tokens_grad, layer_out, small, q_cols, k_cols, tokens):
    vmem = pl.BlockSpec(memory_space=pltpu.VMEM)
    hbm = pl.BlockSpec(memory_space=pl.ANY)
    full = jnp.float32
    down, gate, up, o, qkv = sums
    width = small.shape[1]
    rows = qkv.shape[0]
    shapes = (
        (layer_out.shape, layer_out.dtype, hbm), (tokens_grad.shape, full, hbm), ((width,), full, vmem),
        ((rows, q_cols), full, hbm), ((rows, k_cols), full, hbm), ((rows, k_cols), full, hbm),
        (o.shape, full, hbm), ((width,), full, vmem), (gate.shape, full, hbm), (up.shape, full, hbm),
        (down.shape, full, hbm), ((1, 3), full, vmem),
    )
    slots, tile = 4, 256
    columns = max(part.shape[1] for part in sums)
    out = pl.pallas_call(
        partial(results_kernel, tokens=tokens),
        out_shape=[jax.ShapeDtypeStruct(shape, dtype) for shape, dtype, _ in shapes],
        in_specs=[hbm] * 7 + [vmem],
        out_specs=[space for _, _, space in shapes],
        scratch_shapes=[
            pltpu.VMEM((slots, tile, columns), jnp.bfloat16),
            pltpu.VMEM((slots, tile, columns), full),
            pltpu.VMEM(tokens_grad.shape, full),
            pltpu.VMEM(layer_out.shape, layer_out.dtype),
            pltpu.SemaphoreType.DMA((slots,)),
            pltpu.SemaphoreType.DMA((slots, 3)),
            pltpu.SemaphoreType.DMA((2,)),
        ],
        compiler_params=pltpu.CompilerParams(vmem_limit_bytes=62 << 20),
        cost_estimate=pl.CostEstimate(flops=0, bytes_accessed=78 * 10**6, transcendentals=0),
        name="results",
    )(*sums, tokens_grad, layer_out, small)
    return tuple(part.reshape(-1) if part.shape[0] == 1 else part for part in out)


def dp_sum(terms):
    low = lax.psum(tuple(term.astype(jnp.bfloat16) for term in terms), "dp")
    return tuple(term.astype(jnp.float32) for term in low)


def low_scatter(partial):
    return lax.psum_scatter(
        partial.astype(jnp.bfloat16), "tensor", scatter_dimension=0, tiled=True
    ).astype(jnp.float32)


def body(
    tokens,
    lengths,
    first_gain,
    query_weight,
    key_weight,
    value_weight,
    output_weight,
    second_gain,
    gate_weight,
    up_weight,
    down_weight,
    out_cotangent,
):
    inputs = tokens.astype(jnp.float32)
    normed1, inv_first = norm_rows(inputs, first_gain)
    normed1 = normed1.astype(jnp.bfloat16)
    full_first = lax.all_gather(normed1, "tensor", axis=0, tiled=True)
    total_rows = full_first.shape[0]
    places, segment, cosine_table, sine_table = tables(lengths[0], total_rows, HD // 2)
    kv_heads = key_weight.shape[1] // HD
    groups = query_weight.shape[1] // key_weight.shape[1]
    query = rotate(product(full_first, query_weight), cosine_table, sine_table, 1.0).astype(
        jnp.bfloat16
    )
    keys = rotate(product(full_first, key_weight), cosine_table, sine_table, 1.0).astype(
        jnp.bfloat16
    )
    values = product(full_first, value_weight).astype(jnp.bfloat16)
    block_rows = min(block_limit, total_rows)
    block_count = total_rows // block_rows
    query_blocks = query.reshape(block_count, block_rows, kv_heads, groups, HD)
    seg_blocks = segment.reshape(block_count, block_rows)
    place_blocks = places.reshape(block_count, block_rows)
    key_three = keys.reshape(total_rows, kv_heads, HD)
    value_three = values.reshape(total_rows, kv_heads, HD)
    factor = HD ** (-0.5)

    def scores(query_block, seg_block, place_block):
        raw = (
            jnp.einsum("qcgd,kcd->cgqk", query_block, key_three, preferred_element_type=jnp.float32)
            * factor
        )
        allowed = (seg_block[:, None] == segment[None, :]) & (
            place_block[:, None] >= places[None, :]
        )
        return (jnp.where(allowed[None, None], raw, masked_score), allowed)

    def forward_block(piece_set):
        query_block, seg_block, place_block = piece_set
        masked, allowed = scores(query_block, seg_block, place_block)
        highest = jnp.max(masked, axis=-1, keepdims=True)
        exponent = jnp.exp(masked - highest)
        denominator = jnp.sum(exponent, axis=-1, keepdims=True)
        weights = exponent / denominator
        output = jnp.einsum(
            "cgqk,kcd->qcgd",
            weights.astype(jnp.bfloat16),
            value_three,
            preferred_element_type=jnp.float32,
        )
        stored = (highest + jnp.log(denominator))[..., 0]
        return (output.reshape(block_rows, -1), stored)

    out_blocks, kept_blocks = lax.map(forward_block, (query_blocks, seg_blocks, place_blocks))
    attended = out_blocks.reshape(total_rows, -1).astype(jnp.bfloat16)
    attn_rows = low_scatter(product(attended, output_weight))
    middle = inputs + attn_rows
    normed2, inv_second = norm_rows(middle, second_gain)
    normed2 = normed2.astype(jnp.bfloat16)
    full_second = lax.all_gather(normed2, "tensor", axis=0, tiled=True)
    gate_value = product(full_second, gate_weight)
    upward = product(full_second, up_weight)
    gate_sig = jax.nn.sigmoid(gate_value)
    hidden = (gate_value * gate_sig * upward).astype(jnp.bfloat16)
    mlp_rows = low_scatter(product(hidden, down_weight))
    layer_out = middle + mlp_rows
    squares = jnp.stack(
        [
            jnp.sum(layer_out * layer_out),
            jnp.sum(attn_rows * attn_rows),
            jnp.sum(mlp_rows * mlp_rows),
        ]
    )
    grad_full = lax.all_gather(out_cotangent, "tensor", axis=0, tiled=True)
    grad_hidden = times_cols(grad_full, down_weight)
    down_g = times_rows(hidden, grad_full)
    gate_slope = gate_sig * (1.0 + gate_value * (1.0 - gate_sig))
    grad_gate = (grad_hidden * upward * gate_slope).astype(jnp.bfloat16)
    grad_up = (grad_hidden * gate_value * gate_sig).astype(jnp.bfloat16)
    gate_g = times_rows(full_second, grad_gate)
    up_g = times_rows(full_second, grad_up)
    gate_g, up_g, down_g = dp_sum((gate_g, up_g, down_g))
    grad_normed2 = low_scatter(
        times_cols(grad_gate, gate_weight) + times_cols(grad_up, up_weight)
    )
    second_rows, grad_mid_norm = norm_back(middle, inv_second, second_gain, grad_normed2)
    grad_middle = out_cotangent.astype(jnp.float32) + grad_mid_norm
    grad_attn_full = lax.all_gather(grad_middle.astype(jnp.bfloat16), "tensor", axis=0, tiled=True)
    output_g = times_rows(attended, grad_attn_full)
    grad_out = times_cols(grad_attn_full, output_weight).astype(jnp.bfloat16)
    grad_blocks = grad_out.reshape(block_count, block_rows, kv_heads, groups, HD)

    def backward_block(running, piece_set):
        key_acc, value_acc = running
        query_block, seg_block, place_block, grad_block, stored = piece_set
        masked, allowed = scores(query_block, seg_block, place_block)
        weights = jnp.where(allowed[None, None], jnp.exp(masked - stored[..., None]), 0.0)
        grad_weights = jnp.einsum(
            "qcgd,kcd->cgqk", grad_block, value_three, preferred_element_type=jnp.float32
        )
        row_inner = jnp.sum(weights * grad_weights, axis=-1, keepdims=True)
        grad_scores = (weights * (grad_weights - row_inner)).astype(jnp.bfloat16)
        grad_query = (
            jnp.einsum("cgqk,kcd->qcgd", grad_scores, key_three, preferred_element_type=jnp.float32)
            * factor
        )
        key_acc = (
            key_acc
            + jnp.einsum(
                "cgqk,qcgd->kcd", grad_scores, query_block, preferred_element_type=jnp.float32
            )
            * factor
        )
        value_acc = value_acc + jnp.einsum(
            "cgqk,qcgd->kcd",
            weights.astype(jnp.bfloat16),
            grad_block,
            preferred_element_type=jnp.float32,
        )
        return ((key_acc, value_acc), grad_query.reshape(block_rows, -1))

    zeros_kv = jnp.zeros((total_rows, kv_heads, HD), jnp.float32)
    (key_rot_grad, value_acc_grad), query_rot_grad = lax.scan(
        backward_block,
        (zeros_kv, zeros_kv),
        (query_blocks, seg_blocks, place_blocks, grad_blocks, kept_blocks),
    )
    query_lin = rotate(
        query_rot_grad.reshape(total_rows, -1), cosine_table, sine_table, -1.0
    ).astype(jnp.bfloat16)
    key_lin = rotate(key_rot_grad.reshape(total_rows, -1), cosine_table, sine_table, -1.0).astype(
        jnp.bfloat16
    )
    value_lin = value_acc_grad.reshape(total_rows, -1).astype(jnp.bfloat16)
    query_g = times_rows(full_first, query_lin)
    key_g = times_rows(full_first, key_lin)
    value_g = times_rows(full_first, value_lin)
    grad_normed1 = low_scatter(
        times_cols(query_lin, query_weight)
        + times_cols(key_lin, key_weight)
        + times_cols(value_lin, value_weight)
    )
    first_rows, grad_in_norm = norm_back(inputs, inv_first, first_gain, grad_normed1)
    tokens_grad = grad_middle + grad_in_norm
    gain_rows = jnp.stack([first_rows, second_rows])
    query_g, key_g, value_g, output_g = dp_sum((query_g, key_g, value_g, output_g))
    gain_rows, squares = lax.psum((gain_rows, squares), ("dp", "tensor"))
    rms_values = jnp.sqrt(squares / (total_rows * lax.axis_size("dp")))
    return (
        layer_out.astype(jnp.bfloat16),
        tokens_grad,
        gain_rows[0],
        query_g,
        key_g,
        value_g,
        output_g,
        gain_rows[1],
        gate_g,
        up_g,
        down_g,
        rms_values,
    )


def fused_body(
    tokens,
    lengths,
    first_gain,
    query_weight,
    key_weight,
    value_weight,
    output_weight,
    second_gain,
    gate_weight,
    up_weight,
    down_weight,
    out_cotangent,
):
    half_size = HD // 2
    inverse = (rope_base ** (-2.0 * np.arange(half_size) / (2 * half_size))).astype(np.float32)
    made = forward(
        x=tokens,
        lengths=lengths,
        gain1=first_gain,
        gain2=second_gain,
        inverse=jnp.asarray(np.concatenate([inverse, inverse])[None]),
        q_w=query_weight,
        k_w=key_weight,
        v_w=value_weight,
        out_w=output_weight,
        gate_w=gate_weight,
        up_w=up_weight,
        down_w=down_weight,
        g_own=out_cotangent,
    )
    *sums, tokens_grad, layer_out, small = backward(
        **{name + "_hbm": made[name + "_to"] for name in ("hid", "g", "h2", "d_gate", "d_up", "o", "h1")},
        **{name + "_hbm": made[name + "_to"] for name in ("q", "k", "v", "x1")},
        **{name + "_hbm": made[name] for name in ("cosines", "sines", "starts")},
        x_hbm=tokens,
        out_w=output_weight,
        q_w=query_weight,
        k_w=key_weight,
        v_w=value_weight,
        gate_w=gate_weight,
        up_w=up_weight,
        down_w=down_weight,
        gain1=first_gain,
        gain2=second_gain,
        attn_squares=made["attn_squares"],
    )
    return results(
        sums, tokens_grad, layer_out, small, query_weight.shape[1], key_weight.shape[1],
        2 * tokens.shape[0] * lax.axis_size("dp"),
    )


def solution(mesh):
    in_specs = (
        P(("dp", "tensor"), None),
        P("dp", None),
        P(),
        P(None, "tensor"),
        P(None, "tensor"),
        P(None, "tensor"),
        P("tensor", None),
        P(),
        P(None, "tensor"),
        P(None, "tensor"),
        P("tensor", None),
        P(("dp", "tensor"), None),
    )
    out_specs = (
        P(("dp", "tensor"), None),
        P(("dp", "tensor"), None),
        P(),
        P(None, "tensor"),
        P(None, "tensor"),
        P(None, "tensor"),
        P("tensor", None),
        P(),
        P(None, "tensor"),
        P(None, "tensor"),
        P("tensor", None),
        P(),
    )
    fused = dict(mesh.shape) == {"dp": 16, "tensor": 2}
    chosen = fused_body if fused else body
    return jax.shard_map(chosen, mesh=mesh, in_specs=in_specs, out_specs=out_specs, check_vma=False)
```

```python
from functools import partial

import jax
import jax.numpy as jnp
import numpy as np
from jax import lax
from jax.experimental import pallas as pl
from jax.experimental.pallas import tpu as pltpu
from jax.sharding import PartitionSpec as P

HD = 96


epsilon = 1e-05
rope_base = 10000.0
masked_score = -1e30
block_limit = 512


def product(left_side, right_side):
    return jnp.dot(left_side, right_side, preferred_element_type=jnp.float32)


def times_rows(left_side, right_side):
    return lax.dot_general(
        left_side, right_side, (((0,), (0,)), ((), ())), preferred_element_type=jnp.float32
    )


def times_cols(left_side, right_side):
    return lax.dot_general(
        left_side, right_side, (((1,), (1,)), ((), ())), preferred_element_type=jnp.float32
    )


def tables(lens_row, total_rows, half_size):
    count = lens_row.shape[0]
    earlier = jnp.arange(count)[:, None] <= jnp.arange(count)[None, :]
    seq_ends = jnp.sum(jnp.where(earlier, lens_row[:, None], 0), axis=0, dtype=jnp.int32)
    starts = seq_ends - lens_row
    places = jnp.arange(total_rows, dtype=jnp.int32)
    segment = jnp.sum(
        (places[:, None] >= seq_ends[None, :]).astype(jnp.int32), axis=1, dtype=jnp.int32
    )
    member = segment[:, None] == jnp.arange(lens_row.shape[0], dtype=jnp.int32)[None, :]
    position = places - jnp.sum(jnp.where(member, starts[None, :], 0), axis=1, dtype=jnp.int32)
    inverse = rope_base ** (-2.0 * jnp.arange(half_size, dtype=jnp.float32) / (2 * half_size))
    angles = position.astype(jnp.float32)[:, None] * inverse[None, :]
    return (places, segment, jnp.cos(angles), jnp.sin(angles))


def rotate(values, cosine_table, sine_table, direction):
    total_rows = values.shape[0]
    half_size = cosine_table.shape[1]
    shaped = values.reshape(total_rows, -1, 2 * half_size)
    first_half = shaped[..., :half_size]
    second = shaped[..., half_size:]
    cos_b = cosine_table[:, None, :]
    sin_b = sine_table[:, None, :] * direction
    turned = jnp.concatenate(
        [first_half * cos_b - second * sin_b, second * cos_b + first_half * sin_b], axis=-1
    )
    return turned.reshape(total_rows, -1)


def norm_rows(values, gain):
    inv_rms = lax.rsqrt(jnp.mean(values * values, axis=-1, keepdims=True) + epsilon)
    return (values * inv_rms * gain, inv_rms)


def norm_back(values, inv_rms, gain, upstream):
    scaled = upstream * gain
    row_inner = jnp.mean(scaled * values, axis=-1, keepdims=True)
    gain_rows = jnp.sum(upstream * values * inv_rms, axis=0)
    return (gain_rows, inv_rms * (scaled - values * inv_rms * inv_rms * row_inner))


ORDER = (
    1000, 2, 1001, 102, 205, 204, 1002, 1003, 205, 0, 1, 204, 100, 200, 101, 205, 203, 204, 1004,
    1011, 205, 204, 203, 205, 1012, 204, 200, 205, 202, 203, 1005, 204, 3, 200, 205, 203, 203, 1006,
    200, 201, 1007, 103, 204, 205, 1008, 201, 200, 202, 206, 205, 1009, 201, 203, 200, 1010, 202,
    203, 201, 201, 200, 206, 4, 202, 207, 201, 206, 203, 1013, 104, 202, 201, 207, 208, 209, 206,
    1014, 203, 202, 1015, 206, 209, 208, 202, 200, 206, 207, 208, 209, 205, 206, 207, 207, 208, 202,
    201, 209, 209, 1016, 208, 207, 205, 206, 201, 209, 1017, 204, 207, 208, 202, 1018, 209, 1019,
    207, 203, 201, 208, 201, 206, 209, 1020, 207, 208, 200, 209, 203, 207, 207, 208, 204, 209, 209,
)


MESH = pl.DeviceIdType.MESH
LINE = 4
DOWN, GATE, UP, OUT, QKV = range(5)
UNITS = (
    (2048, 1536, 640, 384, 256, 0, 0),
    (1536, 2048, 512, 256, 256, 1, 0),
    (1536, 2048, 384, 384, 256, 2, 0),
    (768, 1536, 256, 128, 128, 3, 0),
    (1536, 1536, 512, 256, 256, 4, 0),
)
WHOLE = tuple(
    (sum(unit[0] for unit in UNITS if unit[5] == kind), next(unit[1] for unit in UNITS if unit[5] == kind))
    for kind in range(5)
)
COPIES = 20
TILE_BASE = 2 * len(UNITS) * COPIES
TILES = tuple(rows // 2 // tile for rows, _, _, _, tile, _, _ in UNITS)
SMALL_BASE = TILE_BASE + sum(TILES)
SMALL_STEPS = 5
Y_BASE = SMALL_BASE + SMALL_STEPS
N_SEMS = Y_BASE + 4


def rows_at(start, size):
    return pl.ds(pl.multiple_of(start, 16), size)


class Place:
    def __init__(self):
        dp = lax.axis_index("dp")
        self.dp = dp
        self.y = lax.axis_index("tensor")
        self.core = lax.rem(dp, 2)
        self.x = lax.rem(dp // 2, 2)
        self.z = dp // 4

    def at(self, z, x, core, y):
        return ((z * 2 + x) * 2 + core, y)

    def other_core(self):
        return self.at(self.z, self.x, 1 - self.core, self.y)

    def other_x(self):
        return self.at(self.z, 1 - self.x, self.core, self.y)

    def other_y(self):
        return self.at(self.z, self.x, self.core, 1 - self.y)

    def up(self):
        return self.at(self.z + 1, self.x, self.core, self.y)

    def down(self):
        return self.at(self.z - 1, self.x, self.core, self.y)

    def pair_z(self):
        return self.at(self.z + 1 - 2 * lax.rem(self.z, 2), self.x, self.core, self.y)

    def far_z(self):
        return self.at(lax.rem(self.z + 2, LINE), self.x, self.core, self.y)


class Mover:
    def __init__(self, send_sems, recv_sems):
        self.send_sems = send_sems
        self.recv_sems = recv_sems
        self.left = []

    def copy(self, source, target, index, device):
        return pltpu.make_async_remote_copy(
            src_ref=source,
            dst_ref=target,
            send_sem=self.send_sems.at[index],
            recv_sem=self.recv_sems.at[index],
            device_id=device,
            device_id_type=MESH,
        )

    def start(self, source, target, index, device, when=None):
        copy = self.copy(source, target, index, device)
        guarded(when, copy.start)
        self.left.append((when, copy.wait_send))

    def arrived(self, target, index, device):
        self.copy(target, target, index, device).wait_recv()


def guarded(when, action):
    if when is None:
        action()
    else:
        pl.when(when)(action)


def add_rows(target, target_row, source, source_row, size):
    step = 16

    def one(i, _):
        here = rows_at(target_row + i * step, step)
        there = rows_at(source_row + i * step, step)
        total = target[here, :].astype(jnp.float32) + source[there, :].astype(jnp.float32)
        target[here, :] = total.astype(target.dtype)
        return 0

    lax.fori_loop(0, size // step, one, 0)


def fall_slot(step):
    return 0 if step == 0 else 2 + step


class Block:
    def __init__(self, place, mover, held, across, along, result, base, start, size, half_rows, x_first, first):
        self.p = place
        self.m = mover
        self.held = held
        self.across = across
        self.along = along
        self.result = result
        self.base = base
        self.start = start
        self.size = size
        self.half_rows = half_rows
        self.x_first = x_first
        self.first = first
        self.chunk = size // 8 if x_first else size // 4
        self.origin = start + place.x * (size // 2) if x_first else start

    def part(self, chunk):
        return self.held.at[rows_at(self.origin + chunk * self.chunk, self.chunk)]

    def final(self, row, size):
        return self.result.at[rows_at(self.first + self.p.core * self.half_rows + row, size)]

    def final_part(self, chunk):
        return self.final(self.origin + chunk * self.chunk, self.chunk)

    def keep(self, row, size):
        index = self.base // COPIES
        copy = pltpu.make_async_copy(
            self.held.at[rows_at(row, size)], self.final(row, size), self.m.keep_sems.at[index]
        )
        copy.start()
        self.kept = copy

    def events(self):
        line = [self.line_start, lambda: self.line_add(0), lambda: self.line_add(1), lambda: self.line_add(2)]
        spread = [lambda: self.spread(1), lambda: self.spread(2), lambda: self.spread(3)]
        if self.x_first:
            return [self.x_send, self.x_add] + line[1:] + spread + [self.x_done]
        return line + [self.pair_send, self.pair_add, self.pair_done] + spread + [self.z_done]

    def line_start(self):
        p = self.p
        for step in range(3):
            self.m.start(self.part(3 - step), self.along.at[step], self.base + step, p.up(), p.z == 0)
            self.m.start(self.part(step), self.along.at[fall_slot(step)], self.base + 3 + step, p.down(), p.z == LINE - 1)

    def line_add(self, step):
        p = self.p
        rising = jnp.minimum(p.z + 2 - step, 3)
        falling = jnp.maximum(p.z - 2 + step, 0)
        goes_up = (p.z >= 1) & (p.z <= step + 1)
        goes_down = (p.z <= 2) & (p.z >= 2 - step)

        def take_rising():
            self.m.arrived(self.along.at[step], self.base + step, p.down())
            add_rows(self.held, self.origin + rising * self.chunk, self.along.at[step], 0, self.chunk)

        def take_falling():
            self.m.arrived(self.along.at[fall_slot(step)], self.base + 3 + step, p.up())
            add_rows(self.held, self.origin + falling * self.chunk, self.along.at[fall_slot(step)], 0, self.chunk)

        pl.when(goes_up)(take_rising)
        if step < 2:
            self.m.start(self.part(rising), self.along.at[step + 1], self.base + step + 1, p.up(), goes_up)
        pl.when(goes_down)(take_falling)
        if step < 2:
            self.m.start(self.part(falling), self.along.at[fall_slot(step + 1)], self.base + 4 + step, p.down(), goes_down)
        elif self.x_first:
            self.keep(self.origin + p.z * self.chunk, self.chunk)
            self.own_spread(self.part(p.z))
            self.x_return(self.part(p.z), p.z, None)

    def own_spread(self, source):
        p = self.p
        target = self.final_part(p.z)
        self.m.start(source, target, self.base + 6, p.up(), p.z < 3)
        self.m.start(source, target, self.base + 9, p.down(), p.z > 0)

    def spread(self, distance):
        p = self.p
        below = self.final_part(jnp.maximum(p.z - distance, 0))
        above = self.final_part(jnp.minimum(p.z + distance, 3))

        pl.when(p.z >= distance)(lambda: self.m.arrived(below, self.base + 5 + distance, p.down()))
        if distance < 3:
            self.m.start(below, below, self.base + 6 + distance, p.up(), (p.z >= distance) & (p.z < 3))
        if self.x_first:
            self.x_return(below, jnp.maximum(p.z - distance, 0), p.z >= distance)
        pl.when(p.z <= 3 - distance)(lambda: self.m.arrived(above, self.base + 8 + distance, p.up()))
        if distance < 3:
            self.m.start(above, above, self.base + 9 + distance, p.down(), (p.z <= 3 - distance) & (p.z > 0))
        if self.x_first:
            self.x_return(above, jnp.minimum(p.z + distance, 3), p.z <= 3 - distance)
            if distance == 3:
                self.kept.wait()
                self.give(p.x * (self.size // 2), self.size // 2, 14)

    def x_part(self, which):
        half = self.size // 2
        return self.held.at[rows_at(self.start + which * half, half)]

    def x_send(self):
        self.m.start(self.x_part(1 - self.p.x), self.across, self.base + 12, self.p.other_x())

    def x_add(self):
        self.m.arrived(self.across, self.base + 12, self.p.other_x())
        add_rows(self.held, self.origin, self.across, 0, self.size // 2)
        self.line_start()

    def x_return(self, source, chunk, when):
        self.m.start(source, self.final_part(chunk), self.base + 16 + chunk, self.p.other_x(), when)

    def x_done(self):
        p = self.p
        half = (1 - p.x) * (self.size // 2)
        for chunk in range(4):
            place = self.final(self.start + half + chunk * self.chunk, self.chunk)
            self.m.arrived(place, self.base + 16 + chunk, p.other_x())
        self.give(half, self.size // 2, 15)

    def pair_row(self, which):
        return self.start + self.p.z * self.chunk + which * (self.chunk // 2)

    def pair_send(self):
        half = self.chunk // 2
        source = self.held.at[rows_at(self.pair_row(1 - self.p.x), half)]
        self.m.start(source, self.across, self.base + 12, self.p.other_x())

    def pair_add(self):
        p = self.p
        half = self.chunk // 2
        self.m.arrived(self.across, self.base + 12, p.other_x())
        row = self.pair_row(p.x)
        add_rows(self.held, row, self.across, 0, half)
        self.keep(row, half)
        self.m.start(self.held.at[rows_at(row, half)], self.final(row, half), self.base + 13, p.other_x())

    def pair_done(self):
        p = self.p
        half = self.chunk // 2
        self.m.arrived(self.final(self.pair_row(1 - p.x), half), self.base + 13, p.other_x())
        self.kept.wait()
        self.own_spread(self.final_part(p.z))

    def z_done(self):
        self.give(0, self.size, 14)

    def give(self, offset, size, slot):
        p = self.p
        source = self.final(self.start + offset, size)
        self.m.start(source, source, self.base + slot, p.other_core())
        other = self.result.at[
            rows_at(self.first + (1 - p.core) * self.half_rows + self.start + offset, size)
        ]
        self.m.left.append((None, lambda: self.m.arrived(other, self.base + slot, p.other_core())))


def product_tile(left, right, first, tile, width, part):
    columns = pl.ds(pl.multiple_of(first, 128), tile)
    return lax.dot_general(
        left[:, columns], right[:, part * width : (part + 1) * width],
        (((0,), (0,)), ((), ())), preferred_element_type=jnp.float32,
    )


class Unit:
    def __init__(self, index, place, mover, left, right, held, staged, stage_sems):
        self.index = index
        self.rows, self.columns, _, _, self.tile, _, self.first = UNITS[index]
        self.p, self.m = place, mover
        self.left, self.right, self.held = left, right, held
        self.staged, self.stage_sems = staged, stage_sems
        self.base = TILE_BASE + sum(TILES[:index])
        self.width = 512

    def tile_copy(self, i, slot):
        tile = self.tile
        return pltpu.make_async_remote_copy(
            src_ref=self.staged.at[slot, pl.ds(0, tile), pl.ds(0, self.columns)],
            dst_ref=self.held.at[rows_at(i * tile, tile)],
            send_sem=self.stage_sems.at[slot],
            recv_sem=self.m.recv_sems.at[self.base + i],
            device_id=self.p.other_core(),
            device_id_type=MESH,
        )

    def send(self):
        half, tile = self.rows // 2, self.tile

        def one(i, _):
            slot = lax.rem(i, 2)
            pl.when(i >= 2)(lambda: self.tile_copy(i, slot).wait_send())
            first = self.first + (1 - self.p.core) * half + i * tile
            for part in range(self.columns // self.width):
                got = product_tile(self.left, self.right, first, tile, self.width, part)
                self.staged[slot, pl.ds(0, tile), part * self.width : (part + 1) * self.width] = got.astype(
                    jnp.bfloat16
                )
            self.tile_copy(i, slot).start()
            return 0

        lax.fori_loop(0, half // tile, one, 0)
        for slot in range(min(2, half // tile)):
            self.tile_copy(0, slot).wait_send()

    def own(self):
        half, tile = self.rows // 2, self.tile

        def one(i, _):
            self.tile_copy(i, 0).wait_recv()
            first = self.first + self.p.core * half + i * tile
            here = rows_at(i * tile, tile)
            for part in range(self.columns // self.width):
                got = product_tile(self.left, self.right, first, tile, self.width, part)
                cut = slice(part * self.width, (part + 1) * self.width)
                total = got + self.held[here, cut].astype(jnp.float32)
                self.held[here, cut] = total.astype(jnp.bfloat16)
            return 0

        lax.fori_loop(0, half // tile, one, 0)


def row_scale(values):
    return lax.rsqrt(jnp.mean(values * values, axis=-1, keepdims=True) + epsilon)


def eight(values):
    rows, columns = values.shape
    return jnp.sum(values.reshape(rows // 8, 8, columns), axis=0)


def turn_back(values, cosines, sines):
    half = values.shape[1] // 2
    swapped = jnp.concatenate([values[:, half:], values[:, :half]], axis=1)
    return values * cosines + swapped * sines


def nt(left_side, right_side):
    return lax.dot_general(
        left_side, right_side, (((1,), (1,)), ((), ())), preferred_element_type=jnp.float32
    )


def tn(left_side, right_side):
    return lax.dot_general(
        left_side, right_side, (((0,), (0,)), ((), ())), preferred_element_type=jnp.float32
    )


class Layer:
    def __init__(self, place, mover, **refs):
        self.p, self.m = place, mover
        self.__dict__.update(refs)
        self.rows = self.x1.shape[0]
        self.mine = rows_at(place.y * self.rows, self.rows)
        self.theirs = rows_at((1 - place.y) * self.rows, self.rows)

    def load(self, source, target, index):
        copy = pltpu.make_async_copy(source, target, self.local_sems.at[index])
        copy.start()
        return copy

    def begin(self):
        self.waits = {}
        for i, (name, target) in enumerate(LOADED):
            self.waits[target] = self.load(getattr(self, name), getattr(self, target), 16 + i)
        self.waits["out_w"] = self.load(self.out_w, self.wbuf.at[pl.ds(0, 768)], 3)

    def need(self, *targets):
        for target in targets:
            if target in self.waits:
                self.waits.pop(target).wait()

    def stream(self, first, count, fetch, use):
        def go(i):
            for j, (source, target) in enumerate(fetch(i)):
                pltpu.make_async_copy(source, target, self.local_sems.at[8 + 2 * lax.rem(i, 2) + j]).start()

        go(jnp.int32(first))

        def body(i, _):
            pl.when(i + 1 < first + count)(lambda: go(i + 1))
            for j, (source, target) in enumerate(fetch(i)):
                pltpu.make_async_copy(source, target, self.local_sems.at[8 + 2 * lax.rem(i, 2) + j]).wait()
            use(i, lax.rem(i, 2))
            return 0

        lax.fori_loop(first, first + count, body, 0)

    def h2_third(self, third):
        self.need("d_gate", "d_up")

        def fetch(i):
            slot, here = lax.rem(i, 2), rows_at(i * 128, 128)
            return (
                (self.gate_w.at[here], self.staged.at[slot, pl.ds(0, 128)]),
                (self.up_w.at[here], self.staged.at[slot, pl.ds(128, 128)]),
            )

        def use(i, slot):
            cut = pl.ds(pl.multiple_of(i * 128, 128), 128)
            gate_w, up_w = self.staged[slot, 0:128, :], self.staged[slot, 128:256, :]
            for rows, target in ((self.theirs, self.h2_out), (self.mine, self.fbuf)):
                total = nt(self.d_gate[rows, :], gate_w) + nt(self.d_up[rows, :], up_w)
                target[:, cut] = total.astype(target.dtype)

        self.stream(4 * third, 4, fetch, use)
        if third == 2:
            self.h2_sent = self.m.copy(self.h2_out, self.h2_in, Y_BASE, self.p.other_y())
            self.h2_sent.start()

    def mlp_half(self, half):
        self.need("hid")

        rows, target = ((self.theirs, self.mlp_out), (self.mine, self.own))[half]
        self.fbuf[...] = jnp.zeros_like(self.fbuf)

        def fetch(i):
            return ((self.down_w.at[rows_at(i * 256, 256)], self.staged.at[lax.rem(i, 2), :, pl.ds(0, 1536)]),)

        def use(i, slot):
            cut = pl.ds(pl.multiple_of(i * 256, 256), 256)
            self.fbuf[...] += product(self.hid[rows, cut], self.staged[slot, :, 0:1536])

        self.stream(0, self.down_w.shape[0] // 256, fetch, use)
        target[...] = self.fbuf[...].astype(target.dtype)

    def tiles(self, step, body):
        lax.fori_loop(0, self.rows // step, lambda i, _: (body(i * step, step), 0)[1], 0)

    def middle(self):
        self.need("x1", "g")
        self.m.arrived(self.h2_in, Y_BASE, self.p.other_y())
        self.gains[...] = jnp.zeros_like(self.gains)

        def body(start, step):
            here = rows_at(start, step)
            there = rows_at(self.p.y * self.rows + start, step)
            d = self.fbuf[here, :] + self.h2_in[here, :].astype(jnp.float32)
            x1 = self.x1[here, :]
            inv = row_scale(x1)
            scaled = d * self.gain2[...].reshape(1, -1)
            inner = jnp.mean(scaled * x1, axis=-1, keepdims=True)
            self.gains[1] += eight(d * x1 * inv)
            d_x1 = self.g[there, :].astype(jnp.float32) + inv * (scaled - x1 * inv * inv * inner)
            self.d_x1[here, :] = d_x1
            self.d_attn[there, :] = d_x1.astype(jnp.bfloat16)

        self.tiles(16, body)
        own = self.d_attn.at[self.mine]
        self.m.start(own, own, Y_BASE + 1, self.p.other_y())

    def outward(self):
        self.m.arrived(self.d_attn.at[self.theirs], Y_BASE + 1, self.p.other_y())
        self.need("out_w")
        for part in range(3):
            cut = slice(part * 256, (part + 1) * 256)
            self.d_o[:, cut] = nt(self.d_attn[...], self.wbuf[cut, :]).astype(jnp.bfloat16)
        self.w_loads = [
            self.load(self.q_w, self.wbuf.at[:, pl.ds(0, 768)], 3),
            self.load(self.k_w, self.wbuf.at[:, pl.ds(768, 384)], 4),
            self.load(self.v_w, self.wbuf.at[:, pl.ds(1152, 384)], 5),
        ]

    def attention(self, key_head):
        self.need("q", "k", "v", "cosines", "sines", "starts")
        factor = HD ** (-0.5)
        c = key_head * HD
        keys, values = self.k[:, c : c + HD], self.v[:, c : c + HD]
        block = 256
        d_k = [jnp.zeros((block, HD), jnp.float32)] * 2
        d_v = [jnp.zeros((block, HD), jnp.float32)] * 2
        for head in (2 * key_head, 2 * key_head + 1):
            h = head * HD
            for i in range(2):
                here = slice(i * block, (i + 1) * block)
                n = block * (i + 1)
                query, d_out = self.q[here, h : h + HD], self.d_o[here, h : h + HD]
                column = lax.broadcasted_iota(jnp.int32, (block, n), 1)
                row = lax.broadcasted_iota(jnp.int32, (block, n), 0) + i * block
                allowed = (column <= row) & (column >= self.starts[here, :])
                masked = jnp.where(allowed, nt(query, keys[:n]) * factor, masked_score)
                exponent = jnp.exp(masked - jnp.max(masked, axis=1, keepdims=True))
                weights = exponent / jnp.sum(exponent, axis=1, keepdims=True)
                d_weights = nt(d_out, values[:n])
                inner = jnp.sum(weights * d_weights, axis=1, keepdims=True)
                d_scores = (weights * (d_weights - inner)).astype(jnp.bfloat16)
                low = weights.astype(jnp.bfloat16)
                d_query = jnp.dot(d_scores, keys[:n], preferred_element_type=jnp.float32) * factor
                turned = turn_back(d_query, self.cosines[here, :], self.sines[here, :])
                self.d_qkv[here, h : h + HD] = turned.astype(jnp.bfloat16)
                for j in range(i + 1):
                    cut = slice(j * block, (j + 1) * block)
                    d_k[j] = d_k[j] + tn(d_scores[:, cut], query) * factor
                    d_v[j] = d_v[j] + tn(low[:, cut], d_out)
        for j in range(2):
            cut = slice(j * block, (j + 1) * block)
            turned = turn_back(d_k[j], self.cosines[cut, :], self.sines[cut, :])
            self.d_qkv[cut, 768 + c : 768 + c + HD] = turned.astype(jnp.bfloat16)
            self.d_qkv[cut, 1152 + c : 1152 + c + HD] = d_v[j].astype(jnp.bfloat16)

    def h1_part(self, rows, put):
        def body(i, _):
            cut = pl.ds(pl.multiple_of(i * 256, 256), 256)
            put(cut, nt(self.d_qkv[rows, 0:1536], self.wbuf[cut, :]))
            return 0

        lax.fori_loop(0, 6, body, 0)

    def inward(self):
        for copy in self.w_loads:
            copy.wait()

        self.h2_sent.wait_send()
        self.waits["x"] = self.load(self.x_hbm, self.h2_in, 0)

        def put(cut, got):
            self.h2_out[:, cut] = got.astype(jnp.bfloat16)

        self.h1_part(self.theirs, put)
        self.m.start(self.h2_out, self.h1_in, Y_BASE + 2, self.p.other_y())

    def mlp_send(self):
        self.m.start(self.mlp_out, self.mlp_in, Y_BASE + 3, self.p.other_y())

    def finish(self):
        def put(cut, got):
            self.fbuf[:, cut] = got

        self.waits.pop("x").wait()
        self.h1_part(self.mine, put)
        self.m.arrived(self.h1_in, Y_BASE + 2, self.p.other_y())

        def body(start, step):
            here = rows_at(start, step)
            d = self.fbuf[here, :] + self.h1_in[here, :].astype(jnp.float32)
            x = self.h2_in[here, :].astype(jnp.float32)
            inv = row_scale(x)
            scaled = d * self.gain1[...].reshape(1, -1)
            inner = jnp.mean(scaled * x, axis=-1, keepdims=True)
            self.gains[0] += eight(d * x * inv)
            self.d_x1[here, :] = self.d_x1[here, :] + inv * (scaled - x * inv * inv * inner)

        self.tiles(16, body)
        copy = self.load(self.d_x1, self.tokens_out, 6)
        self.m.left.append((None, copy.wait))

    def layer_end(self):
        self.m.arrived(self.mlp_in, Y_BASE + 3, self.p.other_y())

        def body(start, step):
            here = rows_at(start, step)
            mlp = self.own[here, :].astype(jnp.float32) + self.mlp_in[here, :].astype(jnp.float32)
            out = self.x1[here, :] + mlp
            self.gains[2] += eight(out * out)
            self.gains[3] += eight(mlp * mlp)
            self.own[here, :] = out.astype(jnp.bfloat16)

        self.tiles(16, body)
        copy = self.load(self.own, self.layer_out, 7)
        self.m.left.append((None, copy.wait))
        self.totals[0] = jnp.zeros(self.totals.shape[1:], jnp.float32)
        for row in range(4):
            self.totals[0, row : row + 1, :] = jnp.sum(self.gains[row], axis=0, keepdims=True)
        self.totals[0, 4:5, :] = self.attn_squares[...]


def sum_small(place, mover, total, slots, step):
    device = (place.other_core, place.other_x, place.other_y, place.pair_z, place.far_z)[step]()
    copy = mover.copy(total.at[step], slots.at[step], SMALL_BASE + step, device)
    copy.start()
    copy.wait()
    total[step + 1] = total[step] + slots[step]


INPUTS = (
    "hid_hbm", "g_hbm", "h2_hbm", "d_gate_hbm", "d_up_hbm", "o_hbm", "h1_hbm", "q_hbm", "k_hbm", "v_hbm",
    "out_w", "q_w", "k_w", "v_w", "gate_w", "up_w", "down_w", "x1_hbm", "x_hbm", "cosines_hbm", "sines_hbm",
    "starts_hbm", "gain1", "gain2", "attn_squares",
)
IN_VMEM = ("gain1", "gain2", "attn_squares")
LOADED = (
    ("hid_hbm", "hid"), ("g_hbm", "g"), ("h2_hbm", "hbuf"), ("d_gate_hbm", "d_gate"), ("d_up_hbm", "d_up"),
    ("x1_hbm", "x1"), ("o_hbm", "o"), ("q_hbm", "q"), ("k_hbm", "k"), ("v_hbm", "v"),
    ("cosines_hbm", "cosines"), ("sines_hbm", "sines"), ("starts_hbm", "starts"),
)
RESULTS = ("down_out", "gate_out", "up_out", "o_out", "qkv_out", "tokens_out", "layer_out", "small_out")
PLAIN = (
    "staged", "hid", "hbuf", "own", "h2_in", "d_attn", "d_x1", "wbuf", "d_o", "h1_in", "mlp_in", "h2_out",
    "mlp_out", "fbuf", "gains", "totals", "slots", "g", "d_gate", "d_up", "o", "q", "k", "v", "x1",
    "cosines", "sines", "starts",
    "stage_sems", "send_sems", "recv_sems", "keep_sems", "local_sems",
)


def backward_kernel(*refs):
    n = len(UNITS)
    names = INPUTS + RESULTS
    r = dict(zip(names, refs[: len(names)]))
    rest = refs[len(names) :]
    held, across, along = rest[:n], rest[n : 3 * n], rest[3 * n : 5 * n]
    r.update(zip(PLAIN, rest[5 * n :]))
    r["d_qkv"] = r["hid"]
    place = Place()
    mover = Mover(r["send_sems"], r["recv_sems"])
    mover.keep_sems = r["keep_sems"]
    enter(place)
    layer = Layer(place, mover, **r)
    lefts = (r["hid"], r["hbuf"], r["hbuf"], r["o"], r["hbuf"])
    rights = (r["g"], r["d_gate"], r["d_up"], r["d_attn"], r["d_qkv"])
    results = tuple(r[name] for name in RESULTS[:5])
    units = [
        Unit(i, place, mover, lefts[unit[5]], rights[unit[5]], held[i], r["staged"], r["stage_sems"])
        for i, unit in enumerate(UNITS)
    ]
    steps = []
    for i, (rows, columns, x_rows, z_rows, _, kind, first) in enumerate(UNITS):
        for j in range(2):
            b = 2 * i + j
            block = Block(
                place, mover, held[i], across[b], along[b], results[kind], b * COPIES,
                0 if j == 0 else x_rows, x_rows if j == 0 else z_rows, rows // 2, j == 0, first,
            )
            steps.append(block.events())

    def send(i):
        kind, first = UNITS[i][5:]
        layer.need(*((("hid", "g"), ("hbuf", "d_gate"), ("hbuf", "d_up"), ("o",), ())[kind]))
        if kind == QKV and first == 0:
            layer.load(layer.h1_hbm, layer.hbuf, 1).wait()
        units[i].send()

    tasks = [layer.begin]
    tasks += [partial(layer.h2_third, i) for i in range(3)]
    tasks += [layer.middle, layer.outward]
    tasks += [partial(layer.attention, i) for i in range(4)]
    tasks += [layer.inward]
    tasks += [partial(layer.mlp_half, i) for i in range(2)]
    tasks += [layer.mlp_send, layer.finish, layer.layer_end]
    tasks += [partial(sum_small, place, mover, r["totals"], r["slots"], i) for i in range(SMALL_STEPS)]
    for item in ORDER:
        if item < 100:
            send(item)
        elif item < 200:
            units[item - 100].own()
        elif item < 1000:
            steps[item - 200].pop(0)()
        else:
            tasks[item - 1000]()
    r["small_out"][...] = r["totals"][SMALL_STEPS]
    for when, wait in mover.left:
        guarded(when, wait)


def enter(place):
    barrier = pltpu.get_barrier_semaphore()

    def greet(device):
        pl.semaphore_signal(barrier, inc=1, device_id=device, device_id_type=MESH)

    for device in (place.other_core(), place.other_x(), place.other_y(), place.pair_z(), place.far_z()):
        greet(device)
    middle = (place.z == 1) | (place.z == 2)
    pl.when(middle)(lambda: greet(place.at(3 - place.z, place.x, place.core, place.y)))
    pl.semaphore_wait(barrier, 5 + jnp.where(middle, 1, 0))


def backward(**given):
    vmem = pl.BlockSpec(memory_space=pltpu.VMEM)
    hbm = pl.BlockSpec(memory_space=pl.ANY)
    low, full = jnp.bfloat16, jnp.float32
    own_rows, width = given["x1_hbm"].shape
    held = [pltpu.VMEM((rows // 2, columns), low) for rows, columns, *_ in UNITS]
    across, along = [], []
    for _, columns, x_rows, z_rows, *_ in UNITS:
        across += [pltpu.VMEM((x_rows // 2, columns), low), pltpu.VMEM((z_rows // 8, columns), low)]
        along += [pltpu.VMEM((5, x_rows // 8, columns), low), pltpu.VMEM((5, z_rows // 4, columns), low)]
    part = pltpu.VMEM((own_rows, width), low)
    plain = dict(
        staged=pltpu.VMEM((2, 256, 2048), low),
        hid=pltpu.VMEM((512, 2048), low),
        hbuf=pltpu.VMEM((512, width), low),
        own=part,
        h2_in=part,
        d_attn=pltpu.VMEM((512, width), low),
        d_x1=pltpu.VMEM((own_rows, width), full),
        wbuf=pltpu.VMEM((1536, 1536), low),
        d_o=pltpu.VMEM((512, 768), low),
        h1_in=part,
        mlp_in=part,
        h2_out=part,
        mlp_out=part,
        fbuf=pltpu.VMEM((own_rows, width), full),
        gains=pltpu.VMEM((4, 8, width), full),
        totals=pltpu.VMEM((SMALL_STEPS + 1, 8, width), full),
        slots=pltpu.VMEM((SMALL_STEPS, 8, width), full),
        stage_sems=pltpu.SemaphoreType.DMA((2,)),
        send_sems=pltpu.SemaphoreType.DMA((N_SEMS,)),
        recv_sems=pltpu.SemaphoreType.DMA((N_SEMS,)),
        keep_sems=pltpu.SemaphoreType.DMA((2 * len(UNITS),)),
        local_sems=pltpu.SemaphoreType.DMA((16 + len(LOADED),)),
    )
    for name, target in LOADED:
        plain.setdefault(target, pltpu.VMEM(given[name].shape, given[name].dtype))
    flops = sum(2 * 512 * rows * columns for rows, columns, *_ in UNITS)
    return pl.pallas_call(
        backward_kernel,
        out_shape=[jax.ShapeDtypeStruct(shape, low) for shape in WHOLE]
        + [
            jax.ShapeDtypeStruct((own_rows, width), full),
            jax.ShapeDtypeStruct((own_rows, width), low),
            jax.ShapeDtypeStruct((8, width), full),
        ],
        in_specs=[vmem if name in IN_VMEM else hbm for name in INPUTS],
        out_specs=[hbm] * 7 + [vmem],
        scratch_shapes=held + across + along + [plain[name] for name in PLAIN],
        compiler_params=pltpu.CompilerParams(
            collective_id=0, has_side_effects=True, vmem_limit_bytes=62 << 20
        ),
        cost_estimate=pl.CostEstimate(flops=flops, bytes_accessed=80 << 20, transcendentals=0),
        name="backward",
    )(*(given[name] for name in INPUTS))


FORWARD_INPUTS = (
    "x", "lengths", "gain1", "gain2", "inverse", "q_w", "k_w", "v_w", "out_w", "gate_w", "up_w", "down_w", "g_own",
)
FORWARD_RESULTS = (
    "hid_to", "g_to", "h2_to", "d_gate_to", "d_up_to", "o_to", "h1_to", "q_to", "k_to", "v_to", "x1_to",
    "cosines", "sines", "starts", "attn_squares",
)
FORWARD_PLAIN = (
    "x_in", "w_qkv", "w_out", "w_gate", "w_up", "w_down", "g", "h1", "lin", "q", "k", "v", "o", "own_part",
    "sent_part", "got_part", "x1", "h2", "d_hid", "hid", "d_gate", "d_up", "squares",
    "send_sems", "recv_sems", "load_sems", "store_sems",
)
CHUNKS = 2


class Forward:
    def __init__(self, refs):
        self.__dict__.update(refs)
        self.p = Place()
        self.m = Mover(self.send_sems, self.recv_sems)
        self.rows = self.x.shape[0]
        self.step = self.rows // CHUNKS
        self.base = self.p.y * self.rows
        self.far = (1 - self.p.y) * self.rows
        self.stores = 0

    def load(self, source, target, index):
        copy = pltpu.make_async_copy(source, target, self.load_sems.at[index])
        copy.start()
        return copy

    def store(self, source, target):
        copy = pltpu.make_async_copy(source, target, self.store_sems.at[self.stores])
        self.stores += 1
        copy.start()
        self.m.left.append((None, copy.wait))

    def across(self, source, target, index):
        self.m.start(source, target, index, self.p.other_y())

    def arrived(self, target, index):
        self.m.arrived(target, index, self.p.other_y())

    def tiles(self, first, count, step, body):
        lax.fori_loop(0, count // step, lambda i, _: (body(first + i * step, step), 0)[1], 0)

    def run(self):
        step = self.step
        barrier = pltpu.get_barrier_semaphore()
        pl.semaphore_signal(barrier, inc=1, device_id=self.p.other_y(), device_id_type=MESH)
        pl.semaphore_wait(barrier, 1)
        for c in range(CHUNKS):
            part = pl.ds(c * step, step)
            self.across(self.x.at[part], self.x_in.at[part], c)
        self.across(self.g_own, self.g.at[rows_at(self.base, self.rows)], 2 * CHUNKS)
        qkv_loads = [
            self.load(self.q_w, self.w_qkv.at[:, pl.ds(0, 768)], 0),
            self.load(self.k_w, self.w_qkv.at[:, pl.ds(768, 384)], 1),
            self.load(self.v_w, self.w_qkv.at[:, pl.ds(1152, 384)], 2),
        ]
        g_load = self.load(self.g_own, self.g.at[rows_at(self.base, self.rows)], 3)
        out_load = self.load(self.out_w, self.w_out, 4)
        down_load = self.load(self.down_w, self.w_down, 5)
        gate_load = self.load(self.gate_w, self.w_gate, 6)
        up_load = self.load(self.up_w, self.w_up, 7)
        self.tables()
        self.norm1(self.x, 0, self.base, self.rows)
        for copy in qkv_loads:
            copy.wait()
        self.qkv(self.base, self.rows)
        for c in range(CHUNKS):
            self.arrived(self.x_in.at[pl.ds(c * step, step)], c)
            self.norm1(self.x_in, c * step, self.far + c * step, step)
            self.qkv(self.far + c * step, step)
        self.store(self.h1, self.h1_to)
        self.store(self.q, self.q_to)
        self.store(self.k, self.k_to)
        self.store(self.v, self.v_to)
        self.attention(self.far)
        out_load.wait()
        for c in range(CHUNKS):
            part = pl.ds(c * step, step)
            self.project(self.far + c * step, self.sent_part, c * step, step)
            self.across(self.sent_part.at[part], self.got_part.at[part], CHUNKS + c)
        self.attention(self.base)
        self.store(self.o, self.o_to)
        self.project(self.base, self.own_part, 0, self.rows)
        g_load.wait()
        down_load.wait()
        self.hidden_grad(self.base, self.rows)
        self.arrived(self.g.at[rows_at(self.far, self.rows)], 2 * CHUNKS)
        self.store(self.g, self.g_to)
        self.hidden_grad(self.far, self.rows)
        self.squares[...] = jnp.zeros_like(self.squares)
        for c in range(CHUNKS):
            self.arrived(self.got_part.at[pl.ds(c * step, step)], CHUNKS + c)
            self.norm2(c * step)
            mine = self.h2.at[rows_at(self.base + c * step, step)]
            self.across(mine, mine, 2 * CHUNKS + 1 + c)
        self.store(self.x1, self.x1_to)
        self.attn_squares[...] = jnp.sum(self.squares[...], axis=0, keepdims=True)
        gate_load.wait()
        up_load.wait()
        self.feed(self.base, self.rows)
        for c in range(CHUNKS):
            self.arrived(self.h2.at[rows_at(self.far + c * step, step)], 2 * CHUNKS + 1 + c)
            self.feed(self.far + c * step, step)
        for name in ("h2", "hid", "d_gate", "d_up"):
            self.store(getattr(self, name), getattr(self, name + "_to"))
        for when, wait in self.m.left:
            guarded(when, wait)

    def tables(self):
        total = self.starts.shape[0]
        row = lax.broadcasted_iota(jnp.int32, (total, 1), 0)
        first = jnp.zeros((total, 1), jnp.int32)
        end = jnp.int32(0)
        for j in range(self.lengths.shape[1]):
            first = jnp.where(row >= end, end, first)
            end = end + self.lengths[0, j]
        self.starts[...] = first
        angles = (row - first).astype(jnp.float32) * self.inverse[...]
        self.cosines[...] = jnp.cos(angles)
        half = lax.broadcasted_iota(jnp.int32, (total, HD), 1) < HD // 2
        sines = jnp.sin(angles)
        self.sines[...] = jnp.where(half, sines, -sines)

    def norm1(self, source, source_row, row, count):
        def body(i, step):
            x = source[rows_at(source_row + i, step), :].astype(jnp.float32)
            self.h1[rows_at(row + i, step), :] = (x * row_scale(x) * self.gain1[...].reshape(1, -1)).astype(jnp.bfloat16)

        self.tiles(0, count, 32, body)

    def qkv(self, row, count):
        here = rows_at(row, count)
        values = self.h1[here, :]
        for part in range(3):
            cut = slice(part * 512, (part + 1) * 512)
            self.lin[0:count, cut] = product(values, self.w_qkv[:, cut])
        cosines, sines = self.cosines[here, :], -self.sines[here, :]
        for target, first in ((self.q, 0), (self.k, 768)):
            for head in range(target.shape[1] // HD):
                linear = self.lin[0:count, first + head * HD : first + (head + 1) * HD]
                turned = turn_back(linear, cosines, sines)
                target[here, head * HD : (head + 1) * HD] = turned.astype(jnp.bfloat16)
        self.v[here, :] = self.lin[0:count, 1152:1536].astype(jnp.bfloat16)

    def attention(self, row):
        count, total = self.rows, self.q.shape[0]
        here = rows_at(row, count)
        column = lax.broadcasted_iota(jnp.int32, (count, total), 1)
        own = lax.broadcasted_iota(jnp.int32, (count, total), 0) + row
        allowed = (column <= own) & (column >= self.starts[here, :])
        for key_head in range(self.k.shape[1] // HD):
            c = key_head * HD
            keys, values = self.k[:, c : c + HD], self.v[:, c : c + HD]
            for head in (2 * key_head, 2 * key_head + 1):
                h = head * HD
                raw = nt(self.q[here, h : h + HD], keys) * HD ** (-0.5)
                masked = jnp.where(allowed, raw, masked_score)
                exponent = jnp.exp(masked - jnp.max(masked, axis=1, keepdims=True))
                weights = exponent / jnp.sum(exponent, axis=1, keepdims=True)
                out = product(weights.astype(jnp.bfloat16), values)
                self.o[here, h : h + HD] = out.astype(jnp.bfloat16)

    def project(self, row, target, target_row, count):
        values = self.o[rows_at(row, count), :]
        for part in range(3):
            cut = slice(part * 512, (part + 1) * 512)
            target[target_row : target_row + count, cut] = product(values, self.w_out[:, cut]).astype(target.dtype)

    def hidden_grad(self, row, count):
        here = rows_at(row, count)

        def body(i, _):
            cut = pl.ds(pl.multiple_of(i * 256, 256), 256)
            self.d_hid[here, cut] = nt(self.g[here, :], self.w_down[cut, :])
            return 0

        lax.fori_loop(0, self.w_down.shape[0] // 256, body, 0)

    def norm2(self, start):
        def body(i, step):
            here = rows_at(i, step)
            attn = self.own_part[here, :] + self.got_part[here, :].astype(jnp.float32)
            self.squares[...] += eight(attn * attn)
            x1 = self.x[here, :].astype(jnp.float32) + attn
            self.x1[here, :] = x1
            self.h2[rows_at(self.base + i, step), :] = (x1 * row_scale(x1) * self.gain2[...].reshape(1, -1)).astype(jnp.bfloat16)

        self.tiles(start, self.step, 16, body)

    def feed(self, row, count):
        here = rows_at(row, count)

        def body(i, _):
            cut = pl.ds(pl.multiple_of(i * 256, 256), 256)
            values = self.h2[here, :]
            gate = product(values, self.w_gate[:, cut])
            up = product(values, self.w_up[:, cut])
            d_hid = self.d_hid[here, cut]
            sig = 1.0 / (1.0 + jnp.exp(-gate))
            self.hid[here, cut] = (gate * sig * up).astype(jnp.bfloat16)
            self.d_gate[here, cut] = (d_hid * up * sig * (1.0 + gate * (1.0 - sig))).astype(jnp.bfloat16)
            self.d_up[here, cut] = (d_hid * gate * sig).astype(jnp.bfloat16)
            return 0

        lax.fori_loop(0, self.w_gate.shape[1] // 256, body, 0)


def forward_kernel(*refs):
    names = FORWARD_INPUTS + FORWARD_RESULTS + FORWARD_PLAIN
    Forward(dict(zip(names, refs))).run()


def forward(**given):
    vmem = pl.BlockSpec(memory_space=pltpu.VMEM)
    hbm = pl.BlockSpec(memory_space=pl.ANY)
    smem = pl.BlockSpec(memory_space=pltpu.SMEM)
    low, full = jnp.bfloat16, jnp.float32
    own, width = given["x"].shape
    total = 2 * own
    units = given["gate_w"].shape[1]
    q_cols, k_cols = given["q_w"].shape[1], given["k_w"].shape[1]
    shapes = dict(
        hid_to=((total, units), low), g_to=((total, width), low), h2_to=((total, width), low),
        d_gate_to=((total, units), low), d_up_to=((total, units), low), o_to=((total, q_cols), low),
        h1_to=((total, width), low), q_to=((total, q_cols), low), k_to=((total, k_cols), low),
        v_to=((total, k_cols), low), x1_to=((own, width), full), cosines=((total, HD), full), sines=((total, HD), full),
        starts=((total, 1), jnp.int32), attn_squares=((1, width), full),
    )
    plain = dict(
        x_in=((own, width), low), w_qkv=((width, q_cols + 2 * k_cols), low), w_out=((q_cols, width), low),
        w_gate=((width, units), low), w_up=((width, units), low), w_down=((units, width), low),
        g=((total, width), low), h1=((total, width), low), lin=((own, q_cols + 2 * k_cols), full),
        q=((total, q_cols), low), k=((total, k_cols), low), v=((total, k_cols), low), o=((total, q_cols), low),
        own_part=((own, width), full), sent_part=((own, width), low), got_part=((own, width), low),
        x1=((own, width), full), h2=((total, width), low), d_hid=((total, units), full), hid=((total, units), low),
        d_gate=((total, units), low), d_up=((total, units), low), squares=((8, width), full),
    )
    scratch = [pltpu.VMEM(*plain[name]) for name in FORWARD_PLAIN if name in plain]
    copies = 3 * CHUNKS + 1
    scratch += [pltpu.SemaphoreType.DMA((n,)) for n in (copies, copies, 8, 16)]
    spaces = dict.fromkeys(("q_w", "k_w", "v_w", "out_w", "gate_w", "up_w", "down_w", "g_own"), hbm)
    spaces["lengths"] = smem
    out = pl.pallas_call(
        forward_kernel,
        out_shape=[jax.ShapeDtypeStruct(*shapes[name]) for name in FORWARD_RESULTS],
        in_specs=[spaces.get(name, vmem) for name in FORWARD_INPUTS],
        out_specs=[hbm if name.endswith("_to") else vmem for name in FORWARD_RESULTS],
        scratch_shapes=scratch,
        compiler_params=pltpu.CompilerParams(
            collective_id=1, has_side_effects=True, vmem_limit_bytes=62 << 20
        ),
        cost_estimate=pl.CostEstimate(flops=26 * 10**9, bytes_accessed=60 << 20, transcendentals=0),
        name="forward",
    )(*(given[name] for name in FORWARD_INPUTS))
    return dict(zip(FORWARD_RESULTS, out))


def results_kernel(
    down, gate, up, o, qkv, tokens_in, layer_in, small,
    layer_out, tokens_out, gain1_out, q_out, k_out, v_out, o_out, gain2_out, gate_out, up_out, down_out, rms_out,
    taken, made, tokens_held, layer_held, in_sems, out_sems, whole_sems, *, tokens,
):
    held = ((tokens_in, tokens_held, tokens_out), (layer_in, layer_held, layer_out))
    inward = [pltpu.make_async_copy(a, b, whole_sems.at[i]) for i, (a, b, _) in enumerate(held)]
    outward = [pltpu.make_async_copy(b, c, whole_sems.at[i]) for i, (_, b, c) in enumerate(held)]
    for copy in inward:
        copy.start()
    q_cols, k_cols = q_out.shape[1], k_out.shape[1]
    tile = taken.shape[1]
    work = []
    for source, targets in (
        (down, ((down_out, 0),)),
        (gate, ((gate_out, 0),)),
        (up, ((up_out, 0),)),
        (qkv, ((q_out, 0), (k_out, q_cols), (v_out, q_cols + k_cols))),
        (o, ((o_out, 0),)),
    ):
        work += [(source, targets, row) for row in range(0, source.shape[0], tile)]
    slots = taken.shape[0]

    def take(i):
        source, _, row = work[i]
        return pltpu.make_async_copy(
            source.at[pl.ds(row, tile)], taken.at[i % slots, :, pl.ds(0, source.shape[1])], in_sems.at[i % slots]
        )

    def give(i):
        _, targets, row = work[i]
        return [
            pltpu.make_async_copy(
                made.at[i % slots, :, pl.ds(first, target.shape[1])],
                target.at[pl.ds(row, tile)],
                out_sems.at[i % slots, j],
            )
            for j, (target, first) in enumerate(targets)
        ]

    for i in range(min(slots - 1, len(work))):
        take(i).start()
    for i in range(len(work)):
        if i + slots - 1 < len(work):
            take(i + slots - 1).start()
        take(i).wait()
        if i >= slots:
            for copy in give(i - slots):
                copy.wait()
        columns = work[i][0].shape[1]

        def one(j, _, slot=i % slots, columns=columns):
            here = rows_at(j * 32, 32)
            made[slot, here, 0:columns] = taken[slot, here, 0:columns].astype(jnp.float32)
            return 0

        lax.fori_loop(0, tile // 32, one, 0)
        for copy in give(i):
            copy.start()
    for i in range(2):
        inward[i].wait()
        outward[i].start()
    gain1_out[...] = small[0, :]
    gain2_out[...] = small[1, :]
    lane = lax.broadcasted_iota(jnp.int32, (1, 3), 1)
    sums = [jnp.sum(small[row : row + 1, :], axis=1, keepdims=True) for row in (2, 4, 3)]
    squares = jnp.where(lane == 0, sums[0], jnp.where(lane == 1, sums[1], sums[2]))
    rms_out[...] = jnp.sqrt(squares / tokens)
    for i in range(max(0, len(work) - slots), len(work)):
        for copy in give(i):
            copy.wait()
    for copy in outward:
        copy.wait()


def results(sums, tokens_grad, layer_out, small, q_cols, k_cols, tokens):
    vmem = pl.BlockSpec(memory_space=pltpu.VMEM)
    hbm = pl.BlockSpec(memory_space=pl.ANY)
    full = jnp.float32
    down, gate, up, o, qkv = sums
    width = small.shape[1]
    rows = qkv.shape[0]
    shapes = (
        (layer_out.shape, layer_out.dtype, hbm), (tokens_grad.shape, full, hbm), ((width,), full, vmem),
        ((rows, q_cols), full, hbm), ((rows, k_cols), full, hbm), ((rows, k_cols), full, hbm),
        (o.shape, full, hbm), ((width,), full, vmem), (gate.shape, full, hbm), (up.shape, full, hbm),
        (down.shape, full, hbm), ((1, 3), full, vmem),
    )
    slots, tile = 8, 256
    columns = max(part.shape[1] for part in sums)
    out = pl.pallas_call(
        partial(results_kernel, tokens=tokens),
        out_shape=[jax.ShapeDtypeStruct(shape, dtype) for shape, dtype, _ in shapes],
        in_specs=[hbm] * 7 + [vmem],
        out_specs=[space for _, _, space in shapes],
        scratch_shapes=[
            pltpu.VMEM((slots, tile, columns), jnp.bfloat16),
            pltpu.VMEM((slots, tile, columns), full),
            pltpu.VMEM(tokens_grad.shape, full),
            pltpu.VMEM(layer_out.shape, layer_out.dtype),
            pltpu.SemaphoreType.DMA((slots,)),
            pltpu.SemaphoreType.DMA((slots, 3)),
            pltpu.SemaphoreType.DMA((2,)),
        ],
        compiler_params=pltpu.CompilerParams(vmem_limit_bytes=62 << 20),
        cost_estimate=pl.CostEstimate(flops=0, bytes_accessed=78 * 10**6, transcendentals=0),
        name="results",
    )(*sums, tokens_grad, layer_out, small)
    return tuple(part.reshape(-1) if part.shape[0] == 1 else part for part in out)


def dp_sum(terms):
    low = lax.psum(tuple(term.astype(jnp.bfloat16) for term in terms), "dp")
    return tuple(term.astype(jnp.float32) for term in low)


def low_scatter(partial):
    return lax.psum_scatter(
        partial.astype(jnp.bfloat16), "tensor", scatter_dimension=0, tiled=True
    ).astype(jnp.float32)


def body(
    tokens,
    lengths,
    first_gain,
    query_weight,
    key_weight,
    value_weight,
    output_weight,
    second_gain,
    gate_weight,
    up_weight,
    down_weight,
    out_cotangent,
):
    inputs = tokens.astype(jnp.float32)
    normed1, inv_first = norm_rows(inputs, first_gain)
    normed1 = normed1.astype(jnp.bfloat16)
    full_first = lax.all_gather(normed1, "tensor", axis=0, tiled=True)
    total_rows = full_first.shape[0]
    places, segment, cosine_table, sine_table = tables(lengths[0], total_rows, HD // 2)
    kv_heads = key_weight.shape[1] // HD
    groups = query_weight.shape[1] // key_weight.shape[1]
    query = rotate(product(full_first, query_weight), cosine_table, sine_table, 1.0).astype(
        jnp.bfloat16
    )
    keys = rotate(product(full_first, key_weight), cosine_table, sine_table, 1.0).astype(
        jnp.bfloat16
    )
    values = product(full_first, value_weight).astype(jnp.bfloat16)
    block_rows = min(block_limit, total_rows)
    block_count = total_rows // block_rows
    query_blocks = query.reshape(block_count, block_rows, kv_heads, groups, HD)
    seg_blocks = segment.reshape(block_count, block_rows)
    place_blocks = places.reshape(block_count, block_rows)
    key_three = keys.reshape(total_rows, kv_heads, HD)
    value_three = values.reshape(total_rows, kv_heads, HD)
    factor = HD ** (-0.5)

    def scores(query_block, seg_block, place_block):
        raw = (
            jnp.einsum("qcgd,kcd->cgqk", query_block, key_three, preferred_element_type=jnp.float32)
            * factor
        )
        allowed = (seg_block[:, None] == segment[None, :]) & (
            place_block[:, None] >= places[None, :]
        )
        return (jnp.where(allowed[None, None], raw, masked_score), allowed)

    def forward_block(piece_set):
        query_block, seg_block, place_block = piece_set
        masked, allowed = scores(query_block, seg_block, place_block)
        highest = jnp.max(masked, axis=-1, keepdims=True)
        exponent = jnp.exp(masked - highest)
        denominator = jnp.sum(exponent, axis=-1, keepdims=True)
        weights = exponent / denominator
        output = jnp.einsum(
            "cgqk,kcd->qcgd",
            weights.astype(jnp.bfloat16),
            value_three,
            preferred_element_type=jnp.float32,
        )
        stored = (highest + jnp.log(denominator))[..., 0]
        return (output.reshape(block_rows, -1), stored)

    out_blocks, kept_blocks = lax.map(forward_block, (query_blocks, seg_blocks, place_blocks))
    attended = out_blocks.reshape(total_rows, -1).astype(jnp.bfloat16)
    attn_rows = low_scatter(product(attended, output_weight))
    middle = inputs + attn_rows
    normed2, inv_second = norm_rows(middle, second_gain)
    normed2 = normed2.astype(jnp.bfloat16)
    full_second = lax.all_gather(normed2, "tensor", axis=0, tiled=True)
    gate_value = product(full_second, gate_weight)
    upward = product(full_second, up_weight)
    gate_sig = jax.nn.sigmoid(gate_value)
    hidden = (gate_value * gate_sig * upward).astype(jnp.bfloat16)
    mlp_rows = low_scatter(product(hidden, down_weight))
    layer_out = middle + mlp_rows
    squares = jnp.stack(
        [
            jnp.sum(layer_out * layer_out),
            jnp.sum(attn_rows * attn_rows),
            jnp.sum(mlp_rows * mlp_rows),
        ]
    )
    grad_full = lax.all_gather(out_cotangent, "tensor", axis=0, tiled=True)
    grad_hidden = times_cols(grad_full, down_weight)
    down_g = times_rows(hidden, grad_full)
    gate_slope = gate_sig * (1.0 + gate_value * (1.0 - gate_sig))
    grad_gate = (grad_hidden * upward * gate_slope).astype(jnp.bfloat16)
    grad_up = (grad_hidden * gate_value * gate_sig).astype(jnp.bfloat16)
    gate_g = times_rows(full_second, grad_gate)
    up_g = times_rows(full_second, grad_up)
    gate_g, up_g, down_g = dp_sum((gate_g, up_g, down_g))
    grad_normed2 = low_scatter(
        times_cols(grad_gate, gate_weight) + times_cols(grad_up, up_weight)
    )
    second_rows, grad_mid_norm = norm_back(middle, inv_second, second_gain, grad_normed2)
    grad_middle = out_cotangent.astype(jnp.float32) + grad_mid_norm
    grad_attn_full = lax.all_gather(grad_middle.astype(jnp.bfloat16), "tensor", axis=0, tiled=True)
    output_g = times_rows(attended, grad_attn_full)
    grad_out = times_cols(grad_attn_full, output_weight).astype(jnp.bfloat16)
    grad_blocks = grad_out.reshape(block_count, block_rows, kv_heads, groups, HD)

    def backward_block(running, piece_set):
        key_acc, value_acc = running
        query_block, seg_block, place_block, grad_block, stored = piece_set
        masked, allowed = scores(query_block, seg_block, place_block)
        weights = jnp.where(allowed[None, None], jnp.exp(masked - stored[..., None]), 0.0)
        grad_weights = jnp.einsum(
            "qcgd,kcd->cgqk", grad_block, value_three, preferred_element_type=jnp.float32
        )
        row_inner = jnp.sum(weights * grad_weights, axis=-1, keepdims=True)
        grad_scores = (weights * (grad_weights - row_inner)).astype(jnp.bfloat16)
        grad_query = (
            jnp.einsum("cgqk,kcd->qcgd", grad_scores, key_three, preferred_element_type=jnp.float32)
            * factor
        )
        key_acc = (
            key_acc
            + jnp.einsum(
                "cgqk,qcgd->kcd", grad_scores, query_block, preferred_element_type=jnp.float32
            )
            * factor
        )
        value_acc = value_acc + jnp.einsum(
            "cgqk,qcgd->kcd",
            weights.astype(jnp.bfloat16),
            grad_block,
            preferred_element_type=jnp.float32,
        )
        return ((key_acc, value_acc), grad_query.reshape(block_rows, -1))

    zeros_kv = jnp.zeros((total_rows, kv_heads, HD), jnp.float32)
    (key_rot_grad, value_acc_grad), query_rot_grad = lax.scan(
        backward_block,
        (zeros_kv, zeros_kv),
        (query_blocks, seg_blocks, place_blocks, grad_blocks, kept_blocks),
    )
    query_lin = rotate(
        query_rot_grad.reshape(total_rows, -1), cosine_table, sine_table, -1.0
    ).astype(jnp.bfloat16)
    key_lin = rotate(key_rot_grad.reshape(total_rows, -1), cosine_table, sine_table, -1.0).astype(
        jnp.bfloat16
    )
    value_lin = value_acc_grad.reshape(total_rows, -1).astype(jnp.bfloat16)
    query_g = times_rows(full_first, query_lin)
    key_g = times_rows(full_first, key_lin)
    value_g = times_rows(full_first, value_lin)
    grad_normed1 = low_scatter(
        times_cols(query_lin, query_weight)
        + times_cols(key_lin, key_weight)
        + times_cols(value_lin, value_weight)
    )
    first_rows, grad_in_norm = norm_back(inputs, inv_first, first_gain, grad_normed1)
    tokens_grad = grad_middle + grad_in_norm
    gain_rows = jnp.stack([first_rows, second_rows])
    query_g, key_g, value_g, output_g = dp_sum((query_g, key_g, value_g, output_g))
    gain_rows, squares = lax.psum((gain_rows, squares), ("dp", "tensor"))
    rms_values = jnp.sqrt(squares / (total_rows * lax.axis_size("dp")))
    return (
        layer_out.astype(jnp.bfloat16),
        tokens_grad,
        gain_rows[0],
        query_g,
        key_g,
        value_g,
        output_g,
        gain_rows[1],
        gate_g,
        up_g,
        down_g,
        rms_values,
    )


def fused_body(
    tokens,
    lengths,
    first_gain,
    query_weight,
    key_weight,
    value_weight,
    output_weight,
    second_gain,
    gate_weight,
    up_weight,
    down_weight,
    out_cotangent,
):
    half_size = HD // 2
    inverse = (rope_base ** (-2.0 * np.arange(half_size) / (2 * half_size))).astype(np.float32)
    made = forward(
        x=tokens,
        lengths=lengths,
        gain1=first_gain,
        gain2=second_gain,
        inverse=jnp.asarray(np.concatenate([inverse, inverse])[None]),
        q_w=query_weight,
        k_w=key_weight,
        v_w=value_weight,
        out_w=output_weight,
        gate_w=gate_weight,
        up_w=up_weight,
        down_w=down_weight,
        g_own=out_cotangent,
    )
    *sums, tokens_grad, layer_out, small = backward(
        **{name + "_hbm": made[name + "_to"] for name in ("hid", "g", "h2", "d_gate", "d_up", "o", "h1")},
        **{name + "_hbm": made[name + "_to"] for name in ("q", "k", "v", "x1")},
        **{name + "_hbm": made[name] for name in ("cosines", "sines", "starts")},
        x_hbm=tokens,
        out_w=output_weight,
        q_w=query_weight,
        k_w=key_weight,
        v_w=value_weight,
        gate_w=gate_weight,
        up_w=up_weight,
        down_w=down_weight,
        gain1=first_gain,
        gain2=second_gain,
        attn_squares=made["attn_squares"],
    )
    return results(
        sums, tokens_grad, layer_out, small, query_weight.shape[1], key_weight.shape[1],
        2 * tokens.shape[0] * lax.axis_size("dp"),
    )


def solution(mesh):
    in_specs = (
        P(("dp", "tensor"), None),
        P("dp", None),
        P(),
        P(None, "tensor"),
        P(None, "tensor"),
        P(None, "tensor"),
        P("tensor", None),
        P(),
        P(None, "tensor"),
        P(None, "tensor"),
        P("tensor", None),
        P(("dp", "tensor"), None),
    )
    out_specs = (
        P(("dp", "tensor"), None),
        P(("dp", "tensor"), None),
        P(),
        P(None, "tensor"),
        P(None, "tensor"),
        P(None, "tensor"),
        P("tensor", None),
        P(),
        P(None, "tensor"),
        P(None, "tensor"),
        P("tensor", None),
        P(),
    )
    fused = dict(mesh.shape) == {"dp": 16, "tensor": 2}
    chosen = fused_body if fused else body
    return jax.shard_map(chosen, mesh=mesh, in_specs=in_specs, out_specs=out_specs, check_vma=False)
```

```python
from functools import partial

import jax
import jax.numpy as jnp
import numpy as np
from jax import lax
from jax.experimental import pallas as pl
from jax.experimental.pallas import tpu as pltpu
from jax.sharding import PartitionSpec as P

HD = 96


epsilon = 1e-05
rope_base = 10000.0
masked_score = -1e30
block_limit = 512


def product(left_side, right_side):
    return jnp.dot(left_side, right_side, preferred_element_type=jnp.float32)


def times_rows(left_side, right_side):
    return lax.dot_general(
        left_side, right_side, (((0,), (0,)), ((), ())), preferred_element_type=jnp.float32
    )


def times_cols(left_side, right_side):
    return lax.dot_general(
        left_side, right_side, (((1,), (1,)), ((), ())), preferred_element_type=jnp.float32
    )


def tables(lens_row, total_rows, half_size):
    count = lens_row.shape[0]
    earlier = jnp.arange(count)[:, None] <= jnp.arange(count)[None, :]
    seq_ends = jnp.sum(jnp.where(earlier, lens_row[:, None], 0), axis=0, dtype=jnp.int32)
    starts = seq_ends - lens_row
    places = jnp.arange(total_rows, dtype=jnp.int32)
    segment = jnp.sum(
        (places[:, None] >= seq_ends[None, :]).astype(jnp.int32), axis=1, dtype=jnp.int32
    )
    member = segment[:, None] == jnp.arange(lens_row.shape[0], dtype=jnp.int32)[None, :]
    position = places - jnp.sum(jnp.where(member, starts[None, :], 0), axis=1, dtype=jnp.int32)
    inverse = rope_base ** (-2.0 * jnp.arange(half_size, dtype=jnp.float32) / (2 * half_size))
    angles = position.astype(jnp.float32)[:, None] * inverse[None, :]
    return (places, segment, jnp.cos(angles), jnp.sin(angles))


def rotate(values, cosine_table, sine_table, direction):
    total_rows = values.shape[0]
    half_size = cosine_table.shape[1]
    shaped = values.reshape(total_rows, -1, 2 * half_size)
    first_half = shaped[..., :half_size]
    second = shaped[..., half_size:]
    cos_b = cosine_table[:, None, :]
    sin_b = sine_table[:, None, :] * direction
    turned = jnp.concatenate(
        [first_half * cos_b - second * sin_b, second * cos_b + first_half * sin_b], axis=-1
    )
    return turned.reshape(total_rows, -1)


def norm_rows(values, gain):
    inv_rms = lax.rsqrt(jnp.mean(values * values, axis=-1, keepdims=True) + epsilon)
    return (values * inv_rms * gain, inv_rms)


def norm_back(values, inv_rms, gain, upstream):
    scaled = upstream * gain
    row_inner = jnp.mean(scaled * values, axis=-1, keepdims=True)
    gain_rows = jnp.sum(upstream * values * inv_rms, axis=0)
    return (gain_rows, inv_rms * (scaled - values * inv_rms * inv_rms * row_inner))


ORDER = (
    1000, 1, 2, 101, 203, 202, 102, 1001, 203, 205, 1002, 203, 1003, 205, 202, 203, 203, 0, 205,
    203, 204, 100, 202, 203, 205, 1004, 201, 202, 205, 1011, 203, 205, 202, 1012, 201, 205, 200,
    203, 1005, 204, 201, 1006, 202, 1007, 204, 205, 201, 201, 210, 3, 202, 200, 204, 1008, 205, 210,
    201, 204, 200, 103, 206, 210, 201, 207, 1009, 4, 200, 204, 1010, 210, 201, 210, 206, 104, 210,
    204, 1013, 206, 209, 207, 210, 211, 200, 206, 201, 208, 205, 209, 207, 1014, 210, 209, 211, 202,
    200, 204, 1015, 208, 210, 211, 206, 209, 201, 209, 200, 203, 208, 207, 211, 208, 207, 209, 206,
    211, 210, 208, 206, 209, 207, 1016, 1017, 210, 203, 211, 208, 1018, 201, 209, 200, 211, 207,
    206, 202, 204, 208, 1019, 209, 211, 206, 200, 208, 207, 1020, 205, 209, 209, 208, 207, 211, 207,
    207,
)


MESH = pl.DeviceIdType.MESH
LINE = 4
DOWN, GATE, UP, OUT, QKV = range(5)
UNITS = (
    (2048, 1536, 256, 0, 0),
    (1536, 2048, 256, 1, 0),
    (1536, 2048, 256, 2, 0),
    (768, 1536, 128, 3, 0),
    (1536, 1536, 256, 4, 0),
)
BLOCKS = (
    (0, True, 0, 640),
    (0, False, 640, 384),
    (1, True, 0, 512),
    (1, False, 512, 256),
    (2, True, 0, 384),
    (2, False, 384, 256),
    (3, True, 0, 256),
    (3, False, 256, 128),
    (4, True, 0, 256),
    (4, False, 256, 256),
    (2, False, 640, 128),
    (4, True, 512, 256),
)
WHOLE = tuple(
    (sum(unit[0] for unit in UNITS if unit[3] == kind), next(unit[1] for unit in UNITS if unit[3] == kind))
    for kind in range(5)
)
COPIES = 20
TILE_BASE = len(BLOCKS) * COPIES
TILES = tuple(rows // 2 // tile for rows, _, tile, *_ in UNITS)
SMALL_BASE = TILE_BASE + sum(TILES)
SMALL_STEPS = 5
Y_BASE = SMALL_BASE + SMALL_STEPS
N_SEMS = Y_BASE + 4


def rows_at(start, size):
    return pl.ds(pl.multiple_of(start, 16), size)


class Place:
    def __init__(self):
        dp = lax.axis_index("dp")
        self.dp = dp
        self.y = lax.axis_index("tensor")
        self.core = lax.rem(dp, 2)
        self.x = lax.rem(dp // 2, 2)
        self.z = dp // 4

    def at(self, z, x, core, y):
        return ((z * 2 + x) * 2 + core, y)

    def other_core(self):
        return self.at(self.z, self.x, 1 - self.core, self.y)

    def other_x(self):
        return self.at(self.z, 1 - self.x, self.core, self.y)

    def other_y(self):
        return self.at(self.z, self.x, self.core, 1 - self.y)

    def up(self):
        return self.at(self.z + 1, self.x, self.core, self.y)

    def down(self):
        return self.at(self.z - 1, self.x, self.core, self.y)

    def pair_z(self):
        return self.at(self.z + 1 - 2 * lax.rem(self.z, 2), self.x, self.core, self.y)

    def far_z(self):
        return self.at(lax.rem(self.z + 2, LINE), self.x, self.core, self.y)


class Mover:
    def __init__(self, send_sems, recv_sems):
        self.send_sems = send_sems
        self.recv_sems = recv_sems
        self.left = []

    def copy(self, source, target, index, device):
        return pltpu.make_async_remote_copy(
            src_ref=source,
            dst_ref=target,
            send_sem=self.send_sems.at[index],
            recv_sem=self.recv_sems.at[index],
            device_id=device,
            device_id_type=MESH,
        )

    def start(self, source, target, index, device, when=None):
        copy = self.copy(source, target, index, device)
        guarded(when, copy.start)
        self.left.append((when, copy.wait_send))

    def arrived(self, target, index, device):
        self.copy(target, target, index, device).wait_recv()


def guarded(when, action):
    if when is None:
        action()
    else:
        pl.when(when)(action)


def add_rows(target, target_row, source, source_row, size):
    step = 16

    def one(i, _):
        here = rows_at(target_row + i * step, step)
        there = rows_at(source_row + i * step, step)
        total = target[here, :].astype(jnp.float32) + source[there, :].astype(jnp.float32)
        target[here, :] = total.astype(target.dtype)
        return 0

    lax.fori_loop(0, size // step, one, 0)


def fall_slot(step):
    return 0 if step == 0 else 2 + step


class Block:
    def __init__(self, place, mover, held, across, along, result, base, start, size, half_rows, x_first, first):
        self.p = place
        self.m = mover
        self.held = held
        self.across = across
        self.along = along
        self.result = result
        self.base = base
        self.start = start
        self.size = size
        self.half_rows = half_rows
        self.x_first = x_first
        self.first = first
        self.chunk = size // 8 if x_first else size // 4
        self.origin = start + place.x * (size // 2) if x_first else start

    def part(self, chunk):
        return self.held.at[rows_at(self.origin + chunk * self.chunk, self.chunk)]

    def final(self, row, size):
        return self.result.at[rows_at(self.first + self.p.core * self.half_rows + row, size)]

    def final_part(self, chunk):
        return self.final(self.origin + chunk * self.chunk, self.chunk)

    def keep(self, row, size):
        index = self.base // COPIES
        copy = pltpu.make_async_copy(
            self.held.at[rows_at(row, size)], self.final(row, size), self.m.keep_sems.at[index]
        )
        copy.start()
        self.kept = copy

    def events(self):
        line = [self.line_start, lambda: self.line_add(0), lambda: self.line_add(1), lambda: self.line_add(2)]
        spread = [lambda: self.spread(1), lambda: self.spread(2), lambda: self.spread(3)]
        if self.x_first:
            return [self.x_send, self.x_add] + line[1:] + spread + [self.x_done]
        return line + [self.pair_send, self.pair_add, self.pair_done] + spread + [self.z_done]

    def line_start(self):
        p = self.p
        for step in range(3):
            self.m.start(self.part(3 - step), self.along.at[step], self.base + step, p.up(), p.z == 0)
            self.m.start(self.part(step), self.along.at[fall_slot(step)], self.base + 3 + step, p.down(), p.z == LINE - 1)

    def line_add(self, step):
        p = self.p
        rising = jnp.minimum(p.z + 2 - step, 3)
        falling = jnp.maximum(p.z - 2 + step, 0)
        goes_up = (p.z >= 1) & (p.z <= step + 1)
        goes_down = (p.z <= 2) & (p.z >= 2 - step)

        def take_rising():
            self.m.arrived(self.along.at[step], self.base + step, p.down())
            add_rows(self.held, self.origin + rising * self.chunk, self.along.at[step], 0, self.chunk)

        def take_falling():
            self.m.arrived(self.along.at[fall_slot(step)], self.base + 3 + step, p.up())
            add_rows(self.held, self.origin + falling * self.chunk, self.along.at[fall_slot(step)], 0, self.chunk)

        pl.when(goes_up)(take_rising)
        if step < 2:
            self.m.start(self.part(rising), self.along.at[step + 1], self.base + step + 1, p.up(), goes_up)
        pl.when(goes_down)(take_falling)
        if step < 2:
            self.m.start(self.part(falling), self.along.at[fall_slot(step + 1)], self.base + 4 + step, p.down(), goes_down)
        elif self.x_first:
            self.keep(self.origin + p.z * self.chunk, self.chunk)
            self.own_spread(self.part(p.z))
            self.x_return(self.part(p.z), p.z, None)

    def own_spread(self, source):
        p = self.p
        target = self.final_part(p.z)
        self.m.start(source, target, self.base + 6, p.up(), p.z < 3)
        self.m.start(source, target, self.base + 9, p.down(), p.z > 0)

    def spread(self, distance):
        p = self.p
        below = self.final_part(jnp.maximum(p.z - distance, 0))
        above = self.final_part(jnp.minimum(p.z + distance, 3))

        pl.when(p.z >= distance)(lambda: self.m.arrived(below, self.base + 5 + distance, p.down()))
        if distance < 3:
            self.m.start(below, below, self.base + 6 + distance, p.up(), (p.z >= distance) & (p.z < 3))
        if self.x_first:
            self.x_return(below, jnp.maximum(p.z - distance, 0), p.z >= distance)
        pl.when(p.z <= 3 - distance)(lambda: self.m.arrived(above, self.base + 8 + distance, p.up()))
        if distance < 3:
            self.m.start(above, above, self.base + 9 + distance, p.down(), (p.z <= 3 - distance) & (p.z > 0))
        if self.x_first:
            self.x_return(above, jnp.minimum(p.z + distance, 3), p.z <= 3 - distance)
            if distance == 3:
                self.kept.wait()
                self.give(p.x * (self.size // 2), self.size // 2, 14)

    def x_part(self, which):
        half = self.size // 2
        return self.held.at[rows_at(self.start + which * half, half)]

    def x_send(self):
        self.m.start(self.x_part(1 - self.p.x), self.across, self.base + 12, self.p.other_x())

    def x_add(self):
        self.m.arrived(self.across, self.base + 12, self.p.other_x())
        add_rows(self.held, self.origin, self.across, 0, self.size // 2)
        self.line_start()

    def x_return(self, source, chunk, when):
        self.m.start(source, self.final_part(chunk), self.base + 16 + chunk, self.p.other_x(), when)

    def x_done(self):
        p = self.p
        half = (1 - p.x) * (self.size // 2)
        for chunk in range(4):
            place = self.final(self.start + half + chunk * self.chunk, self.chunk)
            self.m.arrived(place, self.base + 16 + chunk, p.other_x())
        self.give(half, self.size // 2, 15)

    def pair_row(self, which):
        return self.start + self.p.z * self.chunk + which * (self.chunk // 2)

    def pair_send(self):
        half = self.chunk // 2
        source = self.held.at[rows_at(self.pair_row(1 - self.p.x), half)]
        self.m.start(source, self.across, self.base + 12, self.p.other_x())

    def pair_add(self):
        p = self.p
        half = self.chunk // 2
        self.m.arrived(self.across, self.base + 12, p.other_x())
        row = self.pair_row(p.x)
        add_rows(self.held, row, self.across, 0, half)
        self.keep(row, half)
        self.m.start(self.held.at[rows_at(row, half)], self.final(row, half), self.base + 13, p.other_x())

    def pair_done(self):
        p = self.p
        half = self.chunk // 2
        self.m.arrived(self.final(self.pair_row(1 - p.x), half), self.base + 13, p.other_x())
        self.kept.wait()
        self.own_spread(self.final_part(p.z))

    def z_done(self):
        self.give(0, self.size, 14)

    def give(self, offset, size, slot):
        p = self.p
        source = self.final(self.start + offset, size)
        self.m.start(source, source, self.base + slot, p.other_core())
        other = self.result.at[
            rows_at(self.first + (1 - p.core) * self.half_rows + self.start + offset, size)
        ]
        self.m.left.append((None, lambda: self.m.arrived(other, self.base + slot, p.other_core())))


def product_tile(left, right, first, tile, width, part):
    columns = pl.ds(pl.multiple_of(first, 128), tile)
    return lax.dot_general(
        left[:, columns], right[:, part * width : (part + 1) * width],
        (((0,), (0,)), ((), ())), preferred_element_type=jnp.float32,
    )


class Unit:
    def __init__(self, index, place, mover, left, right, held, staged, stage_sems):
        self.index = index
        self.rows, self.columns, self.tile, _, self.first = UNITS[index]
        self.p, self.m = place, mover
        self.left, self.right, self.held = left, right, held
        self.staged, self.stage_sems = staged, stage_sems
        self.base = TILE_BASE + sum(TILES[:index])
        self.width = 512

    def tile_copy(self, i, slot):
        tile = self.tile
        return pltpu.make_async_remote_copy(
            src_ref=self.staged.at[slot, pl.ds(0, tile), pl.ds(0, self.columns)],
            dst_ref=self.held.at[rows_at(i * tile, tile)],
            send_sem=self.stage_sems.at[slot],
            recv_sem=self.m.recv_sems.at[self.base + i],
            device_id=self.p.other_core(),
            device_id_type=MESH,
        )

    def send(self):
        half, tile = self.rows // 2, self.tile

        def one(i, _):
            slot = lax.rem(i, 2)
            pl.when(i >= 2)(lambda: self.tile_copy(i, slot).wait_send())
            first = self.first + (1 - self.p.core) * half + i * tile
            for part in range(self.columns // self.width):
                got = product_tile(self.left, self.right, first, tile, self.width, part)
                self.staged[slot, pl.ds(0, tile), part * self.width : (part + 1) * self.width] = got.astype(
                    jnp.bfloat16
                )
            self.tile_copy(i, slot).start()
            return 0

        lax.fori_loop(0, half // tile, one, 0)
        for slot in range(min(2, half // tile)):
            self.tile_copy(0, slot).wait_send()

    def own(self):
        half, tile = self.rows // 2, self.tile

        def one(i, _):
            self.tile_copy(i, 0).wait_recv()
            first = self.first + self.p.core * half + i * tile
            here = rows_at(i * tile, tile)
            for part in range(self.columns // self.width):
                got = product_tile(self.left, self.right, first, tile, self.width, part)
                cut = slice(part * self.width, (part + 1) * self.width)
                total = got + self.held[here, cut].astype(jnp.float32)
                self.held[here, cut] = total.astype(jnp.bfloat16)
            return 0

        lax.fori_loop(0, half // tile, one, 0)


def row_scale(values):
    return lax.rsqrt(jnp.mean(values * values, axis=-1, keepdims=True) + epsilon)


def eight(values):
    rows, columns = values.shape
    return jnp.sum(values.reshape(rows // 8, 8, columns), axis=0)


def turn_back(values, cosines, sines):
    half = values.shape[1] // 2
    swapped = jnp.concatenate([values[:, half:], values[:, :half]], axis=1)
    return values * cosines + swapped * sines


def nt(left_side, right_side):
    return lax.dot_general(
        left_side, right_side, (((1,), (1,)), ((), ())), preferred_element_type=jnp.float32
    )


def tn(left_side, right_side):
    return lax.dot_general(
        left_side, right_side, (((0,), (0,)), ((), ())), preferred_element_type=jnp.float32
    )


class Layer:
    def __init__(self, place, mover, **refs):
        self.p, self.m = place, mover
        self.__dict__.update(refs)
        self.rows = self.x1.shape[0]
        self.mine = rows_at(place.y * self.rows, self.rows)
        self.theirs = rows_at((1 - place.y) * self.rows, self.rows)

    def load(self, source, target, index):
        copy = pltpu.make_async_copy(source, target, self.local_sems.at[index])
        copy.start()
        return copy

    def begin(self):
        self.waits = {}
        for i, (name, target) in enumerate(LOADED):
            self.waits[target] = self.load(getattr(self, name), getattr(self, target), 16 + i)
        self.waits["out_w"] = self.load(self.out_w, self.wbuf.at[pl.ds(0, 768)], 3)

    def need(self, *targets):
        for target in targets:
            if target in self.waits:
                self.waits.pop(target).wait()

    def stream(self, first, count, fetch, use):
        def go(i):
            for j, (source, target) in enumerate(fetch(i)):
                pltpu.make_async_copy(source, target, self.local_sems.at[8 + 2 * lax.rem(i, 2) + j]).start()

        go(jnp.int32(first))

        def body(i, _):
            pl.when(i + 1 < first + count)(lambda: go(i + 1))
            for j, (source, target) in enumerate(fetch(i)):
                pltpu.make_async_copy(source, target, self.local_sems.at[8 + 2 * lax.rem(i, 2) + j]).wait()
            use(i, lax.rem(i, 2))
            return 0

        lax.fori_loop(first, first + count, body, 0)

    def h2_third(self, third):
        self.need("d_gate", "d_up")

        def fetch(i):
            slot, here = lax.rem(i, 2), rows_at(i * 128, 128)
            return (
                (self.gate_w.at[here], self.staged.at[slot, pl.ds(0, 128)]),
                (self.up_w.at[here], self.staged.at[slot, pl.ds(128, 128)]),
            )

        def use(i, slot):
            cut = pl.ds(pl.multiple_of(i * 128, 128), 128)
            gate_w, up_w = self.staged[slot, 0:128, :], self.staged[slot, 128:256, :]
            for rows, target in ((self.theirs, self.h2_out), (self.mine, self.fbuf)):
                total = nt(self.d_gate[rows, :], gate_w) + nt(self.d_up[rows, :], up_w)
                target[:, cut] = total.astype(target.dtype)

        self.stream(4 * third, 4, fetch, use)
        if third == 2:
            self.h2_sent = self.m.copy(self.h2_out, self.h2_in, Y_BASE, self.p.other_y())
            self.h2_sent.start()

    def mlp_half(self, half):
        self.need("hid")

        rows, target = ((self.theirs, self.mlp_out), (self.mine, self.own))[half]
        self.fbuf[...] = jnp.zeros_like(self.fbuf)

        def fetch(i):
            return ((self.down_w.at[rows_at(i * 256, 256)], self.staged.at[lax.rem(i, 2), :, pl.ds(0, 1536)]),)

        def use(i, slot):
            cut = pl.ds(pl.multiple_of(i * 256, 256), 256)
            self.fbuf[...] += product(self.hid[rows, cut], self.staged[slot, :, 0:1536])

        self.stream(0, self.down_w.shape[0] // 256, fetch, use)
        target[...] = self.fbuf[...].astype(target.dtype)

    def tiles(self, step, body):
        lax.fori_loop(0, self.rows // step, lambda i, _: (body(i * step, step), 0)[1], 0)

    def middle(self):
        self.need("x1", "g")
        self.m.arrived(self.h2_in, Y_BASE, self.p.other_y())
        self.gains[...] = jnp.zeros_like(self.gains)

        def body(start, step):
            here = rows_at(start, step)
            there = rows_at(self.p.y * self.rows + start, step)
            d = self.fbuf[here, :] + self.h2_in[here, :].astype(jnp.float32)
            x1 = self.x1[here, :]
            inv = row_scale(x1)
            scaled = d * self.gain2[...].reshape(1, -1)
            inner = jnp.mean(scaled * x1, axis=-1, keepdims=True)
            self.gains[1] += eight(d * x1 * inv)
            d_x1 = self.g[there, :].astype(jnp.float32) + inv * (scaled - x1 * inv * inv * inner)
            self.d_x1[here, :] = d_x1
            self.d_attn[there, :] = d_x1.astype(jnp.bfloat16)

        self.tiles(16, body)
        own = self.d_attn.at[self.mine]
        self.m.start(own, own, Y_BASE + 1, self.p.other_y())

    def outward(self):
        self.m.arrived(self.d_attn.at[self.theirs], Y_BASE + 1, self.p.other_y())
        self.need("out_w")
        for part in range(3):
            cut = slice(part * 256, (part + 1) * 256)
            self.d_o[:, cut] = nt(self.d_attn[...], self.wbuf[cut, :]).astype(jnp.bfloat16)
        self.w_loads = [
            self.load(self.q_w, self.wbuf.at[:, pl.ds(0, 768)], 3),
            self.load(self.k_w, self.wbuf.at[:, pl.ds(768, 384)], 4),
            self.load(self.v_w, self.wbuf.at[:, pl.ds(1152, 384)], 5),
        ]

    def attention(self, key_head):
        self.need("q", "k", "v", "cosines", "sines", "starts")
        factor = HD ** (-0.5)
        c = key_head * HD
        keys, values = self.k[:, c : c + HD], self.v[:, c : c + HD]
        block = 256
        d_k = [jnp.zeros((block, HD), jnp.float32)] * 2
        d_v = [jnp.zeros((block, HD), jnp.float32)] * 2
        for head in (2 * key_head, 2 * key_head + 1):
            h = head * HD
            for i in range(2):
                here = slice(i * block, (i + 1) * block)
                n = block * (i + 1)
                query, d_out = self.q[here, h : h + HD], self.d_o[here, h : h + HD]
                column = lax.broadcasted_iota(jnp.int32, (block, n), 1)
                row = lax.broadcasted_iota(jnp.int32, (block, n), 0) + i * block
                allowed = (column <= row) & (column >= self.starts[here, :])
                masked = jnp.where(allowed, nt(query, keys[:n]) * factor, masked_score)
                exponent = jnp.exp(masked - jnp.max(masked, axis=1, keepdims=True))
                weights = exponent / jnp.sum(exponent, axis=1, keepdims=True)
                d_weights = nt(d_out, values[:n])
                inner = jnp.sum(weights * d_weights, axis=1, keepdims=True)
                d_scores = (weights * (d_weights - inner)).astype(jnp.bfloat16)
                low = weights.astype(jnp.bfloat16)
                d_query = jnp.dot(d_scores, keys[:n], preferred_element_type=jnp.float32) * factor
                turned = turn_back(d_query, self.cosines[here, :], self.sines[here, :])
                self.d_qkv[here, h : h + HD] = turned.astype(jnp.bfloat16)
                for j in range(i + 1):
                    cut = slice(j * block, (j + 1) * block)
                    d_k[j] = d_k[j] + tn(d_scores[:, cut], query) * factor
                    d_v[j] = d_v[j] + tn(low[:, cut], d_out)
        for j in range(2):
            cut = slice(j * block, (j + 1) * block)
            turned = turn_back(d_k[j], self.cosines[cut, :], self.sines[cut, :])
            self.d_qkv[cut, 768 + c : 768 + c + HD] = turned.astype(jnp.bfloat16)
            self.d_qkv[cut, 1152 + c : 1152 + c + HD] = d_v[j].astype(jnp.bfloat16)

    def h1_part(self, rows, put):
        def body(i, _):
            cut = pl.ds(pl.multiple_of(i * 256, 256), 256)
            put(cut, nt(self.d_qkv[rows, 0:1536], self.wbuf[cut, :]))
            return 0

        lax.fori_loop(0, 6, body, 0)

    def inward(self):
        for copy in self.w_loads:
            copy.wait()

        self.h2_sent.wait_send()
        self.waits["x"] = self.load(self.x_hbm, self.h2_in, 0)

        def put(cut, got):
            self.h2_out[:, cut] = got.astype(jnp.bfloat16)

        self.h1_part(self.theirs, put)
        self.m.start(self.h2_out, self.h1_in, Y_BASE + 2, self.p.other_y())

    def mlp_send(self):
        self.m.start(self.mlp_out, self.mlp_in, Y_BASE + 3, self.p.other_y())

    def finish(self):
        def put(cut, got):
            self.fbuf[:, cut] = got

        self.waits.pop("x").wait()
        self.h1_part(self.mine, put)
        self.m.arrived(self.h1_in, Y_BASE + 2, self.p.other_y())

        def body(start, step):
            here = rows_at(start, step)
            d = self.fbuf[here, :] + self.h1_in[here, :].astype(jnp.float32)
            x = self.h2_in[here, :].astype(jnp.float32)
            inv = row_scale(x)
            scaled = d * self.gain1[...].reshape(1, -1)
            inner = jnp.mean(scaled * x, axis=-1, keepdims=True)
            self.gains[0] += eight(d * x * inv)
            self.d_x1[here, :] = self.d_x1[here, :] + inv * (scaled - x * inv * inv * inner)

        self.tiles(16, body)
        copy = self.load(self.d_x1, self.tokens_out, 6)
        self.m.left.append((None, copy.wait))

    def layer_end(self):
        self.m.arrived(self.mlp_in, Y_BASE + 3, self.p.other_y())

        def body(start, step):
            here = rows_at(start, step)
            mlp = self.own[here, :].astype(jnp.float32) + self.mlp_in[here, :].astype(jnp.float32)
            out = self.x1[here, :] + mlp
            self.gains[2] += eight(out * out)
            self.gains[3] += eight(mlp * mlp)
            self.own[here, :] = out.astype(jnp.bfloat16)

        self.tiles(16, body)
        copy = self.load(self.own, self.layer_out, 7)
        self.m.left.append((None, copy.wait))
        self.totals[0] = jnp.zeros(self.totals.shape[1:], jnp.float32)
        for row in range(4):
            self.totals[0, row : row + 1, :] = jnp.sum(self.gains[row], axis=0, keepdims=True)
        self.totals[0, 4:5, :] = self.attn_squares[...]


def sum_small(place, mover, total, slots, step):
    device = (place.other_core, place.other_x, place.other_y, place.pair_z, place.far_z)[step]()
    copy = mover.copy(total.at[step], slots.at[step], SMALL_BASE + step, device)
    copy.start()
    copy.wait()
    total[step + 1] = total[step] + slots[step]


INPUTS = (
    "hid_hbm", "g_hbm", "h2_hbm", "d_gate_hbm", "d_up_hbm", "o_hbm", "h1_hbm", "q_hbm", "k_hbm", "v_hbm",
    "out_w", "q_w", "k_w", "v_w", "gate_w", "up_w", "down_w", "x1_hbm", "x_hbm", "cosines_hbm", "sines_hbm",
    "starts_hbm", "gain1", "gain2", "attn_squares",
)
IN_VMEM = ("gain1", "gain2", "attn_squares")
LOADED = (
    ("hid_hbm", "hid"), ("g_hbm", "g"), ("h2_hbm", "hbuf"), ("d_gate_hbm", "d_gate"), ("d_up_hbm", "d_up"),
    ("x1_hbm", "x1"), ("o_hbm", "o"), ("q_hbm", "q"), ("k_hbm", "k"), ("v_hbm", "v"),
    ("cosines_hbm", "cosines"), ("sines_hbm", "sines"), ("starts_hbm", "starts"),
)
RESULTS = ("down_out", "gate_out", "up_out", "o_out", "qkv_out", "tokens_out", "layer_out", "small_out")
PLAIN = (
    "staged", "hid", "hbuf", "own", "h2_in", "d_attn", "d_x1", "wbuf", "d_o", "h1_in", "mlp_in", "h2_out",
    "mlp_out", "fbuf", "gains", "totals", "slots", "g", "d_gate", "d_up", "o", "q", "k", "v", "x1",
    "cosines", "sines", "starts",
    "stage_sems", "send_sems", "recv_sems", "keep_sems", "local_sems",
)


def backward_kernel(*refs):
    n = len(UNITS)
    names = INPUTS + RESULTS
    r = dict(zip(names, refs[: len(names)]))
    rest = refs[len(names) :]
    b = len(BLOCKS)
    held, across, along = rest[:n], rest[n : n + b], rest[n + b : n + 2 * b]
    r.update(zip(PLAIN, rest[n + 2 * b :]))
    r["d_qkv"] = r["hid"]
    place = Place()
    mover = Mover(r["send_sems"], r["recv_sems"])
    mover.keep_sems = r["keep_sems"]
    enter(place)
    layer = Layer(place, mover, **r)
    lefts = (r["hid"], r["hbuf"], r["hbuf"], r["o"], r["hbuf"])
    rights = (r["g"], r["d_gate"], r["d_up"], r["d_attn"], r["d_qkv"])
    results = tuple(r[name] for name in RESULTS[:5])
    units = [
        Unit(i, place, mover, lefts[unit[3]], rights[unit[3]], held[i], r["staged"], r["stage_sems"])
        for i, unit in enumerate(UNITS)
    ]
    steps = []
    for b, (i, x_first, start, size) in enumerate(BLOCKS):
        rows, _, _, kind, first = UNITS[i]
        block = Block(
            place, mover, held[i], across[b], along[b], results[kind], b * COPIES, start, size, rows // 2, x_first,
            first,
        )
        steps.append(block.events())

    def send(i):
        kind, first = UNITS[i][3:]
        layer.need(*((("hid", "g"), ("hbuf", "d_gate"), ("hbuf", "d_up"), ("o",), ())[kind]))
        if kind == QKV and first == 0:
            layer.load(layer.h1_hbm, layer.hbuf, 1).wait()
        units[i].send()

    tasks = [layer.begin]
    tasks += [partial(layer.h2_third, i) for i in range(3)]
    tasks += [layer.middle, layer.outward]
    tasks += [partial(layer.attention, i) for i in range(4)]
    tasks += [layer.inward]
    tasks += [partial(layer.mlp_half, i) for i in range(2)]
    tasks += [layer.mlp_send, layer.finish, layer.layer_end]
    tasks += [partial(sum_small, place, mover, r["totals"], r["slots"], i) for i in range(SMALL_STEPS)]
    for item in ORDER:
        if item < 100:
            send(item)
        elif item < 200:
            units[item - 100].own()
        elif item < 1000:
            steps[item - 200].pop(0)()
        else:
            tasks[item - 1000]()
    r["small_out"][...] = r["totals"][SMALL_STEPS]
    for when, wait in mover.left:
        guarded(when, wait)


def enter(place):
    barrier = pltpu.get_barrier_semaphore()

    def greet(device):
        pl.semaphore_signal(barrier, inc=1, device_id=device, device_id_type=MESH)

    for device in (place.other_core(), place.other_x(), place.other_y(), place.pair_z(), place.far_z()):
        greet(device)
    middle = (place.z == 1) | (place.z == 2)
    pl.when(middle)(lambda: greet(place.at(3 - place.z, place.x, place.core, place.y)))
    pl.semaphore_wait(barrier, 5 + jnp.where(middle, 1, 0))


def backward(**given):
    vmem = pl.BlockSpec(memory_space=pltpu.VMEM)
    hbm = pl.BlockSpec(memory_space=pl.ANY)
    low, full = jnp.bfloat16, jnp.float32
    own_rows, width = given["x1_hbm"].shape
    held = [pltpu.VMEM((rows // 2, columns), low) for rows, columns, *_ in UNITS]
    across, along = [], []
    for i, x_first, _, size in BLOCKS:
        columns = UNITS[i][1]
        across.append(pltpu.VMEM((size // 2 if x_first else size // 8, columns), low))
        along.append(pltpu.VMEM((5, size // 8 if x_first else size // 4, columns), low))
    part = pltpu.VMEM((own_rows, width), low)
    plain = dict(
        staged=pltpu.VMEM((2, 256, 2048), low),
        hid=pltpu.VMEM((512, 2048), low),
        hbuf=pltpu.VMEM((512, width), low),
        own=part,
        h2_in=part,
        d_attn=pltpu.VMEM((512, width), low),
        d_x1=pltpu.VMEM((own_rows, width), full),
        wbuf=pltpu.VMEM((1536, 1536), low),
        d_o=pltpu.VMEM((512, 768), low),
        h1_in=part,
        mlp_in=part,
        h2_out=part,
        mlp_out=part,
        fbuf=pltpu.VMEM((own_rows, width), full),
        gains=pltpu.VMEM((4, 8, width), full),
        totals=pltpu.VMEM((SMALL_STEPS + 1, 8, width), full),
        slots=pltpu.VMEM((SMALL_STEPS, 8, width), full),
        stage_sems=pltpu.SemaphoreType.DMA((2,)),
        send_sems=pltpu.SemaphoreType.DMA((N_SEMS,)),
        recv_sems=pltpu.SemaphoreType.DMA((N_SEMS,)),
        keep_sems=pltpu.SemaphoreType.DMA((len(BLOCKS),)),
        local_sems=pltpu.SemaphoreType.DMA((16 + len(LOADED),)),
    )
    for name, target in LOADED:
        plain.setdefault(target, pltpu.VMEM(given[name].shape, given[name].dtype))
    flops = sum(2 * 512 * rows * columns for rows, columns, *_ in UNITS)
    return pl.pallas_call(
        backward_kernel,
        out_shape=[jax.ShapeDtypeStruct(shape, low) for shape in WHOLE]
        + [
            jax.ShapeDtypeStruct((own_rows, width), full),
            jax.ShapeDtypeStruct((own_rows, width), low),
            jax.ShapeDtypeStruct((8, width), full),
        ],
        in_specs=[vmem if name in IN_VMEM else hbm for name in INPUTS],
        out_specs=[hbm] * 7 + [vmem],
        scratch_shapes=held + across + along + [plain[name] for name in PLAIN],
        compiler_params=pltpu.CompilerParams(
            collective_id=0, has_side_effects=True, vmem_limit_bytes=62 << 20
        ),
        cost_estimate=pl.CostEstimate(flops=flops, bytes_accessed=80 << 20, transcendentals=0),
        name="backward",
    )(*(given[name] for name in INPUTS))


FORWARD_INPUTS = (
    "x", "lengths", "gain1", "gain2", "inverse", "q_w", "k_w", "v_w", "out_w", "gate_w", "up_w", "down_w", "g_own",
)
FORWARD_RESULTS = (
    "hid_to", "g_to", "h2_to", "d_gate_to", "d_up_to", "o_to", "h1_to", "q_to", "k_to", "v_to", "x1_to",
    "cosines", "sines", "starts", "attn_squares",
)
FORWARD_PLAIN = (
    "x_in", "w_qkv", "w_out", "w_gate", "w_up", "w_down", "g", "h1", "lin", "q", "k", "v", "o", "own_part",
    "sent_part", "got_part", "x1", "h2", "d_hid", "hid", "d_gate", "d_up", "squares",
    "send_sems", "recv_sems", "load_sems", "store_sems",
)
CHUNKS = 2


class Forward:
    def __init__(self, refs):
        self.__dict__.update(refs)
        self.p = Place()
        self.m = Mover(self.send_sems, self.recv_sems)
        self.rows = self.x.shape[0]
        self.step = self.rows // CHUNKS
        self.base = self.p.y * self.rows
        self.far = (1 - self.p.y) * self.rows
        self.stores = 0

    def load(self, source, target, index):
        copy = pltpu.make_async_copy(source, target, self.load_sems.at[index])
        copy.start()
        return copy

    def store(self, source, target):
        copy = pltpu.make_async_copy(source, target, self.store_sems.at[self.stores])
        self.stores += 1
        copy.start()
        self.m.left.append((None, copy.wait))

    def across(self, source, target, index):
        self.m.start(source, target, index, self.p.other_y())

    def arrived(self, target, index):
        self.m.arrived(target, index, self.p.other_y())

    def tiles(self, first, count, step, body):
        lax.fori_loop(0, count // step, lambda i, _: (body(first + i * step, step), 0)[1], 0)

    def run(self):
        step = self.step
        barrier = pltpu.get_barrier_semaphore()
        pl.semaphore_signal(barrier, inc=1, device_id=self.p.other_y(), device_id_type=MESH)
        pl.semaphore_wait(barrier, 1)
        for c in range(CHUNKS):
            part = pl.ds(c * step, step)
            self.across(self.x.at[part], self.x_in.at[part], c)
        self.across(self.g_own, self.g.at[rows_at(self.base, self.rows)], 2 * CHUNKS)
        qkv_loads = [
            self.load(self.q_w, self.w_qkv.at[:, pl.ds(0, 768)], 0),
            self.load(self.k_w, self.w_qkv.at[:, pl.ds(768, 384)], 1),
            self.load(self.v_w, self.w_qkv.at[:, pl.ds(1152, 384)], 2),
        ]
        g_load = self.load(self.g_own, self.g.at[rows_at(self.base, self.rows)], 3)
        out_load = self.load(self.out_w, self.w_out, 4)
        down_load = self.load(self.down_w, self.w_down, 5)
        gate_load = self.load(self.gate_w, self.w_gate, 6)
        up_load = self.load(self.up_w, self.w_up, 7)
        self.tables()
        self.norm1(self.x, 0, self.base, self.rows)
        for copy in qkv_loads:
            copy.wait()
        self.qkv(self.base, self.rows)
        for c in range(CHUNKS):
            self.arrived(self.x_in.at[pl.ds(c * step, step)], c)
            self.norm1(self.x_in, c * step, self.far + c * step, step)
            self.qkv(self.far + c * step, step)
        self.store(self.h1, self.h1_to)
        self.store(self.q, self.q_to)
        self.store(self.k, self.k_to)
        self.store(self.v, self.v_to)
        self.attention(self.far)
        out_load.wait()
        for c in range(CHUNKS):
            part = pl.ds(c * step, step)
            self.project(self.far + c * step, self.sent_part, c * step, step)
            self.across(self.sent_part.at[part], self.got_part.at[part], CHUNKS + c)
        self.attention(self.base)
        self.store(self.o, self.o_to)
        self.project(self.base, self.own_part, 0, self.rows)
        g_load.wait()
        down_load.wait()
        self.hidden_grad(self.base, self.rows)
        self.arrived(self.g.at[rows_at(self.far, self.rows)], 2 * CHUNKS)
        self.store(self.g, self.g_to)
        self.hidden_grad(self.far, self.rows)
        self.squares[...] = jnp.zeros_like(self.squares)
        for c in range(CHUNKS):
            self.arrived(self.got_part.at[pl.ds(c * step, step)], CHUNKS + c)
            self.norm2(c * step)
            mine = self.h2.at[rows_at(self.base + c * step, step)]
            self.across(mine, mine, 2 * CHUNKS + 1 + c)
        self.store(self.x1, self.x1_to)
        self.attn_squares[...] = jnp.sum(self.squares[...], axis=0, keepdims=True)
        gate_load.wait()
        up_load.wait()
        self.feed(self.base, self.rows)
        for c in range(CHUNKS):
            self.arrived(self.h2.at[rows_at(self.far + c * step, step)], 2 * CHUNKS + 1 + c)
            self.feed(self.far + c * step, step)
        for name in ("h2", "hid", "d_gate", "d_up"):
            self.store(getattr(self, name), getattr(self, name + "_to"))
        for when, wait in self.m.left:
            guarded(when, wait)

    def tables(self):
        total = self.starts.shape[0]
        row = lax.broadcasted_iota(jnp.int32, (total, 1), 0)
        first = jnp.zeros((total, 1), jnp.int32)
        end = jnp.int32(0)
        for j in range(self.lengths.shape[1]):
            first = jnp.where(row >= end, end, first)
            end = end + self.lengths[0, j]
        self.starts[...] = first
        angles = (row - first).astype(jnp.float32) * self.inverse[...]
        self.cosines[...] = jnp.cos(angles)
        half = lax.broadcasted_iota(jnp.int32, (total, HD), 1) < HD // 2
        sines = jnp.sin(angles)
        self.sines[...] = jnp.where(half, sines, -sines)

    def norm1(self, source, source_row, row, count):
        def body(i, step):
            x = source[rows_at(source_row + i, step), :].astype(jnp.float32)
            self.h1[rows_at(row + i, step), :] = (x * row_scale(x) * self.gain1[...].reshape(1, -1)).astype(jnp.bfloat16)

        self.tiles(0, count, 32, body)

    def qkv(self, row, count):
        here = rows_at(row, count)
        values = self.h1[here, :]
        for part in range(3):
            cut = slice(part * 512, (part + 1) * 512)
            self.lin[0:count, cut] = product(values, self.w_qkv[:, cut])
        cosines, sines = self.cosines[here, :], -self.sines[here, :]
        for target, first in ((self.q, 0), (self.k, 768)):
            for head in range(target.shape[1] // HD):
                linear = self.lin[0:count, first + head * HD : first + (head + 1) * HD]
                turned = turn_back(linear, cosines, sines)
                target[here, head * HD : (head + 1) * HD] = turned.astype(jnp.bfloat16)
        self.v[here, :] = self.lin[0:count, 1152:1536].astype(jnp.bfloat16)

    def attention(self, row):
        count, total = self.rows, self.q.shape[0]
        here = rows_at(row, count)
        column = lax.broadcasted_iota(jnp.int32, (count, total), 1)
        own = lax.broadcasted_iota(jnp.int32, (count, total), 0) + row
        allowed = (column <= own) & (column >= self.starts[here, :])
        for key_head in range(self.k.shape[1] // HD):
            c = key_head * HD
            keys, values = self.k[:, c : c + HD], self.v[:, c : c + HD]
            for head in (2 * key_head, 2 * key_head + 1):
                h = head * HD
                raw = nt(self.q[here, h : h + HD], keys) * HD ** (-0.5)
                masked = jnp.where(allowed, raw, masked_score)
                exponent = jnp.exp(masked - jnp.max(masked, axis=1, keepdims=True))
                weights = exponent / jnp.sum(exponent, axis=1, keepdims=True)
                out = product(weights.astype(jnp.bfloat16), values)
                self.o[here, h : h + HD] = out.astype(jnp.bfloat16)

    def project(self, row, target, target_row, count):
        values = self.o[rows_at(row, count), :]
        for part in range(3):
            cut = slice(part * 512, (part + 1) * 512)
            target[target_row : target_row + count, cut] = product(values, self.w_out[:, cut]).astype(target.dtype)

    def hidden_grad(self, row, count):
        here = rows_at(row, count)

        def body(i, _):
            cut = pl.ds(pl.multiple_of(i * 256, 256), 256)
            self.d_hid[here, cut] = nt(self.g[here, :], self.w_down[cut, :])
            return 0

        lax.fori_loop(0, self.w_down.shape[0] // 256, body, 0)

    def norm2(self, start):
        def body(i, step):
            here = rows_at(i, step)
            attn = self.own_part[here, :] + self.got_part[here, :].astype(jnp.float32)
            self.squares[...] += eight(attn * attn)
            x1 = self.x[here, :].astype(jnp.float32) + attn
            self.x1[here, :] = x1
            self.h2[rows_at(self.base + i, step), :] = (x1 * row_scale(x1) * self.gain2[...].reshape(1, -1)).astype(jnp.bfloat16)

        self.tiles(start, self.step, 16, body)

    def feed(self, row, count):
        here = rows_at(row, count)

        def body(i, _):
            cut = pl.ds(pl.multiple_of(i * 256, 256), 256)
            values = self.h2[here, :]
            gate = product(values, self.w_gate[:, cut])
            up = product(values, self.w_up[:, cut])
            d_hid = self.d_hid[here, cut]
            sig = 1.0 / (1.0 + jnp.exp(-gate))
            self.hid[here, cut] = (gate * sig * up).astype(jnp.bfloat16)
            self.d_gate[here, cut] = (d_hid * up * sig * (1.0 + gate * (1.0 - sig))).astype(jnp.bfloat16)
            self.d_up[here, cut] = (d_hid * gate * sig).astype(jnp.bfloat16)
            return 0

        lax.fori_loop(0, self.w_gate.shape[1] // 256, body, 0)


def forward_kernel(*refs):
    names = FORWARD_INPUTS + FORWARD_RESULTS + FORWARD_PLAIN
    Forward(dict(zip(names, refs))).run()


def forward(**given):
    vmem = pl.BlockSpec(memory_space=pltpu.VMEM)
    hbm = pl.BlockSpec(memory_space=pl.ANY)
    smem = pl.BlockSpec(memory_space=pltpu.SMEM)
    low, full = jnp.bfloat16, jnp.float32
    own, width = given["x"].shape
    total = 2 * own
    units = given["gate_w"].shape[1]
    q_cols, k_cols = given["q_w"].shape[1], given["k_w"].shape[1]
    shapes = dict(
        hid_to=((total, units), low), g_to=((total, width), low), h2_to=((total, width), low),
        d_gate_to=((total, units), low), d_up_to=((total, units), low), o_to=((total, q_cols), low),
        h1_to=((total, width), low), q_to=((total, q_cols), low), k_to=((total, k_cols), low),
        v_to=((total, k_cols), low), x1_to=((own, width), full), cosines=((total, HD), full), sines=((total, HD), full),
        starts=((total, 1), jnp.int32), attn_squares=((1, width), full),
    )
    plain = dict(
        x_in=((own, width), low), w_qkv=((width, q_cols + 2 * k_cols), low), w_out=((q_cols, width), low),
        w_gate=((width, units), low), w_up=((width, units), low), w_down=((units, width), low),
        g=((total, width), low), h1=((total, width), low), lin=((own, q_cols + 2 * k_cols), full),
        q=((total, q_cols), low), k=((total, k_cols), low), v=((total, k_cols), low), o=((total, q_cols), low),
        own_part=((own, width), full), sent_part=((own, width), low), got_part=((own, width), low),
        x1=((own, width), full), h2=((total, width), low), d_hid=((total, units), full), hid=((total, units), low),
        d_gate=((total, units), low), d_up=((total, units), low), squares=((8, width), full),
    )
    scratch = [pltpu.VMEM(*plain[name]) for name in FORWARD_PLAIN if name in plain]
    copies = 3 * CHUNKS + 1
    scratch += [pltpu.SemaphoreType.DMA((n,)) for n in (copies, copies, 8, 16)]
    spaces = dict.fromkeys(("q_w", "k_w", "v_w", "out_w", "gate_w", "up_w", "down_w", "g_own"), hbm)
    spaces["lengths"] = smem
    out = pl.pallas_call(
        forward_kernel,
        out_shape=[jax.ShapeDtypeStruct(*shapes[name]) for name in FORWARD_RESULTS],
        in_specs=[spaces.get(name, vmem) for name in FORWARD_INPUTS],
        out_specs=[hbm if name.endswith("_to") else vmem for name in FORWARD_RESULTS],
        scratch_shapes=scratch,
        compiler_params=pltpu.CompilerParams(
            collective_id=1, has_side_effects=True, vmem_limit_bytes=62 << 20
        ),
        cost_estimate=pl.CostEstimate(flops=26 * 10**9, bytes_accessed=60 << 20, transcendentals=0),
        name="forward",
    )(*(given[name] for name in FORWARD_INPUTS))
    return dict(zip(FORWARD_RESULTS, out))


def results_kernel(
    down, gate, up, o, qkv, tokens_in, layer_in, small,
    layer_out, tokens_out, gain1_out, q_out, k_out, v_out, o_out, gain2_out, gate_out, up_out, down_out, rms_out,
    taken, made, tokens_held, layer_held, in_sems, out_sems, whole_sems, *, tokens,
):
    held = ((tokens_in, tokens_held, tokens_out), (layer_in, layer_held, layer_out))
    inward = [pltpu.make_async_copy(a, b, whole_sems.at[i]) for i, (a, b, _) in enumerate(held)]
    outward = [pltpu.make_async_copy(b, c, whole_sems.at[i]) for i, (_, b, c) in enumerate(held)]
    for copy in inward:
        copy.start()
    q_cols, k_cols = q_out.shape[1], k_out.shape[1]
    tile = taken.shape[1]
    work = []
    for source, targets in (
        (down, ((down_out, 0),)),
        (gate, ((gate_out, 0),)),
        (up, ((up_out, 0),)),
        (qkv, ((q_out, 0), (k_out, q_cols), (v_out, q_cols + k_cols))),
        (o, ((o_out, 0),)),
    ):
        work += [(source, targets, row) for row in range(0, source.shape[0], tile)]
    slots = taken.shape[0]

    def take(i):
        source, _, row = work[i]
        return pltpu.make_async_copy(
            source.at[pl.ds(row, tile)], taken.at[i % slots, :, pl.ds(0, source.shape[1])], in_sems.at[i % slots]
        )

    def give(i):
        _, targets, row = work[i]
        return [
            pltpu.make_async_copy(
                made.at[i % slots, :, pl.ds(first, target.shape[1])],
                target.at[pl.ds(row, tile)],
                out_sems.at[i % slots, j],
            )
            for j, (target, first) in enumerate(targets)
        ]

    for i in range(min(slots - 1, len(work))):
        take(i).start()
    for i in range(len(work)):
        if i + slots - 1 < len(work):
            take(i + slots - 1).start()
        take(i).wait()
        if i >= slots:
            for copy in give(i - slots):
                copy.wait()
        columns = work[i][0].shape[1]

        def one(j, _, slot=i % slots, columns=columns):
            here = rows_at(j * 32, 32)
            made[slot, here, 0:columns] = taken[slot, here, 0:columns].astype(jnp.float32)
            return 0

        lax.fori_loop(0, tile // 32, one, 0)
        for copy in give(i):
            copy.start()
    for i in range(2):
        inward[i].wait()
        outward[i].start()
    gain1_out[...] = small[0, :]
    gain2_out[...] = small[1, :]
    lane = lax.broadcasted_iota(jnp.int32, (1, 3), 1)
    sums = [jnp.sum(small[row : row + 1, :], axis=1, keepdims=True) for row in (2, 4, 3)]
    squares = jnp.where(lane == 0, sums[0], jnp.where(lane == 1, sums[1], sums[2]))
    rms_out[...] = jnp.sqrt(squares / tokens)
    for i in range(max(0, len(work) - slots), len(work)):
        for copy in give(i):
            copy.wait()
    for copy in outward:
        copy.wait()


def results(sums, tokens_grad, layer_out, small, q_cols, k_cols, tokens):
    vmem = pl.BlockSpec(memory_space=pltpu.VMEM)
    hbm = pl.BlockSpec(memory_space=pl.ANY)
    full = jnp.float32
    down, gate, up, o, qkv = sums
    width = small.shape[1]
    rows = qkv.shape[0]
    shapes = (
        (layer_out.shape, layer_out.dtype, hbm), (tokens_grad.shape, full, hbm), ((width,), full, vmem),
        ((rows, q_cols), full, hbm), ((rows, k_cols), full, hbm), ((rows, k_cols), full, hbm),
        (o.shape, full, hbm), ((width,), full, vmem), (gate.shape, full, hbm), (up.shape, full, hbm),
        (down.shape, full, hbm), ((1, 3), full, vmem),
    )
    slots, tile = 8, 256
    columns = max(part.shape[1] for part in sums)
    out = pl.pallas_call(
        partial(results_kernel, tokens=tokens),
        out_shape=[jax.ShapeDtypeStruct(shape, dtype) for shape, dtype, _ in shapes],
        in_specs=[hbm] * 7 + [vmem],
        out_specs=[space for _, _, space in shapes],
        scratch_shapes=[
            pltpu.VMEM((slots, tile, columns), jnp.bfloat16),
            pltpu.VMEM((slots, tile, columns), full),
            pltpu.VMEM(tokens_grad.shape, full),
            pltpu.VMEM(layer_out.shape, layer_out.dtype),
            pltpu.SemaphoreType.DMA((slots,)),
            pltpu.SemaphoreType.DMA((slots, 3)),
            pltpu.SemaphoreType.DMA((2,)),
        ],
        compiler_params=pltpu.CompilerParams(vmem_limit_bytes=62 << 20),
        cost_estimate=pl.CostEstimate(flops=0, bytes_accessed=78 * 10**6, transcendentals=0),
        name="results",
    )(*sums, tokens_grad, layer_out, small)
    return tuple(part.reshape(-1) if part.shape[0] == 1 else part for part in out)


def dp_sum(terms):
    low = lax.psum(tuple(term.astype(jnp.bfloat16) for term in terms), "dp")
    return tuple(term.astype(jnp.float32) for term in low)


def low_scatter(partial):
    return lax.psum_scatter(
        partial.astype(jnp.bfloat16), "tensor", scatter_dimension=0, tiled=True
    ).astype(jnp.float32)


def body(
    tokens,
    lengths,
    first_gain,
    query_weight,
    key_weight,
    value_weight,
    output_weight,
    second_gain,
    gate_weight,
    up_weight,
    down_weight,
    out_cotangent,
):
    inputs = tokens.astype(jnp.float32)
    normed1, inv_first = norm_rows(inputs, first_gain)
    normed1 = normed1.astype(jnp.bfloat16)
    full_first = lax.all_gather(normed1, "tensor", axis=0, tiled=True)
    total_rows = full_first.shape[0]
    places, segment, cosine_table, sine_table = tables(lengths[0], total_rows, HD // 2)
    kv_heads = key_weight.shape[1] // HD
    groups = query_weight.shape[1] // key_weight.shape[1]
    query = rotate(product(full_first, query_weight), cosine_table, sine_table, 1.0).astype(
        jnp.bfloat16
    )
    keys = rotate(product(full_first, key_weight), cosine_table, sine_table, 1.0).astype(
        jnp.bfloat16
    )
    values = product(full_first, value_weight).astype(jnp.bfloat16)
    block_rows = min(block_limit, total_rows)
    block_count = total_rows // block_rows
    query_blocks = query.reshape(block_count, block_rows, kv_heads, groups, HD)
    seg_blocks = segment.reshape(block_count, block_rows)
    place_blocks = places.reshape(block_count, block_rows)
    key_three = keys.reshape(total_rows, kv_heads, HD)
    value_three = values.reshape(total_rows, kv_heads, HD)
    factor = HD ** (-0.5)

    def scores(query_block, seg_block, place_block):
        raw = (
            jnp.einsum("qcgd,kcd->cgqk", query_block, key_three, preferred_element_type=jnp.float32)
            * factor
        )
        allowed = (seg_block[:, None] == segment[None, :]) & (
            place_block[:, None] >= places[None, :]
        )
        return (jnp.where(allowed[None, None], raw, masked_score), allowed)

    def forward_block(piece_set):
        query_block, seg_block, place_block = piece_set
        masked, allowed = scores(query_block, seg_block, place_block)
        highest = jnp.max(masked, axis=-1, keepdims=True)
        exponent = jnp.exp(masked - highest)
        denominator = jnp.sum(exponent, axis=-1, keepdims=True)
        weights = exponent / denominator
        output = jnp.einsum(
            "cgqk,kcd->qcgd",
            weights.astype(jnp.bfloat16),
            value_three,
            preferred_element_type=jnp.float32,
        )
        stored = (highest + jnp.log(denominator))[..., 0]
        return (output.reshape(block_rows, -1), stored)

    out_blocks, kept_blocks = lax.map(forward_block, (query_blocks, seg_blocks, place_blocks))
    attended = out_blocks.reshape(total_rows, -1).astype(jnp.bfloat16)
    attn_rows = low_scatter(product(attended, output_weight))
    middle = inputs + attn_rows
    normed2, inv_second = norm_rows(middle, second_gain)
    normed2 = normed2.astype(jnp.bfloat16)
    full_second = lax.all_gather(normed2, "tensor", axis=0, tiled=True)
    gate_value = product(full_second, gate_weight)
    upward = product(full_second, up_weight)
    gate_sig = jax.nn.sigmoid(gate_value)
    hidden = (gate_value * gate_sig * upward).astype(jnp.bfloat16)
    mlp_rows = low_scatter(product(hidden, down_weight))
    layer_out = middle + mlp_rows
    squares = jnp.stack(
        [
            jnp.sum(layer_out * layer_out),
            jnp.sum(attn_rows * attn_rows),
            jnp.sum(mlp_rows * mlp_rows),
        ]
    )
    grad_full = lax.all_gather(out_cotangent, "tensor", axis=0, tiled=True)
    grad_hidden = times_cols(grad_full, down_weight)
    down_g = times_rows(hidden, grad_full)
    gate_slope = gate_sig * (1.0 + gate_value * (1.0 - gate_sig))
    grad_gate = (grad_hidden * upward * gate_slope).astype(jnp.bfloat16)
    grad_up = (grad_hidden * gate_value * gate_sig).astype(jnp.bfloat16)
    gate_g = times_rows(full_second, grad_gate)
    up_g = times_rows(full_second, grad_up)
    gate_g, up_g, down_g = dp_sum((gate_g, up_g, down_g))
    grad_normed2 = low_scatter(
        times_cols(grad_gate, gate_weight) + times_cols(grad_up, up_weight)
    )
    second_rows, grad_mid_norm = norm_back(middle, inv_second, second_gain, grad_normed2)
    grad_middle = out_cotangent.astype(jnp.float32) + grad_mid_norm
    grad_attn_full = lax.all_gather(grad_middle.astype(jnp.bfloat16), "tensor", axis=0, tiled=True)
    output_g = times_rows(attended, grad_attn_full)
    grad_out = times_cols(grad_attn_full, output_weight).astype(jnp.bfloat16)
    grad_blocks = grad_out.reshape(block_count, block_rows, kv_heads, groups, HD)

    def backward_block(running, piece_set):
        key_acc, value_acc = running
        query_block, seg_block, place_block, grad_block, stored = piece_set
        masked, allowed = scores(query_block, seg_block, place_block)
        weights = jnp.where(allowed[None, None], jnp.exp(masked - stored[..., None]), 0.0)
        grad_weights = jnp.einsum(
            "qcgd,kcd->cgqk", grad_block, value_three, preferred_element_type=jnp.float32
        )
        row_inner = jnp.sum(weights * grad_weights, axis=-1, keepdims=True)
        grad_scores = (weights * (grad_weights - row_inner)).astype(jnp.bfloat16)
        grad_query = (
            jnp.einsum("cgqk,kcd->qcgd", grad_scores, key_three, preferred_element_type=jnp.float32)
            * factor
        )
        key_acc = (
            key_acc
            + jnp.einsum(
                "cgqk,qcgd->kcd", grad_scores, query_block, preferred_element_type=jnp.float32
            )
            * factor
        )
        value_acc = value_acc + jnp.einsum(
            "cgqk,qcgd->kcd",
            weights.astype(jnp.bfloat16),
            grad_block,
            preferred_element_type=jnp.float32,
        )
        return ((key_acc, value_acc), grad_query.reshape(block_rows, -1))

    zeros_kv = jnp.zeros((total_rows, kv_heads, HD), jnp.float32)
    (key_rot_grad, value_acc_grad), query_rot_grad = lax.scan(
        backward_block,
        (zeros_kv, zeros_kv),
        (query_blocks, seg_blocks, place_blocks, grad_blocks, kept_blocks),
    )
    query_lin = rotate(
        query_rot_grad.reshape(total_rows, -1), cosine_table, sine_table, -1.0
    ).astype(jnp.bfloat16)
    key_lin = rotate(key_rot_grad.reshape(total_rows, -1), cosine_table, sine_table, -1.0).astype(
        jnp.bfloat16
    )
    value_lin = value_acc_grad.reshape(total_rows, -1).astype(jnp.bfloat16)
    query_g = times_rows(full_first, query_lin)
    key_g = times_rows(full_first, key_lin)
    value_g = times_rows(full_first, value_lin)
    grad_normed1 = low_scatter(
        times_cols(query_lin, query_weight)
        + times_cols(key_lin, key_weight)
        + times_cols(value_lin, value_weight)
    )
    first_rows, grad_in_norm = norm_back(inputs, inv_first, first_gain, grad_normed1)
    tokens_grad = grad_middle + grad_in_norm
    gain_rows = jnp.stack([first_rows, second_rows])
    query_g, key_g, value_g, output_g = dp_sum((query_g, key_g, value_g, output_g))
    gain_rows, squares = lax.psum((gain_rows, squares), ("dp", "tensor"))
    rms_values = jnp.sqrt(squares / (total_rows * lax.axis_size("dp")))
    return (
        layer_out.astype(jnp.bfloat16),
        tokens_grad,
        gain_rows[0],
        query_g,
        key_g,
        value_g,
        output_g,
        gain_rows[1],
        gate_g,
        up_g,
        down_g,
        rms_values,
    )


def fused_body(
    tokens,
    lengths,
    first_gain,
    query_weight,
    key_weight,
    value_weight,
    output_weight,
    second_gain,
    gate_weight,
    up_weight,
    down_weight,
    out_cotangent,
):
    half_size = HD // 2
    inverse = (rope_base ** (-2.0 * np.arange(half_size) / (2 * half_size))).astype(np.float32)
    made = forward(
        x=tokens,
        lengths=lengths,
        gain1=first_gain,
        gain2=second_gain,
        inverse=jnp.asarray(np.concatenate([inverse, inverse])[None]),
        q_w=query_weight,
        k_w=key_weight,
        v_w=value_weight,
        out_w=output_weight,
        gate_w=gate_weight,
        up_w=up_weight,
        down_w=down_weight,
        g_own=out_cotangent,
    )
    *sums, tokens_grad, layer_out, small = backward(
        **{name + "_hbm": made[name + "_to"] for name in ("hid", "g", "h2", "d_gate", "d_up", "o", "h1")},
        **{name + "_hbm": made[name + "_to"] for name in ("q", "k", "v", "x1")},
        **{name + "_hbm": made[name] for name in ("cosines", "sines", "starts")},
        x_hbm=tokens,
        out_w=output_weight,
        q_w=query_weight,
        k_w=key_weight,
        v_w=value_weight,
        gate_w=gate_weight,
        up_w=up_weight,
        down_w=down_weight,
        gain1=first_gain,
        gain2=second_gain,
        attn_squares=made["attn_squares"],
    )
    return results(
        sums, tokens_grad, layer_out, small, query_weight.shape[1], key_weight.shape[1],
        2 * tokens.shape[0] * lax.axis_size("dp"),
    )


def solution(mesh):
    in_specs = (
        P(("dp", "tensor"), None),
        P("dp", None),
        P(),
        P(None, "tensor"),
        P(None, "tensor"),
        P(None, "tensor"),
        P("tensor", None),
        P(),
        P(None, "tensor"),
        P(None, "tensor"),
        P("tensor", None),
        P(("dp", "tensor"), None),
    )
    out_specs = (
        P(("dp", "tensor"), None),
        P(("dp", "tensor"), None),
        P(),
        P(None, "tensor"),
        P(None, "tensor"),
        P(None, "tensor"),
        P("tensor", None),
        P(),
        P(None, "tensor"),
        P(None, "tensor"),
        P("tensor", None),
        P(),
    )
    fused = dict(mesh.shape) == {"dp": 16, "tensor": 2}
    chosen = fused_body if fused else body
    return jax.shard_map(chosen, mesh=mesh, in_specs=in_specs, out_specs=out_specs, check_vma=False)
```

```python
from functools import partial

import jax
import jax.numpy as jnp
import numpy as np
from jax import lax
from jax.experimental import pallas as pl
from jax.experimental.pallas import tpu as pltpu
from jax.sharding import PartitionSpec as P

HD = 96


epsilon = 1e-05
rope_base = 10000.0
masked_score = -1e30
block_limit = 512


def product(left_side, right_side):
    return jnp.dot(left_side, right_side, preferred_element_type=jnp.float32)


def times_rows(left_side, right_side):
    return lax.dot_general(
        left_side, right_side, (((0,), (0,)), ((), ())), preferred_element_type=jnp.float32
    )


def times_cols(left_side, right_side):
    return lax.dot_general(
        left_side, right_side, (((1,), (1,)), ((), ())), preferred_element_type=jnp.float32
    )


def tables(lens_row, total_rows, half_size):
    count = lens_row.shape[0]
    earlier = jnp.arange(count)[:, None] <= jnp.arange(count)[None, :]
    seq_ends = jnp.sum(jnp.where(earlier, lens_row[:, None], 0), axis=0, dtype=jnp.int32)
    starts = seq_ends - lens_row
    places = jnp.arange(total_rows, dtype=jnp.int32)
    segment = jnp.sum(
        (places[:, None] >= seq_ends[None, :]).astype(jnp.int32), axis=1, dtype=jnp.int32
    )
    member = segment[:, None] == jnp.arange(lens_row.shape[0], dtype=jnp.int32)[None, :]
    position = places - jnp.sum(jnp.where(member, starts[None, :], 0), axis=1, dtype=jnp.int32)
    inverse = rope_base ** (-2.0 * jnp.arange(half_size, dtype=jnp.float32) / (2 * half_size))
    angles = position.astype(jnp.float32)[:, None] * inverse[None, :]
    return (places, segment, jnp.cos(angles), jnp.sin(angles))


def rotate(values, cosine_table, sine_table, direction):
    total_rows = values.shape[0]
    half_size = cosine_table.shape[1]
    shaped = values.reshape(total_rows, -1, 2 * half_size)
    first_half = shaped[..., :half_size]
    second = shaped[..., half_size:]
    cos_b = cosine_table[:, None, :]
    sin_b = sine_table[:, None, :] * direction
    turned = jnp.concatenate(
        [first_half * cos_b - second * sin_b, second * cos_b + first_half * sin_b], axis=-1
    )
    return turned.reshape(total_rows, -1)


def norm_rows(values, gain):
    inv_rms = lax.rsqrt(jnp.mean(values * values, axis=-1, keepdims=True) + epsilon)
    return (values * inv_rms * gain, inv_rms)


def norm_back(values, inv_rms, gain, upstream):
    scaled = upstream * gain
    row_inner = jnp.mean(scaled * values, axis=-1, keepdims=True)
    gain_rows = jnp.sum(upstream * values * inv_rms, axis=0)
    return (gain_rows, inv_rms * (scaled - values * inv_rms * inv_rms * row_inner))


ORDER = (
    1000, 1, 2, 101, 203, 202, 102, 1001, 203, 205, 1002, 203, 1003, 205, 202, 203, 203, 0, 205,
    203, 204, 100, 202, 203, 205, 1004, 201, 202, 205, 1011, 203, 205, 202, 1012, 201, 205, 200,
    203, 1005, 204, 201, 1006, 202, 1007, 204, 205, 201, 201, 210, 3, 202, 200, 204, 1008, 205, 210,
    201, 204, 200, 103, 206, 210, 201, 207, 1009, 4, 200, 204, 1010, 210, 201, 210, 206, 104, 210,
    204, 1013, 206, 209, 207, 210, 211, 200, 206, 201, 208, 205, 209, 207, 1014, 210, 209, 211, 202,
    200, 204, 1015, 208, 210, 211, 206, 209, 201, 209, 200, 203, 208, 207, 211, 208, 207, 209, 206,
    211, 210, 208, 206, 209, 207, 1016, 1017, 210, 203, 211, 208, 1018, 206, 201, 209, 200, 211,
    207, 202, 206, 204, 208, 1019, 209, 211, 200, 208, 207, 1020, 205, 209, 209, 208, 207, 211, 207,
    207,
)


MESH = pl.DeviceIdType.MESH
LINE = 4
DOWN, GATE, UP, OUT, QKV = range(5)
UNITS = (
    (2048, 1536, 256, 0, 0),
    (1536, 2048, 256, 1, 0),
    (1536, 2048, 256, 2, 0),
    (768, 1536, 128, 3, 0),
    (1536, 1536, 256, 4, 0),
)
BLOCKS = (
    (0, True, 0, 640),
    (0, False, 640, 384),
    (1, True, 0, 512),
    (1, False, 512, 256),
    (2, True, 0, 384),
    (2, False, 384, 256),
    (3, True, 0, 256),
    (3, False, 256, 128),
    (4, True, 0, 256),
    (4, False, 256, 256),
    (2, False, 640, 128),
    (4, True, 512, 256),
)
WHOLE = tuple(
    (sum(unit[0] for unit in UNITS if unit[3] == kind), next(unit[1] for unit in UNITS if unit[3] == kind))
    for kind in range(5)
)
COPIES = 20
TILE_BASE = len(BLOCKS) * COPIES
TILES = tuple(rows // 2 // tile for rows, _, tile, *_ in UNITS)
SMALL_BASE = TILE_BASE + sum(TILES)
SMALL_STEPS = 5
Y_BASE = SMALL_BASE + SMALL_STEPS
N_SEMS = Y_BASE + 4


def rows_at(start, size):
    return pl.ds(pl.multiple_of(start, 16), size)


class Place:
    def __init__(self):
        dp = lax.axis_index("dp")
        self.dp = dp
        self.y = lax.axis_index("tensor")
        self.core = lax.rem(dp, 2)
        self.x = lax.rem(dp // 2, 2)
        self.z = dp // 4

    def at(self, z, x, core, y):
        return ((z * 2 + x) * 2 + core, y)

    def other_core(self):
        return self.at(self.z, self.x, 1 - self.core, self.y)

    def other_x(self):
        return self.at(self.z, 1 - self.x, self.core, self.y)

    def other_y(self):
        return self.at(self.z, self.x, self.core, 1 - self.y)

    def up(self):
        return self.at(self.z + 1, self.x, self.core, self.y)

    def down(self):
        return self.at(self.z - 1, self.x, self.core, self.y)

    def pair_z(self):
        return self.at(self.z + 1 - 2 * lax.rem(self.z, 2), self.x, self.core, self.y)

    def far_z(self):
        return self.at(lax.rem(self.z + 2, LINE), self.x, self.core, self.y)


class Mover:
    def __init__(self, send_sems, recv_sems):
        self.send_sems = send_sems
        self.recv_sems = recv_sems
        self.left = []

    def copy(self, source, target, index, device):
        return pltpu.make_async_remote_copy(
            src_ref=source,
            dst_ref=target,
            send_sem=self.send_sems.at[index],
            recv_sem=self.recv_sems.at[index],
            device_id=device,
            device_id_type=MESH,
        )

    def start(self, source, target, index, device, when=None):
        copy = self.copy(source, target, index, device)
        guarded(when, copy.start)
        self.left.append((when, copy.wait_send))

    def arrived(self, target, index, device):
        self.copy(target, target, index, device).wait_recv()


def guarded(when, action):
    if when is None:
        action()
    else:
        pl.when(when)(action)


def add_rows(target, target_row, source, source_row, size):
    step = 16

    def one(i, _):
        here = rows_at(target_row + i * step, step)
        there = rows_at(source_row + i * step, step)
        total = target[here, :].astype(jnp.float32) + source[there, :].astype(jnp.float32)
        target[here, :] = total.astype(target.dtype)
        return 0

    lax.fori_loop(0, size // step, one, 0)


def fall_slot(step):
    return 0 if step == 0 else 2 + step


class Block:
    def __init__(self, place, mover, held, across, along, result, base, start, size, half_rows, x_first, first):
        self.p = place
        self.m = mover
        self.held = held
        self.across = across
        self.along = along
        self.result = result
        self.base = base
        self.start = start
        self.size = size
        self.half_rows = half_rows
        self.x_first = x_first
        self.first = first
        self.chunk = size // 8 if x_first else size // 4
        self.origin = start + place.x * (size // 2) if x_first else start

    def part(self, chunk):
        return self.held.at[rows_at(self.origin + chunk * self.chunk, self.chunk)]

    def final(self, row, size):
        return self.result.at[rows_at(self.first + self.p.core * self.half_rows + row, size)]

    def final_part(self, chunk):
        return self.final(self.origin + chunk * self.chunk, self.chunk)

    def keep(self, row, size):
        index = self.base // COPIES
        copy = pltpu.make_async_copy(
            self.held.at[rows_at(row, size)], self.final(row, size), self.m.keep_sems.at[index]
        )
        copy.start()
        self.kept = copy

    def events(self):
        line = [self.line_start, lambda: self.line_add(0), lambda: self.line_add(1), lambda: self.line_add(2)]
        spread = [lambda: self.spread(1), lambda: self.spread(2), lambda: self.spread(3)]
        if self.x_first:
            return [self.x_send, self.x_add] + line[1:] + spread + [self.x_done]
        return line + [self.pair_send, self.pair_add, self.pair_done] + spread + [self.z_done]

    def line_start(self):
        p = self.p
        for step in range(3):
            self.m.start(self.part(3 - step), self.along.at[step], self.base + step, p.up(), p.z == 0)
            self.m.start(self.part(step), self.along.at[fall_slot(step)], self.base + 3 + step, p.down(), p.z == LINE - 1)

    def line_add(self, step):
        p = self.p
        rising = jnp.minimum(p.z + 2 - step, 3)
        falling = jnp.maximum(p.z - 2 + step, 0)
        goes_up = (p.z >= 1) & (p.z <= step + 1)
        goes_down = (p.z <= 2) & (p.z >= 2 - step)

        def take_rising():
            self.m.arrived(self.along.at[step], self.base + step, p.down())
            add_rows(self.held, self.origin + rising * self.chunk, self.along.at[step], 0, self.chunk)

        def take_falling():
            self.m.arrived(self.along.at[fall_slot(step)], self.base + 3 + step, p.up())
            add_rows(self.held, self.origin + falling * self.chunk, self.along.at[fall_slot(step)], 0, self.chunk)

        pl.when(goes_up)(take_rising)
        if step < 2:
            self.m.start(self.part(rising), self.along.at[step + 1], self.base + step + 1, p.up(), goes_up)
        pl.when(goes_down)(take_falling)
        if step < 2:
            self.m.start(self.part(falling), self.along.at[fall_slot(step + 1)], self.base + 4 + step, p.down(), goes_down)
        elif self.x_first:
            self.keep(self.origin + p.z * self.chunk, self.chunk)
            self.own_spread(self.part(p.z))
            self.x_return(self.part(p.z), p.z, None)

    def own_spread(self, source):
        p = self.p
        target = self.final_part(p.z)
        self.m.start(source, target, self.base + 6, p.up(), p.z < 3)
        self.m.start(source, target, self.base + 9, p.down(), p.z > 0)

    def spread(self, distance):
        p = self.p
        below = self.final_part(jnp.maximum(p.z - distance, 0))
        above = self.final_part(jnp.minimum(p.z + distance, 3))

        pl.when(p.z >= distance)(lambda: self.m.arrived(below, self.base + 5 + distance, p.down()))
        if distance < 3:
            self.m.start(below, below, self.base + 6 + distance, p.up(), (p.z >= distance) & (p.z < 3))
        if self.x_first:
            self.x_return(below, jnp.maximum(p.z - distance, 0), p.z >= distance)
        pl.when(p.z <= 3 - distance)(lambda: self.m.arrived(above, self.base + 8 + distance, p.up()))
        if distance < 3:
            self.m.start(above, above, self.base + 9 + distance, p.down(), (p.z <= 3 - distance) & (p.z > 0))
        if self.x_first:
            self.x_return(above, jnp.minimum(p.z + distance, 3), p.z <= 3 - distance)
            if distance == 3:
                self.kept.wait()
                self.give(p.x * (self.size // 2), self.size // 2, 14)

    def x_part(self, which):
        half = self.size // 2
        return self.held.at[rows_at(self.start + which * half, half)]

    def x_send(self):
        self.m.start(self.x_part(1 - self.p.x), self.across, self.base + 12, self.p.other_x())

    def x_add(self):
        self.m.arrived(self.across, self.base + 12, self.p.other_x())
        add_rows(self.held, self.origin, self.across, 0, self.size // 2)
        self.line_start()

    def x_return(self, source, chunk, when):
        self.m.start(source, self.final_part(chunk), self.base + 16 + chunk, self.p.other_x(), when)

    def x_done(self):
        p = self.p
        half = (1 - p.x) * (self.size // 2)
        for chunk in range(4):
            place = self.final(self.start + half + chunk * self.chunk, self.chunk)
            self.m.arrived(place, self.base + 16 + chunk, p.other_x())
        self.give(half, self.size // 2, 15)

    def pair_row(self, which):
        return self.start + self.p.z * self.chunk + which * (self.chunk // 2)

    def pair_send(self):
        half = self.chunk // 2
        source = self.held.at[rows_at(self.pair_row(1 - self.p.x), half)]
        self.m.start(source, self.across, self.base + 12, self.p.other_x())

    def pair_add(self):
        p = self.p
        half = self.chunk // 2
        self.m.arrived(self.across, self.base + 12, p.other_x())
        row = self.pair_row(p.x)
        add_rows(self.held, row, self.across, 0, half)
        self.keep(row, half)
        self.m.start(self.held.at[rows_at(row, half)], self.final(row, half), self.base + 13, p.other_x())

    def pair_done(self):
        p = self.p
        half = self.chunk // 2
        self.m.arrived(self.final(self.pair_row(1 - p.x), half), self.base + 13, p.other_x())
        self.kept.wait()
        self.own_spread(self.final_part(p.z))

    def z_done(self):
        self.give(0, self.size, 14)

    def give(self, offset, size, slot):
        p = self.p
        source = self.final(self.start + offset, size)
        self.m.start(source, source, self.base + slot, p.other_core())
        other = self.result.at[
            rows_at(self.first + (1 - p.core) * self.half_rows + self.start + offset, size)
        ]
        self.m.left.append((None, lambda: self.m.arrived(other, self.base + slot, p.other_core())))


def product_tile(left, right, first, tile, width, part):
    columns = pl.ds(pl.multiple_of(first, 128), tile)
    return lax.dot_general(
        left[:, columns], right[:, part * width : (part + 1) * width],
        (((0,), (0,)), ((), ())), preferred_element_type=jnp.float32,
    )


class Unit:
    def __init__(self, index, place, mover, left, right, held, staged, stage_sems):
        self.index = index
        self.rows, self.columns, self.tile, _, self.first = UNITS[index]
        self.p, self.m = place, mover
        self.left, self.right, self.held = left, right, held
        self.staged, self.stage_sems = staged, stage_sems
        self.base = TILE_BASE + sum(TILES[:index])
        self.width = 512

    def tile_copy(self, i, slot):
        tile = self.tile
        return pltpu.make_async_remote_copy(
            src_ref=self.staged.at[slot, pl.ds(0, tile), pl.ds(0, self.columns)],
            dst_ref=self.held.at[rows_at(i * tile, tile)],
            send_sem=self.stage_sems.at[slot],
            recv_sem=self.m.recv_sems.at[self.base + i],
            device_id=self.p.other_core(),
            device_id_type=MESH,
        )

    def send(self):
        half, tile = self.rows // 2, self.tile

        def one(i, _):
            slot = lax.rem(i, 2)
            pl.when(i >= 2)(lambda: self.tile_copy(i, slot).wait_send())
            first = self.first + (1 - self.p.core) * half + i * tile
            for part in range(self.columns // self.width):
                got = product_tile(self.left, self.right, first, tile, self.width, part)
                self.staged[slot, pl.ds(0, tile), part * self.width : (part + 1) * self.width] = got.astype(
                    jnp.bfloat16
                )
            self.tile_copy(i, slot).start()
            return 0

        lax.fori_loop(0, half // tile, one, 0)
        for slot in range(min(2, half // tile)):
            self.tile_copy(0, slot).wait_send()

    def own(self):
        half, tile = self.rows // 2, self.tile

        def one(i, _):
            self.tile_copy(i, 0).wait_recv()
            first = self.first + self.p.core * half + i * tile
            here = rows_at(i * tile, tile)
            for part in range(self.columns // self.width):
                got = product_tile(self.left, self.right, first, tile, self.width, part)
                cut = slice(part * self.width, (part + 1) * self.width)
                total = got + self.held[here, cut].astype(jnp.float32)
                self.held[here, cut] = total.astype(jnp.bfloat16)
            return 0

        lax.fori_loop(0, half // tile, one, 0)


def row_scale(values):
    return lax.rsqrt(jnp.mean(values * values, axis=-1, keepdims=True) + epsilon)


def eight(values):
    rows, columns = values.shape
    return jnp.sum(values.reshape(rows // 8, 8, columns), axis=0)


def turn_back(values, cosines, sines):
    half = values.shape[1] // 2
    swapped = jnp.concatenate([values[:, half:], values[:, :half]], axis=1)
    return values * cosines + swapped * sines


def nt(left_side, right_side):
    return lax.dot_general(
        left_side, right_side, (((1,), (1,)), ((), ())), preferred_element_type=jnp.float32
    )


def tn(left_side, right_side):
    return lax.dot_general(
        left_side, right_side, (((0,), (0,)), ((), ())), preferred_element_type=jnp.float32
    )


class Layer:
    def __init__(self, place, mover, **refs):
        self.p, self.m = place, mover
        self.__dict__.update(refs)
        self.rows = self.x1.shape[0]
        self.mine = rows_at(place.y * self.rows, self.rows)
        self.theirs = rows_at((1 - place.y) * self.rows, self.rows)

    def load(self, source, target, index):
        copy = pltpu.make_async_copy(source, target, self.local_sems.at[index])
        copy.start()
        return copy

    def begin(self):
        self.waits = {}
        for i, (name, target) in enumerate(LOADED):
            self.waits[target] = self.load(getattr(self, name), getattr(self, target), 16 + i)
        self.waits["out_w"] = self.load(self.out_w, self.wbuf.at[pl.ds(0, 768)], 3)

    def need(self, *targets):
        for target in targets:
            if target in self.waits:
                self.waits.pop(target).wait()

    def stream(self, first, count, fetch, use):
        def go(i):
            for j, (source, target) in enumerate(fetch(i)):
                pltpu.make_async_copy(source, target, self.local_sems.at[8 + 2 * lax.rem(i, 2) + j]).start()

        go(jnp.int32(first))

        def body(i, _):
            pl.when(i + 1 < first + count)(lambda: go(i + 1))
            for j, (source, target) in enumerate(fetch(i)):
                pltpu.make_async_copy(source, target, self.local_sems.at[8 + 2 * lax.rem(i, 2) + j]).wait()
            use(i, lax.rem(i, 2))
            return 0

        lax.fori_loop(first, first + count, body, 0)

    def h2_third(self, third):
        self.need("d_gate", "d_up")
        first, count = 2 * third, 2

        def fetch(i, which):
            source = (self.gate_w, self.up_w)[which].at[rows_at(i * 256, 256)]
            return pltpu.make_async_copy(source, self.staged.at[which], self.local_sems.at[8 + which])

        def use(i, which):
            fetch(i, which).wait()
            cut = pl.ds(pl.multiple_of(i * 256, 256), 256)
            weight, grad = self.staged[which], (self.d_gate, self.d_up)[which]
            theirs, mine = nt(grad[self.theirs, :], weight), nt(grad[self.mine, :], weight)
            if which == 0:
                self.d_x1[:, cut] = theirs
                self.fbuf[:, cut] = mine
            else:
                self.h2_out[:, cut] = (self.d_x1[:, cut] + theirs).astype(jnp.bfloat16)
                self.fbuf[:, cut] += mine
            pl.when(i + 1 < first + count)(lambda: fetch(i + 1, which).start())

        fetch(first, 0).start()
        fetch(first, 1).start()

        def body(i, _):
            use(i, 0)
            use(i, 1)
            return 0

        lax.fori_loop(first, first + count, body, 0)
        if third == 2:
            self.h2_sent = self.m.copy(self.h2_out, self.h2_in, Y_BASE, self.p.other_y())
            self.h2_sent.start()

    def mlp_half(self, half):
        self.need("hid")

        rows, target = ((self.theirs, self.mlp_out), (self.mine, self.own))[half]
        self.fbuf[...] = jnp.zeros_like(self.fbuf)

        def fetch(i):
            return ((self.down_w.at[rows_at(i * 256, 256)], self.staged.at[lax.rem(i, 2), :, pl.ds(0, 1536)]),)

        def use(i, slot):
            cut = pl.ds(pl.multiple_of(i * 256, 256), 256)
            self.fbuf[...] += product(self.hid[rows, cut], self.staged[slot, :, 0:1536])

        self.stream(0, self.down_w.shape[0] // 256, fetch, use)
        target[...] = self.fbuf[...].astype(target.dtype)

    def tiles(self, step, body):
        lax.fori_loop(0, self.rows // step, lambda i, _: (body(i * step, step), 0)[1], 0)

    def middle(self):
        self.need("x1", "g")
        self.m.arrived(self.h2_in, Y_BASE, self.p.other_y())
        self.gains[...] = jnp.zeros_like(self.gains)

        def body(start, step):
            here = rows_at(start, step)
            there = rows_at(self.p.y * self.rows + start, step)
            d = self.fbuf[here, :] + self.h2_in[here, :].astype(jnp.float32)
            x1 = self.x1[here, :]
            inv = row_scale(x1)
            scaled = d * self.gain2[...].reshape(1, -1)
            inner = jnp.mean(scaled * x1, axis=-1, keepdims=True)
            self.gains[1] += eight(d * x1 * inv)
            d_x1 = self.g[there, :].astype(jnp.float32) + inv * (scaled - x1 * inv * inv * inner)
            self.d_x1[here, :] = d_x1
            self.d_attn[there, :] = d_x1.astype(jnp.bfloat16)

        self.tiles(16, body)
        own = self.d_attn.at[self.mine]
        self.m.start(own, own, Y_BASE + 1, self.p.other_y())

    def outward(self):
        self.m.arrived(self.d_attn.at[self.theirs], Y_BASE + 1, self.p.other_y())
        self.need("out_w")
        for part in range(3):
            cut = slice(part * 256, (part + 1) * 256)
            self.d_o[:, cut] = nt(self.d_attn[...], self.wbuf[cut, :]).astype(jnp.bfloat16)
        self.w_loads = [
            self.load(self.q_w, self.wbuf.at[:, pl.ds(0, 768)], 3),
            self.load(self.k_w, self.wbuf.at[:, pl.ds(768, 384)], 4),
            self.load(self.v_w, self.wbuf.at[:, pl.ds(1152, 384)], 5),
        ]

    def attention(self, key_head):
        self.need("q", "k", "v", "cosines", "sines", "starts")
        factor = HD ** (-0.5)
        c = key_head * HD
        keys, values = self.k[:, c : c + HD], self.v[:, c : c + HD]
        block = 256
        d_k = [jnp.zeros((block, HD), jnp.float32)] * 2
        d_v = [jnp.zeros((block, HD), jnp.float32)] * 2
        for head in (2 * key_head, 2 * key_head + 1):
            h = head * HD
            for i in range(2):
                here = slice(i * block, (i + 1) * block)
                n = block * (i + 1)
                query, d_out = self.q[here, h : h + HD], self.d_o[here, h : h + HD]
                column = lax.broadcasted_iota(jnp.int32, (block, n), 1)
                row = lax.broadcasted_iota(jnp.int32, (block, n), 0) + i * block
                allowed = (column <= row) & (column >= self.starts[here, :])
                masked = jnp.where(allowed, nt(query, keys[:n]) * factor, masked_score)
                exponent = jnp.exp(masked - jnp.max(masked, axis=1, keepdims=True))
                weights = exponent / jnp.sum(exponent, axis=1, keepdims=True)
                d_weights = nt(d_out, values[:n])
                inner = jnp.sum(weights * d_weights, axis=1, keepdims=True)
                d_scores = (weights * (d_weights - inner)).astype(jnp.bfloat16)
                low = weights.astype(jnp.bfloat16)
                d_query = jnp.dot(d_scores, keys[:n], preferred_element_type=jnp.float32) * factor
                turned = turn_back(d_query, self.cosines[here, :], self.sines[here, :])
                self.d_qkv[here, h : h + HD] = turned.astype(jnp.bfloat16)
                for j in range(i + 1):
                    cut = slice(j * block, (j + 1) * block)
                    d_k[j] = d_k[j] + tn(d_scores[:, cut], query) * factor
                    d_v[j] = d_v[j] + tn(low[:, cut], d_out)
        for j in range(2):
            cut = slice(j * block, (j + 1) * block)
            turned = turn_back(d_k[j], self.cosines[cut, :], self.sines[cut, :])
            self.d_qkv[cut, 768 + c : 768 + c + HD] = turned.astype(jnp.bfloat16)
            self.d_qkv[cut, 1152 + c : 1152 + c + HD] = d_v[j].astype(jnp.bfloat16)

    def h1_part(self, rows, put):
        def body(i, _):
            cut = pl.ds(pl.multiple_of(i * 256, 256), 256)
            put(cut, nt(self.d_qkv[rows, 0:1536], self.wbuf[cut, :]))
            return 0

        lax.fori_loop(0, 6, body, 0)

    def inward(self):
        for copy in self.w_loads:
            copy.wait()

        self.h2_sent.wait_send()
        self.waits["x"] = self.load(self.x_hbm, self.h2_in, 0)

        def put(cut, got):
            self.h2_out[:, cut] = got.astype(jnp.bfloat16)

        self.h1_part(self.theirs, put)
        self.m.start(self.h2_out, self.h1_in, Y_BASE + 2, self.p.other_y())

    def mlp_send(self):
        self.m.start(self.mlp_out, self.mlp_in, Y_BASE + 3, self.p.other_y())

    def finish(self):
        def put(cut, got):
            self.fbuf[:, cut] = got

        self.waits.pop("x").wait()
        self.h1_part(self.mine, put)
        self.m.arrived(self.h1_in, Y_BASE + 2, self.p.other_y())

        def body(start, step):
            here = rows_at(start, step)
            d = self.fbuf[here, :] + self.h1_in[here, :].astype(jnp.float32)
            x = self.h2_in[here, :].astype(jnp.float32)
            inv = row_scale(x)
            scaled = d * self.gain1[...].reshape(1, -1)
            inner = jnp.mean(scaled * x, axis=-1, keepdims=True)
            self.gains[0] += eight(d * x * inv)
            self.d_x1[here, :] = self.d_x1[here, :] + inv * (scaled - x * inv * inv * inner)

        self.tiles(16, body)
        copy = self.load(self.d_x1, self.tokens_out, 6)
        self.m.left.append((None, copy.wait))

    def layer_end(self):
        self.m.arrived(self.mlp_in, Y_BASE + 3, self.p.other_y())

        def body(start, step):
            here = rows_at(start, step)
            mlp = self.own[here, :].astype(jnp.float32) + self.mlp_in[here, :].astype(jnp.float32)
            out = self.x1[here, :] + mlp
            self.gains[2] += eight(out * out)
            self.gains[3] += eight(mlp * mlp)
            self.own[here, :] = out.astype(jnp.bfloat16)

        self.tiles(16, body)
        copy = self.load(self.own, self.layer_out, 7)
        self.m.left.append((None, copy.wait))
        self.totals[0] = jnp.zeros(self.totals.shape[1:], jnp.float32)
        for row in range(4):
            self.totals[0, row : row + 1, :] = jnp.sum(self.gains[row], axis=0, keepdims=True)
        self.totals[0, 4:5, :] = self.attn_squares[...]


def sum_small(place, mover, total, slots, step):
    device = (place.other_core, place.other_x, place.other_y, place.pair_z, place.far_z)[step]()
    copy = mover.copy(total.at[step], slots.at[step], SMALL_BASE + step, device)
    copy.start()
    copy.wait()
    total[step + 1] = total[step] + slots[step]


INPUTS = (
    "hid_hbm", "g_hbm", "h2_hbm", "d_gate_hbm", "d_up_hbm", "o_hbm", "h1_hbm", "q_hbm", "k_hbm", "v_hbm",
    "out_w", "q_w", "k_w", "v_w", "gate_w", "up_w", "down_w", "x1_hbm", "x_hbm", "cosines_hbm", "sines_hbm",
    "starts_hbm", "gain1", "gain2", "attn_squares",
)
IN_VMEM = ("gain1", "gain2", "attn_squares")
LOADED = (
    ("hid_hbm", "hid"), ("g_hbm", "g"), ("h2_hbm", "hbuf"), ("d_gate_hbm", "d_gate"), ("d_up_hbm", "d_up"),
    ("x1_hbm", "x1"), ("o_hbm", "o"), ("q_hbm", "q"), ("k_hbm", "k"), ("v_hbm", "v"),
    ("cosines_hbm", "cosines"), ("sines_hbm", "sines"), ("starts_hbm", "starts"),
)
RESULTS = ("down_out", "gate_out", "up_out", "o_out", "qkv_out", "tokens_out", "layer_out", "small_out")
PLAIN = (
    "staged", "hid", "hbuf", "own", "h2_in", "d_attn", "d_x1", "wbuf", "d_o", "h1_in", "mlp_in", "h2_out",
    "mlp_out", "fbuf", "gains", "totals", "slots", "g", "d_gate", "d_up", "o", "q", "k", "v", "x1",
    "cosines", "sines", "starts",
    "stage_sems", "send_sems", "recv_sems", "keep_sems", "local_sems",
)


def backward_kernel(*refs):
    n = len(UNITS)
    names = INPUTS + RESULTS
    r = dict(zip(names, refs[: len(names)]))
    rest = refs[len(names) :]
    b = len(BLOCKS)
    held, across, along = rest[:n], rest[n : n + b], rest[n + b : n + 2 * b]
    r.update(zip(PLAIN, rest[n + 2 * b :]))
    r["d_qkv"] = r["hid"]
    place = Place()
    mover = Mover(r["send_sems"], r["recv_sems"])
    mover.keep_sems = r["keep_sems"]
    enter(place)
    layer = Layer(place, mover, **r)
    lefts = (r["hid"], r["hbuf"], r["hbuf"], r["o"], r["hbuf"])
    rights = (r["g"], r["d_gate"], r["d_up"], r["d_attn"], r["d_qkv"])
    results = tuple(r[name] for name in RESULTS[:5])
    units = [
        Unit(i, place, mover, lefts[unit[3]], rights[unit[3]], held[i], r["staged"], r["stage_sems"])
        for i, unit in enumerate(UNITS)
    ]
    steps = []
    for b, (i, x_first, start, size) in enumerate(BLOCKS):
        rows, _, _, kind, first = UNITS[i]
        block = Block(
            place, mover, held[i], across[b], along[b], results[kind], b * COPIES, start, size, rows // 2, x_first,
            first,
        )
        steps.append(block.events())

    def send(i):
        kind, first = UNITS[i][3:]
        layer.need(*((("hid", "g"), ("hbuf", "d_gate"), ("hbuf", "d_up"), ("o",), ())[kind]))
        if kind == QKV and first == 0:
            layer.load(layer.h1_hbm, layer.hbuf, 1).wait()
        units[i].send()

    tasks = [layer.begin]
    tasks += [partial(layer.h2_third, i) for i in range(3)]
    tasks += [layer.middle, layer.outward]
    tasks += [partial(layer.attention, i) for i in range(4)]
    tasks += [layer.inward]
    tasks += [partial(layer.mlp_half, i) for i in range(2)]
    tasks += [layer.mlp_send, layer.finish, layer.layer_end]
    tasks += [partial(sum_small, place, mover, r["totals"], r["slots"], i) for i in range(SMALL_STEPS)]
    for item in ORDER:
        if item < 100:
            send(item)
        elif item < 200:
            units[item - 100].own()
        elif item < 1000:
            steps[item - 200].pop(0)()
        else:
            tasks[item - 1000]()
    r["small_out"][...] = r["totals"][SMALL_STEPS]
    for when, wait in mover.left:
        guarded(when, wait)


def enter(place):
    barrier = pltpu.get_barrier_semaphore()

    def greet(device):
        pl.semaphore_signal(barrier, inc=1, device_id=device, device_id_type=MESH)

    for device in (place.other_core(), place.other_x(), place.other_y(), place.pair_z(), place.far_z()):
        greet(device)
    middle = (place.z == 1) | (place.z == 2)
    pl.when(middle)(lambda: greet(place.at(3 - place.z, place.x, place.core, place.y)))
    pl.semaphore_wait(barrier, 5 + jnp.where(middle, 1, 0))


def backward(**given):
    vmem = pl.BlockSpec(memory_space=pltpu.VMEM)
    hbm = pl.BlockSpec(memory_space=pl.ANY)
    low, full = jnp.bfloat16, jnp.float32
    own_rows, width = given["x1_hbm"].shape
    held = [pltpu.VMEM((rows // 2, columns), low) for rows, columns, *_ in UNITS]
    across, along = [], []
    for i, x_first, _, size in BLOCKS:
        columns = UNITS[i][1]
        across.append(pltpu.VMEM((size // 2 if x_first else size // 8, columns), low))
        along.append(pltpu.VMEM((5, size // 8 if x_first else size // 4, columns), low))
    part = pltpu.VMEM((own_rows, width), low)
    plain = dict(
        staged=pltpu.VMEM((2, 256, 2048), low),
        hid=pltpu.VMEM((512, 2048), low),
        hbuf=pltpu.VMEM((512, width), low),
        own=part,
        h2_in=part,
        d_attn=pltpu.VMEM((512, width), low),
        d_x1=pltpu.VMEM((own_rows, width), full),
        wbuf=pltpu.VMEM((1536, 1536), low),
        d_o=pltpu.VMEM((512, 768), low),
        h1_in=part,
        mlp_in=part,
        h2_out=part,
        mlp_out=part,
        fbuf=pltpu.VMEM((own_rows, width), full),
        gains=pltpu.VMEM((4, 8, width), full),
        totals=pltpu.VMEM((SMALL_STEPS + 1, 8, width), full),
        slots=pltpu.VMEM((SMALL_STEPS, 8, width), full),
        stage_sems=pltpu.SemaphoreType.DMA((2,)),
        send_sems=pltpu.SemaphoreType.DMA((N_SEMS,)),
        recv_sems=pltpu.SemaphoreType.DMA((N_SEMS,)),
        keep_sems=pltpu.SemaphoreType.DMA((len(BLOCKS),)),
        local_sems=pltpu.SemaphoreType.DMA((16 + len(LOADED),)),
    )
    for name, target in LOADED:
        plain.setdefault(target, pltpu.VMEM(given[name].shape, given[name].dtype))
    flops = sum(2 * 512 * rows * columns for rows, columns, *_ in UNITS)
    return pl.pallas_call(
        backward_kernel,
        out_shape=[jax.ShapeDtypeStruct(shape, low) for shape in WHOLE]
        + [
            jax.ShapeDtypeStruct((own_rows, width), full),
            jax.ShapeDtypeStruct((own_rows, width), low),
            jax.ShapeDtypeStruct((8, width), full),
        ],
        in_specs=[vmem if name in IN_VMEM else hbm for name in INPUTS],
        out_specs=[hbm] * 7 + [vmem],
        scratch_shapes=held + across + along + [plain[name] for name in PLAIN],
        compiler_params=pltpu.CompilerParams(
            collective_id=0, has_side_effects=True, vmem_limit_bytes=62 << 20
        ),
        cost_estimate=pl.CostEstimate(flops=flops, bytes_accessed=80 << 20, transcendentals=0),
        name="backward",
    )(*(given[name] for name in INPUTS))


FORWARD_INPUTS = (
    "x", "lengths", "gain1", "gain2", "inverse", "q_w", "k_w", "v_w", "out_w", "gate_w", "up_w", "down_w", "g_own",
)
FORWARD_RESULTS = (
    "hid_to", "g_to", "h2_to", "d_gate_to", "d_up_to", "o_to", "h1_to", "q_to", "k_to", "v_to", "x1_to",
    "cosines", "sines", "starts", "attn_squares",
)
FORWARD_PLAIN = (
    "x_in", "w_qkv", "w_out", "w_gate", "w_up", "w_down", "g", "h1", "lin", "q", "k", "v", "o", "own_part",
    "sent_part", "got_part", "x1", "h2", "d_hid", "hid", "d_gate", "d_up", "squares",
    "send_sems", "recv_sems", "load_sems", "store_sems",
)
CHUNKS = 2


class Forward:
    def __init__(self, refs):
        self.__dict__.update(refs)
        self.p = Place()
        self.m = Mover(self.send_sems, self.recv_sems)
        self.rows = self.x.shape[0]
        self.step = self.rows // CHUNKS
        self.base = self.p.y * self.rows
        self.far = (1 - self.p.y) * self.rows
        self.stores = 0

    def load(self, source, target, index):
        copy = pltpu.make_async_copy(source, target, self.load_sems.at[index])
        copy.start()
        return copy

    def store(self, source, target):
        copy = pltpu.make_async_copy(source, target, self.store_sems.at[self.stores])
        self.stores += 1
        copy.start()
        self.m.left.append((None, copy.wait))

    def store_rows(self, row, count):
        here = rows_at(row, count)
        for name in ("h2", "hid", "d_gate", "d_up"):
            self.store(getattr(self, name).at[here], getattr(self, name + "_to").at[here])

    def across(self, source, target, index):
        self.m.start(source, target, index, self.p.other_y())

    def arrived(self, target, index):
        self.m.arrived(target, index, self.p.other_y())

    def tiles(self, first, count, step, body):
        lax.fori_loop(0, count // step, lambda i, _: (body(first + i * step, step), 0)[1], 0)

    def run(self):
        step = self.step
        barrier = pltpu.get_barrier_semaphore()
        pl.semaphore_signal(barrier, inc=1, device_id=self.p.other_y(), device_id_type=MESH)
        pl.semaphore_wait(barrier, 1)
        for c in range(CHUNKS):
            part = pl.ds(c * step, step)
            self.across(self.x.at[part], self.x_in.at[part], c)
        self.across(self.g_own, self.g.at[rows_at(self.base, self.rows)], 2 * CHUNKS)
        qkv_loads = [
            self.load(self.q_w, self.w_qkv.at[:, pl.ds(0, 768)], 0),
            self.load(self.k_w, self.w_qkv.at[:, pl.ds(768, 384)], 1),
            self.load(self.v_w, self.w_qkv.at[:, pl.ds(1152, 384)], 2),
        ]
        g_load = self.load(self.g_own, self.g.at[rows_at(self.base, self.rows)], 3)
        out_load = self.load(self.out_w, self.w_out, 4)
        down_load = self.load(self.down_w, self.w_down, 5)
        gate_load = self.load(self.gate_w, self.w_gate, 6)
        up_load = self.load(self.up_w, self.w_up, 7)
        self.tables()
        self.norm1(self.x, 0, self.base, self.rows)
        for copy in qkv_loads:
            copy.wait()
        self.qkv(self.base, self.rows)
        for c in range(CHUNKS):
            self.arrived(self.x_in.at[pl.ds(c * step, step)], c)
            self.norm1(self.x_in, c * step, self.far + c * step, step)
            self.qkv(self.far + c * step, step)
        self.store(self.h1, self.h1_to)
        self.store(self.q, self.q_to)
        self.store(self.k, self.k_to)
        self.store(self.v, self.v_to)
        self.attention(self.far)
        out_load.wait()
        for c in range(CHUNKS):
            part = pl.ds(c * step, step)
            self.project(self.far + c * step, self.sent_part, c * step, step)
            self.across(self.sent_part.at[part], self.got_part.at[part], CHUNKS + c)
        self.attention(self.base)
        self.store(self.o, self.o_to)
        self.project(self.base, self.own_part, 0, self.rows)
        g_load.wait()
        down_load.wait()
        self.hidden_grad(self.base, self.rows)
        self.arrived(self.g.at[rows_at(self.far, self.rows)], 2 * CHUNKS)
        self.store(self.g, self.g_to)
        self.hidden_grad(self.far, self.rows)
        self.squares[...] = jnp.zeros_like(self.squares)
        for c in range(CHUNKS):
            self.arrived(self.got_part.at[pl.ds(c * step, step)], CHUNKS + c)
            self.norm2(c * step)
            mine = self.h2.at[rows_at(self.base + c * step, step)]
            self.across(mine, mine, 2 * CHUNKS + 1 + c)
        self.store(self.x1, self.x1_to)
        self.attn_squares[...] = jnp.sum(self.squares[...], axis=0, keepdims=True)
        gate_load.wait()
        up_load.wait()
        self.feed(self.base, self.rows)
        self.store_rows(self.base, self.rows)
        for c in range(CHUNKS):
            self.arrived(self.h2.at[rows_at(self.far + c * step, step)], 2 * CHUNKS + 1 + c)
            self.feed(self.far + c * step, step)
            self.store_rows(self.far + c * step, step)
        for when, wait in self.m.left:
            guarded(when, wait)

    def tables(self):
        total = self.starts.shape[0]
        row = lax.broadcasted_iota(jnp.int32, (total, 1), 0)
        first = jnp.zeros((total, 1), jnp.int32)
        end = jnp.int32(0)
        for j in range(self.lengths.shape[1]):
            first = jnp.where(row >= end, end, first)
            end = end + self.lengths[0, j]
        self.starts[...] = first
        angles = (row - first).astype(jnp.float32) * self.inverse[...]
        self.cosines[...] = jnp.cos(angles)
        half = lax.broadcasted_iota(jnp.int32, (total, HD), 1) < HD // 2
        sines = jnp.sin(angles)
        self.sines[...] = jnp.where(half, sines, -sines)

    def norm1(self, source, source_row, row, count):
        def body(i, step):
            x = source[rows_at(source_row + i, step), :].astype(jnp.float32)
            self.h1[rows_at(row + i, step), :] = (x * row_scale(x) * self.gain1[...].reshape(1, -1)).astype(jnp.bfloat16)

        self.tiles(0, count, 32, body)

    def qkv(self, row, count):
        here = rows_at(row, count)
        values = self.h1[here, :]
        for part in range(3):
            cut = slice(part * 512, (part + 1) * 512)
            self.lin[0:count, cut] = product(values, self.w_qkv[:, cut])
        cosines, sines = self.cosines[here, :], -self.sines[here, :]
        for target, first in ((self.q, 0), (self.k, 768)):
            for head in range(target.shape[1] // HD):
                linear = self.lin[0:count, first + head * HD : first + (head + 1) * HD]
                turned = turn_back(linear, cosines, sines)
                target[here, head * HD : (head + 1) * HD] = turned.astype(jnp.bfloat16)
        self.v[here, :] = self.lin[0:count, 1152:1536].astype(jnp.bfloat16)

    def attention(self, row):
        count, total = self.rows, self.q.shape[0]
        here = rows_at(row, count)
        column = lax.broadcasted_iota(jnp.int32, (count, total), 1)
        own = lax.broadcasted_iota(jnp.int32, (count, total), 0) + row
        allowed = (column <= own) & (column >= self.starts[here, :])
        for key_head in range(self.k.shape[1] // HD):
            c = key_head * HD
            keys, values = self.k[:, c : c + HD], self.v[:, c : c + HD]
            for head in (2 * key_head, 2 * key_head + 1):
                h = head * HD
                raw = nt(self.q[here, h : h + HD], keys) * HD ** (-0.5)
                masked = jnp.where(allowed, raw, masked_score)
                exponent = jnp.exp(masked - jnp.max(masked, axis=1, keepdims=True))
                weights = exponent / jnp.sum(exponent, axis=1, keepdims=True)
                out = product(weights.astype(jnp.bfloat16), values)
                self.o[here, h : h + HD] = out.astype(jnp.bfloat16)

    def project(self, row, target, target_row, count):
        values = self.o[rows_at(row, count), :]
        for part in range(3):
            cut = slice(part * 512, (part + 1) * 512)
            target[target_row : target_row + count, cut] = product(values, self.w_out[:, cut]).astype(target.dtype)

    def hidden_grad(self, row, count):
        here = rows_at(row, count)

        def body(i, _):
            cut = pl.ds(pl.multiple_of(i * 256, 256), 256)
            self.d_hid[here, cut] = nt(self.g[here, :], self.w_down[cut, :])
            return 0

        lax.fori_loop(0, self.w_down.shape[0] // 256, body, 0)

    def norm2(self, start):
        def body(i, step):
            here = rows_at(i, step)
            attn = self.own_part[here, :] + self.got_part[here, :].astype(jnp.float32)
            self.squares[...] += eight(attn * attn)
            x1 = self.x[here, :].astype(jnp.float32) + attn
            self.x1[here, :] = x1
            self.h2[rows_at(self.base + i, step), :] = (x1 * row_scale(x1) * self.gain2[...].reshape(1, -1)).astype(jnp.bfloat16)

        self.tiles(start, self.step, 16, body)

    def feed(self, row, count):
        here = rows_at(row, count)

        def body(i, _):
            cut = pl.ds(pl.multiple_of(i * 256, 256), 256)
            values = self.h2[here, :]
            gate = product(values, self.w_gate[:, cut])
            up = product(values, self.w_up[:, cut])
            d_hid = self.d_hid[here, cut]
            sig = 1.0 / (1.0 + jnp.exp(-gate))
            self.hid[here, cut] = (gate * sig * up).astype(jnp.bfloat16)
            self.d_gate[here, cut] = (d_hid * up * sig * (1.0 + gate * (1.0 - sig))).astype(jnp.bfloat16)
            self.d_up[here, cut] = (d_hid * gate * sig).astype(jnp.bfloat16)
            return 0

        lax.fori_loop(0, self.w_gate.shape[1] // 256, body, 0)


def forward_kernel(*refs):
    names = FORWARD_INPUTS + FORWARD_RESULTS + FORWARD_PLAIN
    Forward(dict(zip(names, refs))).run()


def forward(**given):
    vmem = pl.BlockSpec(memory_space=pltpu.VMEM)
    hbm = pl.BlockSpec(memory_space=pl.ANY)
    smem = pl.BlockSpec(memory_space=pltpu.SMEM)
    low, full = jnp.bfloat16, jnp.float32
    own, width = given["x"].shape
    total = 2 * own
    units = given["gate_w"].shape[1]
    q_cols, k_cols = given["q_w"].shape[1], given["k_w"].shape[1]
    shapes = dict(
        hid_to=((total, units), low), g_to=((total, width), low), h2_to=((total, width), low),
        d_gate_to=((total, units), low), d_up_to=((total, units), low), o_to=((total, q_cols), low),
        h1_to=((total, width), low), q_to=((total, q_cols), low), k_to=((total, k_cols), low),
        v_to=((total, k_cols), low), x1_to=((own, width), full), cosines=((total, HD), full), sines=((total, HD), full),
        starts=((total, 1), jnp.int32), attn_squares=((1, width), full),
    )
    plain = dict(
        x_in=((own, width), low), w_qkv=((width, q_cols + 2 * k_cols), low), w_out=((q_cols, width), low),
        w_gate=((width, units), low), w_up=((width, units), low), w_down=((units, width), low),
        g=((total, width), low), h1=((total, width), low), lin=((own, q_cols + 2 * k_cols), full),
        q=((total, q_cols), low), k=((total, k_cols), low), v=((total, k_cols), low), o=((total, q_cols), low),
        own_part=((own, width), full), sent_part=((own, width), low), got_part=((own, width), low),
        x1=((own, width), full), h2=((total, width), low), d_hid=((total, units), full), hid=((total, units), low),
        d_gate=((total, units), low), d_up=((total, units), low), squares=((8, width), full),
    )
    scratch = [pltpu.VMEM(*plain[name]) for name in FORWARD_PLAIN if name in plain]
    copies = 3 * CHUNKS + 1
    scratch += [pltpu.SemaphoreType.DMA((n,)) for n in (copies, copies, 8, 24)]
    spaces = dict.fromkeys(("q_w", "k_w", "v_w", "out_w", "gate_w", "up_w", "down_w", "g_own"), hbm)
    spaces["lengths"] = smem
    out = pl.pallas_call(
        forward_kernel,
        out_shape=[jax.ShapeDtypeStruct(*shapes[name]) for name in FORWARD_RESULTS],
        in_specs=[spaces.get(name, vmem) for name in FORWARD_INPUTS],
        out_specs=[hbm if name.endswith("_to") else vmem for name in FORWARD_RESULTS],
        scratch_shapes=scratch,
        compiler_params=pltpu.CompilerParams(
            collective_id=1, has_side_effects=True, vmem_limit_bytes=62 << 20
        ),
        cost_estimate=pl.CostEstimate(flops=26 * 10**9, bytes_accessed=60 << 20, transcendentals=0),
        name="forward",
    )(*(given[name] for name in FORWARD_INPUTS))
    return dict(zip(FORWARD_RESULTS, out))


def results_kernel(
    down, gate, up, o, qkv, tokens_in, layer_in, small,
    layer_out, tokens_out, gain1_out, q_out, k_out, v_out, o_out, gain2_out, gate_out, up_out, down_out, rms_out,
    taken, made, tokens_held, layer_held, in_sems, out_sems, whole_sems, *, tokens,
):
    held = ((tokens_in, tokens_held, tokens_out), (layer_in, layer_held, layer_out))
    inward = [pltpu.make_async_copy(a, b, whole_sems.at[i]) for i, (a, b, _) in enumerate(held)]
    outward = [pltpu.make_async_copy(b, c, whole_sems.at[i]) for i, (_, b, c) in enumerate(held)]
    for copy in inward:
        copy.start()
    q_cols, k_cols = q_out.shape[1], k_out.shape[1]
    tile = taken.shape[1]
    work = []
    for source, targets in (
        (down, ((down_out, 0),)),
        (gate, ((gate_out, 0),)),
        (up, ((up_out, 0),)),
        (qkv, ((q_out, 0), (k_out, q_cols), (v_out, q_cols + k_cols))),
        (o, ((o_out, 0),)),
    ):
        work += [(source, targets, row) for row in range(0, source.shape[0], tile)]
    slots = taken.shape[0]

    def take(i):
        source, _, row = work[i]
        return pltpu.make_async_copy(
            source.at[pl.ds(row, tile)], taken.at[i % slots, :, pl.ds(0, source.shape[1])], in_sems.at[i % slots]
        )

    def give(i):
        _, targets, row = work[i]
        return [
            pltpu.make_async_copy(
                made.at[i % slots, :, pl.ds(first, target.shape[1])],
                target.at[pl.ds(row, tile)],
                out_sems.at[i % slots, j],
            )
            for j, (target, first) in enumerate(targets)
        ]

    for i in range(min(slots - 1, len(work))):
        take(i).start()
    for i in range(len(work)):
        if i + slots - 1 < len(work):
            take(i + slots - 1).start()
        take(i).wait()
        if i >= slots:
            for copy in give(i - slots):
                copy.wait()
        columns = work[i][0].shape[1]

        def one(j, _, slot=i % slots, columns=columns):
            here = rows_at(j * 32, 32)
            made[slot, here, 0:columns] = taken[slot, here, 0:columns].astype(jnp.float32)
            return 0

        lax.fori_loop(0, tile // 32, one, 0)
        for copy in give(i):
            copy.start()
    for i in range(2):
        inward[i].wait()
        outward[i].start()
    gain1_out[...] = small[0, :]
    gain2_out[...] = small[1, :]
    lane = lax.broadcasted_iota(jnp.int32, (1, 3), 1)
    sums = [jnp.sum(small[row : row + 1, :], axis=1, keepdims=True) for row in (2, 4, 3)]
    squares = jnp.where(lane == 0, sums[0], jnp.where(lane == 1, sums[1], sums[2]))
    rms_out[...] = jnp.sqrt(squares / tokens)
    for i in range(max(0, len(work) - slots), len(work)):
        for copy in give(i):
            copy.wait()
    for copy in outward:
        copy.wait()


def results(sums, tokens_grad, layer_out, small, q_cols, k_cols, tokens):
    vmem = pl.BlockSpec(memory_space=pltpu.VMEM)
    hbm = pl.BlockSpec(memory_space=pl.ANY)
    full = jnp.float32
    down, gate, up, o, qkv = sums
    width = small.shape[1]
    rows = qkv.shape[0]
    shapes = (
        (layer_out.shape, layer_out.dtype, hbm), (tokens_grad.shape, full, hbm), ((width,), full, vmem),
        ((rows, q_cols), full, hbm), ((rows, k_cols), full, hbm), ((rows, k_cols), full, hbm),
        (o.shape, full, hbm), ((width,), full, vmem), (gate.shape, full, hbm), (up.shape, full, hbm),
        (down.shape, full, hbm), ((1, 3), full, vmem),
    )
    slots, tile = 8, 256
    columns = max(part.shape[1] for part in sums)
    out = pl.pallas_call(
        partial(results_kernel, tokens=tokens),
        out_shape=[jax.ShapeDtypeStruct(shape, dtype) for shape, dtype, _ in shapes],
        in_specs=[hbm] * 7 + [vmem],
        out_specs=[space for _, _, space in shapes],
        scratch_shapes=[
            pltpu.VMEM((slots, tile, columns), jnp.bfloat16),
            pltpu.VMEM((slots, tile, columns), full),
            pltpu.VMEM(tokens_grad.shape, full),
            pltpu.VMEM(layer_out.shape, layer_out.dtype),
            pltpu.SemaphoreType.DMA((slots,)),
            pltpu.SemaphoreType.DMA((slots, 3)),
            pltpu.SemaphoreType.DMA((2,)),
        ],
        compiler_params=pltpu.CompilerParams(vmem_limit_bytes=62 << 20),
        cost_estimate=pl.CostEstimate(flops=0, bytes_accessed=78 * 10**6, transcendentals=0),
        name="results",
    )(*sums, tokens_grad, layer_out, small)
    return tuple(part.reshape(-1) if part.shape[0] == 1 else part for part in out)


def dp_sum(terms):
    low = lax.psum(tuple(term.astype(jnp.bfloat16) for term in terms), "dp")
    return tuple(term.astype(jnp.float32) for term in low)


def low_scatter(partial):
    return lax.psum_scatter(
        partial.astype(jnp.bfloat16), "tensor", scatter_dimension=0, tiled=True
    ).astype(jnp.float32)


def body(
    tokens,
    lengths,
    first_gain,
    query_weight,
    key_weight,
    value_weight,
    output_weight,
    second_gain,
    gate_weight,
    up_weight,
    down_weight,
    out_cotangent,
):
    inputs = tokens.astype(jnp.float32)
    normed1, inv_first = norm_rows(inputs, first_gain)
    normed1 = normed1.astype(jnp.bfloat16)
    full_first = lax.all_gather(normed1, "tensor", axis=0, tiled=True)
    total_rows = full_first.shape[0]
    places, segment, cosine_table, sine_table = tables(lengths[0], total_rows, HD // 2)
    kv_heads = key_weight.shape[1] // HD
    groups = query_weight.shape[1] // key_weight.shape[1]
    query = rotate(product(full_first, query_weight), cosine_table, sine_table, 1.0).astype(
        jnp.bfloat16
    )
    keys = rotate(product(full_first, key_weight), cosine_table, sine_table, 1.0).astype(
        jnp.bfloat16
    )
    values = product(full_first, value_weight).astype(jnp.bfloat16)
    block_rows = min(block_limit, total_rows)
    block_count = total_rows // block_rows
    query_blocks = query.reshape(block_count, block_rows, kv_heads, groups, HD)
    seg_blocks = segment.reshape(block_count, block_rows)
    place_blocks = places.reshape(block_count, block_rows)
    key_three = keys.reshape(total_rows, kv_heads, HD)
    value_three = values.reshape(total_rows, kv_heads, HD)
    factor = HD ** (-0.5)

    def scores(query_block, seg_block, place_block):
        raw = (
            jnp.einsum("qcgd,kcd->cgqk", query_block, key_three, preferred_element_type=jnp.float32)
            * factor
        )
        allowed = (seg_block[:, None] == segment[None, :]) & (
            place_block[:, None] >= places[None, :]
        )
        return (jnp.where(allowed[None, None], raw, masked_score), allowed)

    def forward_block(piece_set):
        query_block, seg_block, place_block = piece_set
        masked, allowed = scores(query_block, seg_block, place_block)
        highest = jnp.max(masked, axis=-1, keepdims=True)
        exponent = jnp.exp(masked - highest)
        denominator = jnp.sum(exponent, axis=-1, keepdims=True)
        weights = exponent / denominator
        output = jnp.einsum(
            "cgqk,kcd->qcgd",
            weights.astype(jnp.bfloat16),
            value_three,
            preferred_element_type=jnp.float32,
        )
        stored = (highest + jnp.log(denominator))[..., 0]
        return (output.reshape(block_rows, -1), stored)

    out_blocks, kept_blocks = lax.map(forward_block, (query_blocks, seg_blocks, place_blocks))
    attended = out_blocks.reshape(total_rows, -1).astype(jnp.bfloat16)
    attn_rows = low_scatter(product(attended, output_weight))
    middle = inputs + attn_rows
    normed2, inv_second = norm_rows(middle, second_gain)
    normed2 = normed2.astype(jnp.bfloat16)
    full_second = lax.all_gather(normed2, "tensor", axis=0, tiled=True)
    gate_value = product(full_second, gate_weight)
    upward = product(full_second, up_weight)
    gate_sig = jax.nn.sigmoid(gate_value)
    hidden = (gate_value * gate_sig * upward).astype(jnp.bfloat16)
    mlp_rows = low_scatter(product(hidden, down_weight))
    layer_out = middle + mlp_rows
    squares = jnp.stack(
        [
            jnp.sum(layer_out * layer_out),
            jnp.sum(attn_rows * attn_rows),
            jnp.sum(mlp_rows * mlp_rows),
        ]
    )
    grad_full = lax.all_gather(out_cotangent, "tensor", axis=0, tiled=True)
    grad_hidden = times_cols(grad_full, down_weight)
    down_g = times_rows(hidden, grad_full)
    gate_slope = gate_sig * (1.0 + gate_value * (1.0 - gate_sig))
    grad_gate = (grad_hidden * upward * gate_slope).astype(jnp.bfloat16)
    grad_up = (grad_hidden * gate_value * gate_sig).astype(jnp.bfloat16)
    gate_g = times_rows(full_second, grad_gate)
    up_g = times_rows(full_second, grad_up)
    gate_g, up_g, down_g = dp_sum((gate_g, up_g, down_g))
    grad_normed2 = low_scatter(
        times_cols(grad_gate, gate_weight) + times_cols(grad_up, up_weight)
    )
    second_rows, grad_mid_norm = norm_back(middle, inv_second, second_gain, grad_normed2)
    grad_middle = out_cotangent.astype(jnp.float32) + grad_mid_norm
    grad_attn_full = lax.all_gather(grad_middle.astype(jnp.bfloat16), "tensor", axis=0, tiled=True)
    output_g = times_rows(attended, grad_attn_full)
    grad_out = times_cols(grad_attn_full, output_weight).astype(jnp.bfloat16)
    grad_blocks = grad_out.reshape(block_count, block_rows, kv_heads, groups, HD)

    def backward_block(running, piece_set):
        key_acc, value_acc = running
        query_block, seg_block, place_block, grad_block, stored = piece_set
        masked, allowed = scores(query_block, seg_block, place_block)
        weights = jnp.where(allowed[None, None], jnp.exp(masked - stored[..., None]), 0.0)
        grad_weights = jnp.einsum(
            "qcgd,kcd->cgqk", grad_block, value_three, preferred_element_type=jnp.float32
        )
        row_inner = jnp.sum(weights * grad_weights, axis=-1, keepdims=True)
        grad_scores = (weights * (grad_weights - row_inner)).astype(jnp.bfloat16)
        grad_query = (
            jnp.einsum("cgqk,kcd->qcgd", grad_scores, key_three, preferred_element_type=jnp.float32)
            * factor
        )
        key_acc = (
            key_acc
            + jnp.einsum(
                "cgqk,qcgd->kcd", grad_scores, query_block, preferred_element_type=jnp.float32
            )
            * factor
        )
        value_acc = value_acc + jnp.einsum(
            "cgqk,qcgd->kcd",
            weights.astype(jnp.bfloat16),
            grad_block,
            preferred_element_type=jnp.float32,
        )
        return ((key_acc, value_acc), grad_query.reshape(block_rows, -1))

    zeros_kv = jnp.zeros((total_rows, kv_heads, HD), jnp.float32)
    (key_rot_grad, value_acc_grad), query_rot_grad = lax.scan(
        backward_block,
        (zeros_kv, zeros_kv),
        (query_blocks, seg_blocks, place_blocks, grad_blocks, kept_blocks),
    )
    query_lin = rotate(
        query_rot_grad.reshape(total_rows, -1), cosine_table, sine_table, -1.0
    ).astype(jnp.bfloat16)
    key_lin = rotate(key_rot_grad.reshape(total_rows, -1), cosine_table, sine_table, -1.0).astype(
        jnp.bfloat16
    )
    value_lin = value_acc_grad.reshape(total_rows, -1).astype(jnp.bfloat16)
    query_g = times_rows(full_first, query_lin)
    key_g = times_rows(full_first, key_lin)
    value_g = times_rows(full_first, value_lin)
    grad_normed1 = low_scatter(
        times_cols(query_lin, query_weight)
        + times_cols(key_lin, key_weight)
        + times_cols(value_lin, value_weight)
    )
    first_rows, grad_in_norm = norm_back(inputs, inv_first, first_gain, grad_normed1)
    tokens_grad = grad_middle + grad_in_norm
    gain_rows = jnp.stack([first_rows, second_rows])
    query_g, key_g, value_g, output_g = dp_sum((query_g, key_g, value_g, output_g))
    gain_rows, squares = lax.psum((gain_rows, squares), ("dp", "tensor"))
    rms_values = jnp.sqrt(squares / (total_rows * lax.axis_size("dp")))
    return (
        layer_out.astype(jnp.bfloat16),
        tokens_grad,
        gain_rows[0],
        query_g,
        key_g,
        value_g,
        output_g,
        gain_rows[1],
        gate_g,
        up_g,
        down_g,
        rms_values,
    )


def fused_body(
    tokens,
    lengths,
    first_gain,
    query_weight,
    key_weight,
    value_weight,
    output_weight,
    second_gain,
    gate_weight,
    up_weight,
    down_weight,
    out_cotangent,
):
    half_size = HD // 2
    inverse = (rope_base ** (-2.0 * np.arange(half_size) / (2 * half_size))).astype(np.float32)
    made = forward(
        x=tokens,
        lengths=lengths,
        gain1=first_gain,
        gain2=second_gain,
        inverse=jnp.asarray(np.concatenate([inverse, inverse])[None]),
        q_w=query_weight,
        k_w=key_weight,
        v_w=value_weight,
        out_w=output_weight,
        gate_w=gate_weight,
        up_w=up_weight,
        down_w=down_weight,
        g_own=out_cotangent,
    )
    *sums, tokens_grad, layer_out, small = backward(
        **{name + "_hbm": made[name + "_to"] for name in ("hid", "g", "h2", "d_gate", "d_up", "o", "h1")},
        **{name + "_hbm": made[name + "_to"] for name in ("q", "k", "v", "x1")},
        **{name + "_hbm": made[name] for name in ("cosines", "sines", "starts")},
        x_hbm=tokens,
        out_w=output_weight,
        q_w=query_weight,
        k_w=key_weight,
        v_w=value_weight,
        gate_w=gate_weight,
        up_w=up_weight,
        down_w=down_weight,
        gain1=first_gain,
        gain2=second_gain,
        attn_squares=made["attn_squares"],
    )
    return results(
        sums, tokens_grad, layer_out, small, query_weight.shape[1], key_weight.shape[1],
        2 * tokens.shape[0] * lax.axis_size("dp"),
    )


def solution(mesh):
    in_specs = (
        P(("dp", "tensor"), None),
        P("dp", None),
        P(),
        P(None, "tensor"),
        P(None, "tensor"),
        P(None, "tensor"),
        P("tensor", None),
        P(),
        P(None, "tensor"),
        P(None, "tensor"),
        P("tensor", None),
        P(("dp", "tensor"), None),
    )
    out_specs = (
        P(("dp", "tensor"), None),
        P(("dp", "tensor"), None),
        P(),
        P(None, "tensor"),
        P(None, "tensor"),
        P(None, "tensor"),
        P("tensor", None),
        P(),
        P(None, "tensor"),
        P(None, "tensor"),
        P("tensor", None),
        P(),
    )
    fused = dict(mesh.shape) == {"dp": 16, "tensor": 2}
    chosen = fused_body if fused else body
    return jax.shard_map(chosen, mesh=mesh, in_specs=in_specs, out_specs=out_specs, check_vma=False)
```

```python
from functools import partial

import jax
import jax.numpy as jnp
import numpy as np
from jax import lax
from jax.experimental import pallas as pl
from jax.experimental.pallas import tpu as pltpu
from jax.sharding import PartitionSpec as P

HD = 96


epsilon = 1e-05
rope_base = 10000.0
masked_score = -1e30
block_limit = 512


def product(left_side, right_side):
    return jnp.dot(left_side, right_side, preferred_element_type=jnp.float32)


def times_rows(left_side, right_side):
    return lax.dot_general(
        left_side, right_side, (((0,), (0,)), ((), ())), preferred_element_type=jnp.float32
    )


def times_cols(left_side, right_side):
    return lax.dot_general(
        left_side, right_side, (((1,), (1,)), ((), ())), preferred_element_type=jnp.float32
    )


def tables(lens_row, total_rows, half_size):
    count = lens_row.shape[0]
    earlier = jnp.arange(count)[:, None] <= jnp.arange(count)[None, :]
    seq_ends = jnp.sum(jnp.where(earlier, lens_row[:, None], 0), axis=0, dtype=jnp.int32)
    starts = seq_ends - lens_row
    places = jnp.arange(total_rows, dtype=jnp.int32)
    segment = jnp.sum(
        (places[:, None] >= seq_ends[None, :]).astype(jnp.int32), axis=1, dtype=jnp.int32
    )
    member = segment[:, None] == jnp.arange(lens_row.shape[0], dtype=jnp.int32)[None, :]
    position = places - jnp.sum(jnp.where(member, starts[None, :], 0), axis=1, dtype=jnp.int32)
    inverse = rope_base ** (-2.0 * jnp.arange(half_size, dtype=jnp.float32) / (2 * half_size))
    angles = position.astype(jnp.float32)[:, None] * inverse[None, :]
    return (places, segment, jnp.cos(angles), jnp.sin(angles))


def rotate(values, cosine_table, sine_table, direction):
    total_rows = values.shape[0]
    half_size = cosine_table.shape[1]
    shaped = values.reshape(total_rows, -1, 2 * half_size)
    first_half = shaped[..., :half_size]
    second = shaped[..., half_size:]
    cos_b = cosine_table[:, None, :]
    sin_b = sine_table[:, None, :] * direction
    turned = jnp.concatenate(
        [first_half * cos_b - second * sin_b, second * cos_b + first_half * sin_b], axis=-1
    )
    return turned.reshape(total_rows, -1)


def norm_rows(values, gain):
    inv_rms = lax.rsqrt(jnp.mean(values * values, axis=-1, keepdims=True) + epsilon)
    return (values * inv_rms * gain, inv_rms)


def norm_back(values, inv_rms, gain, upstream):
    scaled = upstream * gain
    row_inner = jnp.mean(scaled * values, axis=-1, keepdims=True)
    gain_rows = jnp.sum(upstream * values * inv_rms, axis=0)
    return (gain_rows, inv_rms * (scaled - values * inv_rms * inv_rms * row_inner))


ORDER = (
    1000, 1, 2, 101, 203, 202, 102, 1001, 203, 205, 1002, 203, 1003, 205, 202, 203, 203, 0, 205,
    203, 204, 100, 202, 203, 205, 1004, 201, 202, 205, 1011, 203, 205, 202, 1012, 201, 205, 200,
    203, 1005, 204, 201, 1006, 202, 1007, 204, 205, 201, 201, 210, 3, 202, 200, 204, 1008, 205, 210,
    201, 204, 200, 103, 206, 210, 201, 207, 1009, 4, 200, 204, 1010, 210, 201, 210, 206, 104, 210,
    204, 1013, 206, 209, 207, 210, 211, 200, 206, 201, 208, 205, 209, 207, 1014, 210, 209, 211, 202,
    200, 204, 1015, 208, 210, 211, 206, 209, 201, 209, 200, 203, 208, 207, 211, 208, 207, 209, 206,
    211, 210, 208, 206, 209, 207, 1016, 1017, 210, 203, 211, 208, 1018, 206, 201, 209, 200, 211,
    207, 202, 206, 204, 208, 1019, 209, 211, 200, 208, 207, 1020, 205, 209, 209, 208, 207, 211, 207,
    207,
)


MESH = pl.DeviceIdType.MESH
LINE = 4
DOWN, GATE, UP, OUT, QKV = range(5)
UNITS = (
    (2048, 1536, 256, 0, 0),
    (1536, 2048, 256, 1, 0),
    (1536, 2048, 256, 2, 0),
    (768, 1536, 128, 3, 0),
    (1536, 1536, 256, 4, 0),
)
BLOCKS = (
    (0, True, 0, 640),
    (0, False, 640, 384),
    (1, True, 0, 512),
    (1, False, 512, 256),
    (2, True, 0, 384),
    (2, False, 384, 256),
    (3, True, 0, 256),
    (3, False, 256, 128),
    (4, True, 0, 256),
    (4, False, 256, 256),
    (2, False, 640, 128),
    (4, True, 512, 256),
)
WHOLE = tuple(
    (sum(unit[0] for unit in UNITS if unit[3] == kind), next(unit[1] for unit in UNITS if unit[3] == kind))
    for kind in range(5)
)
COPIES = 20
TILE_BASE = len(BLOCKS) * COPIES
TILES = tuple(rows // 2 // tile for rows, _, tile, *_ in UNITS)
SMALL_BASE = TILE_BASE + sum(TILES)
SMALL_STEPS = 5
Y_BASE = SMALL_BASE + SMALL_STEPS
N_SEMS = Y_BASE + 4


def rows_at(start, size):
    return pl.ds(pl.multiple_of(start, 16), size)


class Place:
    def __init__(self):
        dp = lax.axis_index("dp")
        self.dp = dp
        self.y = lax.axis_index("tensor")
        self.core = lax.rem(dp, 2)
        self.x = lax.rem(dp // 2, 2)
        self.z = dp // 4

    def at(self, z, x, core, y):
        return ((z * 2 + x) * 2 + core, y)

    def other_core(self):
        return self.at(self.z, self.x, 1 - self.core, self.y)

    def other_x(self):
        return self.at(self.z, 1 - self.x, self.core, self.y)

    def other_y(self):
        return self.at(self.z, self.x, self.core, 1 - self.y)

    def up(self):
        return self.at(self.z + 1, self.x, self.core, self.y)

    def down(self):
        return self.at(self.z - 1, self.x, self.core, self.y)

    def pair_z(self):
        return self.at(self.z + 1 - 2 * lax.rem(self.z, 2), self.x, self.core, self.y)

    def far_z(self):
        return self.at(lax.rem(self.z + 2, LINE), self.x, self.core, self.y)


class Mover:
    def __init__(self, send_sems, recv_sems):
        self.send_sems = send_sems
        self.recv_sems = recv_sems
        self.left = []

    def copy(self, source, target, index, device):
        return pltpu.make_async_remote_copy(
            src_ref=source,
            dst_ref=target,
            send_sem=self.send_sems.at[index],
            recv_sem=self.recv_sems.at[index],
            device_id=device,
            device_id_type=MESH,
        )

    def start(self, source, target, index, device, when=None):
        copy = self.copy(source, target, index, device)
        guarded(when, copy.start)
        self.left.append((when, copy.wait_send))

    def arrived(self, target, index, device):
        self.copy(target, target, index, device).wait_recv()


def guarded(when, action):
    if when is None:
        action()
    else:
        pl.when(when)(action)


def add_rows(target, target_row, source, source_row, size):
    step = 16

    def one(i, _):
        here = rows_at(target_row + i * step, step)
        there = rows_at(source_row + i * step, step)
        total = target[here, :].astype(jnp.float32) + source[there, :].astype(jnp.float32)
        target[here, :] = total.astype(target.dtype)
        return 0

    lax.fori_loop(0, size // step, one, 0)


def fall_slot(step):
    return 0 if step == 0 else 2 + step


class Block:
    def __init__(self, place, mover, held, across, along, result, base, start, size, half_rows, x_first, first):
        self.p = place
        self.m = mover
        self.held = held
        self.across = across
        self.along = along
        self.result = result
        self.base = base
        self.start = start
        self.size = size
        self.half_rows = half_rows
        self.x_first = x_first
        self.first = first
        self.chunk = size // 8 if x_first else size // 4
        self.origin = start + place.x * (size // 2) if x_first else start

    def part(self, chunk):
        return self.held.at[rows_at(self.origin + chunk * self.chunk, self.chunk)]

    def final(self, row, size):
        return self.result.at[rows_at(self.first + self.p.core * self.half_rows + row, size)]

    def final_part(self, chunk):
        return self.final(self.origin + chunk * self.chunk, self.chunk)

    def keep(self, row, size):
        index = self.base // COPIES
        copy = pltpu.make_async_copy(
            self.held.at[rows_at(row, size)], self.final(row, size), self.m.keep_sems.at[index]
        )
        copy.start()
        self.kept = copy

    def events(self):
        line = [self.line_start, lambda: self.line_add(0), lambda: self.line_add(1), lambda: self.line_add(2)]
        spread = [lambda: self.spread(1), lambda: self.spread(2), lambda: self.spread(3)]
        if self.x_first:
            return [self.x_send, self.x_add] + line[1:] + spread + [self.x_done]
        return line + [self.pair_send, self.pair_add, self.pair_done] + spread + [self.z_done]

    def line_start(self):
        p = self.p
        for step in range(3):
            self.m.start(self.part(3 - step), self.along.at[step], self.base + step, p.up(), p.z == 0)
            self.m.start(self.part(step), self.along.at[fall_slot(step)], self.base + 3 + step, p.down(), p.z == LINE - 1)

    def line_add(self, step):
        p = self.p
        rising = jnp.minimum(p.z + 2 - step, 3)
        falling = jnp.maximum(p.z - 2 + step, 0)
        goes_up = (p.z >= 1) & (p.z <= step + 1)
        goes_down = (p.z <= 2) & (p.z >= 2 - step)

        def take_rising():
            self.m.arrived(self.along.at[step], self.base + step, p.down())
            add_rows(self.held, self.origin + rising * self.chunk, self.along.at[step], 0, self.chunk)

        def take_falling():
            self.m.arrived(self.along.at[fall_slot(step)], self.base + 3 + step, p.up())
            add_rows(self.held, self.origin + falling * self.chunk, self.along.at[fall_slot(step)], 0, self.chunk)

        pl.when(goes_up)(take_rising)
        if step < 2:
            self.m.start(self.part(rising), self.along.at[step + 1], self.base + step + 1, p.up(), goes_up)
        pl.when(goes_down)(take_falling)
        if step < 2:
            self.m.start(self.part(falling), self.along.at[fall_slot(step + 1)], self.base + 4 + step, p.down(), goes_down)
        elif self.x_first:
            self.keep(self.origin + p.z * self.chunk, self.chunk)
            self.own_spread(self.part(p.z))
            self.x_return(self.part(p.z), p.z, None)

    def own_spread(self, source):
        p = self.p
        target = self.final_part(p.z)
        self.m.start(source, target, self.base + 6, p.up(), p.z < 3)
        self.m.start(source, target, self.base + 9, p.down(), p.z > 0)

    def spread(self, distance):
        p = self.p
        below = self.final_part(jnp.maximum(p.z - distance, 0))
        above = self.final_part(jnp.minimum(p.z + distance, 3))

        pl.when(p.z >= distance)(lambda: self.m.arrived(below, self.base + 5 + distance, p.down()))
        if distance < 3:
            self.m.start(below, below, self.base + 6 + distance, p.up(), (p.z >= distance) & (p.z < 3))
        if self.x_first:
            self.x_return(below, jnp.maximum(p.z - distance, 0), p.z >= distance)
        pl.when(p.z <= 3 - distance)(lambda: self.m.arrived(above, self.base + 8 + distance, p.up()))
        if distance < 3:
            self.m.start(above, above, self.base + 9 + distance, p.down(), (p.z <= 3 - distance) & (p.z > 0))
        if self.x_first:
            self.x_return(above, jnp.minimum(p.z + distance, 3), p.z <= 3 - distance)
            if distance == 3:
                self.kept.wait()
                self.give(p.x * (self.size // 2), self.size // 2, 14)

    def x_part(self, which):
        half = self.size // 2
        return self.held.at[rows_at(self.start + which * half, half)]

    def x_send(self):
        self.m.start(self.x_part(1 - self.p.x), self.across, self.base + 12, self.p.other_x())

    def x_add(self):
        self.m.arrived(self.across, self.base + 12, self.p.other_x())
        add_rows(self.held, self.origin, self.across, 0, self.size // 2)
        self.line_start()

    def x_return(self, source, chunk, when):
        self.m.start(source, self.final_part(chunk), self.base + 16 + chunk, self.p.other_x(), when)

    def x_done(self):
        p = self.p
        half = (1 - p.x) * (self.size // 2)
        for chunk in range(4):
            place = self.final(self.start + half + chunk * self.chunk, self.chunk)
            self.m.arrived(place, self.base + 16 + chunk, p.other_x())
        self.give(half, self.size // 2, 15)

    def pair_row(self, which):
        return self.start + self.p.z * self.chunk + which * (self.chunk // 2)

    def pair_send(self):
        half = self.chunk // 2
        source = self.held.at[rows_at(self.pair_row(1 - self.p.x), half)]
        self.m.start(source, self.across, self.base + 12, self.p.other_x())

    def pair_add(self):
        p = self.p
        half = self.chunk // 2
        self.m.arrived(self.across, self.base + 12, p.other_x())
        row = self.pair_row(p.x)
        add_rows(self.held, row, self.across, 0, half)
        self.keep(row, half)
        self.m.start(self.held.at[rows_at(row, half)], self.final(row, half), self.base + 13, p.other_x())

    def pair_done(self):
        p = self.p
        half = self.chunk // 2
        self.m.arrived(self.final(self.pair_row(1 - p.x), half), self.base + 13, p.other_x())
        self.kept.wait()
        self.own_spread(self.final_part(p.z))

    def z_done(self):
        self.give(0, self.size, 14)

    def give(self, offset, size, slot):
        p = self.p
        source = self.final(self.start + offset, size)
        self.m.start(source, source, self.base + slot, p.other_core())
        other = self.result.at[
            rows_at(self.first + (1 - p.core) * self.half_rows + self.start + offset, size)
        ]
        self.m.left.append((None, lambda: self.m.arrived(other, self.base + slot, p.other_core())))


def product_tile(left, right, first, tile, width, part):
    columns = pl.ds(pl.multiple_of(first, 128), tile)
    return lax.dot_general(
        left[:, columns], right[:, part * width : (part + 1) * width],
        (((0,), (0,)), ((), ())), preferred_element_type=jnp.float32,
    )


class Unit:
    def __init__(self, index, place, mover, left, right, held, staged, stage_sems):
        self.index = index
        self.rows, self.columns, self.tile, _, self.first = UNITS[index]
        self.p, self.m = place, mover
        self.left, self.right, self.held = left, right, held
        self.staged, self.stage_sems = staged, stage_sems
        self.base = TILE_BASE + sum(TILES[:index])
        self.width = 512

    def tile_copy(self, i, slot):
        tile = self.tile
        return pltpu.make_async_remote_copy(
            src_ref=self.staged.at[slot, pl.ds(0, tile), pl.ds(0, self.columns)],
            dst_ref=self.held.at[rows_at(i * tile, tile)],
            send_sem=self.stage_sems.at[slot],
            recv_sem=self.m.recv_sems.at[self.base + i],
            device_id=self.p.other_core(),
            device_id_type=MESH,
        )

    def send(self):
        half, tile = self.rows // 2, self.tile

        def one(i, _):
            slot = lax.rem(i, 2)
            pl.when(i >= 2)(lambda: self.tile_copy(i, slot).wait_send())
            first = self.first + (1 - self.p.core) * half + i * tile
            for part in range(self.columns // self.width):
                got = product_tile(self.left, self.right, first, tile, self.width, part)
                self.staged[slot, pl.ds(0, tile), part * self.width : (part + 1) * self.width] = got.astype(
                    jnp.bfloat16
                )
            self.tile_copy(i, slot).start()
            return 0

        lax.fori_loop(0, half // tile, one, 0)
        for slot in range(min(2, half // tile)):
            self.tile_copy(0, slot).wait_send()

    def own(self):
        half, tile = self.rows // 2, self.tile

        def one(i, _):
            self.tile_copy(i, 0).wait_recv()
            first = self.first + self.p.core * half + i * tile
            here = rows_at(i * tile, tile)
            for part in range(self.columns // self.width):
                got = product_tile(self.left, self.right, first, tile, self.width, part)
                cut = slice(part * self.width, (part + 1) * self.width)
                total = got + self.held[here, cut].astype(jnp.float32)
                self.held[here, cut] = total.astype(jnp.bfloat16)
            return 0

        lax.fori_loop(0, half // tile, one, 0)


def row_scale(values):
    return lax.rsqrt(jnp.mean(values * values, axis=-1, keepdims=True) + epsilon)


def eight(values):
    rows, columns = values.shape
    return jnp.sum(values.reshape(rows // 8, 8, columns), axis=0)


def turn_back(values, cosines, sines):
    half = values.shape[1] // 2
    swapped = jnp.concatenate([values[:, half:], values[:, :half]], axis=1)
    return values * cosines + swapped * sines


def nt(left_side, right_side):
    return lax.dot_general(
        left_side, right_side, (((1,), (1,)), ((), ())), preferred_element_type=jnp.float32
    )


def tn(left_side, right_side):
    return lax.dot_general(
        left_side, right_side, (((0,), (0,)), ((), ())), preferred_element_type=jnp.float32
    )


class Layer:
    def __init__(self, place, mover, **refs):
        self.p, self.m = place, mover
        self.__dict__.update(refs)
        self.rows = self.x1.shape[0]
        self.mine = rows_at(place.y * self.rows, self.rows)
        self.theirs = rows_at((1 - place.y) * self.rows, self.rows)

    def load(self, source, target, index):
        copy = pltpu.make_async_copy(source, target, self.local_sems.at[index])
        copy.start()
        return copy

    def begin(self):
        self.waits = {}
        for i, (name, target) in enumerate(LOADED):
            self.waits[target] = self.load(getattr(self, name), getattr(self, target), 16 + i)
        self.waits["out_w"] = self.load(self.out_w, self.wbuf.at[pl.ds(0, 768)], 3)

    def need(self, *targets):
        for target in targets:
            if target in self.waits:
                self.waits.pop(target).wait()

    def stream(self, first, count, fetch, use):
        def go(i):
            for j, (source, target) in enumerate(fetch(i)):
                pltpu.make_async_copy(source, target, self.local_sems.at[8 + 2 * lax.rem(i, 2) + j]).start()

        go(jnp.int32(first))

        def body(i, _):
            pl.when(i + 1 < first + count)(lambda: go(i + 1))
            for j, (source, target) in enumerate(fetch(i)):
                pltpu.make_async_copy(source, target, self.local_sems.at[8 + 2 * lax.rem(i, 2) + j]).wait()
            use(i, lax.rem(i, 2))
            return 0

        lax.fori_loop(first, first + count, body, 0)

    def h2_third(self, third):
        self.need("d_gate", "d_up")
        first, count = 2 * third, 2

        def fetch(i, which):
            source = (self.gate_w, self.up_w)[which].at[rows_at(i * 256, 256)]
            return pltpu.make_async_copy(source, self.staged.at[which], self.local_sems.at[8 + which])

        def use(i, which):
            fetch(i, which).wait()
            cut = pl.ds(pl.multiple_of(i * 256, 256), 256)
            weight, grad = self.staged[which], (self.d_gate, self.d_up)[which]
            theirs, mine = nt(grad[self.theirs, :], weight), nt(grad[self.mine, :], weight)
            if which == 0:
                self.d_x1[:, cut] = theirs
                self.fbuf[:, cut] = mine
            else:
                self.h2_out[:, cut] = (self.d_x1[:, cut] + theirs).astype(jnp.bfloat16)
                self.fbuf[:, cut] += mine
            pl.when(i + 1 < first + count)(lambda: fetch(i + 1, which).start())

        fetch(first, 0).start()
        fetch(first, 1).start()

        def body(i, _):
            use(i, 0)
            use(i, 1)
            return 0

        lax.fori_loop(first, first + count, body, 0)
        if third == 2:
            self.h2_sent = self.m.copy(self.h2_out, self.h2_in, Y_BASE, self.p.other_y())
            self.h2_sent.start()

    def mlp_half(self, half):
        self.need("hid")

        rows, target = ((self.theirs, self.mlp_out), (self.mine, self.own))[half]
        self.fbuf[...] = jnp.zeros_like(self.fbuf)

        def fetch(i):
            return ((self.down_w.at[rows_at(i * 256, 256)], self.staged.at[lax.rem(i, 2), :, pl.ds(0, 1536)]),)

        def use(i, slot):
            cut = pl.ds(pl.multiple_of(i * 256, 256), 256)
            self.fbuf[...] += product(self.hid[rows, cut], self.staged[slot, :, 0:1536])

        self.stream(0, self.down_w.shape[0] // 256, fetch, use)
        target[...] = self.fbuf[...].astype(target.dtype)

    def tiles(self, step, body):
        lax.fori_loop(0, self.rows // step, lambda i, _: (body(i * step, step), 0)[1], 0)

    def middle(self):
        self.need("x1", "g")
        self.m.arrived(self.h2_in, Y_BASE, self.p.other_y())
        self.gains[...] = jnp.zeros_like(self.gains)

        def body(start, step):
            here = rows_at(start, step)
            there = rows_at(self.p.y * self.rows + start, step)
            d = self.fbuf[here, :] + self.h2_in[here, :].astype(jnp.float32)
            x1 = self.x1[here, :]
            inv = row_scale(x1)
            scaled = d * self.gain2[...].reshape(1, -1)
            inner = jnp.mean(scaled * x1, axis=-1, keepdims=True)
            self.gains[1] += eight(d * x1 * inv)
            d_x1 = self.g[there, :].astype(jnp.float32) + inv * (scaled - x1 * inv * inv * inner)
            self.d_x1[here, :] = d_x1
            self.d_attn[there, :] = d_x1.astype(jnp.bfloat16)

        self.tiles(16, body)
        own = self.d_attn.at[self.mine]
        self.m.start(own, own, Y_BASE + 1, self.p.other_y())

    def outward(self):
        self.m.arrived(self.d_attn.at[self.theirs], Y_BASE + 1, self.p.other_y())
        self.need("out_w")
        for part in range(3):
            cut = slice(part * 256, (part + 1) * 256)
            self.d_o[:, cut] = nt(self.d_attn[...], self.wbuf[cut, :]).astype(jnp.bfloat16)
        self.w_loads = [
            self.load(self.q_w, self.wbuf.at[:, pl.ds(0, 768)], 3),
            self.load(self.k_w, self.wbuf.at[:, pl.ds(768, 384)], 4),
            self.load(self.v_w, self.wbuf.at[:, pl.ds(1152, 384)], 5),
        ]

    def attention(self, key_head):
        self.need("q", "k", "v", "cosines", "sines", "starts")
        factor = HD ** (-0.5)
        c = key_head * HD
        keys, values = self.k[:, c : c + HD], self.v[:, c : c + HD]
        block = 256
        d_k = [jnp.zeros((block, HD), jnp.float32)] * 2
        d_v = [jnp.zeros((block, HD), jnp.float32)] * 2
        for head in (2 * key_head, 2 * key_head + 1):
            h = head * HD
            for i in range(2):
                here = slice(i * block, (i + 1) * block)
                n = block * (i + 1)
                query, d_out = self.q[here, h : h + HD], self.d_o[here, h : h + HD]
                column = lax.broadcasted_iota(jnp.int32, (block, n), 1)
                row = lax.broadcasted_iota(jnp.int32, (block, n), 0) + i * block
                allowed = (column <= row) & (column >= self.starts[here, :])
                masked = jnp.where(allowed, nt(query, keys[:n]) * factor, masked_score)
                exponent = jnp.exp(masked - jnp.max(masked, axis=1, keepdims=True))
                weights = exponent / jnp.sum(exponent, axis=1, keepdims=True)
                d_weights = nt(d_out, values[:n])
                inner = jnp.sum(weights * d_weights, axis=1, keepdims=True)
                d_scores = (weights * (d_weights - inner)).astype(jnp.bfloat16)
                low = weights.astype(jnp.bfloat16)
                d_query = jnp.dot(d_scores, keys[:n], preferred_element_type=jnp.float32) * factor
                turned = turn_back(d_query, self.cosines[here, :], self.sines[here, :])
                self.d_qkv[here, h : h + HD] = turned.astype(jnp.bfloat16)
                for j in range(i + 1):
                    cut = slice(j * block, (j + 1) * block)
                    d_k[j] = d_k[j] + tn(d_scores[:, cut], query) * factor
                    d_v[j] = d_v[j] + tn(low[:, cut], d_out)
        for j in range(2):
            cut = slice(j * block, (j + 1) * block)
            turned = turn_back(d_k[j], self.cosines[cut, :], self.sines[cut, :])
            self.d_qkv[cut, 768 + c : 768 + c + HD] = turned.astype(jnp.bfloat16)
            self.d_qkv[cut, 1152 + c : 1152 + c + HD] = d_v[j].astype(jnp.bfloat16)

    def h1_part(self, rows, put):
        def body(i, _):
            cut = pl.ds(pl.multiple_of(i * 256, 256), 256)
            put(cut, nt(self.d_qkv[rows, 0:1536], self.wbuf[cut, :]))
            return 0

        lax.fori_loop(0, 6, body, 0)

    def inward(self):
        for copy in self.w_loads:
            copy.wait()

        self.h2_sent.wait_send()
        self.waits["x"] = self.load(self.x_hbm, self.h2_in, 0)

        def put(cut, got):
            self.h2_out[:, cut] = got.astype(jnp.bfloat16)

        self.h1_part(self.theirs, put)
        self.m.start(self.h2_out, self.h1_in, Y_BASE + 2, self.p.other_y())

    def mlp_send(self):
        self.m.start(self.mlp_out, self.mlp_in, Y_BASE + 3, self.p.other_y())

    def finish(self):
        def put(cut, got):
            self.fbuf[:, cut] = got

        self.waits.pop("x").wait()
        self.h1_part(self.mine, put)
        self.m.arrived(self.h1_in, Y_BASE + 2, self.p.other_y())

        def body(start, step):
            here = rows_at(start, step)
            d = self.fbuf[here, :] + self.h1_in[here, :].astype(jnp.float32)
            x = self.h2_in[here, :].astype(jnp.float32)
            inv = row_scale(x)
            scaled = d * self.gain1[...].reshape(1, -1)
            inner = jnp.mean(scaled * x, axis=-1, keepdims=True)
            self.gains[0] += eight(d * x * inv)
            self.d_x1[here, :] = self.d_x1[here, :] + inv * (scaled - x * inv * inv * inner)

        self.tiles(16, body)
        copy = self.load(self.d_x1, self.tokens_out, 6)
        self.m.left.append((None, copy.wait))

    def layer_end(self):
        self.m.arrived(self.mlp_in, Y_BASE + 3, self.p.other_y())

        def body(start, step):
            here = rows_at(start, step)
            mlp = self.own[here, :].astype(jnp.float32) + self.mlp_in[here, :].astype(jnp.float32)
            out = self.x1[here, :] + mlp
            self.gains[2] += eight(out * out)
            self.gains[3] += eight(mlp * mlp)
            self.own[here, :] = out.astype(jnp.bfloat16)

        self.tiles(16, body)
        copy = self.load(self.own, self.layer_out, 7)
        self.m.left.append((None, copy.wait))
        self.totals[0] = jnp.zeros(self.totals.shape[1:], jnp.float32)
        for row in range(4):
            self.totals[0, row : row + 1, :] = jnp.sum(self.gains[row], axis=0, keepdims=True)
        self.totals[0, 4:5, :] = self.attn_squares[...]


def sum_small(place, mover, total, slots, step):
    device = (place.other_core, place.other_x, place.other_y, place.pair_z, place.far_z)[step]()
    copy = mover.copy(total.at[step], slots.at[step], SMALL_BASE + step, device)
    copy.start()
    copy.wait()
    total[step + 1] = total[step] + slots[step]


INPUTS = (
    "hid_hbm", "g_hbm", "h2_hbm", "d_gate_hbm", "d_up_hbm", "o_hbm", "h1_hbm", "q_hbm", "k_hbm", "v_hbm",
    "out_w", "q_w", "k_w", "v_w", "gate_w", "up_w", "down_w", "x1_hbm", "x_hbm", "cosines_hbm", "sines_hbm",
    "starts_hbm", "gain1", "gain2", "attn_squares",
)
IN_VMEM = ("gain1", "gain2", "attn_squares")
LOADED = (
    ("hid_hbm", "hid"), ("g_hbm", "g"), ("h2_hbm", "hbuf"), ("d_gate_hbm", "d_gate"), ("d_up_hbm", "d_up"),
    ("x1_hbm", "x1"), ("o_hbm", "o"), ("q_hbm", "q"), ("k_hbm", "k"), ("v_hbm", "v"),
    ("cosines_hbm", "cosines"), ("sines_hbm", "sines"), ("starts_hbm", "starts"),
)
RESULTS = ("down_out", "gate_out", "up_out", "o_out", "qkv_out", "tokens_out", "layer_out", "small_out")
PLAIN = (
    "staged", "hid", "hbuf", "own", "h2_in", "d_attn", "d_x1", "wbuf", "d_o", "h1_in", "mlp_in", "h2_out",
    "mlp_out", "fbuf", "gains", "totals", "slots", "g", "d_gate", "d_up", "o", "q", "k", "v", "x1",
    "cosines", "sines", "starts",
    "stage_sems", "send_sems", "recv_sems", "keep_sems", "local_sems",
)


def backward_kernel(*refs):
    n = len(UNITS)
    names = INPUTS + RESULTS
    r = dict(zip(names, refs[: len(names)]))
    rest = refs[len(names) :]
    b = len(BLOCKS)
    held, across, along = rest[:n], rest[n : n + b], rest[n + b : n + 2 * b]
    r.update(zip(PLAIN, rest[n + 2 * b :]))
    r["d_qkv"] = r["hid"]
    place = Place()
    mover = Mover(r["send_sems"], r["recv_sems"])
    mover.keep_sems = r["keep_sems"]
    enter(place)
    layer = Layer(place, mover, **r)
    lefts = (r["hid"], r["hbuf"], r["hbuf"], r["o"], r["hbuf"])
    rights = (r["g"], r["d_gate"], r["d_up"], r["d_attn"], r["d_qkv"])
    results = tuple(r[name] for name in RESULTS[:5])
    units = [
        Unit(i, place, mover, lefts[unit[3]], rights[unit[3]], held[i], r["staged"], r["stage_sems"])
        for i, unit in enumerate(UNITS)
    ]
    steps = []
    for b, (i, x_first, start, size) in enumerate(BLOCKS):
        rows, _, _, kind, first = UNITS[i]
        block = Block(
            place, mover, held[i], across[b], along[b], results[kind], b * COPIES, start, size, rows // 2, x_first,
            first,
        )
        steps.append(block.events())

    def send(i):
        kind, first = UNITS[i][3:]
        layer.need(*((("hid", "g"), ("hbuf", "d_gate"), ("hbuf", "d_up"), ("o",), ())[kind]))
        if kind == QKV and first == 0:
            layer.load(layer.h1_hbm, layer.hbuf, 1).wait()
        units[i].send()

    tasks = [layer.begin]
    tasks += [partial(layer.h2_third, i) for i in range(3)]
    tasks += [layer.middle, layer.outward]
    tasks += [partial(layer.attention, i) for i in range(4)]
    tasks += [layer.inward]
    tasks += [partial(layer.mlp_half, i) for i in range(2)]
    tasks += [layer.mlp_send, layer.finish, layer.layer_end]
    tasks += [partial(sum_small, place, mover, r["totals"], r["slots"], i) for i in range(SMALL_STEPS)]
    for item in ORDER:
        if item < 100:
            send(item)
        elif item < 200:
            units[item - 100].own()
        elif item < 1000:
            steps[item - 200].pop(0)()
        else:
            tasks[item - 1000]()
    r["small_out"][...] = r["totals"][SMALL_STEPS]
    for when, wait in mover.left:
        guarded(when, wait)


def enter(place):
    barrier = pltpu.get_barrier_semaphore()

    def greet(device):
        pl.semaphore_signal(barrier, inc=1, device_id=device, device_id_type=MESH)

    for device in (place.other_core(), place.other_x(), place.other_y(), place.pair_z(), place.far_z()):
        greet(device)
    middle = (place.z == 1) | (place.z == 2)
    pl.when(middle)(lambda: greet(place.at(3 - place.z, place.x, place.core, place.y)))
    pl.semaphore_wait(barrier, 5 + jnp.where(middle, 1, 0))


def backward(**given):
    vmem = pl.BlockSpec(memory_space=pltpu.VMEM)
    hbm = pl.BlockSpec(memory_space=pl.ANY)
    low, full = jnp.bfloat16, jnp.float32
    own_rows, width = given["x1_hbm"].shape
    held = [pltpu.VMEM((rows // 2, columns), low) for rows, columns, *_ in UNITS]
    across, along = [], []
    for i, x_first, _, size in BLOCKS:
        columns = UNITS[i][1]
        across.append(pltpu.VMEM((size // 2 if x_first else size // 8, columns), low))
        along.append(pltpu.VMEM((5, size // 8 if x_first else size // 4, columns), low))
    part = pltpu.VMEM((own_rows, width), low)
    plain = dict(
        staged=pltpu.VMEM((2, 256, 2048), low),
        hid=pltpu.VMEM((512, 2048), low),
        hbuf=pltpu.VMEM((512, width), low),
        own=part,
        h2_in=part,
        d_attn=pltpu.VMEM((512, width), low),
        d_x1=pltpu.VMEM((own_rows, width), full),
        wbuf=pltpu.VMEM((1536, 1536), low),
        d_o=pltpu.VMEM((512, 768), low),
        h1_in=part,
        mlp_in=part,
        h2_out=part,
        mlp_out=part,
        fbuf=pltpu.VMEM((own_rows, width), full),
        gains=pltpu.VMEM((4, 8, width), full),
        totals=pltpu.VMEM((SMALL_STEPS + 1, 8, width), full),
        slots=pltpu.VMEM((SMALL_STEPS, 8, width), full),
        stage_sems=pltpu.SemaphoreType.DMA((2,)),
        send_sems=pltpu.SemaphoreType.DMA((N_SEMS,)),
        recv_sems=pltpu.SemaphoreType.DMA((N_SEMS,)),
        keep_sems=pltpu.SemaphoreType.DMA((len(BLOCKS),)),
        local_sems=pltpu.SemaphoreType.DMA((16 + len(LOADED),)),
    )
    for name, target in LOADED:
        plain.setdefault(target, pltpu.VMEM(given[name].shape, given[name].dtype))
    flops = sum(2 * 512 * rows * columns for rows, columns, *_ in UNITS)
    return pl.pallas_call(
        backward_kernel,
        out_shape=[jax.ShapeDtypeStruct(shape, low) for shape in WHOLE]
        + [
            jax.ShapeDtypeStruct((own_rows, width), full),
            jax.ShapeDtypeStruct((own_rows, width), low),
            jax.ShapeDtypeStruct((8, width), full),
        ],
        in_specs=[vmem if name in IN_VMEM else hbm for name in INPUTS],
        out_specs=[hbm] * 7 + [vmem],
        scratch_shapes=held + across + along + [plain[name] for name in PLAIN],
        compiler_params=pltpu.CompilerParams(
            collective_id=0, has_side_effects=True, vmem_limit_bytes=62 << 20
        ),
        cost_estimate=pl.CostEstimate(flops=flops, bytes_accessed=80 << 20, transcendentals=0),
        name="backward",
    )(*(given[name] for name in INPUTS))


FORWARD_INPUTS = (
    "x", "lengths", "gain1", "gain2", "inverse", "q_w", "k_w", "v_w", "out_w", "gate_w", "up_w", "down_w", "g_own",
)
FORWARD_RESULTS = (
    "hid_to", "g_to", "h2_to", "d_gate_to", "d_up_to", "o_to", "h1_to", "q_to", "k_to", "v_to", "x1_to",
    "cosines", "sines", "starts", "attn_squares",
)
FORWARD_PLAIN = (
    "x_in", "w_qkv", "w_out", "w_gate", "w_up", "w_down", "g", "h1", "lin", "q", "k", "v", "o", "own_part",
    "sent_part", "got_part", "x1", "h2", "d_hid", "hid", "d_gate", "d_up", "squares",
    "send_sems", "recv_sems", "load_sems", "store_sems",
)
CHUNKS = 2


class Forward:
    def __init__(self, refs):
        self.__dict__.update(refs)
        self.p = Place()
        self.m = Mover(self.send_sems, self.recv_sems)
        self.rows = self.x.shape[0]
        self.step = self.rows // CHUNKS
        self.base = self.p.y * self.rows
        self.far = (1 - self.p.y) * self.rows
        self.stores = 0

    def load(self, source, target, index):
        copy = pltpu.make_async_copy(source, target, self.load_sems.at[index])
        copy.start()
        return copy

    def store(self, source, target):
        copy = pltpu.make_async_copy(source, target, self.store_sems.at[self.stores])
        self.stores += 1
        copy.start()
        self.m.left.append((None, copy.wait))

    def store_rows(self, row, count):
        here = rows_at(row, count)
        for name in ("h2", "hid", "d_gate", "d_up"):
            self.store(getattr(self, name).at[here], getattr(self, name + "_to").at[here])

    def across(self, source, target, index):
        self.m.start(source, target, index, self.p.other_y())

    def arrived(self, target, index):
        self.m.arrived(target, index, self.p.other_y())

    def tiles(self, first, count, step, body):
        lax.fori_loop(0, count // step, lambda i, _: (body(first + i * step, step), 0)[1], 0)

    def run(self):
        step = self.step
        barrier = pltpu.get_barrier_semaphore()
        pl.semaphore_signal(barrier, inc=1, device_id=self.p.other_y(), device_id_type=MESH)
        pl.semaphore_wait(barrier, 1)
        for c in range(CHUNKS):
            part = pl.ds(c * step, step)
            self.across(self.x.at[part], self.x_in.at[part], c)
        self.across(self.g_own, self.g.at[rows_at(self.base, self.rows)], 2 * CHUNKS)
        qkv_loads = [
            self.load(self.q_w, self.w_qkv.at[:, pl.ds(0, 768)], 0),
            self.load(self.k_w, self.w_qkv.at[:, pl.ds(768, 384)], 1),
            self.load(self.v_w, self.w_qkv.at[:, pl.ds(1152, 384)], 2),
        ]
        g_load = self.load(self.g_own, self.g.at[rows_at(self.base, self.rows)], 3)
        out_load = self.load(self.out_w, self.w_out, 4)
        down_load = self.load(self.down_w, self.w_down, 5)
        gate_load = self.load(self.gate_w, self.w_gate, 6)
        up_load = self.load(self.up_w, self.w_up, 7)
        self.tables()
        self.norm1(self.x, 0, self.base, self.rows)
        for copy in qkv_loads:
            copy.wait()
        self.qkv(self.base, self.rows)
        for c in range(CHUNKS):
            self.arrived(self.x_in.at[pl.ds(c * step, step)], c)
            self.norm1(self.x_in, c * step, self.far + c * step, step)
            self.qkv(self.far + c * step, step)
        self.store(self.h1, self.h1_to)
        self.store(self.q, self.q_to)
        self.store(self.k, self.k_to)
        self.store(self.v, self.v_to)
        self.attention(self.far)
        out_load.wait()
        for c in range(CHUNKS):
            part = pl.ds(c * step, step)
            self.project(self.far + c * step, self.sent_part, c * step, step)
            self.across(self.sent_part.at[part], self.got_part.at[part], CHUNKS + c)
        self.attention(self.base)
        self.store(self.o, self.o_to)
        self.project(self.base, self.own_part, 0, self.rows)
        g_load.wait()
        down_load.wait()
        self.hidden_grad(self.base, self.rows)
        self.arrived(self.g.at[rows_at(self.far, self.rows)], 2 * CHUNKS)
        self.store(self.g, self.g_to)
        self.hidden_grad(self.far, self.rows)
        self.squares[...] = jnp.zeros_like(self.squares)
        for c in range(CHUNKS):
            self.arrived(self.got_part.at[pl.ds(c * step, step)], CHUNKS + c)
            self.norm2(c * step)
            mine = self.h2.at[rows_at(self.base + c * step, step)]
            self.across(mine, mine, 2 * CHUNKS + 1 + c)
        self.store(self.x1, self.x1_to)
        self.attn_squares[...] = jnp.sum(self.squares[...], axis=0, keepdims=True)
        gate_load.wait()
        up_load.wait()
        self.feed(self.base, self.rows)
        self.store_rows(self.base, self.rows)
        for c in range(CHUNKS):
            self.arrived(self.h2.at[rows_at(self.far + c * step, step)], 2 * CHUNKS + 1 + c)
            self.feed(self.far + c * step, step)
            self.store_rows(self.far + c * step, step)
        for when, wait in self.m.left:
            guarded(when, wait)

    def tables(self):
        total = self.starts.shape[0]
        row = lax.broadcasted_iota(jnp.int32, (total, 1), 0)
        first = jnp.zeros((total, 1), jnp.int32)
        end = jnp.int32(0)
        for j in range(self.lengths.shape[1]):
            first = jnp.where(row >= end, end, first)
            end = end + self.lengths[0, j]
        self.starts[...] = first
        angles = (row - first).astype(jnp.float32) * self.inverse[...]
        self.cosines[...] = jnp.cos(angles)
        half = lax.broadcasted_iota(jnp.int32, (total, HD), 1) < HD // 2
        sines = jnp.sin(angles)
        self.sines[...] = jnp.where(half, sines, -sines)

    def norm1(self, source, source_row, row, count):
        def body(i, step):
            x = source[rows_at(source_row + i, step), :].astype(jnp.float32)
            self.h1[rows_at(row + i, step), :] = (x * row_scale(x) * self.gain1[...].reshape(1, -1)).astype(jnp.bfloat16)

        self.tiles(0, count, 32, body)

    def qkv(self, row, count):
        here = rows_at(row, count)
        values = self.h1[here, :]
        for part in range(3):
            cut = slice(part * 512, (part + 1) * 512)
            self.lin[0:count, cut] = product(values, self.w_qkv[:, cut])
        cosines, sines = self.cosines[here, :], -self.sines[here, :]
        for target, first in ((self.q, 0), (self.k, 768)):
            for head in range(target.shape[1] // HD):
                linear = self.lin[0:count, first + head * HD : first + (head + 1) * HD]
                turned = turn_back(linear, cosines, sines)
                target[here, head * HD : (head + 1) * HD] = turned.astype(jnp.bfloat16)
        self.v[here, :] = self.lin[0:count, 1152:1536].astype(jnp.bfloat16)

    def attention(self, row):
        count, total = self.rows, self.q.shape[0]
        here = rows_at(row, count)
        column = lax.broadcasted_iota(jnp.int32, (count, total), 1)
        own = lax.broadcasted_iota(jnp.int32, (count, total), 0) + row
        allowed = (column <= own) & (column >= self.starts[here, :])
        for key_head in range(self.k.shape[1] // HD):
            c = key_head * HD
            keys, values = self.k[:, c : c + HD], self.v[:, c : c + HD]
            for head in (2 * key_head, 2 * key_head + 1):
                h = head * HD
                raw = nt(self.q[here, h : h + HD], keys) * HD ** (-0.5)
                masked = jnp.where(allowed, raw, masked_score)
                exponent = jnp.exp(masked - jnp.max(masked, axis=1, keepdims=True))
                weights = exponent / jnp.sum(exponent, axis=1, keepdims=True)
                out = product(weights.astype(jnp.bfloat16), values)
                self.o[here, h : h + HD] = out.astype(jnp.bfloat16)

    def project(self, row, target, target_row, count):
        values = self.o[rows_at(row, count), :]
        for part in range(3):
            cut = slice(part * 512, (part + 1) * 512)
            target[target_row : target_row + count, cut] = product(values, self.w_out[:, cut]).astype(target.dtype)

    def hidden_grad(self, row, count):
        here = rows_at(row, count)

        def body(i, _):
            cut = pl.ds(pl.multiple_of(i * 256, 256), 256)
            self.d_hid[here, cut] = nt(self.g[here, :], self.w_down[cut, :])
            return 0

        lax.fori_loop(0, self.w_down.shape[0] // 256, body, 0)

    def norm2(self, start):
        def body(i, step):
            here = rows_at(i, step)
            attn = self.own_part[here, :] + self.got_part[here, :].astype(jnp.float32)
            self.squares[...] += eight(attn * attn)
            x1 = self.x[here, :].astype(jnp.float32) + attn
            self.x1[here, :] = x1
            self.h2[rows_at(self.base + i, step), :] = (x1 * row_scale(x1) * self.gain2[...].reshape(1, -1)).astype(jnp.bfloat16)

        self.tiles(start, self.step, 16, body)

    def feed(self, row, count):
        here = rows_at(row, count)

        def body(i, _):
            cut = pl.ds(pl.multiple_of(i * 256, 256), 256)
            values = self.h2[here, :]
            gate = product(values, self.w_gate[:, cut])
            up = product(values, self.w_up[:, cut])
            d_hid = self.d_hid[here, cut]
            sig = 1.0 / (1.0 + jnp.exp(-gate))
            self.hid[here, cut] = (gate * sig * up).astype(jnp.bfloat16)
            self.d_gate[here, cut] = (d_hid * up * sig * (1.0 + gate * (1.0 - sig))).astype(jnp.bfloat16)
            self.d_up[here, cut] = (d_hid * gate * sig).astype(jnp.bfloat16)
            return 0

        lax.fori_loop(0, self.w_gate.shape[1] // 256, body, 0)


def forward_kernel(*refs):
    names = FORWARD_INPUTS + FORWARD_RESULTS + FORWARD_PLAIN
    Forward(dict(zip(names, refs))).run()


def forward(**given):
    vmem = pl.BlockSpec(memory_space=pltpu.VMEM)
    hbm = pl.BlockSpec(memory_space=pl.ANY)
    smem = pl.BlockSpec(memory_space=pltpu.SMEM)
    low, full = jnp.bfloat16, jnp.float32
    own, width = given["x"].shape
    total = 2 * own
    units = given["gate_w"].shape[1]
    q_cols, k_cols = given["q_w"].shape[1], given["k_w"].shape[1]
    shapes = dict(
        hid_to=((total, units), low), g_to=((total, width), low), h2_to=((total, width), low),
        d_gate_to=((total, units), low), d_up_to=((total, units), low), o_to=((total, q_cols), low),
        h1_to=((total, width), low), q_to=((total, q_cols), low), k_to=((total, k_cols), low),
        v_to=((total, k_cols), low), x1_to=((own, width), full), cosines=((total, HD), full), sines=((total, HD), full),
        starts=((total, 1), jnp.int32), attn_squares=((1, width), full),
    )
    plain = dict(
        x_in=((own, width), low), w_qkv=((width, q_cols + 2 * k_cols), low), w_out=((q_cols, width), low),
        w_gate=((width, units), low), w_up=((width, units), low), w_down=((units, width), low),
        g=((total, width), low), h1=((total, width), low), lin=((own, q_cols + 2 * k_cols), full),
        q=((total, q_cols), low), k=((total, k_cols), low), v=((total, k_cols), low), o=((total, q_cols), low),
        own_part=((own, width), full), sent_part=((own, width), low), got_part=((own, width), low),
        x1=((own, width), full), h2=((total, width), low), d_hid=((total, units), full), hid=((total, units), low),
        d_gate=((total, units), low), d_up=((total, units), low), squares=((8, width), full),
    )
    scratch = [pltpu.VMEM(*plain[name]) for name in FORWARD_PLAIN if name in plain]
    copies = 3 * CHUNKS + 1
    scratch += [pltpu.SemaphoreType.DMA((n,)) for n in (copies, copies, 8, 24)]
    spaces = dict.fromkeys(("q_w", "k_w", "v_w", "out_w", "gate_w", "up_w", "down_w", "g_own"), hbm)
    spaces["lengths"] = smem
    out = pl.pallas_call(
        forward_kernel,
        out_shape=[jax.ShapeDtypeStruct(*shapes[name]) for name in FORWARD_RESULTS],
        in_specs=[spaces.get(name, vmem) for name in FORWARD_INPUTS],
        out_specs=[hbm if name.endswith("_to") else vmem for name in FORWARD_RESULTS],
        scratch_shapes=scratch,
        compiler_params=pltpu.CompilerParams(
            collective_id=1, has_side_effects=True, vmem_limit_bytes=62 << 20
        ),
        cost_estimate=pl.CostEstimate(flops=26 * 10**9, bytes_accessed=60 << 20, transcendentals=0),
        name="forward",
    )(*(given[name] for name in FORWARD_INPUTS))
    return dict(zip(FORWARD_RESULTS, out))


def results_kernel(
    down, gate, up, o, qkv, tokens_in, layer_in, small,
    layer_out, tokens_out, gain1_out, q_out, k_out, v_out, o_out, gain2_out, gate_out, up_out, down_out, rms_out,
    taken, made, tokens_held, layer_held, in_sems, out_sems, whole_sems, *, tokens,
):
    held = ((tokens_in, tokens_held, tokens_out), (layer_in, layer_held, layer_out))
    inward = [pltpu.make_async_copy(a, b, whole_sems.at[i]) for i, (a, b, _) in enumerate(held)]
    outward = [pltpu.make_async_copy(b, c, whole_sems.at[i]) for i, (_, b, c) in enumerate(held)]
    for copy in inward:
        copy.start()
    q_cols, k_cols = q_out.shape[1], k_out.shape[1]
    tile = taken.shape[1]
    work = []
    for source, targets in (
        (down, ((down_out, 0),)),
        (gate, ((gate_out, 0),)),
        (up, ((up_out, 0),)),
        (qkv, ((q_out, 0), (k_out, q_cols), (v_out, q_cols + k_cols))),
        (o, ((o_out, 0),)),
    ):
        work += [(source, targets, row) for row in range(0, source.shape[0], tile)]
    slots = taken.shape[0]

    def take(i):
        source, _, row = work[i]
        return pltpu.make_async_copy(
            source.at[pl.ds(row, tile)], taken.at[i % slots, :, pl.ds(0, source.shape[1])], in_sems.at[i % slots]
        )

    def give(i):
        _, targets, row = work[i]
        return [
            pltpu.make_async_copy(
                made.at[i % slots, :, pl.ds(first, target.shape[1])],
                target.at[pl.ds(row, tile)],
                out_sems.at[i % slots, j],
            )
            for j, (target, first) in enumerate(targets)
        ]

    for i in range(min(slots - 1, len(work))):
        take(i).start()
    for i in range(len(work)):
        if i + slots - 1 < len(work):
            take(i + slots - 1).start()
        take(i).wait()
        if i >= slots:
            for copy in give(i - slots):
                copy.wait()
        columns = work[i][0].shape[1]

        def one(j, _, slot=i % slots, columns=columns):
            here = rows_at(j * 32, 32)
            made[slot, here, 0:columns] = taken[slot, here, 0:columns].astype(jnp.float32)
            return 0

        lax.fori_loop(0, tile // 32, one, 0)
        for copy in give(i):
            copy.start()
    for i in range(2):
        inward[i].wait()
        outward[i].start()
    gain1_out[...] = small[0, :]
    gain2_out[...] = small[1, :]
    lane = lax.broadcasted_iota(jnp.int32, (1, 3), 1)
    sums = [jnp.sum(small[row : row + 1, :], axis=1, keepdims=True) for row in (2, 4, 3)]
    squares = jnp.where(lane == 0, sums[0], jnp.where(lane == 1, sums[1], sums[2]))
    rms_out[...] = jnp.sqrt(squares / tokens)
    for i in range(max(0, len(work) - slots), len(work)):
        for copy in give(i):
            copy.wait()
    for copy in outward:
        copy.wait()


def results(sums, tokens_grad, layer_out, small, q_cols, k_cols, tokens):
    vmem = pl.BlockSpec(memory_space=pltpu.VMEM)
    hbm = pl.BlockSpec(memory_space=pl.ANY)
    full = jnp.float32
    down, gate, up, o, qkv = sums
    width = small.shape[1]
    rows = qkv.shape[0]
    shapes = (
        (layer_out.shape, layer_out.dtype, hbm), (tokens_grad.shape, full, hbm), ((width,), full, vmem),
        ((rows, q_cols), full, hbm), ((rows, k_cols), full, hbm), ((rows, k_cols), full, hbm),
        (o.shape, full, hbm), ((width,), full, vmem), (gate.shape, full, hbm), (up.shape, full, hbm),
        (down.shape, full, hbm), ((1, 3), full, vmem),
    )
    slots, tile = 12, 256
    columns = max(part.shape[1] for part in sums)
    out = pl.pallas_call(
        partial(results_kernel, tokens=tokens),
        out_shape=[jax.ShapeDtypeStruct(shape, dtype) for shape, dtype, _ in shapes],
        in_specs=[hbm] * 7 + [vmem],
        out_specs=[space for _, _, space in shapes],
        scratch_shapes=[
            pltpu.VMEM((slots, tile, columns), jnp.bfloat16),
            pltpu.VMEM((slots, tile, columns), full),
            pltpu.VMEM(tokens_grad.shape, full),
            pltpu.VMEM(layer_out.shape, layer_out.dtype),
            pltpu.SemaphoreType.DMA((slots,)),
            pltpu.SemaphoreType.DMA((slots, 3)),
            pltpu.SemaphoreType.DMA((2,)),
        ],
        compiler_params=pltpu.CompilerParams(vmem_limit_bytes=62 << 20),
        cost_estimate=pl.CostEstimate(flops=0, bytes_accessed=78 * 10**6, transcendentals=0),
        name="results",
    )(*sums, tokens_grad, layer_out, small)
    return tuple(part.reshape(-1) if part.shape[0] == 1 else part for part in out)


def dp_sum(terms):
    low = lax.psum(tuple(term.astype(jnp.bfloat16) for term in terms), "dp")
    return tuple(term.astype(jnp.float32) for term in low)


def low_scatter(partial):
    return lax.psum_scatter(
        partial.astype(jnp.bfloat16), "tensor", scatter_dimension=0, tiled=True
    ).astype(jnp.float32)


def body(
    tokens,
    lengths,
    first_gain,
    query_weight,
    key_weight,
    value_weight,
    output_weight,
    second_gain,
    gate_weight,
    up_weight,
    down_weight,
    out_cotangent,
):
    inputs = tokens.astype(jnp.float32)
    normed1, inv_first = norm_rows(inputs, first_gain)
    normed1 = normed1.astype(jnp.bfloat16)
    full_first = lax.all_gather(normed1, "tensor", axis=0, tiled=True)
    total_rows = full_first.shape[0]
    places, segment, cosine_table, sine_table = tables(lengths[0], total_rows, HD // 2)
    kv_heads = key_weight.shape[1] // HD
    groups = query_weight.shape[1] // key_weight.shape[1]
    query = rotate(product(full_first, query_weight), cosine_table, sine_table, 1.0).astype(
        jnp.bfloat16
    )
    keys = rotate(product(full_first, key_weight), cosine_table, sine_table, 1.0).astype(
        jnp.bfloat16
    )
    values = product(full_first, value_weight).astype(jnp.bfloat16)
    block_rows = min(block_limit, total_rows)
    block_count = total_rows // block_rows
    query_blocks = query.reshape(block_count, block_rows, kv_heads, groups, HD)
    seg_blocks = segment.reshape(block_count, block_rows)
    place_blocks = places.reshape(block_count, block_rows)
    key_three = keys.reshape(total_rows, kv_heads, HD)
    value_three = values.reshape(total_rows, kv_heads, HD)
    factor = HD ** (-0.5)

    def scores(query_block, seg_block, place_block):
        raw = (
            jnp.einsum("qcgd,kcd->cgqk", query_block, key_three, preferred_element_type=jnp.float32)
            * factor
        )
        allowed = (seg_block[:, None] == segment[None, :]) & (
            place_block[:, None] >= places[None, :]
        )
        return (jnp.where(allowed[None, None], raw, masked_score), allowed)

    def forward_block(piece_set):
        query_block, seg_block, place_block = piece_set
        masked, allowed = scores(query_block, seg_block, place_block)
        highest = jnp.max(masked, axis=-1, keepdims=True)
        exponent = jnp.exp(masked - highest)
        denominator = jnp.sum(exponent, axis=-1, keepdims=True)
        weights = exponent / denominator
        output = jnp.einsum(
            "cgqk,kcd->qcgd",
            weights.astype(jnp.bfloat16),
            value_three,
            preferred_element_type=jnp.float32,
        )
        stored = (highest + jnp.log(denominator))[..., 0]
        return (output.reshape(block_rows, -1), stored)

    out_blocks, kept_blocks = lax.map(forward_block, (query_blocks, seg_blocks, place_blocks))
    attended = out_blocks.reshape(total_rows, -1).astype(jnp.bfloat16)
    attn_rows = low_scatter(product(attended, output_weight))
    middle = inputs + attn_rows
    normed2, inv_second = norm_rows(middle, second_gain)
    normed2 = normed2.astype(jnp.bfloat16)
    full_second = lax.all_gather(normed2, "tensor", axis=0, tiled=True)
    gate_value = product(full_second, gate_weight)
    upward = product(full_second, up_weight)
    gate_sig = jax.nn.sigmoid(gate_value)
    hidden = (gate_value * gate_sig * upward).astype(jnp.bfloat16)
    mlp_rows = low_scatter(product(hidden, down_weight))
    layer_out = middle + mlp_rows
    squares = jnp.stack(
        [
            jnp.sum(layer_out * layer_out),
            jnp.sum(attn_rows * attn_rows),
            jnp.sum(mlp_rows * mlp_rows),
        ]
    )
    grad_full = lax.all_gather(out_cotangent, "tensor", axis=0, tiled=True)
    grad_hidden = times_cols(grad_full, down_weight)
    down_g = times_rows(hidden, grad_full)
    gate_slope = gate_sig * (1.0 + gate_value * (1.0 - gate_sig))
    grad_gate = (grad_hidden * upward * gate_slope).astype(jnp.bfloat16)
    grad_up = (grad_hidden * gate_value * gate_sig).astype(jnp.bfloat16)
    gate_g = times_rows(full_second, grad_gate)
    up_g = times_rows(full_second, grad_up)
    gate_g, up_g, down_g = dp_sum((gate_g, up_g, down_g))
    grad_normed2 = low_scatter(
        times_cols(grad_gate, gate_weight) + times_cols(grad_up, up_weight)
    )
    second_rows, grad_mid_norm = norm_back(middle, inv_second, second_gain, grad_normed2)
    grad_middle = out_cotangent.astype(jnp.float32) + grad_mid_norm
    grad_attn_full = lax.all_gather(grad_middle.astype(jnp.bfloat16), "tensor", axis=0, tiled=True)
    output_g = times_rows(attended, grad_attn_full)
    grad_out = times_cols(grad_attn_full, output_weight).astype(jnp.bfloat16)
    grad_blocks = grad_out.reshape(block_count, block_rows, kv_heads, groups, HD)

    def backward_block(running, piece_set):
        key_acc, value_acc = running
        query_block, seg_block, place_block, grad_block, stored = piece_set
        masked, allowed = scores(query_block, seg_block, place_block)
        weights = jnp.where(allowed[None, None], jnp.exp(masked - stored[..., None]), 0.0)
        grad_weights = jnp.einsum(
            "qcgd,kcd->cgqk", grad_block, value_three, preferred_element_type=jnp.float32
        )
        row_inner = jnp.sum(weights * grad_weights, axis=-1, keepdims=True)
        grad_scores = (weights * (grad_weights - row_inner)).astype(jnp.bfloat16)
        grad_query = (
            jnp.einsum("cgqk,kcd->qcgd", grad_scores, key_three, preferred_element_type=jnp.float32)
            * factor
        )
        key_acc = (
            key_acc
            + jnp.einsum(
                "cgqk,qcgd->kcd", grad_scores, query_block, preferred_element_type=jnp.float32
            )
            * factor
        )
        value_acc = value_acc + jnp.einsum(
            "cgqk,qcgd->kcd",
            weights.astype(jnp.bfloat16),
            grad_block,
            preferred_element_type=jnp.float32,
        )
        return ((key_acc, value_acc), grad_query.reshape(block_rows, -1))

    zeros_kv = jnp.zeros((total_rows, kv_heads, HD), jnp.float32)
    (key_rot_grad, value_acc_grad), query_rot_grad = lax.scan(
        backward_block,
        (zeros_kv, zeros_kv),
        (query_blocks, seg_blocks, place_blocks, grad_blocks, kept_blocks),
    )
    query_lin = rotate(
        query_rot_grad.reshape(total_rows, -1), cosine_table, sine_table, -1.0
    ).astype(jnp.bfloat16)
    key_lin = rotate(key_rot_grad.reshape(total_rows, -1), cosine_table, sine_table, -1.0).astype(
        jnp.bfloat16
    )
    value_lin = value_acc_grad.reshape(total_rows, -1).astype(jnp.bfloat16)
    query_g = times_rows(full_first, query_lin)
    key_g = times_rows(full_first, key_lin)
    value_g = times_rows(full_first, value_lin)
    grad_normed1 = low_scatter(
        times_cols(query_lin, query_weight)
        + times_cols(key_lin, key_weight)
        + times_cols(value_lin, value_weight)
    )
    first_rows, grad_in_norm = norm_back(inputs, inv_first, first_gain, grad_normed1)
    tokens_grad = grad_middle + grad_in_norm
    gain_rows = jnp.stack([first_rows, second_rows])
    query_g, key_g, value_g, output_g = dp_sum((query_g, key_g, value_g, output_g))
    gain_rows, squares = lax.psum((gain_rows, squares), ("dp", "tensor"))
    rms_values = jnp.sqrt(squares / (total_rows * lax.axis_size("dp")))
    return (
        layer_out.astype(jnp.bfloat16),
        tokens_grad,
        gain_rows[0],
        query_g,
        key_g,
        value_g,
        output_g,
        gain_rows[1],
        gate_g,
        up_g,
        down_g,
        rms_values,
    )


def fused_body(
    tokens,
    lengths,
    first_gain,
    query_weight,
    key_weight,
    value_weight,
    output_weight,
    second_gain,
    gate_weight,
    up_weight,
    down_weight,
    out_cotangent,
):
    half_size = HD // 2
    inverse = (rope_base ** (-2.0 * np.arange(half_size) / (2 * half_size))).astype(np.float32)
    made = forward(
        x=tokens,
        lengths=lengths,
        gain1=first_gain,
        gain2=second_gain,
        inverse=jnp.asarray(np.concatenate([inverse, inverse])[None]),
        q_w=query_weight,
        k_w=key_weight,
        v_w=value_weight,
        out_w=output_weight,
        gate_w=gate_weight,
        up_w=up_weight,
        down_w=down_weight,
        g_own=out_cotangent,
    )
    *sums, tokens_grad, layer_out, small = backward(
        **{name + "_hbm": made[name + "_to"] for name in ("hid", "g", "h2", "d_gate", "d_up", "o", "h1")},
        **{name + "_hbm": made[name + "_to"] for name in ("q", "k", "v", "x1")},
        **{name + "_hbm": made[name] for name in ("cosines", "sines", "starts")},
        x_hbm=tokens,
        out_w=output_weight,
        q_w=query_weight,
        k_w=key_weight,
        v_w=value_weight,
        gate_w=gate_weight,
        up_w=up_weight,
        down_w=down_weight,
        gain1=first_gain,
        gain2=second_gain,
        attn_squares=made["attn_squares"],
    )
    return results(
        sums, tokens_grad, layer_out, small, query_weight.shape[1], key_weight.shape[1],
        2 * tokens.shape[0] * lax.axis_size("dp"),
    )


def solution(mesh):
    in_specs = (
        P(("dp", "tensor"), None),
        P("dp", None),
        P(),
        P(None, "tensor"),
        P(None, "tensor"),
        P(None, "tensor"),
        P("tensor", None),
        P(),
        P(None, "tensor"),
        P(None, "tensor"),
        P("tensor", None),
        P(("dp", "tensor"), None),
    )
    out_specs = (
        P(("dp", "tensor"), None),
        P(("dp", "tensor"), None),
        P(),
        P(None, "tensor"),
        P(None, "tensor"),
        P(None, "tensor"),
        P("tensor", None),
        P(),
        P(None, "tensor"),
        P(None, "tensor"),
        P("tensor", None),
        P(),
    )
    fused = dict(mesh.shape) == {"dp": 16, "tensor": 2}
    chosen = fused_body if fused else body
    return jax.shard_map(chosen, mesh=mesh, in_specs=in_specs, out_specs=out_specs, check_vma=False)
```
